32 devices in a mesh: dp: 8 (over z, y), mp: 4 (over x, core).
Axes of the slice: x: 2, y: 2, z: 4, core: 2. Of those that a mesh axis runs over, the one named last changes fastest.
Arguments:
- patches: bfloat16 [40, 198, 384], P('dp'), may hold values from -6 to 6
- targets: bfloat16 [40, 198, 384], P('dp'), may hold values from -6 to 6
- keep_mask: int32 [40, 196], P('dp'), may hold values from 0 to 1
- attn_weights: bfloat16 [2, 384, 1536], P(None, None, ('dp', 'mp')), may hold values from -0.8164966 to 0.8164966
- vectors: bfloat16 [2, 4608], P(None, ('dp', 'mp')), may hold values from -1.2 to 1.8
- up_weights: bfloat16 [2, 384, 1536], P(None, 'dp', 'mp'), may hold values from -0.3125 to 0.3125
- down_weights: bfloat16 [2, 1536, 384], P(None, 'mp', 'dp'), may hold values from -0.15625 to 0.15625
Outputs:
- activations: float32 [8192, 384], P('dp')
- input_grads: float32 [40, 198, 384], P('dp')
- attn_grads: float32 [2, 384, 1536], P(None, None, ('dp', 'mp'))
- vector_grads: float32 [2, 4608], P(None, ('dp', 'mp'))
- up_grads: float32 [2, 384, 1536], P(None, 'dp', 'mp')
- down_grads: float32 [2, 1536, 384], P(None, 'mp', 'dp')
The draws below stay inside these ranges and needn't reach their ends.
All inputs are finite; a program needn't handle non-finite values.
Results may differ from the reference program's by a relative error of at most 0.013.
Values may be sent and summed in bfloat16 or wider, within the bound.
No kernel may reach another device: no remote copies, remote signals or barrier semaphores. Data moves between devices by JAX's collectives and lax.ppermute only.
A program may use at most 128 MiB of HBM per device.

```python
import jax
import jax.numpy as jnp
from jax import lax

D = 384
HEADS = 6
HD = 64
FF = 1536
PATCHES = 196
LAYERS = 2
SLOTS = 1024
ROWS = 198
IMG_DEV = 5
IMAGES = 40
N_DP = 8


def draw_keep_mask(key, part):
    key = jax.random.fold_in(key, 11)
    codes = jax.random.randint(key, (IMAGES, PATCHES), 0, 1000)
    device_no = jnp.arange(IMAGES) // IMG_DEV
    device_count = IMAGES // IMG_DEV
    threshold = 280 + 640 * device_no // max(device_count - 1, 1)
    return (codes < threshold[:, None]).astype(jnp.int32)


def draw_attn_weights(key, part):
    key = jax.random.fold_in(key, 23)
    values = jax.random.truncated_normal(key, -4.0, 4.0, (LAYERS, D, 4 * D), jnp.float32)
    column = jnp.arange(4 * D)
    factor = jnp.where(column < 3 * D, 1.0, 4.0) * D ** (-0.5)
    return (values * factor).astype(jnp.bfloat16)


def draw_vectors(key, part):
    key = jax.random.fold_in(key, 37)
    values = jax.random.truncated_normal(key, -4.0, 4.0, (LAYERS, 8 * D + FF), jnp.float32)
    column = jnp.arange(8 * D + FF)
    is_gain = (column < D) | (column >= 2 * D) & (column < 3 * D)
    return jnp.where(is_gain, 1.0 + 0.2 * values, 0.3 * values).astype(jnp.bfloat16)


def block_levels(stream_key, shape, shards, least, high):
    loudness = 1.0
    for axis_at, parts in shards:
        draws = jax.random.uniform(jax.random.fold_in(jax.random.fold_in(stream_key, 6), axis_at), (parts,), jnp.float32, least / len(shards), high / len(shards))
        loudness = loudness * jnp.repeat(jnp.exp(draws), shape[axis_at] // parts).reshape((-1,) + (1,) * (len(shape) - 1 - axis_at))
    return loudness


def scatter_about(rng, extent, scale, bound, cuts=(), kind=jnp.bfloat16):
    values = jax.random.normal(rng, extent, jnp.float32) * scale
    if len(cuts) > 0:
        values = block_levels(rng, extent, cuts, -0.22, 0.18) * values
    return jnp.clip(values, min=-bound, max=bound).astype(kind)


def setup_inputs(seed: int = 0) -> dict:
    seeds = jax.random.split(jax.random.key(seed), 8)
    return {
        "patches": scatter_about(seeds[0], (IMAGES, ROWS, D), 1.0, 6.0, ((0, 8),)),
        "targets": scatter_about(seeds[1], (IMAGES, ROWS, D), 1.0, 6.0, ((0, 8),)),
        "keep_mask": draw_keep_mask(jax.random.fold_in(seeds[7], 71), 0),
        "attn_weights": draw_attn_weights(jax.random.fold_in(seeds[7], 71), 0),
        "vectors": draw_vectors(jax.random.fold_in(seeds[7], 71), 0),
        "up_weights": scatter_about(seeds[5], (LAYERS, D, FF), D ** -0.5, 0.3125, ((1, 8), (2, 4))),
        "down_weights": scatter_about(seeds[6], (LAYERS, FF, D), FF ** -0.5, 0.15625, ((1, 4), (2, 8))),
    }


@jax.custom_vjp
def low(v):
    return lax.optimization_barrier(v.astype(jnp.bfloat16)).astype(jnp.float32)

@jax.custom_vjp
def low_back(v):
    return v

def low_keep(v):
    return (low(v), None)

def low_pass(kept, grad):
    return (grad,)

def back_keep(v):
    return (v, None)

def back_low(kept, grad):
    return (low(grad),)
low.defvjp(low_keep, low_pass)
low_back.defvjp(back_keep, back_low)
HIGHEST = lax.Precision.HIGHEST
EPSILON = 1e-06

def matmul(left, right):
    return jnp.dot(left, right, precision=HIGHEST, preferred_element_type=jnp.float32)

def layer_norm(values, gain_vec, shift_vec):
    centred = values - lax.optimization_barrier(jnp.mean(values, axis=-1, keepdims=True))
    variance = lax.optimization_barrier(jnp.mean(centred * centred, axis=-1, keepdims=True))
    return centred * lax.rsqrt(variance + EPSILON) * gain_vec + shift_vec

def pack_rows(keep_mask, slot_count):
    image_count, patch_count = keep_mask.shape
    row_keep = jnp.concatenate([jnp.ones((image_count, 2), jnp.int32), keep_mask.astype(jnp.int32)], axis=1).reshape(-1)
    position = jnp.cumsum(row_keep) - row_keep
    target_slot = jnp.where(row_keep == 1, position, slot_count).astype(jnp.int32)
    row_count = row_keep.shape[0]
    row_ids = jnp.arange(row_count, dtype=jnp.int32)
    source = jnp.zeros((slot_count,), jnp.int32).at[target_slot].set(row_ids, mode='drop')
    image_of = row_ids // (patch_count + 2)
    segment = jnp.full((slot_count,), -1, jnp.int32).at[target_slot].set(image_of, mode='drop')
    live_count = jnp.sum(row_keep)
    live_slot = jnp.arange(slot_count, dtype=jnp.int32) < live_count
    return (row_keep, target_slot, source, segment, live_slot, live_count)

def attend_block(query_block, seg_block, key_rows, value_rows, segment):
    scores = low_back(jnp.einsum('qhd,khd->hqk', query_block, key_rows, precision=HIGHEST) * HD ** (-0.5))
    scores = jnp.where(seg_block[None, :, None] == segment[None, None, :], scores, -1e+30)
    row_top = lax.optimization_barrier(jnp.max(scores, axis=-1, keepdims=True))
    exp_scores = jnp.exp(scores - row_top)
    soft_probs = exp_scores / lax.optimization_barrier(jnp.sum(exp_scores, axis=-1, keepdims=True))
    return jnp.einsum('hqk,khd->qhd', low(soft_probs), value_rows, precision=HIGHEST)

def forward(stream, attn_weights, vectors, up_weights, down_weights, segment):
    block_rows = min(512, SLOTS)
    checked = jax.checkpoint(attend_block)
    seg_blocks = segment.reshape(SLOTS // block_rows, block_rows)
    for layer_no in range(LAYERS):
        attn_mat = attn_weights[layer_no]
        params = vectors[layer_no]
        normed_one = low(layer_norm(stream, params[0:D], params[D:2 * D]))
        qkv_bias = jnp.concatenate([params[4 * D:5 * D], jnp.zeros((D,), jnp.float32), params[5 * D:6 * D]])
        project = low(low_back(matmul(normed_one, attn_mat[:, :3 * D]) + qkv_bias))
        queries = project[:, :D].reshape(SLOTS // block_rows, block_rows, HEADS, HD)
        key_rows = project[:, D:2 * D].reshape(SLOTS, HEADS, HD)
        value_rows = project[:, 2 * D:].reshape(SLOTS, HEADS, HD)

        def run_block(block_pair):
            return checked(block_pair[0], block_pair[1], key_rows, value_rows, segment)
        mixed_rows = lax.map(run_block, (queries, seg_blocks)).reshape(SLOTS, D)
        attended = low(low_back(mixed_rows))
        stream = stream + low_back(matmul(attended, attn_mat[:, 3 * D:])) + params[6 * D:7 * D]
        normed_two = low(layer_norm(stream, params[2 * D:3 * D], params[3 * D:4 * D]))
        hidden = low_back(matmul(normed_two, up_weights[layer_no]) + params[7 * D:7 * D + FF])
        activated = low(jax.nn.gelu(hidden, approximate=False))
        stream = stream + low_back(matmul(activated, down_weights[layer_no])) + params[7 * D + FF:]
    return stream

def reference(patches, targets, keep_mask, attn_weights, vectors, up_weights, down_weights):
    kept_total = jnp.sum(keep_mask).astype(jnp.float32) + 2.0 * IMAGES
    loss_scale = SLOTS * N_DP / kept_total
    attn_full = attn_weights.astype(jnp.float32)
    vector_full = vectors.astype(jnp.float32)
    up_full = up_weights.astype(jnp.float32)
    down_full = down_weights.astype(jnp.float32)
    patch_packs = patches.reshape(N_DP, IMG_DEV * ROWS, D)
    goal_packs = targets.reshape(N_DP, IMG_DEV * ROWS, D)
    keep_packs = keep_mask.reshape(N_DP, IMG_DEV, PATCHES)

    def one_pack(totals, pack_data):
        rows_in, goal_in, keep_in = pack_data
        row_keep, target_slot, source, segment, live_slot, live_count = pack_rows(keep_in, SLOTS)
        live_col = live_slot[:, None]
        stream_in = jnp.where(live_col, rows_in[source].astype(jnp.float32), 0.0)
        goal_rows = jnp.where(live_col, goal_in[source].astype(jnp.float32), 0.0) * loss_scale

        def run_layers(stream_arg, attn_arg, vector_arg, up_arg, down_arg):
            return forward(stream_arg, attn_arg, vector_arg, up_arg, down_arg, segment)
        output, pull_back = jax.vjp(run_layers, stream_in, attn_full, vector_full, up_full, down_full)
        gradients = pull_back(goal_rows)
        kept_col = row_keep[:, None] == 1
        input_rows = jnp.where(kept_col, gradients[0][jnp.minimum(target_slot, SLOTS - 1)], 0.0)
        totals = tuple((before + after for before, after in zip(totals, gradients[1:])))
        return (totals, (jnp.where(live_col, output, 0.0), input_rows))
    zero_totals = (jnp.zeros_like(attn_full), jnp.zeros_like(vector_full), jnp.zeros_like(up_full), jnp.zeros_like(down_full))
    totals, (outputs, input_rows) = lax.scan(one_pack, zero_totals, (patch_packs, goal_packs, keep_packs))
    return (outputs.reshape(SLOTS * N_DP, D), input_rows.reshape(IMAGES, ROWS, D), totals[0], totals[1], totals[2], totals[3])
```

```python
import functools

import jax
import jax.numpy as jnp
from jax import lax
from jax.experimental import pallas as pl
from jax.experimental.pallas import tpu as pltpu
from jax.sharding import PartitionSpec as P

HD = 64
SLOTS = 1024
EPSILON = 1e-06
MASKED = -1e30
STEP = 16

F32 = jnp.float32
BF16 = jnp.bfloat16


def dot_nn(left, right):
    return lax.dot_general(left, right, (((1,), (0,)), ((), ())), preferred_element_type=F32)


def dot_nt(left, right):
    return lax.dot_general(left, right, (((1,), (1,)), ((), ())), preferred_element_type=F32)


def dot_tn(left, right):
    return lax.dot_general(left, right, (((0,), (0,)), ((), ())), preferred_element_type=F32)


def block_rows(index, step):
    return pl.ds(pl.multiple_of(index * step, step), step)


def fold_rows(values):
    return jnp.sum(values.reshape(values.shape[0] // 8, 8, values.shape[1]), axis=0)


def low_halves(rows):
    lane = lax.broadcasted_iota(jnp.int32, (rows, 2 * HD), 1)
    return lane < HD


def stack_heads(pair):
    low = low_halves(pair.shape[0])
    zero = jnp.zeros_like(pair)
    return jnp.concatenate([jnp.where(low, pair, zero), jnp.where(low, zero, pair)], axis=0)


def unstack_heads(stacked):
    rows = stacked.shape[0] // 2
    return jnp.where(low_halves(rows), stacked[:rows], stacked[rows:])


def norm_rows(x_ref, out_ref, gain, shift):
    def body(index, carry):
        at = block_rows(index, STEP)
        values = x_ref[at, :]
        centred = values - jnp.mean(values, axis=-1, keepdims=True)
        variance = jnp.mean(centred * centred, axis=-1, keepdims=True)
        out_ref[at, :] = (centred * lax.rsqrt(variance + EPSILON) * gain + shift).astype(BF16)
        return carry

    lax.fori_loop(0, x_ref.shape[0] // STEP, body, 0)


def norm_back(x_ref, grad_ref, base_ref, out_ref, low_ref, gain, images):
    rows = x_ref.shape[0] // images
    width = x_ref.shape[1]
    sums = []
    for image in range(images):

        def body(index, carry, image=image):
            at = pl.ds(pl.multiple_of(image * rows + index * STEP, STEP), STEP)
            values = x_ref[at, :]
            grad = grad_ref[at, :]
            centred = values - jnp.mean(values, axis=-1, keepdims=True)
            variance = jnp.mean(centred * centred, axis=-1, keepdims=True)
            inverse = lax.rsqrt(variance + EPSILON)
            unit = centred * inverse
            scaled = grad * gain
            mean_one = jnp.mean(scaled, axis=-1, keepdims=True)
            mean_two = jnp.mean(scaled * unit, axis=-1, keepdims=True)
            out = base_ref[at, :] + inverse * (scaled - mean_one - unit * mean_two)
            out_ref[at, :] = out
            if low_ref is not None:
                low_ref[at, :] = out.astype(BF16)
            return (
                carry[0] + fold_rows(grad * unit),
                carry[1] + fold_rows(grad),
                carry[2] + fold_rows(out),
            )

        zero = jnp.zeros((8, width), F32)
        sums.append(lax.fori_loop(0, rows // STEP, body, (zero, zero, zero)))
    return sums


def weigh(sums, share):
    total = sums[0]
    for more in sums[1:]:
        total = total + more * share
    return jnp.sum(total, axis=0, keepdims=True)


def forward_layer(x_ref, bias_ref, vec_ref, attn_ref, up_ref, down_ref, keep, scratch, out_ref):
    n1_ref, proj_ref, p_ref, att_ref, mid_ref, n2_ref, a_ref, gp_ref = keep
    (h_ref,) = scratch
    images = bias_ref.shape[0]
    rows = x_ref.shape[0] // images
    width = x_ref.shape[1]
    pairs = width // (2 * HD)
    scale = HD**-0.5

    norm_rows(x_ref, n1_ref, vec_ref[0:1, :], vec_ref[1:2, :])
    for part, bias_row in enumerate((4, None, 5)):
        value = dot_nt(n1_ref[...], attn_ref[part])
        if bias_row is not None:
            value = value + vec_ref[bias_row : bias_row + 1, :]
        proj_ref[part] = value.astype(BF16)

    def image_body(image, carry):
        at = block_rows(image, rows)
        for pair in range(pairs):
            lanes = slice(pair * 2 * HD, (pair + 1) * 2 * HD)
            query = stack_heads(proj_ref[0, at, lanes])
            scores = dot_nt(query, proj_ref[1, at, lanes]) * scale + bias_ref[image]
            top = jnp.max(scores, axis=-1, keepdims=True)
            powers = jnp.exp(scores - top)
            total = jnp.sum(powers, axis=-1, keepdims=True)
            probs = (powers * (1.0 / total)).astype(BF16)
            p_ref[image, pair] = probs
            att_ref[at, lanes] = unstack_heads(dot_nn(probs, proj_ref[2, at, lanes])).astype(BF16)
        return carry

    lax.fori_loop(0, images, image_body, 0)
    mid_ref[...] = x_ref[...] + dot_nt(att_ref[...], attn_ref[3]) + vec_ref[6:7, :]
    norm_rows(mid_ref, n2_ref, vec_ref[2:3, :], vec_ref[3:4, :])
    out_ref[...] = mid_ref[...] + vec_ref[11:12, :]

    def part_body(part, carry):
        h_ref[...] = dot_nn(n2_ref[...], up_ref[part])
        bias = vec_ref[pl.ds(7 + part, 1), :]

        def gelu_body(index, inner):
            at = block_rows(index, STEP)
            hidden = h_ref[at, :] + bias
            share = 0.5 + 0.5 * lax.erf(hidden * 0.7071067811865476)
            a_ref[part, at, :] = (hidden * share).astype(BF16)
            bell = jnp.exp(-0.5 * hidden * hidden) * 0.3989422804014327
            gp_ref[part, at, :] = (share + hidden * bell).astype(gp_ref.dtype)
            return inner

        lax.fori_loop(0, h_ref.shape[0] // STEP, gelu_body, 0)
        out_ref[...] += dot_nt(a_ref[part], down_ref[part])
        return carry

    lax.fori_loop(0, up_ref.shape[0], part_body, 0)


def drop_shared(flag_ref, keep, images):
    n1_ref, proj_ref, p_ref, att_ref, mid_ref, n2_ref, a_ref, gp_ref = keep

    @pl.when(flag_ref[0] == 0)
    def _():
        rows = n1_ref.shape[0] // images
        at = slice(rows, images * rows)
        for ref in (n1_ref, att_ref, n2_ref):
            ref[at, :] = jnp.zeros((rows * (images - 1), ref.shape[1]), BF16)
        a_ref[:, at, :] = jnp.zeros((a_ref.shape[0], rows * (images - 1), a_ref.shape[2]), BF16)


def backward_layer(
    g_ref, x_ref, vec_ref, attn_ref, up_ref, down_ref, flag_ref, keep, scratch, outs
):
    n1_ref, proj_ref, p_ref, att_ref, mid_ref, n2_ref, a_ref, gp_ref = keep
    go_ref, gh_ref, acc_ref, h_ref, gm_ref, ga_ref, dproj_ref = scratch
    gx_ref, gattn_ref, gup_ref, gdown_ref, gvec_ref = outs
    images = p_ref.shape[0]
    rows = x_ref.shape[0] // images
    width = x_ref.shape[1]
    pairs = width // (2 * HD)
    scale = HD**-0.5
    share = flag_ref[0].astype(F32)

    sums = []
    for image in range(images):

        def low_body(index, carry, image=image):
            at = pl.ds(pl.multiple_of(image * rows + index * STEP, STEP), STEP)
            grad = g_ref[at, :]
            go_ref[at, :] = grad.astype(BF16)
            return carry + fold_rows(grad)

        sums.append(lax.fori_loop(0, rows // STEP, low_body, jnp.zeros((8, width), F32)))
    gvec_ref[11:12, :] = weigh(sums, share)
    acc_ref[...] = jnp.zeros_like(acc_ref)

    def part_body(part, carry):
        gdown_ref[part] = dot_tn(go_ref[...], a_ref[part]).astype(gdown_ref.dtype)
        h_ref[...] = dot_nn(go_ref[...], down_ref[part])
        inner_sums = []
        for image in range(images):

            def hidden_body(index, inner, image=image):
                at = pl.ds(pl.multiple_of(image * rows + index * STEP, STEP), STEP)
                grad = (h_ref[at, :] * gp_ref[part, at, :].astype(F32)).astype(BF16)
                gh_ref[at, :] = grad
                return inner + fold_rows(grad.astype(F32))

            inner_sums.append(
                lax.fori_loop(0, rows // STEP, hidden_body, jnp.zeros((8, width), F32))
            )
        gvec_ref[pl.ds(7 + part, 1), :] = weigh(inner_sums, share)
        gup_ref[part] = dot_tn(n2_ref[...], gh_ref[...]).astype(gup_ref.dtype)
        acc_ref[...] += dot_nt(gh_ref[...], up_ref[part])
        return carry

    lax.fori_loop(0, up_ref.shape[0], part_body, 0)
    sums = norm_back(mid_ref, acc_ref, g_ref, gm_ref, go_ref, vec_ref[2:3, :], images)
    for place, row in enumerate((2, 3, 6)):
        gvec_ref[row : row + 1, :] = weigh([one[place] for one in sums], share)
    gattn_ref[3] = dot_tn(go_ref[...], att_ref[...]).astype(gattn_ref.dtype)
    ga_ref[...] = dot_nn(go_ref[...], attn_ref[3]).astype(BF16)

    def image_body(image, carry):
        at = block_rows(image, rows)
        for pair in range(pairs):
            lanes = slice(pair * 2 * HD, (pair + 1) * 2 * HD)
            query = stack_heads(proj_ref[0, at, lanes])
            keys = proj_ref[1, at, lanes]
            grad_out = stack_heads(ga_ref[at, lanes])
            probs = p_ref[image, pair]
            grad_probs = dot_nt(grad_out, proj_ref[2, at, lanes])
            dproj_ref[2, at, lanes] = dot_tn(probs, grad_out).astype(BF16)
            wide = probs.astype(F32)
            inner = jnp.sum(grad_probs * wide, axis=-1, keepdims=True)
            grad_scores = (wide * (grad_probs - inner)).astype(BF16)
            dproj_ref[0, at, lanes] = (unstack_heads(dot_nn(grad_scores, keys)) * scale).astype(BF16)
            dproj_ref[1, at, lanes] = (dot_tn(grad_scores, query) * scale).astype(BF16)
        return carry

    lax.fori_loop(0, images, image_body, 0)
    for part, row in enumerate((4, None, 5)):
        gattn_ref[part] = dot_tn(dproj_ref[part], n1_ref[...]).astype(gattn_ref.dtype)
        value = dot_nn(dproj_ref[part], attn_ref[part])
        if part == 0:
            acc_ref[...] = value
        else:
            acc_ref[...] += value
        if row is not None:
            sums = [
                fold_rows(dproj_ref[part, image * rows : (image + 1) * rows, :].astype(F32))
                for image in range(images)
            ]
            gvec_ref[row : row + 1, :] = weigh(sums, share)
    sums = norm_back(x_ref, acc_ref, gm_ref, gx_ref, None, vec_ref[0:1, :], images)
    for place, row in enumerate((0, 1)):
        gvec_ref[row : row + 1, :] = weigh([one[place] for one in sums], share)


def first_kernel(flag_ref, x_ref, bias_ref, vec_ref, attn_ref, up_ref, down_ref, *refs):
    out_ref, keep, h_ref = refs[0], refs[1:9], refs[9]
    forward_layer(x_ref, bias_ref, vec_ref, attn_ref, up_ref, down_ref, keep, (h_ref,), out_ref)
    drop_shared(flag_ref, keep, bias_ref.shape[0])


def last_kernel(flag_ref, x_ref, bias_ref, g_ref, vec_ref, attn_ref, up_ref, down_ref, *refs):
    out_ref, outs, keep, scratch = refs[0], refs[1:6], refs[6:14], refs[14:]
    forward_layer(
        x_ref, bias_ref, vec_ref, attn_ref, up_ref, down_ref, keep, (scratch[3],), out_ref
    )
    drop_shared(flag_ref, keep, bias_ref.shape[0])
    backward_layer(
        g_ref, x_ref, vec_ref, attn_ref, up_ref, down_ref, flag_ref, keep, scratch, outs
    )


def back_kernel(flag_ref, x_ref, g_ref, vec_ref, attn_ref, up_ref, down_ref, *refs):
    keep, outs, scratch = refs[0:8], refs[8:13], refs[13:]
    backward_layer(
        g_ref, x_ref, vec_ref, attn_ref, up_ref, down_ref, flag_ref, keep, scratch, outs
    )


def call(kernel, operands, outs, scratch, flops):
    smem = pl.BlockSpec(memory_space=pltpu.SMEM)
    vmem = pl.BlockSpec(memory_space=pltpu.VMEM)
    return pl.pallas_call(
        kernel,
        out_shape=[jax.ShapeDtypeStruct(shape, dtype) for shape, dtype in outs],
        in_specs=[smem] + [vmem] * (len(operands) - 1),
        out_specs=[vmem] * len(outs),
        scratch_shapes=[pltpu.VMEM(shape, dtype) for shape, dtype in scratch],
        compiler_params=pltpu.CompilerParams(vmem_limit_bytes=56 * 1024 * 1024),
        cost_estimate=pl.CostEstimate(flops=flops, bytes_accessed=8 << 20, transcendentals=0),
    )(*operands)


def shards(patches, targets, keep_mask, attn_weights, vectors, up_weights, down_weights):
    image_count, patch_rows, width = patches.shape
    layers = attn_weights.shape[0]
    dp_size, mp_size = lax.axis_size("dp"), lax.axis_size("mp")
    devices = dp_size * mp_size
    rank = lax.axis_index("mp")
    slice_rows = attn_weights.shape[2]
    vec_rows = vectors.shape[1]
    parts = attn_weights.shape[2] * devices // width
    assert image_count == mp_size + 1 and layers == 2
    images = 2
    rows = -(-patch_rows // 16) * 16
    total = images * rows

    gathered = []
    for layer in range(layers):
        tail = jnp.pad(vectors[layer], (0, 16 * width - vec_rows)).reshape(16, width)
        packed = jnp.concatenate(
            [attn_weights[layer].T, up_weights[layer], down_weights[layer].T, tail], axis=0
        )
        gathered.append(lax.all_gather(packed, ("dp", "mp")))

    def unpack(whole):
        attn = whole[:, :slice_rows].reshape(parts, width, width)

        def by_part(rows_of):
            split = rows_of.reshape(dp_size, mp_size, slice_rows, width)
            return split.transpose(1, 0, 2, 3).reshape(parts, width, width)

        up = by_part(whole[:, slice_rows : 2 * slice_rows])
        down = by_part(whole[:, 2 * slice_rows : 3 * slice_rows])
        vec = whole[:, 3 * slice_rows :].reshape(devices, 16 * width)[:, :vec_rows]
        vec = vec.reshape(-1, width).astype(F32)
        return vec, attn, up, down

    keep_rows = jnp.concatenate([jnp.ones((image_count, 2), jnp.int32), keep_mask], axis=1)
    keep_rows = jnp.pad(keep_rows, ((0, 0), (0, rows - patch_rows)))
    live = jnp.sum(keep_rows).astype(F32)
    loss_scale = SLOTS * dp_size / lax.psum(live, "dp")
    flat = keep_rows.reshape(-1)
    slot = jnp.cumsum(flat) - flat
    picks = (jnp.where(flat == 1, slot, SLOTS)[None, :] == jnp.arange(SLOTS)[:, None]).astype(BF16)

    def mine(array):
        own = lax.dynamic_slice_in_dim(array, rank, 1, 0)
        return jnp.concatenate([own, array[mp_size:]], axis=0)

    def padded(array):
        return jnp.pad(mine(array), ((0, 0), (0, rows - patch_rows), (0, 0))).astype(F32)

    kept = mine(keep_rows)
    stream = padded(patches).reshape(total, width)
    bias = jnp.where(kept == 1, 0.0, MASKED).astype(F32)[:, None, :]
    grad = (padded(targets) * (kept == 1)[:, :, None] * loss_scale).reshape(total, width)
    flag = (rank == 0).astype(jnp.int32).reshape(1)

    pairs = width // (2 * HD)
    wide = (parts, width, width)
    keep_shapes = [
        ((total, width), BF16),
        ((3, total, width), BF16),
        ((images, pairs, 2 * rows, rows), BF16),
        ((total, width), BF16),
        ((total, width), F32),
        ((total, width), BF16),
        ((parts, total, width), BF16),
        ((parts, total, width), F32),
    ]
    scratch_shapes = [
        ((total, width), BF16),
        ((total, width), BF16),
        ((total, width), F32),
        ((total, width), F32),
        ((total, width), F32),
        ((total, width), BF16),
        ((3, total, width), BF16),
    ]
    stream_shape = ((total, width), F32)
    grad_shapes = [
        stream_shape,
        (wide, BF16),
        (wide, BF16),
        (wide, BF16),
        ((2 * parts + 4, width), F32),
    ]
    first_weights = unpack(gathered[0])
    last_weights = unpack(gathered[1])
    forward_flops = 8 * total * parts * width * width
    first = call(
        first_kernel,
        (flag, stream, bias, *first_weights),
        [stream_shape] + keep_shapes,
        [stream_shape],
        forward_flops,
    )
    middle, saved = first[0], first[1:]
    last = call(
        last_kernel,
        (flag, middle, bias, grad, *last_weights),
        [stream_shape] + grad_shapes,
        keep_shapes + scratch_shapes,
        3 * forward_flops,
    )
    output, grad_middle, last_grads = last[0], last[1], last[2:]
    back = call(
        back_kernel,
        (flag, stream, grad_middle, *first_weights, *saved),
        grad_shapes,
        scratch_shapes,
        2 * forward_flops,
    )
    grad_first, first_grads = back[0], back[1:]

    def scatter(gattn, gup, gdown, gvec):
        def by_owner(grads):
            split = grads.reshape(mp_size, dp_size, slice_rows, width)
            return split.transpose(1, 0, 2, 3).reshape(devices, slice_rows, width)

        tail = gvec.reshape(devices, vec_rows).astype(BF16)
        tail = jnp.pad(tail, ((0, 0), (0, 16 * width - vec_rows))).reshape(devices, 16, width)
        packed = jnp.concatenate(
            [gattn.reshape(devices, slice_rows, width), by_owner(gup), by_owner(gdown), tail], axis=1
        )
        owned = lax.psum_scatter(packed, ("dp", "mp"), scatter_dimension=0, tiled=False)
        owned = owned.astype(F32)
        return (
            owned[:slice_rows].T,
            owned[3 * slice_rows :].reshape(16 * width)[:vec_rows],
            owned[slice_rows : 2 * slice_rows],
            owned[2 * slice_rows : 3 * slice_rows].T,
        )

    late = scatter(*last_grads)
    early = scatter(*first_grads)
    attn_grads, vector_grads, up_grads, down_grads = (
        jnp.stack([one, two]) for one, two in zip(early, late)
    )

    def everywhere(array):
        low = array.astype(BF16).reshape(images, rows, width)
        shared = lax.all_gather(low[0], "mp")
        return jnp.concatenate([shared, low[1:]], axis=0)

    final_rows = everywhere(output).reshape(image_count * rows, width)
    activations = dot_nn(picks, final_rows)
    input_grads = jnp.where(
        keep_rows[:, :patch_rows, None] == 1, everywhere(grad_first)[:, :patch_rows].astype(F32), 0.0
    )
    return (activations, input_grads, attn_grads, vector_grads, up_grads, down_grads)


def solution(mesh):
    in_specs = (
        P("dp", None, None),
        P("dp", None, None),
        P("dp", None),
        P(None, None, ("dp", "mp")),
        P(None, ("dp", "mp")),
        P(None, "dp", "mp"),
        P(None, "mp", "dp"),
    )
    out_specs = (
        P("dp", None),
        P("dp", None, None),
        P(None, None, ("dp", "mp")),
        P(None, ("dp", "mp")),
        P(None, "dp", "mp"),
        P(None, "mp", "dp"),
    )
    return jax.shard_map(shards, mesh=mesh, in_specs=in_specs, out_specs=out_specs, check_vma=False)
```

```python
import dataclasses
import functools

import jax
import jax.numpy as jnp
from jax import lax
from jax.experimental import pallas as pl
from jax.experimental.pallas import tpu as pltpu
from jax.sharding import PartitionSpec as P

HD = 64
SLOTS = 1024
EPSILON = 1e-06
MASKED = -1e30
STEP = 16

F32 = jnp.float32
BF16 = jnp.bfloat16


def dot_nn(left, right):
    return lax.dot_general(left, right, (((1,), (0,)), ((), ())), preferred_element_type=F32)


def dot_nt(left, right):
    return lax.dot_general(left, right, (((1,), (1,)), ((), ())), preferred_element_type=F32)


def dot_tn(left, right):
    return lax.dot_general(left, right, (((0,), (0,)), ((), ())), preferred_element_type=F32)


def block_rows(index, step):
    return pl.ds(pl.multiple_of(index * step, step), step)


def fold_rows(values):
    return jnp.sum(values.reshape(values.shape[0] // 8, 8, values.shape[1]), axis=0)


def low_halves(rows):
    lane = lax.broadcasted_iota(jnp.int32, (rows, 2 * HD), 1)
    return lane < HD


def stack_heads(pair):
    low = low_halves(pair.shape[0])
    zero = jnp.zeros_like(pair)
    return jnp.concatenate([jnp.where(low, pair, zero), jnp.where(low, zero, pair)], axis=0)


def unstack_heads(stacked):
    rows = stacked.shape[0] // 2
    return jnp.where(low_halves(rows), stacked[:rows], stacked[rows:])


def norm_rows(x_ref, out_ref, gain, shift):
    def body(index, carry):
        at = block_rows(index, STEP)
        values = x_ref[at, :].astype(F32)
        centred = values - jnp.mean(values, axis=-1, keepdims=True)
        variance = jnp.mean(centred * centred, axis=-1, keepdims=True)
        out_ref[at, :] = (centred * lax.rsqrt(variance + EPSILON) * gain + shift).astype(BF16)
        return carry

    lax.fori_loop(0, x_ref.shape[0] // STEP, body, 0)


def norm_back(x_ref, grad_ref, base_ref, out_ref, low_ref, gain, images):
    rows = x_ref.shape[0] // images
    width = x_ref.shape[1]
    sums = []
    for image in range(images):

        def body(index, carry, image=image):
            at = pl.ds(pl.multiple_of(image * rows + index * STEP, STEP), STEP)
            values = x_ref[at, :].astype(F32)
            grad = grad_ref[at, :]
            centred = values - jnp.mean(values, axis=-1, keepdims=True)
            variance = jnp.mean(centred * centred, axis=-1, keepdims=True)
            inverse = lax.rsqrt(variance + EPSILON)
            unit = centred * inverse
            scaled = grad * gain
            mean_one = jnp.mean(scaled, axis=-1, keepdims=True)
            mean_two = jnp.mean(scaled * unit, axis=-1, keepdims=True)
            out = base_ref[at, :] + inverse * (scaled - mean_one - unit * mean_two)
            out_ref[at, :] = out.astype(out_ref.dtype)
            if low_ref is not None:
                low_ref[at, :] = out.astype(BF16)
            return (
                carry[0] + fold_rows(grad * unit),
                carry[1] + fold_rows(grad),
                carry[2] + fold_rows(out),
            )

        zero = jnp.zeros((8, width), F32)
        sums.append(lax.fori_loop(0, rows // STEP, body, (zero, zero, zero)))
    return sums


def weigh(sums, share):
    total = sums[0]
    for more in sums[1:]:
        total = total + more * share
    return jnp.sum(total, axis=0, keepdims=True)


def as_square(ref, part):
    rows, width = ref.shape[1:]
    per = width // rows
    return ref[pl.ds(part * per, per)].reshape(width, width)


def forward_layer(x_ref, bias_ref, vec_ref, weights, keep, scratch, out_ref):
    attn_ref, up_ref, down_ref = weights
    n1_ref, proj_ref, p_ref, att_ref, mid_ref, n2_ref, a_ref, gp_ref = keep
    h_ref, acc_ref = scratch
    images = bias_ref.shape[0]
    rows = x_ref.shape[0] // images
    width = x_ref.shape[1]
    pairs = width // (2 * HD)
    scale = HD**-0.5

    norm_rows(x_ref, n1_ref, vec_ref[0:1, :], vec_ref[1:2, :])
    for part, bias_row in enumerate((4, None, 5)):
        value = dot_nt(n1_ref[...], as_square(attn_ref, part))
        if bias_row is not None:
            value = value + vec_ref[bias_row : bias_row + 1, :]
        proj_ref[part] = value.astype(BF16)

    def image_body(image, carry):
        at = block_rows(image, rows)
        for pair in range(pairs):
            lanes = slice(pair * 2 * HD, (pair + 1) * 2 * HD)
            query = stack_heads(proj_ref[0, at, lanes])
            scores = dot_nt(query, proj_ref[1, at, lanes]) * scale + bias_ref[image]
            top = jnp.max(scores, axis=-1, keepdims=True)
            powers = jnp.exp(scores - top)
            total = jnp.sum(powers, axis=-1, keepdims=True)
            probs = (powers * (1.0 / total)).astype(BF16)
            p_ref[image, pair] = probs
            att_ref[at, lanes] = unstack_heads(dot_nn(probs, proj_ref[2, at, lanes])).astype(BF16)
        return carry

    lax.fori_loop(0, images, image_body, 0)
    mid_ref[...] = x_ref[...].astype(F32) + dot_nt(att_ref[...], as_square(attn_ref, 3)) + vec_ref[6:7, :]
    norm_rows(mid_ref, n2_ref, vec_ref[2:3, :], vec_ref[3:4, :])
    acc_ref[...] = mid_ref[...] + vec_ref[11:12, :]

    def part_body(part, carry):
        h_ref[...] = dot_nn(n2_ref[...], as_square(up_ref, part))
        bias = vec_ref[pl.ds(7 + part, 1), :]

        def gelu_body(index, inner):
            at = block_rows(index, STEP)
            hidden = h_ref[at, :] + bias
            share = 0.5 + 0.5 * lax.erf(hidden * 0.7071067811865476)
            a_ref[part, at, :] = (hidden * share).astype(BF16)
            bell = jnp.exp(-0.5 * hidden * hidden) * 0.3989422804014327
            gp_ref[part, at, :] = (share + hidden * bell).astype(gp_ref.dtype)
            return inner

        lax.fori_loop(0, h_ref.shape[0] // STEP, gelu_body, 0)
        acc_ref[...] += dot_nt(a_ref[part], as_square(down_ref, part))
        return carry

    lax.fori_loop(0, a_ref.shape[0], part_body, 0)
    out_ref[...] = acc_ref[...].astype(out_ref.dtype)


def drop_shared(rank_ref, keep, images):
    n1_ref, proj_ref, p_ref, att_ref, mid_ref, n2_ref, a_ref, gp_ref = keep

    @pl.when(rank_ref[4] == 0)
    def _():
        rows = n1_ref.shape[0] // images
        at = slice(rows, images * rows)
        for ref in (n1_ref, att_ref, n2_ref):
            ref[at, :] = jnp.zeros((rows * (images - 1), ref.shape[1]), BF16)
        a_ref[:, at, :] = jnp.zeros((a_ref.shape[0], rows * (images - 1), a_ref.shape[2]), BF16)


def backward_layer(plan, g_ref, x_ref, vec_ref, weights, rank_ref, keep, scratch, gx_ref, store):
    attn_ref, up_ref, down_ref = weights
    n1_ref, proj_ref, p_ref, att_ref, mid_ref, n2_ref, a_ref, gp_ref = keep
    go_ref, gh_ref, acc_ref, h_ref, gm_ref, ga_ref, dproj_ref, gvec_ref = scratch
    gvec_ref[...] = jnp.zeros_like(gvec_ref)
    images = p_ref.shape[0]
    rows = x_ref.shape[0] // images
    width = x_ref.shape[1]
    pairs = width // (2 * HD)
    scale = HD**-0.5
    share = rank_ref[4].astype(F32)

    sums = []
    for image in range(images):

        def low_body(index, carry, image=image):
            at = pl.ds(pl.multiple_of(image * rows + index * STEP, STEP), STEP)
            grad = g_ref[at, :]
            go_ref[at, :] = grad.astype(BF16)
            return carry + fold_rows(grad)

        sums.append(lax.fori_loop(0, rows // STEP, low_body, jnp.zeros((8, width), F32)))
    gvec_ref[11:12, :] = weigh(sums, share)
    acc_ref[...] = jnp.zeros_like(acc_ref)

    def part_body(part, carry):
        store(2, part, dot_tn(go_ref[...], a_ref[part]))
        h_ref[...] = dot_nn(go_ref[...], as_square(down_ref, part))
        inner_sums = []
        for image in range(images):

            def hidden_body(index, inner, image=image):
                at = pl.ds(pl.multiple_of(image * rows + index * STEP, STEP), STEP)
                grad = (h_ref[at, :] * gp_ref[part, at, :].astype(F32)).astype(BF16)
                gh_ref[at, :] = grad
                return inner + fold_rows(grad.astype(F32))

            inner_sums.append(
                lax.fori_loop(0, rows // STEP, hidden_body, jnp.zeros((8, width), F32))
            )
        gvec_ref[pl.ds(7 + part, 1), :] = weigh(inner_sums, share)
        store(1, part, dot_tn(n2_ref[...], gh_ref[...]))
        acc_ref[...] += dot_nt(gh_ref[...], as_square(up_ref, part))
        return carry

    lax.fori_loop(0, a_ref.shape[0], part_body, 0)
    sums = norm_back(mid_ref, acc_ref, g_ref, gm_ref, go_ref, vec_ref[2:3, :], images)
    for place, row in enumerate((2, 3, 6)):
        gvec_ref[row : row + 1, :] = weigh([one[place] for one in sums], share)
    store(0, 3, dot_tn(go_ref[...], att_ref[...]))
    ga_ref[...] = dot_nn(go_ref[...], as_square(attn_ref, 3)).astype(BF16)

    def image_body(image, carry):
        at = block_rows(image, rows)
        for pair in range(pairs):
            lanes = slice(pair * 2 * HD, (pair + 1) * 2 * HD)
            query = stack_heads(proj_ref[0, at, lanes])
            keys = proj_ref[1, at, lanes]
            grad_out = stack_heads(ga_ref[at, lanes])
            probs = p_ref[image, pair]
            grad_probs = dot_nt(grad_out, proj_ref[2, at, lanes])
            dproj_ref[2, at, lanes] = dot_tn(probs, grad_out).astype(BF16)
            wide = probs.astype(F32)
            inner = jnp.sum(grad_probs * wide, axis=-1, keepdims=True)
            grad_scores = (wide * (grad_probs - inner)).astype(BF16)
            dproj_ref[0, at, lanes] = (unstack_heads(dot_nn(grad_scores, keys)) * scale).astype(BF16)
            dproj_ref[1, at, lanes] = (dot_tn(grad_scores, query) * scale).astype(BF16)
        return carry

    lax.fori_loop(0, images, image_body, 0)
    for part, row in enumerate((4, None, 5)):
        store(0, part, dot_tn(dproj_ref[part], n1_ref[...]))
        value = dot_nn(dproj_ref[part], as_square(attn_ref, part))
        if part == 0:
            acc_ref[...] = value
        else:
            acc_ref[...] += value
        if row is not None:
            sums = [
                fold_rows(dproj_ref[part, image * rows : (image + 1) * rows, :].astype(F32))
                for image in range(images)
            ]
            gvec_ref[row : row + 1, :] = weigh(sums, share)
    sums = norm_back(x_ref, acc_ref, gm_ref, gx_ref, None, vec_ref[0:1, :], images)
    for place, row in enumerate((0, 1)):
        gvec_ref[row : row + 1, :] = weigh([one[place] for one in sums], share)
    store(3, 0, gvec_ref[...])


def load_weights(plan, layer, source, weights, tiles_ref, sems):
    attn_ref, up_ref, down_ref = weights
    thin, tile = plan.thin, plan.tile
    copies = []

    def copy(src, dst):
        copies.append(pltpu.make_async_copy(src, dst, sems.at[len(copies)]))

    base = layer * plan.block
    for i in range(plan.outer):
        to = pl.ds(i * plan.inner, plan.inner)
        copy(source.at[i, :, pl.ds(base, thin)], attn_ref.at[to])
        copy(source.at[i, :, pl.ds(base + 3 * thin, tile)], tiles_ref.at[to])
    first = len(copies)
    for m in range(plan.inner):
        to = pl.ds(m * plan.outer, plan.outer)
        copy(source.at[:, m, pl.ds(base + thin, thin)], up_ref.at[to])
        copy(source.at[:, m, pl.ds(base + 2 * thin, thin)], down_ref.at[to])
    for one in copies:
        one.start()
    return copies[:first], copies[first:]


def wait_all(copies):
    for one in copies:
        one.wait()


def sum_tiles(tiles_ref, vec_ref):
    vec_ref[...] = jnp.sum(tiles_ref[...].astype(F32), axis=0)


def storer(plan, rank_ref, packed_ref):
    thin, width = plan.thin, plan.width
    per = width // thin

    def put(owner, row, block):
        c, x, y = owner % 2, owner // 2 % 2, owner // 4 % 2
        z = owner // 8
        at = (c ^ rank_ref[3], y ^ rank_ref[1], x ^ rank_ref[2], z ^ rank_ref[0])
        packed_ref[at[0], at[1], at[2], at[3], row : row + block.shape[0], :] = block

    def store(kind, part, value):
        low = value.astype(BF16)
        if kind == 3:
            for owner in range(plan.outer * plan.inner):
                put(owner, 3 * thin, low)
            return
        blocks = low.reshape(per, thin, width)
        for i in range(per):
            owner = part * per + i if kind == 0 else i * plan.inner + part
            put(owner, kind * thin, blocks[i])

    return store


def first_kernel(plan, rank_ref, x_ref, bias_ref, source, *refs):
    out_ref, keep, (h_ref, acc_ref, vec_ref, tiles_ref, *weights, sems) = refs[0], refs[1:9], refs[9:]
    early, late = load_weights(plan, 0, source, weights, tiles_ref, sems)
    wait_all(early)
    sum_tiles(tiles_ref, vec_ref)
    wait_all(late)
    forward_layer(x_ref, bias_ref, vec_ref, weights, keep, (h_ref, acc_ref), out_ref)
    drop_shared(rank_ref, keep, bias_ref.shape[0])


def send_out(packed_ref, outs, sems):
    copies = [pltpu.make_async_copy(packed_ref.at[i], outs[i], sems.at[i]) for i in range(2)]
    for one in copies:
        one.start()
    wait_all(copies)


def last_kernel(plan, rank_ref, x_ref, bias_ref, goal_ref, source, *refs):
    out_ref, gx_ref, outs, keep, scratch = refs[0], refs[1], refs[2:4], refs[4:12], refs[12:20]
    g_ref, packed_ref, vec_ref, tiles_ref, *weights, sems = refs[20:]
    early, late = load_weights(plan, 1, source, weights, tiles_ref, sems)
    wait_all(early)
    sum_tiles(tiles_ref, vec_ref)
    wait_all(late)
    forward_layer(x_ref, bias_ref, vec_ref, weights, keep, (scratch[3], scratch[2]), out_ref)
    drop_shared(rank_ref, keep, bias_ref.shape[0])
    high = jnp.sum(vec_ref[12:13, :], axis=-1, keepdims=True)
    rest = jnp.sum(vec_ref[13:14, :], axis=-1, keepdims=True)
    loss_scale = float(plan.slots) / (high * 32.0 + rest)
    g_ref[...] = goal_ref[...].astype(F32) * loss_scale
    store = storer(plan, rank_ref, packed_ref)
    backward_layer(plan, g_ref, x_ref, vec_ref, weights, rank_ref, keep, scratch, gx_ref, store)
    send_out(packed_ref, outs, sems)


def back_kernel(plan, rank_ref, x_ref, g_ref, source, *refs):
    keep, gx_ref, outs, scratch = refs[0:8], refs[8], refs[9:11], refs[11:19]
    packed_ref, vec_ref, tiles_ref, *weights, sems = refs[19:]
    early, late = load_weights(plan, 0, source, weights, tiles_ref, sems)
    wait_all(early)
    sum_tiles(tiles_ref, vec_ref)
    wait_all(late)
    store = storer(plan, rank_ref, packed_ref)
    backward_layer(plan, g_ref, x_ref, vec_ref, weights, rank_ref, keep, scratch, gx_ref, store)
    send_out(packed_ref, outs, sems)


def place_kernel(rank_ref, own_ref, *refs):
    others, out_ref = refs[:-1], refs[-1]
    rows = own_ref.shape[0] // 2
    kept = out_ref.shape[1]
    mine = rank_ref[2] * 2 + rank_ref[3]
    out_ref[mine] = own_ref[0:rows, :].astype(F32)[:kept]
    for i, ref in enumerate(others):
        out_ref[mine ^ (i + 1)] = ref[...].astype(F32)[:kept]
    out_ref[out_ref.shape[0] - 1] = own_ref[rows : 2 * rows, :].astype(F32)[:kept]


def pack_kernel(slot_ref, own_ref, *refs):
    others, out_ref = refs[:-1], refs[-1]
    rows = own_ref.shape[0] // 2
    sources = [own_ref[0:rows, :]] + [ref[...] for ref in others] + [own_ref[rows : 2 * rows, :]]
    step = 256

    def body(index, carry):
        slots = lax.broadcasted_iota(jnp.int32, (step, rows), 0) + index * step
        total = None
        for i, values in enumerate(sources):
            picks = jnp.where(slots == slot_ref[i], 1.0, 0.0).astype(BF16)
            term = dot_nn(picks, values)
            total = term if total is None else total + term
        out_ref[block_rows(index, step), :] = total
        return carry

    lax.fori_loop(0, out_ref.shape[0] // step, body, 0)


VMEM = pl.BlockSpec(memory_space=pltpu.VMEM)
SMEM = pl.BlockSpec(memory_space=pltpu.SMEM)
ANY = pl.BlockSpec(memory_space=pl.ANY)


def call(kernel, operands, specs, outs, out_specs, scratch, flops):
    return pl.pallas_call(
        kernel,
        out_shape=[jax.ShapeDtypeStruct(shape, dtype) for shape, dtype in outs],
        in_specs=specs,
        out_specs=out_specs,
        scratch_shapes=scratch,
        compiler_params=pltpu.CompilerParams(vmem_limit_bytes=56 * 1024 * 1024),
        cost_estimate=pl.CostEstimate(flops=flops, bytes_accessed=8 << 20, transcendentals=0),
    )(*operands)


@dataclasses.dataclass(frozen=True)
class Plan:
    outer: int
    inner: int
    thin: int
    tile: int
    width: int
    slots: int

    @property
    def block(self):
        return 3 * self.thin + self.tile


def flip(array, mask, devices):
    return lax.ppermute(array, ("dp", "mp"), [(d, d ^ mask) for d in range(devices)])


def scatter_sum(kept, sent, devices):
    got = flip(sent, 1, devices)
    plane = {
        at: kept[at].astype(F32) + got[at].astype(F32) for at in ((0, 0), (0, 1), (1, 0), (1, 1))
    }
    total = plane[0, 0]
    for at, mask in (((1, 1), 6), ((0, 1), 2), ((1, 0), 4)):
        total = total + flip(plane[at].astype(BF16), mask, devices).astype(F32)
    result = total[0]
    for k in range(1, total.shape[0]):
        result = result + flip(total[k].astype(BF16), 8 * k, devices).astype(F32)
    return result


def shards(patches, targets, keep_mask, attn_weights, vectors, up_weights, down_weights):
    image_count, patch_rows, width = patches.shape
    layers = attn_weights.shape[0]
    dp_size, mp_size = lax.axis_size("dp"), lax.axis_size("mp")
    devices = dp_size * mp_size
    rank = lax.axis_index("mp")
    lane_rank = lax.axis_index("dp")
    device = lane_rank * mp_size + rank
    thin = attn_weights.shape[2]
    vec_rows = vectors.shape[1]
    parts = thin * devices // width
    assert image_count == mp_size + 1 and layers == 2 and parts == mp_size == 4
    direct = thin % 16 == 0
    images, tile = 2, 16
    rows = -(-patch_rows // 16) * 16
    total = images * rows
    block = 3 * thin + tile

    keep_rows = jnp.concatenate([jnp.ones((image_count, 2), jnp.int32), keep_mask], axis=1)
    keep_rows = jnp.pad(keep_rows, ((0, 0), (0, rows - patch_rows)))
    live = jnp.where(rank == 0, jnp.sum(keep_rows), 0)

    packed = []
    for layer in range(layers):
        piece = lax.dynamic_update_slice(
            jnp.zeros((tile * width,), BF16), vectors[layer], (device * vec_rows,)
        ).reshape(tile, width)
        if layer == layers - 1:
            row = lax.broadcasted_iota(jnp.int32, (tile, width), 0)
            here = lax.broadcasted_iota(jnp.int32, (tile, width), 1) == lane_rank
            piece = jnp.where(here & (row == 12), (live // 32).astype(BF16), piece)
            piece = jnp.where(here & (row == 13), (live % 32).astype(BF16), piece)
        packed += [attn_weights[layer].T, up_weights[layer], down_weights[layer].T, piece]
    whole = lax.all_gather(jnp.concatenate(packed, axis=0), ("dp", "mp"))
    if direct:
        plan = Plan(dp_size, mp_size, thin, tile, width, SLOTS * dp_size)
        source = whole.reshape(dp_size, mp_size, layers * block, width)
    else:
        plan = Plan(1, parts, width, tile, width, SLOTS * dp_size)
        pieces = []
        for layer in range(layers):
            mine_of = whole[:, layer * block : (layer + 1) * block]
            pieces.append(mine_of[:, :thin].reshape(parts, width, width))
            for kind in (1, 2):
                split = mine_of[:, kind * thin : (kind + 1) * thin]
                split = split.reshape(dp_size, mp_size, thin, width).transpose(1, 0, 2, 3)
                pieces.append(split.reshape(parts, width, width))
            summed = jnp.sum(mine_of[:, 3 * thin :].astype(F32), axis=0).astype(BF16)
            pieces.append(jnp.pad(summed[None], ((0, parts - 1), (0, 0), (0, 0))))
        source = jnp.concatenate(pieces, axis=1)[None]

    flat = keep_rows.reshape(-1)
    slot = jnp.where(flat == 1, jnp.cumsum(flat) - flat, SLOTS).reshape(image_count, 1, rows)

    def mine(array):
        return jnp.concatenate(
            [lax.dynamic_slice_in_dim(array, rank, 1, 0), array[mp_size:]], axis=0
        )

    def padded(array):
        return jnp.pad(mine(array), ((0, 0), (0, rows - patch_rows), (0, 0)))

    kept = mine(keep_rows)
    stream = padded(patches).reshape(total, width)
    bias = jnp.where(kept == 1, 0.0, MASKED).astype(F32)[:, None, :]
    goal = jnp.where((kept == 1)[:, :, None], padded(targets), 0).reshape(total, width)
    slots = jnp.concatenate(
        [lax.dynamic_slice_in_dim(slot, rank ^ k, 1, 0) for k in range(mp_size)] + [slot[mp_size:]],
        axis=0,
    )
    plane = (lane_rank // 2, lane_rank % 2) if direct else (0, 0)
    ranks = jnp.stack(
        [jnp.int32(k) for k in (*plane, rank // 2, rank % 2)] + [(rank == 0).astype(jnp.int32)]
    )

    pairs = width // (2 * HD)
    stream_shape = ((total, width), F32)
    low_shape = ((total, width), BF16)
    keep_shapes = [
        low_shape,
        ((3, total, width), BF16),
        ((images, pairs, 2 * rows, rows), BF16),
        low_shape,
        stream_shape,
        low_shape,
        ((parts, total, width), BF16),
        ((parts, total, width), F32),
    ]
    scratch_shapes = [
        low_shape,
        low_shape,
        stream_shape,
        stream_shape,
        stream_shape,
        low_shape,
        ((3, total, width), BF16),
        ((tile, width), F32),
    ]
    blocks = plan.outer * plan.inner
    weight_shapes = [
        ((tile, width), F32),
        ((blocks, tile, width), BF16),
        ((blocks, plan.thin, width), BF16),
        ((blocks, plan.thin, width), BF16),
        ((blocks, plan.thin, width), BF16),
    ]
    zs = max(blocks // 8, 1)
    half_shape = ((2, 2, zs, plan.block, width), BF16)
    packed_shape = ((2, 2, 2, zs, plan.block, width), BF16)
    sems = [pltpu.SemaphoreType.DMA((2 * (plan.outer + plan.inner),))]

    def vmem(shapes):
        return [pltpu.VMEM(shape, dtype) for shape, dtype in shapes]

    forward_flops = 8 * total * parts * width * width
    first = call(
        functools.partial(first_kernel, plan),
        (ranks, stream, bias, source),
        [SMEM, VMEM, VMEM, ANY],
        [stream_shape] + keep_shapes,
        [VMEM] * 9,
        vmem([stream_shape, stream_shape] + weight_shapes) + sems,
        forward_flops,
    )
    middle, saved = first[0], first[1:]
    output, grad_middle, *late_halves = call(
        functools.partial(last_kernel, plan),
        (ranks, middle, bias, goal, source),
        [SMEM, VMEM, VMEM, VMEM, ANY],
        [low_shape, stream_shape, half_shape, half_shape],
        [VMEM, VMEM, ANY, ANY],
        vmem(keep_shapes + scratch_shapes + [stream_shape, packed_shape] + weight_shapes) + sems,
        3 * forward_flops,
    )
    grad_first, *early_halves = call(
        functools.partial(back_kernel, plan),
        (ranks, stream, grad_middle, source, *saved),
        [SMEM, VMEM, VMEM, ANY] + [VMEM] * 8,
        [low_shape, half_shape, half_shape],
        [VMEM, ANY, ANY],
        vmem(scratch_shapes + [packed_shape] + weight_shapes) + sems,
        2 * forward_flops,
    )

    def owned_block(halves):
        if direct:
            return scatter_sum(*halves, devices)
        both = jnp.stack(halves)[:, 0, :, 0]
        both = jnp.stack([both[k % 2, k // 2] for k in range(parts)])
        both = jnp.stack([lax.dynamic_index_in_dim(both, rank ^ k, 0, False) for k in range(parts)])
        attn = both[:, :width].reshape(devices, thin, width)
        pieces = [attn]
        for kind in (1, 2):
            split = both[:, kind * width : (kind + 1) * width]
            split = split.reshape(mp_size, dp_size, thin, width).transpose(1, 0, 2, 3)
            pieces.append(split.reshape(devices, thin, width))
        pieces.append(jnp.broadcast_to(both[0, 3 * width :], (devices, tile, width)))
        summed = lax.psum_scatter(
            jnp.concatenate(pieces, axis=1), ("dp", "mp"), scatter_dimension=0, tiled=False
        )
        return summed.astype(F32)

    def outputs_of(halves):
        owned = owned_block(halves)
        vec = lax.dynamic_slice_in_dim(owned[3 * thin :].reshape(-1), device * vec_rows, vec_rows)
        return owned[:thin].T, vec, owned[thin : 2 * thin], owned[2 * thin : 3 * thin].T

    late = outputs_of(late_halves)
    early = outputs_of(early_halves)
    attn_grads, vector_grads, up_grads, down_grads = (
        jnp.stack([one, two]) for one, two in zip(early, late)
    )

    def others(array):
        return [flip(array[:rows], k, devices) for k in range(1, mp_size)]

    (activations,) = call(
        pack_kernel,
        (slots, output, *others(output)),
        [VMEM] * (mp_size + 1),
        [((SLOTS, width), F32)],
        [VMEM],
        [],
        2 * SLOTS * image_count * rows * width,
    )
    (input_grads,) = call(
        place_kernel,
        (ranks, grad_first, *others(grad_first)),
        [SMEM] + [VMEM] * mp_size,
        [((image_count, patch_rows, width), F32)],
        [VMEM],
        [],
        image_count * patch_rows * width,
    )
    return (activations, input_grads, attn_grads, vector_grads, up_grads, down_grads)


def solution(mesh):
    in_specs = (
        P("dp", None, None),
        P("dp", None, None),
        P("dp", None),
        P(None, None, ("dp", "mp")),
        P(None, ("dp", "mp")),
        P(None, "dp", "mp"),
        P(None, "mp", "dp"),
    )
    out_specs = (
        P("dp", None),
        P("dp", None, None),
        P(None, None, ("dp", "mp")),
        P(None, ("dp", "mp")),
        P(None, "dp", "mp"),
        P(None, "mp", "dp"),
    )
    return jax.shard_map(shards, mesh=mesh, in_specs=in_specs, out_specs=out_specs, check_vma=False)
```

```python
import dataclasses
import functools

import jax
import jax.numpy as jnp
from jax import lax
from jax.experimental import pallas as pl
from jax.experimental.pallas import tpu as pltpu
from jax.sharding import PartitionSpec as P

HD = 64
SLOTS = 1024
EPSILON = 1e-06
MASKED = -1e30
STEP = 16
UNROLL = 13

F32 = jnp.float32
BF16 = jnp.bfloat16


def dot_nn(left, right):
    return lax.dot_general(left, right, (((1,), (0,)), ((), ())), preferred_element_type=F32)


def dot_nt(left, right):
    return lax.dot_general(left, right, (((1,), (1,)), ((), ())), preferred_element_type=F32)


def dot_tn(left, right):
    return lax.dot_general(left, right, (((0,), (0,)), ((), ())), preferred_element_type=F32)


def block_rows(index, step):
    return pl.ds(pl.multiple_of(index * step, step), step)


def fold_rows(values):
    return jnp.sum(values.reshape(values.shape[0] // 8, 8, values.shape[1]), axis=0)


def low_halves(rows):
    lane = lax.broadcasted_iota(jnp.int32, (rows, 2 * HD), 1)
    return lane < HD


def stack_heads(pair):
    low = low_halves(pair.shape[0])
    zero = jnp.zeros_like(pair)
    return jnp.concatenate([jnp.where(low, pair, zero), jnp.where(low, zero, pair)], axis=0)


def unstack_heads(stacked):
    rows = stacked.shape[0] // 2
    return jnp.where(low_halves(rows), stacked[:rows], stacked[rows:])


def norm_rows(x_ref, out_ref, gain, shift):
    def body(index, carry):
        at = block_rows(index, STEP)
        values = x_ref[at, :].astype(F32)
        centred = values - jnp.mean(values, axis=-1, keepdims=True)
        variance = jnp.mean(centred * centred, axis=-1, keepdims=True)
        out_ref[at, :] = (centred * lax.rsqrt(variance + EPSILON) * gain + shift).astype(BF16)
        return carry

    lax.fori_loop(0, x_ref.shape[0] // STEP, body, 0, unroll=UNROLL)


def norm_back(x_ref, grad_ref, base_ref, out_ref, low_ref, gain, images):
    rows = x_ref.shape[0] // images
    width = x_ref.shape[1]
    sums = []
    for image in range(images):

        def body(index, carry, image=image):
            at = pl.ds(pl.multiple_of(image * rows + index * STEP, STEP), STEP)
            values = x_ref[at, :].astype(F32)
            grad = grad_ref[at, :]
            centred = values - jnp.mean(values, axis=-1, keepdims=True)
            variance = jnp.mean(centred * centred, axis=-1, keepdims=True)
            inverse = lax.rsqrt(variance + EPSILON)
            unit = centred * inverse
            scaled = grad * gain
            mean_one = jnp.mean(scaled, axis=-1, keepdims=True)
            mean_two = jnp.mean(scaled * unit, axis=-1, keepdims=True)
            out = base_ref[at, :] + inverse * (scaled - mean_one - unit * mean_two)
            out_ref[at, :] = out.astype(out_ref.dtype)
            if low_ref is not None:
                low_ref[at, :] = out.astype(BF16)
            return (
                carry[0] + fold_rows(grad * unit),
                carry[1] + fold_rows(grad),
                carry[2] + fold_rows(out),
            )

        zero = jnp.zeros((8, width), F32)
        sums.append(lax.fori_loop(0, rows // STEP, body, (zero, zero, zero), unroll=UNROLL))
    return sums


def weigh(sums, share):
    total = sums[0]
    for more in sums[1:]:
        total = total + more * share
    return jnp.sum(total, axis=0, keepdims=True)


def as_square(ref, part):
    rows, width = ref.shape[1:]
    per = width // rows
    return ref[pl.ds(part * per, per)].reshape(width, width)


def forward_layer(x_ref, bias_ref, vec_ref, weights, keep, scratch, out_ref):
    attn_ref, up_ref, down_ref = weights
    n1_ref, proj_ref, p_ref, att_ref, mid_ref, n2_ref, a_ref, gp_ref = keep
    h_ref, acc_ref = scratch
    images = bias_ref.shape[0]
    rows = x_ref.shape[0] // images
    width = x_ref.shape[1]
    pairs = width // (2 * HD)
    scale = HD**-0.5

    norm_rows(x_ref, n1_ref, vec_ref[0:1, :], vec_ref[1:2, :])
    for part, bias_row in enumerate((4, None, 5)):
        value = dot_nt(n1_ref[...], as_square(attn_ref, part))
        if bias_row is not None:
            value = value + vec_ref[bias_row : bias_row + 1, :]
        proj_ref[part] = value.astype(BF16)

    def image_body(image, carry):
        at = block_rows(image, rows)
        for pair in range(pairs):
            lanes = slice(pair * 2 * HD, (pair + 1) * 2 * HD)
            query = stack_heads(proj_ref[0, at, lanes])
            scores = dot_nt(query, proj_ref[1, at, lanes]) * scale + bias_ref[image]
            top = jnp.max(scores, axis=-1, keepdims=True)
            powers = jnp.exp(scores - top)
            total = jnp.sum(powers, axis=-1, keepdims=True)
            probs = (powers * (1.0 / total)).astype(BF16)
            p_ref[image, pair] = probs
            att_ref[at, lanes] = unstack_heads(dot_nn(probs, proj_ref[2, at, lanes])).astype(BF16)
        return carry

    lax.fori_loop(0, images, image_body, 0)
    mid_ref[...] = x_ref[...].astype(F32) + dot_nt(att_ref[...], as_square(attn_ref, 3)) + vec_ref[6:7, :]
    norm_rows(mid_ref, n2_ref, vec_ref[2:3, :], vec_ref[3:4, :])
    acc_ref[...] = mid_ref[...] + vec_ref[11:12, :]

    def part_body(part, carry):
        h_ref[...] = dot_nn(n2_ref[...], as_square(up_ref, part))
        bias = vec_ref[pl.ds(7 + part, 1), :]

        def gelu_body(index, inner):
            at = block_rows(index, STEP)
            hidden = h_ref[at, :] + bias
            share = 0.5 + 0.5 * lax.erf(hidden * 0.7071067811865476)
            a_ref[part, at, :] = (hidden * share).astype(BF16)
            bell = jnp.exp(-0.5 * hidden * hidden) * 0.3989422804014327
            gp_ref[part, at, :] = (share + hidden * bell).astype(gp_ref.dtype)
            return inner

        lax.fori_loop(0, h_ref.shape[0] // STEP, gelu_body, 0, unroll=UNROLL)
        acc_ref[...] += dot_nt(a_ref[part], as_square(down_ref, part))
        return carry

    lax.fori_loop(0, a_ref.shape[0], part_body, 0)
    out_ref[...] = acc_ref[...].astype(out_ref.dtype)


def drop_shared(rank_ref, keep, images):
    n1_ref, proj_ref, p_ref, att_ref, mid_ref, n2_ref, a_ref, gp_ref = keep

    @pl.when(rank_ref[4] == 0)
    def _():
        rows = n1_ref.shape[0] // images
        at = slice(rows, images * rows)
        for ref in (n1_ref, att_ref, n2_ref):
            ref[at, :] = jnp.zeros((rows * (images - 1), ref.shape[1]), BF16)
        a_ref[:, at, :] = jnp.zeros((a_ref.shape[0], rows * (images - 1), a_ref.shape[2]), BF16)


def backward_layer(plan, g_ref, x_ref, vec_ref, weights, rank_ref, keep, scratch, gx_ref, store):
    attn_ref, up_ref, down_ref = weights
    n1_ref, proj_ref, p_ref, att_ref, mid_ref, n2_ref, a_ref, gp_ref = keep
    go_ref, gh_ref, acc_ref, h_ref, gm_ref, ga_ref, dproj_ref, gvec_ref, got_ref, n2t_ref = scratch
    gvec_ref[...] = jnp.zeros_like(gvec_ref)
    images = p_ref.shape[0]
    rows = x_ref.shape[0] // images
    width = x_ref.shape[1]
    pairs = width // (2 * HD)
    scale = HD**-0.5
    share = rank_ref[4].astype(F32)

    sums = []
    for image in range(images):

        def low_body(index, carry, image=image):
            at = pl.ds(pl.multiple_of(image * rows + index * STEP, STEP), STEP)
            grad = g_ref[at, :]
            go_ref[at, :] = grad.astype(BF16)
            return carry + fold_rows(grad)

        sums.append(
            lax.fori_loop(0, rows // STEP, low_body, jnp.zeros((8, width), F32), unroll=UNROLL)
        )
    gvec_ref[11:12, :] = weigh(sums, share)
    acc_ref[...] = jnp.zeros_like(acc_ref)
    got_ref[...] = go_ref[...].T
    n2t_ref[...] = n2_ref[...].T

    def part_body(part, carry):
        store(2, part, dot_nn(got_ref[...], a_ref[part]))
        h_ref[...] = dot_nn(go_ref[...], as_square(down_ref, part))
        inner_sums = []
        for image in range(images):

            def hidden_body(index, inner, image=image):
                at = pl.ds(pl.multiple_of(image * rows + index * STEP, STEP), STEP)
                grad = (h_ref[at, :] * gp_ref[part, at, :].astype(F32)).astype(BF16)
                gh_ref[at, :] = grad
                return inner + fold_rows(grad.astype(F32))

            start = jnp.zeros((8, width), F32)
            inner_sums.append(
                lax.fori_loop(0, rows // STEP, hidden_body, start, unroll=UNROLL)
            )
        gvec_ref[pl.ds(7 + part, 1), :] = weigh(inner_sums, share)
        store(1, part, dot_nn(n2t_ref[...], gh_ref[...]))
        acc_ref[...] += dot_nt(gh_ref[...], as_square(up_ref, part))
        return carry

    lax.fori_loop(0, a_ref.shape[0], part_body, 0)
    sums = norm_back(mid_ref, acc_ref, g_ref, gm_ref, go_ref, vec_ref[2:3, :], images)
    for place, row in enumerate((2, 3, 6)):
        gvec_ref[row : row + 1, :] = weigh([one[place] for one in sums], share)
    store(0, 3, dot_tn(go_ref[...], att_ref[...]))
    ga_ref[...] = dot_nn(go_ref[...], as_square(attn_ref, 3)).astype(BF16)

    def image_body(image, carry):
        at = block_rows(image, rows)
        for pair in range(pairs):
            lanes = slice(pair * 2 * HD, (pair + 1) * 2 * HD)
            query = stack_heads(proj_ref[0, at, lanes])
            keys = proj_ref[1, at, lanes]
            grad_out = stack_heads(ga_ref[at, lanes])
            probs = p_ref[image, pair]
            grad_probs = dot_nt(grad_out, proj_ref[2, at, lanes])
            dproj_ref[2, at, lanes] = dot_tn(probs, grad_out).astype(BF16)
            wide = probs.astype(F32)
            inner = jnp.sum(grad_probs * wide, axis=-1, keepdims=True)
            grad_scores = (wide * (grad_probs - inner)).astype(BF16)
            dproj_ref[0, at, lanes] = (unstack_heads(dot_nn(grad_scores, keys)) * scale).astype(BF16)
            dproj_ref[1, at, lanes] = (dot_tn(grad_scores, query) * scale).astype(BF16)
        return carry

    lax.fori_loop(0, images, image_body, 0)
    for part, row in enumerate((4, None, 5)):
        store(0, part, dot_tn(dproj_ref[part], n1_ref[...]))
        value = dot_nn(dproj_ref[part], as_square(attn_ref, part))
        if part == 0:
            acc_ref[...] = value
        else:
            acc_ref[...] += value
        if row is not None:
            sums = [
                fold_rows(dproj_ref[part, image * rows : (image + 1) * rows, :].astype(F32))
                for image in range(images)
            ]
            gvec_ref[row : row + 1, :] = weigh(sums, share)
    sums = norm_back(x_ref, acc_ref, gm_ref, gx_ref, None, vec_ref[0:1, :], images)
    for place, row in enumerate((0, 1)):
        gvec_ref[row : row + 1, :] = weigh([one[place] for one in sums], share)
    store(3, 0, gvec_ref[...])


def load_weights(plan, layer, source, weights, tiles_ref, sems):
    attn_ref, up_ref, down_ref = weights
    thin, tile = plan.thin, plan.tile
    copies = []

    def copy(src, dst):
        copies.append(pltpu.make_async_copy(src, dst, sems.at[len(copies)]))

    base = layer * plan.block
    for i in range(plan.outer):
        to = pl.ds(i * plan.inner, plan.inner)
        copy(source.at[i, :, pl.ds(base, thin)], attn_ref.at[to])
        copy(source.at[i, :, pl.ds(base + 3 * thin, tile)], tiles_ref.at[to])
    first = len(copies)
    for m in range(plan.inner):
        to = pl.ds(m * plan.outer, plan.outer)
        copy(source.at[:, m, pl.ds(base + thin, thin)], up_ref.at[to])
        copy(source.at[:, m, pl.ds(base + 2 * thin, thin)], down_ref.at[to])
    for one in copies:
        one.start()
    return copies[:first], copies[first:]


def wait_all(copies):
    for one in copies:
        one.wait()


def sum_tiles(tiles_ref, vec_ref):
    vec_ref[...] = jnp.sum(tiles_ref[...].astype(F32), axis=0)


def storer(plan, rank_ref, packed_ref):
    thin, width = plan.thin, plan.width
    per = width // thin

    def put(owner, row, block):
        c, x, y = owner % 2, owner // 2 % 2, owner // 4 % 2
        z = owner // 8
        at = (c ^ rank_ref[3], y ^ rank_ref[1], x ^ rank_ref[2], z ^ rank_ref[0])
        packed_ref[at[0], at[1], at[2], at[3], row : row + block.shape[0], :] = block

    def store(kind, part, value):
        low = value.astype(BF16)
        if kind == 3:
            for owner in range(plan.outer * plan.inner):
                put(owner, 3 * thin, low)
            return
        blocks = low.reshape(per, thin, width)
        for i in range(per):
            owner = part * per + i if kind == 0 else i * plan.inner + part
            put(owner, kind * thin, blocks[i])

    return store


def first_kernel(plan, rank_ref, x_ref, bias_ref, source, *refs):
    out_ref, keep, (h_ref, acc_ref, vec_ref, tiles_ref, *weights, sems) = refs[0], refs[1:9], refs[9:]
    early, late = load_weights(plan, 0, source, weights, tiles_ref, sems)
    wait_all(early)
    sum_tiles(tiles_ref, vec_ref)
    wait_all(late)
    forward_layer(x_ref, bias_ref, vec_ref, weights, keep, (h_ref, acc_ref), out_ref)
    drop_shared(rank_ref, keep, bias_ref.shape[0])


def send_out(packed_ref, outs, sems):
    copies = [pltpu.make_async_copy(packed_ref.at[i], outs[i], sems.at[i]) for i in range(2)]
    for one in copies:
        one.start()
    wait_all(copies)


def last_kernel(plan, rank_ref, x_ref, bias_ref, goal_ref, source, *refs):
    out_ref, gx_ref, outs, keep, scratch = refs[0], refs[1], refs[2:4], refs[4:12], refs[12:22]
    g_ref, packed_ref, vec_ref, tiles_ref, *weights, sems = refs[22:]
    early, late = load_weights(plan, 1, source, weights, tiles_ref, sems)
    wait_all(early)
    sum_tiles(tiles_ref, vec_ref)
    wait_all(late)
    forward_layer(x_ref, bias_ref, vec_ref, weights, keep, (scratch[3], scratch[2]), out_ref)
    drop_shared(rank_ref, keep, bias_ref.shape[0])
    high = jnp.sum(vec_ref[12:13, :], axis=-1, keepdims=True)
    rest = jnp.sum(vec_ref[13:14, :], axis=-1, keepdims=True)
    loss_scale = float(plan.slots) / (high * 32.0 + rest)
    g_ref[...] = goal_ref[...].astype(F32) * loss_scale
    store = storer(plan, rank_ref, packed_ref)
    backward_layer(plan, g_ref, x_ref, vec_ref, weights, rank_ref, keep, scratch, gx_ref, store)
    send_out(packed_ref, outs, sems)


def back_kernel(plan, rank_ref, x_ref, g_ref, source, *refs):
    keep, gx_ref, outs, scratch = refs[0:8], refs[8], refs[9:11], refs[11:21]
    packed_ref, vec_ref, tiles_ref, *weights, sems = refs[21:]
    early, late = load_weights(plan, 0, source, weights, tiles_ref, sems)
    wait_all(early)
    sum_tiles(tiles_ref, vec_ref)
    wait_all(late)
    store = storer(plan, rank_ref, packed_ref)
    backward_layer(plan, g_ref, x_ref, vec_ref, weights, rank_ref, keep, scratch, gx_ref, store)
    send_out(packed_ref, outs, sems)


def place_kernel(rank_ref, own_ref, *refs):
    others, out_ref = refs[:-1], refs[-1]
    rows = own_ref.shape[0] // 2
    kept = out_ref.shape[1]
    mine = rank_ref[2] * 2 + rank_ref[3]
    out_ref[mine] = own_ref[0:rows, :].astype(F32)[:kept]
    for i, ref in enumerate(others):
        out_ref[mine ^ (i + 1)] = ref[...].astype(F32)[:kept]
    out_ref[out_ref.shape[0] - 1] = own_ref[rows : 2 * rows, :].astype(F32)[:kept]


def pack_kernel(slot_ref, own_ref, *refs):
    others, out_ref = refs[:-1], refs[-1]
    rows = own_ref.shape[0] // 2
    sources = [own_ref[0:rows, :]] + [ref[...] for ref in others] + [own_ref[rows : 2 * rows, :]]
    step = 256

    def body(index, carry):
        slots = lax.broadcasted_iota(jnp.int32, (step, rows), 0) + index * step
        total = None
        for i, values in enumerate(sources):
            picks = jnp.where(slots == slot_ref[i], 1.0, 0.0).astype(BF16)
            term = dot_nn(picks, values)
            total = term if total is None else total + term
        out_ref[block_rows(index, step), :] = total
        return carry

    lax.fori_loop(0, out_ref.shape[0] // step, body, 0)


VMEM = pl.BlockSpec(memory_space=pltpu.VMEM)
SMEM = pl.BlockSpec(memory_space=pltpu.SMEM)
ANY = pl.BlockSpec(memory_space=pl.ANY)


def call(kernel, operands, specs, outs, out_specs, scratch, flops):
    return pl.pallas_call(
        kernel,
        out_shape=[jax.ShapeDtypeStruct(shape, dtype) for shape, dtype in outs],
        in_specs=specs,
        out_specs=out_specs,
        scratch_shapes=scratch,
        compiler_params=pltpu.CompilerParams(vmem_limit_bytes=56 * 1024 * 1024),
        cost_estimate=pl.CostEstimate(flops=flops, bytes_accessed=8 << 20, transcendentals=0),
    )(*operands)


@dataclasses.dataclass(frozen=True)
class Plan:
    outer: int
    inner: int
    thin: int
    tile: int
    width: int
    slots: int

    @property
    def block(self):
        return 3 * self.thin + self.tile


def flip(array, mask, devices):
    return lax.ppermute(array, ("dp", "mp"), [(d, d ^ mask) for d in range(devices)])


def scatter_sum(kept, sent, devices):
    got = flip(sent, 1, devices)
    plane = {
        at: kept[at].astype(F32) + got[at].astype(F32) for at in ((0, 0), (0, 1), (1, 0), (1, 1))
    }
    total = plane[0, 0]
    for at, mask in (((1, 1), 6), ((0, 1), 2), ((1, 0), 4)):
        total = total + flip(plane[at].astype(BF16), mask, devices).astype(F32)
    result = total[0]
    for k in range(1, total.shape[0]):
        result = result + flip(total[k].astype(BF16), 8 * k, devices).astype(F32)
    return result


def shards(patches, targets, keep_mask, attn_weights, vectors, up_weights, down_weights):
    image_count, patch_rows, width = patches.shape
    layers = attn_weights.shape[0]
    dp_size, mp_size = lax.axis_size("dp"), lax.axis_size("mp")
    devices = dp_size * mp_size
    rank = lax.axis_index("mp")
    lane_rank = lax.axis_index("dp")
    device = lane_rank * mp_size + rank
    thin = attn_weights.shape[2]
    vec_rows = vectors.shape[1]
    parts = thin * devices // width
    assert image_count == mp_size + 1 and layers == 2 and parts == mp_size == 4
    direct = thin % 16 == 0
    images, tile = 2, 16
    rows = -(-patch_rows // 16) * 16
    total = images * rows
    block = 3 * thin + tile

    keep_rows = jnp.concatenate([jnp.ones((image_count, 2), jnp.int32), keep_mask], axis=1)
    keep_rows = jnp.pad(keep_rows, ((0, 0), (0, rows - patch_rows)))
    live = jnp.where(rank == 0, jnp.sum(keep_rows), 0)

    packed = []
    for layer in range(layers):
        piece = lax.dynamic_update_slice(
            jnp.zeros((tile * width,), BF16), vectors[layer], (device * vec_rows,)
        ).reshape(tile, width)
        if layer == layers - 1:
            row = lax.broadcasted_iota(jnp.int32, (tile, width), 0)
            here = lax.broadcasted_iota(jnp.int32, (tile, width), 1) == lane_rank
            piece = jnp.where(here & (row == 12), (live // 32).astype(BF16), piece)
            piece = jnp.where(here & (row == 13), (live % 32).astype(BF16), piece)
        packed += [attn_weights[layer].T, up_weights[layer], down_weights[layer].T, piece]
    whole = lax.all_gather(jnp.concatenate(packed, axis=0), ("dp", "mp"))
    if direct:
        plan = Plan(dp_size, mp_size, thin, tile, width, SLOTS * dp_size)
        source = whole.reshape(dp_size, mp_size, layers * block, width)
    else:
        plan = Plan(1, parts, width, tile, width, SLOTS * dp_size)
        pieces = []
        for layer in range(layers):
            mine_of = whole[:, layer * block : (layer + 1) * block]
            pieces.append(mine_of[:, :thin].reshape(parts, width, width))
            for kind in (1, 2):
                split = mine_of[:, kind * thin : (kind + 1) * thin]
                split = split.reshape(dp_size, mp_size, thin, width).transpose(1, 0, 2, 3)
                pieces.append(split.reshape(parts, width, width))
            summed = jnp.sum(mine_of[:, 3 * thin :].astype(F32), axis=0).astype(BF16)
            pieces.append(jnp.pad(summed[None], ((0, parts - 1), (0, 0), (0, 0))))
        source = jnp.concatenate(pieces, axis=1)[None]

    flat = keep_rows.reshape(-1)
    slot = jnp.where(flat == 1, jnp.cumsum(flat) - flat, SLOTS).reshape(image_count, 1, rows)

    def mine(array):
        return jnp.concatenate(
            [lax.dynamic_slice_in_dim(array, rank, 1, 0), array[mp_size:]], axis=0
        )

    def padded(array):
        return jnp.pad(mine(array), ((0, 0), (0, rows - patch_rows), (0, 0)))

    kept = mine(keep_rows)
    stream = padded(patches).reshape(total, width)
    bias = jnp.where(kept == 1, 0.0, MASKED).astype(F32)[:, None, :]
    goal = jnp.where((kept == 1)[:, :, None], padded(targets), 0).reshape(total, width)
    slots = jnp.concatenate(
        [lax.dynamic_slice_in_dim(slot, rank ^ k, 1, 0) for k in range(mp_size)] + [slot[mp_size:]],
        axis=0,
    )
    plane = (lane_rank // 2, lane_rank % 2) if direct else (0, 0)
    ranks = jnp.stack(
        [jnp.int32(k) for k in (*plane, rank // 2, rank % 2)] + [(rank == 0).astype(jnp.int32)]
    )

    pairs = width // (2 * HD)
    stream_shape = ((total, width), F32)
    low_shape = ((total, width), BF16)
    keep_shapes = [
        low_shape,
        ((3, total, width), BF16),
        ((images, pairs, 2 * rows, rows), BF16),
        low_shape,
        stream_shape,
        low_shape,
        ((parts, total, width), BF16),
        ((parts, total, width), F32),
    ]
    scratch_shapes = [
        low_shape,
        low_shape,
        stream_shape,
        stream_shape,
        stream_shape,
        low_shape,
        ((3, total, width), BF16),
        ((tile, width), F32),
        ((width, total), BF16),
        ((width, total), BF16),
    ]
    blocks = plan.outer * plan.inner
    weight_shapes = [
        ((tile, width), F32),
        ((blocks, tile, width), BF16),
        ((blocks, plan.thin, width), BF16),
        ((blocks, plan.thin, width), BF16),
        ((blocks, plan.thin, width), BF16),
    ]
    zs = max(blocks // 8, 1)
    half_shape = ((2, 2, zs, plan.block, width), BF16)
    packed_shape = ((2, 2, 2, zs, plan.block, width), BF16)
    sems = [pltpu.SemaphoreType.DMA((2 * (plan.outer + plan.inner),))]

    def vmem(shapes):
        return [pltpu.VMEM(shape, dtype) for shape, dtype in shapes]

    forward_flops = 8 * total * parts * width * width
    first = call(
        functools.partial(first_kernel, plan),
        (ranks, stream, bias, source),
        [SMEM, VMEM, VMEM, ANY],
        [stream_shape] + keep_shapes,
        [VMEM] * 9,
        vmem([stream_shape, stream_shape] + weight_shapes) + sems,
        forward_flops,
    )
    middle, saved = first[0], first[1:]
    output, grad_middle, *late_halves = call(
        functools.partial(last_kernel, plan),
        (ranks, middle, bias, goal, source),
        [SMEM, VMEM, VMEM, VMEM, ANY],
        [low_shape, stream_shape, half_shape, half_shape],
        [VMEM, VMEM, ANY, ANY],
        vmem(keep_shapes + scratch_shapes + [stream_shape, packed_shape] + weight_shapes) + sems,
        3 * forward_flops,
    )
    grad_first, *early_halves = call(
        functools.partial(back_kernel, plan),
        (ranks, stream, grad_middle, source, *saved),
        [SMEM, VMEM, VMEM, ANY] + [VMEM] * 8,
        [low_shape, half_shape, half_shape],
        [VMEM, ANY, ANY],
        vmem(scratch_shapes + [packed_shape] + weight_shapes) + sems,
        2 * forward_flops,
    )

    def owned_block(halves):
        if direct:
            return scatter_sum(*halves, devices)
        both = jnp.stack(halves)[:, 0, :, 0]
        both = jnp.stack([both[k % 2, k // 2] for k in range(parts)])
        both = jnp.stack([lax.dynamic_index_in_dim(both, rank ^ k, 0, False) for k in range(parts)])
        attn = both[:, :width].reshape(devices, thin, width)
        pieces = [attn]
        for kind in (1, 2):
            split = both[:, kind * width : (kind + 1) * width]
            split = split.reshape(mp_size, dp_size, thin, width).transpose(1, 0, 2, 3)
            pieces.append(split.reshape(devices, thin, width))
        pieces.append(jnp.broadcast_to(both[0, 3 * width :], (devices, tile, width)))
        summed = lax.psum_scatter(
            jnp.concatenate(pieces, axis=1), ("dp", "mp"), scatter_dimension=0, tiled=False
        )
        return summed.astype(F32)

    def outputs_of(halves):
        owned = owned_block(halves)
        vec = lax.dynamic_slice_in_dim(owned[3 * thin :].reshape(-1), device * vec_rows, vec_rows)
        return owned[:thin].T, vec, owned[thin : 2 * thin], owned[2 * thin : 3 * thin].T

    late = outputs_of(late_halves)
    early = outputs_of(early_halves)
    attn_grads, vector_grads, up_grads, down_grads = (
        jnp.stack([one, two]) for one, two in zip(early, late)
    )

    def others(array):
        return [flip(array[:rows], k, devices) for k in range(1, mp_size)]

    (activations,) = call(
        pack_kernel,
        (slots, output, *others(output)),
        [VMEM] * (mp_size + 1),
        [((SLOTS, width), F32)],
        [VMEM],
        [],
        2 * SLOTS * image_count * rows * width,
    )
    (input_grads,) = call(
        place_kernel,
        (ranks, grad_first, *others(grad_first)),
        [SMEM] + [VMEM] * mp_size,
        [((image_count, patch_rows, width), F32)],
        [VMEM],
        [],
        image_count * patch_rows * width,
    )
    return (activations, input_grads, attn_grads, vector_grads, up_grads, down_grads)


def solution(mesh):
    in_specs = (
        P("dp", None, None),
        P("dp", None, None),
        P("dp", None),
        P(None, None, ("dp", "mp")),
        P(None, ("dp", "mp")),
        P(None, "dp", "mp"),
        P(None, "mp", "dp"),
    )
    out_specs = (
        P("dp", None),
        P("dp", None, None),
        P(None, None, ("dp", "mp")),
        P(None, ("dp", "mp")),
        P(None, "dp", "mp"),
        P(None, "mp", "dp"),
    )
    return jax.shard_map(shards, mesh=mesh, in_specs=in_specs, out_specs=out_specs, check_vma=False)
```

```python
import dataclasses
import functools

import jax
import jax.numpy as jnp
from jax import lax
from jax.experimental import pallas as pl
from jax.experimental.pallas import tpu as pltpu
from jax.sharding import PartitionSpec as P

HD = 64
SLOTS = 1024
EPSILON = 1e-06
MASKED = -1e30
STEP = 16
UNROLL = 13

F32 = jnp.float32
BF16 = jnp.bfloat16


def dot_nn(left, right):
    return lax.dot_general(left, right, (((1,), (0,)), ((), ())), preferred_element_type=F32)


def dot_nt(left, right):
    return lax.dot_general(left, right, (((1,), (1,)), ((), ())), preferred_element_type=F32)


def dot_tn(left, right):
    return lax.dot_general(left, right, (((0,), (0,)), ((), ())), preferred_element_type=F32)


def block_rows(index, step):
    return pl.ds(pl.multiple_of(index * step, step), step)


def fold_rows(values):
    return jnp.sum(values.reshape(values.shape[0] // 8, 8, values.shape[1]), axis=0)


def low_halves(rows):
    lane = lax.broadcasted_iota(jnp.int32, (rows, 2 * HD), 1)
    return lane < HD


def stack_heads(pair):
    low = low_halves(pair.shape[0])
    zero = jnp.zeros_like(pair)
    return jnp.concatenate([jnp.where(low, pair, zero), jnp.where(low, zero, pair)], axis=0)


def unstack_heads(stacked):
    rows = stacked.shape[0] // 2
    return jnp.where(low_halves(rows), stacked[:rows], stacked[rows:])


def norm_rows(x_ref, out_ref, gain, shift):
    def body(index, carry):
        at = block_rows(index, STEP)
        values = x_ref[at, :].astype(F32)
        centred = values - jnp.mean(values, axis=-1, keepdims=True)
        variance = jnp.mean(centred * centred, axis=-1, keepdims=True)
        out_ref[at, :] = (centred * lax.rsqrt(variance + EPSILON) * gain + shift).astype(BF16)
        return carry

    lax.fori_loop(0, x_ref.shape[0] // STEP, body, 0, unroll=UNROLL)


def norm_back(x_ref, grad_ref, base_ref, out_ref, low_ref, gain, images):
    rows = x_ref.shape[0] // images
    width = x_ref.shape[1]
    sums = []
    for image in range(images):

        def body(index, carry, image=image):
            at = pl.ds(pl.multiple_of(image * rows + index * STEP, STEP), STEP)
            values = x_ref[at, :].astype(F32)
            grad = grad_ref[at, :]
            centred = values - jnp.mean(values, axis=-1, keepdims=True)
            variance = jnp.mean(centred * centred, axis=-1, keepdims=True)
            inverse = lax.rsqrt(variance + EPSILON)
            unit = centred * inverse
            scaled = grad * gain
            mean_one = jnp.mean(scaled, axis=-1, keepdims=True)
            mean_two = jnp.mean(scaled * unit, axis=-1, keepdims=True)
            out = base_ref[at, :] + inverse * (scaled - mean_one - unit * mean_two)
            out_ref[at, :] = out.astype(out_ref.dtype)
            if low_ref is not None:
                low_ref[at, :] = out.astype(BF16)
            return (
                carry[0] + fold_rows(grad * unit),
                carry[1] + fold_rows(grad),
                carry[2] + fold_rows(out),
            )

        zero = jnp.zeros((8, width), F32)
        sums.append(lax.fori_loop(0, rows // STEP, body, (zero, zero, zero), unroll=UNROLL))
    return sums


def weigh(sums, share):
    total = sums[0]
    for more in sums[1:]:
        total = total + more * share
    return jnp.sum(total, axis=0, keepdims=True)


def as_square(ref, part):
    rows, width = ref.shape[1:]
    per = width // rows
    return ref[pl.ds(part * per, per)].reshape(width, width)


def forward_attention(x_ref, bias_ref, vec_ref, attn_ref, keep, mid_ref):
    n1_ref, proj_ref, p_ref, att_ref = keep
    images = bias_ref.shape[0]
    rows = x_ref.shape[0] // images
    width = x_ref.shape[1]
    pairs = width // (2 * HD)
    scale = HD**-0.5

    norm_rows(x_ref, n1_ref, vec_ref[0:1, :], vec_ref[1:2, :])
    for part, bias_row in enumerate((4, None, 5)):
        value = dot_nt(n1_ref[...], as_square(attn_ref, part))
        if bias_row is not None:
            value = value + vec_ref[bias_row : bias_row + 1, :]
        proj_ref[part] = value.astype(BF16)

    def image_body(image, carry):
        at = block_rows(image, rows)
        for pair in range(pairs):
            lanes = slice(pair * 2 * HD, (pair + 1) * 2 * HD)
            query = stack_heads(proj_ref[0, at, lanes])
            scores = dot_nt(query, proj_ref[1, at, lanes]) * scale + bias_ref[image]
            top = jnp.max(scores, axis=-1, keepdims=True)
            powers = jnp.exp(scores - top)
            total = jnp.sum(powers, axis=-1, keepdims=True)
            probs = (powers * (1.0 / total)).astype(BF16)
            p_ref[image, pair] = probs
            att_ref[at, lanes] = unstack_heads(dot_nn(probs, proj_ref[2, at, lanes])).astype(BF16)
        return carry

    lax.fori_loop(0, images, image_body, 0)
    mid_ref[...] = x_ref[...].astype(F32) + dot_nt(att_ref[...], as_square(attn_ref, 3)) + vec_ref[6:7, :]


def forward_hidden(mid_ref, vec_ref, up_ref, down_ref, keep, scratch, out_ref):
    n2_ref, a_ref, gp_ref = keep
    h_ref, acc_ref = scratch
    norm_rows(mid_ref, n2_ref, vec_ref[2:3, :], vec_ref[3:4, :])
    acc_ref[...] = mid_ref[...] + vec_ref[11:12, :]

    def part_body(part, carry):
        h_ref[...] = dot_nn(n2_ref[...], as_square(up_ref, part))
        bias = vec_ref[pl.ds(7 + part, 1), :]

        def gelu_body(index, inner):
            at = block_rows(index, STEP)
            hidden = h_ref[at, :] + bias
            share = 0.5 + 0.5 * lax.erf(hidden * 0.7071067811865476)
            a_ref[part, at, :] = (hidden * share).astype(BF16)
            bell = jnp.exp(-0.5 * hidden * hidden) * 0.3989422804014327
            gp_ref[part, at, :] = (share + hidden * bell).astype(gp_ref.dtype)
            return inner

        lax.fori_loop(0, h_ref.shape[0] // STEP, gelu_body, 0, unroll=UNROLL)
        acc_ref[...] += dot_nt(a_ref[part], as_square(down_ref, part))
        return carry

    lax.fori_loop(0, a_ref.shape[0], part_body, 0)
    out_ref[...] = acc_ref[...].astype(out_ref.dtype)


def drop_shared(rank_ref, refs):
    @pl.when(rank_ref[4] == 0)
    def _():
        for ref in refs:
            rows = ref.shape[-2] // 2
            ref[..., rows:, :] = jnp.zeros((*ref.shape[:-2], rows, ref.shape[-1]), ref.dtype)


def backward_hidden(g_ref, mid_ref, vec_ref, up_ref, down_ref, share, keep, scratch, gm_ref, gvec_ref, store):
    n2_ref, a_ref, gp_ref = keep
    go_ref, gh_ref, acc_ref, h_ref, got_ref, n2t_ref = scratch
    images = 2
    rows = mid_ref.shape[0] // images
    width = mid_ref.shape[1]
    zero = jnp.zeros((8, width), F32)
    sums = []
    for image in range(images):

        def low_body(index, carry, image=image):
            at = pl.ds(pl.multiple_of(image * rows + index * STEP, STEP), STEP)
            grad = g_ref[at, :]
            go_ref[at, :] = grad.astype(BF16)
            return carry + fold_rows(grad)

        sums.append(lax.fori_loop(0, rows // STEP, low_body, zero, unroll=UNROLL))
    gvec_ref[11:12, :] = weigh(sums, share)
    acc_ref[...] = jnp.zeros_like(acc_ref)
    got_ref[...] = go_ref[...].T
    n2t_ref[...] = n2_ref[...].T

    def part_body(part, carry):
        store(2, part, dot_nn(got_ref[...], a_ref[part]))
        h_ref[...] = dot_nn(go_ref[...], as_square(down_ref, part))
        inner_sums = []
        for image in range(images):

            def hidden_body(index, inner, image=image):
                at = pl.ds(pl.multiple_of(image * rows + index * STEP, STEP), STEP)
                grad = (h_ref[at, :] * gp_ref[part, at, :].astype(F32)).astype(BF16)
                gh_ref[at, :] = grad
                return inner + fold_rows(grad.astype(F32))

            inner_sums.append(lax.fori_loop(0, rows // STEP, hidden_body, zero, unroll=UNROLL))
        gvec_ref[pl.ds(7 + part, 1), :] = weigh(inner_sums, share)
        store(1, part, dot_nn(n2t_ref[...], gh_ref[...]))
        acc_ref[...] += dot_nt(gh_ref[...], as_square(up_ref, part))
        return carry

    lax.fori_loop(0, a_ref.shape[0], part_body, 0)
    sums = norm_back(mid_ref, acc_ref, g_ref, gm_ref, None, vec_ref[2:3, :], images)
    for place, row in enumerate((2, 3, 6)):
        gvec_ref[row : row + 1, :] = weigh([one[place] for one in sums], share)


def backward_attention(gm_ref, x_ref, vec_ref, attn_ref, share, keep, scratch, gx_ref, gvec_ref, store):
    n1_ref, proj_ref, p_ref, att_ref = keep
    go_ref, acc_ref, ga_ref, dproj_ref = scratch
    images = p_ref.shape[0]
    rows = x_ref.shape[0] // images
    width = x_ref.shape[1]
    pairs = width // (2 * HD)
    scale = HD**-0.5
    go_ref[...] = gm_ref[...].astype(BF16)
    store(0, 3, dot_tn(go_ref[...], att_ref[...]))
    ga_ref[...] = dot_nn(go_ref[...], as_square(attn_ref, 3)).astype(BF16)

    def image_body(image, carry):
        at = block_rows(image, rows)
        for pair in range(pairs):
            lanes = slice(pair * 2 * HD, (pair + 1) * 2 * HD)
            query = stack_heads(proj_ref[0, at, lanes])
            keys = proj_ref[1, at, lanes]
            grad_out = stack_heads(ga_ref[at, lanes])
            probs = p_ref[image, pair]
            grad_probs = dot_nt(grad_out, proj_ref[2, at, lanes])
            dproj_ref[2, at, lanes] = dot_tn(probs, grad_out).astype(BF16)
            wide = probs.astype(F32)
            inner = jnp.sum(grad_probs * wide, axis=-1, keepdims=True)
            grad_scores = (wide * (grad_probs - inner)).astype(BF16)
            dproj_ref[0, at, lanes] = (unstack_heads(dot_nn(grad_scores, keys)) * scale).astype(BF16)
            dproj_ref[1, at, lanes] = (dot_tn(grad_scores, query) * scale).astype(BF16)
        return carry

    lax.fori_loop(0, images, image_body, 0)
    for part, row in enumerate((4, None, 5)):
        store(0, part, dot_tn(dproj_ref[part], n1_ref[...]))
        value = dot_nn(dproj_ref[part], as_square(attn_ref, part))
        if part == 0:
            acc_ref[...] = value
        else:
            acc_ref[...] += value
        if row is not None:
            sums = [
                fold_rows(dproj_ref[part, image * rows : (image + 1) * rows, :].astype(F32))
                for image in range(images)
            ]
            gvec_ref[row : row + 1, :] = weigh(sums, share)
    sums = norm_back(x_ref, acc_ref, gm_ref, gx_ref, None, vec_ref[0:1, :], images)
    for place, row in enumerate((0, 1)):
        gvec_ref[row : row + 1, :] = weigh([one[place] for one in sums], share)
    store(3, 0, gvec_ref[...])


def load_weights(plan, source, weights, tiles_ref, sems):
    attn_ref, up_ref, down_ref = weights
    thin, tile = plan.thin, plan.tile
    copies = []

    def copy(src, dst):
        copies.append(pltpu.make_async_copy(src, dst, sems.at[len(copies)]))

    for i in range(plan.outer):
        to = pl.ds(i * plan.inner, plan.inner)
        copy(source.at[i, :, pl.ds(0, thin)], attn_ref.at[to])
        copy(source.at[i, :, pl.ds(3 * thin, tile)], tiles_ref.at[to])
    first = len(copies)
    for m in range(plan.inner):
        to = pl.ds(m * plan.outer, plan.outer)
        copy(source.at[:, m, pl.ds(thin, thin)], up_ref.at[to])
        copy(source.at[:, m, pl.ds(2 * thin, thin)], down_ref.at[to])
    for one in copies:
        one.start()
    return copies[:first], copies[first:]


def wait_all(copies):
    for one in copies:
        one.wait()


def sum_tiles(tiles_ref, vec_ref):
    vec_ref[...] = jnp.sum(tiles_ref[...].astype(F32), axis=0)


def place_blocks(plan, rank_ref, pieces, put):
    if not plan.direct:
        for owner in range(plan.inner):
            put(owner, pieces[0][owner])
        return
    for i, piece in enumerate(pieces):
        c, x, y = i % 2, i // 2 % 2, i // 4
        low = ((rank_ref[1] ^ y) * 2 + (rank_ref[2] ^ x)) * 2 + (rank_ref[3] ^ c)
        for k in range(piece.shape[0]):
            put((rank_ref[0] ^ k) * 8 + low, piece[k])


def storer(plan, rank_ref, packed_ref, places):
    thin, width = plan.thin, plan.width
    per = width // thin

    def put(owner, row, block):
        c, x, y = owner % 2, owner // 2 % 2, owner // 4 % 2
        z = owner // 8
        at = (c ^ rank_ref[3], y ^ rank_ref[1], x ^ rank_ref[2], z ^ rank_ref[0])
        packed_ref[at[0], at[1], at[2], at[3], row : row + block.shape[0], :] = block

    def store(kind, part, value):
        low = value.astype(BF16)
        if kind == 3:
            for owner in range(plan.outer * plan.inner):
                put(owner, places[3], low)
            return
        blocks = low.reshape(per, thin, width)
        for i in range(per):
            owner = part * per + i if kind == 0 else i * plan.inner + part
            put(owner, places[kind], blocks[i])

    return store


def send_out(packed_ref, outs, sems):
    copies = [pltpu.make_async_copy(packed_ref.at[i], outs[i], sems.at[i]) for i in range(2)]
    for one in copies:
        one.start()
    wait_all(copies)


def attend_kernel(plan, pieces, rank_ref, x_ref, bias_ref, *refs):
    sources, (attn_ref, vec_ref, mid_ref, *keep) = refs[:pieces], refs[pieces:]
    thin = plan.thin
    vec_ref[...] = jnp.zeros_like(vec_ref)

    def put(owner, block):
        attn_ref[owner] = block[:thin]
        vec_ref[...] += block[thin : thin + plan.tile].astype(F32)

    place_blocks(plan, rank_ref, sources, put)
    forward_attention(x_ref, bias_ref, vec_ref, attn_ref, keep, mid_ref)
    drop_shared(rank_ref, (keep[0], keep[3]))


def hidden_kernel(plan, pieces, rank_ref, mid_ref, vec_ref, *refs):
    sources, (up_ref, down_ref, out_ref, n2_ref, a_ref, gp_ref, h_ref, acc_ref) = refs[:pieces], refs[pieces:]
    thin = plan.thin

    def put(owner, block):
        at = owner % plan.inner * plan.outer + owner // plan.inner
        up_ref[at] = block[:thin]
        down_ref[at] = block[thin : 2 * thin]

    place_blocks(plan, rank_ref, sources, put)
    forward_hidden(mid_ref, vec_ref, up_ref, down_ref, (n2_ref, a_ref, gp_ref), (h_ref, acc_ref), out_ref)
    drop_shared(rank_ref, (n2_ref, a_ref))


def last_kernel(plan, rank_ref, x_ref, bias_ref, goal_ref, source, *refs):
    out_ref, gx_ref, outs, refs = refs[0], refs[1], refs[2:4], refs[4:]
    attn_keep, hidden_keep, refs = refs[0:4], refs[4:7], refs[7:]
    mid_ref, g_ref, gm_ref, gvec_ref, go_ref, gh_ref, ga_ref, acc_ref, h_ref, got_ref, n2t_ref, dproj_ref = refs[:12]
    packed_ref, vec_ref, tiles_ref, attn_ref, up_ref, down_ref, sems = refs[12:]
    early, late = load_weights(plan, source, (attn_ref, up_ref, down_ref), tiles_ref, sems)
    wait_all(early)
    sum_tiles(tiles_ref, vec_ref)
    forward_attention(x_ref, bias_ref, vec_ref, attn_ref, attn_keep, mid_ref)
    wait_all(late)
    forward_hidden(mid_ref, vec_ref, up_ref, down_ref, hidden_keep, (h_ref, acc_ref), out_ref)
    drop_shared(rank_ref, (attn_keep[0], attn_keep[3], hidden_keep[0], hidden_keep[1]))
    high = jnp.sum(vec_ref[12:13, :], axis=-1, keepdims=True)
    rest = jnp.sum(vec_ref[13:14, :], axis=-1, keepdims=True)
    loss_scale = float(plan.slots) / (high * 32.0 + rest)
    g_ref[...] = goal_ref[...].astype(F32) * loss_scale
    gvec_ref[...] = jnp.zeros_like(gvec_ref)
    share = rank_ref[4].astype(F32)
    thin = plan.thin
    store = storer(plan, rank_ref, packed_ref, (0, thin, 2 * thin, 3 * thin))
    scratch = (go_ref, gh_ref, acc_ref, h_ref, got_ref, n2t_ref)
    backward_hidden(g_ref, mid_ref, vec_ref, up_ref, down_ref, share, hidden_keep, scratch, gm_ref, gvec_ref, store)
    scratch = (go_ref, acc_ref, ga_ref, dproj_ref)
    backward_attention(gm_ref, x_ref, vec_ref, attn_ref, share, attn_keep, scratch, gx_ref, gvec_ref, store)
    send_out(packed_ref, outs, sems)


def back_hidden_kernel(plan, rank_ref, g_ref, mid_ref, vec_ref, up_ref, down_ref, *refs):
    keep, gm_ref, gvec_ref, outs, scratch, (packed_ref, sems) = refs[:3], refs[3], refs[4], refs[5:7], refs[7:13], refs[13:]
    gvec_ref[...] = jnp.zeros_like(gvec_ref)
    share = rank_ref[4].astype(F32)
    store = storer(plan, rank_ref, packed_ref, (None, 0, plan.thin, None))
    backward_hidden(g_ref, mid_ref, vec_ref, up_ref, down_ref, share, keep, scratch, gm_ref, gvec_ref, store)
    send_out(packed_ref, outs, sems)


def back_attend_kernel(plan, rank_ref, gm_ref, x_ref, vec_ref, attn_ref, early_ref, *refs):
    keep, gx_ref, outs, scratch, (gvec_ref, packed_ref, sems) = refs[:4], refs[4], refs[5:7], refs[7:11], refs[11:]
    gvec_ref[...] = early_ref[...]
    share = rank_ref[4].astype(F32)
    store = storer(plan, rank_ref, packed_ref, (0, None, None, plan.thin))
    backward_attention(gm_ref, x_ref, vec_ref, attn_ref, share, keep, scratch, gx_ref, gvec_ref, store)
    send_out(packed_ref, outs, sems)


def finish_kernel(plan, terms, rank_ref, *refs):
    sources, (attn_out, vec_out, up_out, down_out, *tiles) = refs[: 3 * terms], refs[3 * terms :]
    thin, tile, width = plan.thin, plan.tile, plan.width

    def total(which, start, count):
        value = None
        for ref in sources[which * terms : (which + 1) * terms]:
            term = ref[start : start + count, :].astype(F32)
            value = term if value is None else value + term
        return value

    count = vec_out.shape[1]
    device = ((rank_ref[0] * 2 + rank_ref[1]) * 2 + rank_ref[2]) * 2 + rank_ref[3]
    for layer, (attn, hidden) in enumerate((((2, 0), (1, 0)), ((0, 0), (0, thin)))):
        tile_at = thin if layer == 0 else 3 * thin
        attn_out[layer] = total(attn[0], attn[1], thin).T
        up_out[layer] = total(hidden[0], hidden[1], thin)
        down_out[layer] = total(hidden[0], hidden[1] + thin, thin).T
        tiles[layer][...] = total(attn[0], tile_at, tile)
        row = device * count // width
        offset = device * count - row * width
        both = jnp.concatenate([tiles[layer][pl.ds(row, 1), :], tiles[layer][pl.ds(row + 1, 1), :]], axis=1)
        both = jnp.broadcast_to(both, (8, 2 * width))
        moved = pltpu.roll(both, 2 * width - offset, 1)
        vec_out[layer : layer + 1, :] = moved[0:1, :count]


def place_kernel(rank_ref, own_ref, *refs):
    others, out_ref = refs[:-1], refs[-1]
    rows = own_ref.shape[0] // 2
    kept = out_ref.shape[1]
    mine = rank_ref[2] * 2 + rank_ref[3]
    out_ref[mine] = own_ref[0:rows, :].astype(F32)[:kept]
    for i, ref in enumerate(others):
        out_ref[mine ^ (i + 1)] = ref[...].astype(F32)[:kept]
    out_ref[out_ref.shape[0] - 1] = own_ref[rows : 2 * rows, :].astype(F32)[:kept]


def pack_kernel(slot_ref, own_ref, *refs):
    others, out_ref = refs[:-1], refs[-1]
    rows = own_ref.shape[0] // 2
    sources = [own_ref[0:rows, :]] + [ref[...] for ref in others] + [own_ref[rows : 2 * rows, :]]
    step = 256

    def body(index, carry):
        slots = lax.broadcasted_iota(jnp.int32, (step, rows), 0) + index * step
        total = None
        for i, values in enumerate(sources):
            picks = jnp.where(slots == slot_ref[i], 1.0, 0.0).astype(BF16)
            term = dot_nn(picks, values)
            total = term if total is None else total + term
        out_ref[block_rows(index, step), :] = total
        return carry

    lax.fori_loop(0, out_ref.shape[0] // step, body, 0)


VMEM = pl.BlockSpec(memory_space=pltpu.VMEM)
SMEM = pl.BlockSpec(memory_space=pltpu.SMEM)
ANY = pl.BlockSpec(memory_space=pl.ANY)


def call(kernel, operands, specs, outs, out_specs, scratch, flops):
    return pl.pallas_call(
        kernel,
        out_shape=[jax.ShapeDtypeStruct(shape, dtype) for shape, dtype in outs],
        in_specs=specs,
        out_specs=out_specs,
        scratch_shapes=scratch,
        compiler_params=pltpu.CompilerParams(vmem_limit_bytes=56 * 1024 * 1024),
        cost_estimate=pl.CostEstimate(flops=flops, bytes_accessed=8 << 20, transcendentals=0),
    )(*operands)


@dataclasses.dataclass(frozen=True)
class Plan:
    outer: int
    inner: int
    thin: int
    tile: int
    width: int
    slots: int
    direct: bool


def flip(array, mask, devices):
    return lax.ppermute(array, ("dp", "mp"), [(d, d ^ mask) for d in range(devices)])


def gather_column(block, devices):
    column = [block] + [flip(block, 8 * k, devices) for k in range(1, devices // 8)]
    column = jnp.stack(column)
    return column


def gather_plane(column, devices):
    plane = [column] + [flip(column, mask, devices) for mask in (2, 4, 6)]
    pieces = []
    for piece in plane:
        pieces += [piece, flip(piece, 1, devices)]
    return pieces


PLANE = ((0, 0), (0, 1), (1, 0), (1, 1))


def sum_cores(halves, devices):
    kept, sent = halves
    got = flip(sent, 1, devices)
    sums = [kept[at].astype(F32) + got[at].astype(F32) for at in PLANE]
    return [sums[0]] + [one.astype(BF16) for one in sums[1:]]


def sum_plane(sums, devices):
    total = sums[0]
    for one, mask in zip(sums[1:], (2, 4, 6)):
        total = total + flip(one, mask, devices).astype(F32)
    return total


def sum_column(total, devices):
    return [total[0]] + [
        flip(total[k].astype(BF16), 8 * k, devices) for k in range(1, total.shape[0])
    ]


def shards(patches, targets, keep_mask, attn_weights, vectors, up_weights, down_weights):
    image_count, patch_rows, width = patches.shape
    layers = attn_weights.shape[0]
    dp_size, mp_size = lax.axis_size("dp"), lax.axis_size("mp")
    devices = dp_size * mp_size
    rank = lax.axis_index("mp")
    lane_rank = lax.axis_index("dp")
    device = lane_rank * mp_size + rank
    thin = attn_weights.shape[2]
    vec_rows = vectors.shape[1]
    parts = thin * devices // width
    assert image_count == mp_size + 1 and layers == 2 and parts == mp_size == 4
    direct = thin % 16 == 0
    images, tile = 2, 16
    rows = -(-patch_rows // 16) * 16
    total = images * rows

    keep_rows = jnp.concatenate([jnp.ones((image_count, 2), jnp.int32), keep_mask], axis=1)
    keep_rows = jnp.pad(keep_rows, ((0, 0), (0, rows - patch_rows)))
    live = jnp.where(rank == 0, jnp.sum(keep_rows), 0)

    tiles = []
    for layer in range(layers):
        piece = lax.dynamic_update_slice(
            jnp.zeros((tile * width,), BF16), vectors[layer], (device * vec_rows,)
        ).reshape(tile, width)
        if layer == layers - 1:
            row = lax.broadcasted_iota(jnp.int32, (tile, width), 0)
            here = lax.broadcasted_iota(jnp.int32, (tile, width), 1) == lane_rank
            piece = jnp.where(here & (row == 12), (live // 32).astype(BF16), piece)
            piece = jnp.where(here & (row == 13), (live % 32).astype(BF16), piece)
        tiles.append(piece)
    attn_block = jnp.concatenate([attn_weights[0].T, tiles[0]], axis=0)
    hidden_block = jnp.concatenate([up_weights[0], down_weights[0].T], axis=0)
    last_block = jnp.concatenate(
        [attn_weights[1].T, up_weights[1], down_weights[1].T, tiles[1]], axis=0
    )
    if direct:
        plan = Plan(dp_size, mp_size, thin, tile, width, SLOTS * dp_size, True)
        attn_column = gather_column(attn_block, devices)
        hidden_column = gather_column(hidden_block, devices)
        attn_pieces = gather_plane(attn_column, devices)
        hidden_pieces = gather_plane(hidden_column, devices)
        source = lax.all_gather(last_block, ("dp", "mp"))
        source = source.reshape(dp_size, mp_size, 3 * thin + tile, width)
    else:
        plan = Plan(1, parts, width, tile, width, SLOTS * dp_size, False)

        def squares(array):
            return array.reshape(parts, width, width)

        def by_part(array):
            split = array.reshape(dp_size, mp_size, thin, width).transpose(1, 0, 2, 3)
            return squares(split)

        def one_tile(array):
            summed = jnp.sum(array.astype(F32), axis=0).astype(BF16)
            return jnp.pad(summed[None], ((0, parts - 1), (0, 0), (0, 0)))

        attn_all, hidden_all, last_all = (
            lax.all_gather(one, ("dp", "mp")) for one in (attn_block, hidden_block, last_block)
        )
        attn_pieces = [
            jnp.concatenate([squares(attn_all[:, :thin]), one_tile(attn_all[:, thin:])], axis=1)
        ]
        hidden_pieces = [
            jnp.concatenate([by_part(hidden_all[:, :thin]), by_part(hidden_all[:, thin:])], axis=1)
        ]
        source = jnp.concatenate(
            [
                squares(last_all[:, :thin]),
                by_part(last_all[:, thin : 2 * thin]),
                by_part(last_all[:, 2 * thin : 3 * thin]),
                one_tile(last_all[:, 3 * thin :]),
            ],
            axis=1,
        )[None]

    flat = keep_rows.reshape(-1)
    slot = jnp.where(flat == 1, jnp.cumsum(flat) - flat, SLOTS).reshape(image_count, 1, rows)

    def mine(array):
        return jnp.concatenate(
            [lax.dynamic_slice_in_dim(array, rank, 1, 0), array[mp_size:]], axis=0
        )

    def padded(array):
        return jnp.pad(mine(array), ((0, 0), (0, rows - patch_rows), (0, 0)))

    kept = mine(keep_rows)
    stream = padded(patches).reshape(total, width)
    bias = jnp.where(kept == 1, 0.0, MASKED).astype(F32)[:, None, :]
    goal = jnp.where((kept == 1)[:, :, None], padded(targets), 0).reshape(total, width)
    slots = jnp.concatenate(
        [lax.dynamic_slice_in_dim(slot, rank ^ k, 1, 0) for k in range(mp_size)] + [slot[mp_size:]],
        axis=0,
    )
    plane = (lane_rank // 2, lane_rank % 2) if direct else (0, 0)
    ranks = jnp.stack(
        [jnp.int32(k) for k in (*plane, rank // 2, rank % 2)] + [(rank == 0).astype(jnp.int32)]
    )

    pairs = width // (2 * HD)
    stream_shape = ((total, width), F32)
    low_shape = ((total, width), BF16)
    three_shape = ((3, total, width), BF16)
    turned_shape = ((width, total), BF16)
    vec_shape = ((tile, width), F32)
    attn_keep = [low_shape, three_shape, ((images, pairs, 2 * rows, rows), BF16), low_shape]
    hidden_keep = [low_shape, ((parts, total, width), BF16), ((parts, total, width), F32)]
    blocks = plan.outer * plan.inner
    weight_shape = ((blocks, plan.thin, width), BF16)
    zs = max(blocks // 8, 1)

    def half(count):
        return ((2, 2, zs, count, width), BF16)

    def both(count):
        return ((2, 2, 2, zs, count, width), BF16)

    sems = [pltpu.SemaphoreType.DMA((2 * (plan.outer + plan.inner),))]

    def vmem(shapes):
        return [pltpu.VMEM(shape, dtype) for shape, dtype in shapes]

    layer_flops = 8 * total * parts * width * width
    attn_rows, hidden_rows = plan.thin + tile, 2 * plan.thin
    last_rows = attn_rows + hidden_rows

    attn_full, vec, mid, *attn_kept = call(
        functools.partial(attend_kernel, plan, len(attn_pieces)),
        (ranks, stream, bias, *attn_pieces),
        [SMEM] + [VMEM] * (2 + len(attn_pieces)),
        [weight_shape, vec_shape, stream_shape] + attn_keep,
        [VMEM] * 7,
        [],
        layer_flops // 2,
    )
    up_full, down_full, middle, *hidden_kept = call(
        functools.partial(hidden_kernel, plan, len(hidden_pieces)),
        (ranks, mid, vec, *hidden_pieces),
        [SMEM] + [VMEM] * (2 + len(hidden_pieces)),
        [weight_shape, weight_shape, stream_shape] + hidden_keep,
        [VMEM] * 6,
        vmem([stream_shape, stream_shape]),
        layer_flops,
    )
    output, grad_middle, *last_halves = call(
        functools.partial(last_kernel, plan),
        (ranks, middle, bias, goal, source),
        [SMEM, VMEM, VMEM, VMEM, ANY],
        [low_shape, stream_shape, half(last_rows), half(last_rows)],
        [VMEM, VMEM, ANY, ANY],
        vmem(
            attn_keep
            + hidden_keep
            + [stream_shape, stream_shape, stream_shape, vec_shape, low_shape, low_shape, low_shape]
            + [stream_shape, stream_shape, turned_shape, turned_shape, three_shape]
            + [both(last_rows), vec_shape, ((blocks, tile, width), BF16)]
            + [weight_shape] * 3
        )
        + sems,
        3 * layer_flops,
    )
    grad_mid, early_vec, *hidden_halves = call(
        functools.partial(back_hidden_kernel, plan),
        (ranks, grad_middle, mid, vec, up_full, down_full, *hidden_kept),
        [SMEM] + [VMEM] * 8,
        [stream_shape, vec_shape, half(hidden_rows), half(hidden_rows)],
        [VMEM, VMEM, ANY, ANY],
        vmem(
            [low_shape, low_shape, stream_shape, stream_shape, turned_shape, turned_shape]
            + [both(hidden_rows)]
        )
        + sems,
        2 * layer_flops,
    )
    if direct:
        last_sums = sum_cores(last_halves, devices)
        grad_mid, last_sums = lax.optimization_barrier((grad_mid, last_sums))
    grad_first, *attn_halves = call(
        functools.partial(back_attend_kernel, plan),
        (ranks, grad_mid, stream, vec, attn_full, early_vec, *attn_kept),
        [SMEM] + [VMEM] * 9,
        [low_shape, half(attn_rows), half(attn_rows)],
        [VMEM, ANY, ANY],
        vmem([low_shape, stream_shape, low_shape, three_shape, vec_shape, both(attn_rows)]) + sems,
        layer_flops,
    )

    if direct:
        hidden_sums = sum_cores(hidden_halves, devices)
        last_total = sum_plane(last_sums, devices)
        attn_sums = sum_cores(attn_halves, devices)
        hidden_total = sum_plane(hidden_sums, devices)
        last_terms = sum_column(last_total, devices)
        attn_total = sum_plane(attn_sums, devices)
        hidden_terms = sum_column(hidden_total, devices)
        attn_terms = sum_column(attn_total, devices)
        terms = (*last_terms, *hidden_terms, *attn_terms)
        attn_grads, vector_grads, up_grads, down_grads = call(
            functools.partial(finish_kernel, plan, len(last_terms)),
            (ranks, *terms),
            [SMEM] + [VMEM] * len(terms),
            [
                (attn_weights.shape, F32),
                (vectors.shape, F32),
                (up_weights.shape, F32),
                (down_weights.shape, F32),
            ],
            [VMEM] * 4,
            vmem([vec_shape, vec_shape]),
            1 << 20,
        )
    else:

        def square_blocks(halves):
            stacked = jnp.stack(halves)[:, 0, :, 0]
            stacked = jnp.stack([stacked[k % 2, k // 2] for k in range(parts)])
            return jnp.stack(
                [lax.dynamic_index_in_dim(stacked, rank ^ k, 0, False) for k in range(parts)]
            )

        def outputs_of(attn, up, down, tail):
            def by_owner(array):
                split = array.reshape(mp_size, dp_size, thin, width).transpose(1, 0, 2, 3)
                return split.reshape(devices, thin, width)

            pieces = [
                attn.reshape(devices, thin, width),
                by_owner(up),
                by_owner(down),
                jnp.broadcast_to(tail[0], (devices, tile, width)),
            ]
            owned = lax.psum_scatter(
                jnp.concatenate(pieces, axis=1), ("dp", "mp"), scatter_dimension=0, tiled=False
            ).astype(F32)
            own_vec = lax.dynamic_slice_in_dim(
                owned[3 * thin :].reshape(-1), device * vec_rows, vec_rows
            )
            return owned[:thin].T, own_vec, owned[thin : 2 * thin], owned[2 * thin : 3 * thin].T

        last_all = square_blocks(last_halves)
        attn_all, hidden_all = square_blocks(attn_halves), square_blocks(hidden_halves)
        late = outputs_of(
            last_all[:, :width],
            last_all[:, width : 2 * width],
            last_all[:, 2 * width : 3 * width],
            last_all[:, 3 * width :],
        )
        early = outputs_of(
            attn_all[:, :width], hidden_all[:, :width], hidden_all[:, width:], attn_all[:, width:]
        )
        attn_grads, vector_grads, up_grads, down_grads = (
            jnp.stack([one, two]) for one, two in zip(early, late)
        )

    def others(array):
        return [flip(array[:rows], k, devices) for k in range(1, mp_size)]

    (activations,) = call(
        pack_kernel,
        (slots, output, *others(output)),
        [VMEM] * (mp_size + 1),
        [((SLOTS, width), F32)],
        [VMEM],
        [],
        2 * SLOTS * image_count * rows * width,
    )
    (input_grads,) = call(
        place_kernel,
        (ranks, grad_first, *others(grad_first)),
        [SMEM] + [VMEM] * mp_size,
        [((image_count, patch_rows, width), F32)],
        [VMEM],
        [],
        image_count * patch_rows * width,
    )
    return (activations, input_grads, attn_grads, vector_grads, up_grads, down_grads)


def solution(mesh):
    in_specs = (
        P("dp", None, None),
        P("dp", None, None),
        P("dp", None),
        P(None, None, ("dp", "mp")),
        P(None, ("dp", "mp")),
        P(None, "dp", "mp"),
        P(None, "mp", "dp"),
    )
    out_specs = (
        P("dp", None),
        P("dp", None, None),
        P(None, None, ("dp", "mp")),
        P(None, ("dp", "mp")),
        P(None, "dp", "mp"),
        P(None, "mp", "dp"),
    )
    return jax.shard_map(shards, mesh=mesh, in_specs=in_specs, out_specs=out_specs, check_vma=False)
```

```python
import dataclasses
import functools

import jax
import jax.numpy as jnp
from jax import lax
from jax.experimental import pallas as pl
from jax.experimental.pallas import tpu as pltpu
from jax.sharding import PartitionSpec as P

HD = 64
SLOTS = 1024
EPSILON = 1e-06
MASKED = -1e30
STEP = 16
UNROLL = 13

F32 = jnp.float32
BF16 = jnp.bfloat16


def dot_nn(left, right):
    return lax.dot_general(left, right, (((1,), (0,)), ((), ())), preferred_element_type=F32)


def dot_nt(left, right):
    return lax.dot_general(left, right, (((1,), (1,)), ((), ())), preferred_element_type=F32)


def dot_tn(left, right):
    return lax.dot_general(left, right, (((0,), (0,)), ((), ())), preferred_element_type=F32)


def block_rows(index, step):
    return pl.ds(pl.multiple_of(index * step, step), step)


def fold_rows(values):
    return jnp.sum(values.reshape(values.shape[0] // 8, 8, values.shape[1]), axis=0)


def low_halves(rows):
    lane = lax.broadcasted_iota(jnp.int32, (rows, 2 * HD), 1)
    return lane < HD


def stack_heads(pair):
    low = low_halves(pair.shape[0])
    zero = jnp.zeros_like(pair)
    return jnp.concatenate([jnp.where(low, pair, zero), jnp.where(low, zero, pair)], axis=0)


def unstack_heads(stacked):
    rows = stacked.shape[0] // 2
    return jnp.where(low_halves(rows), stacked[:rows], stacked[rows:])


def norm_rows(x_ref, out_ref, gain, shift):
    def body(index, carry):
        at = block_rows(index, STEP)
        values = x_ref[at, :].astype(F32)
        centred = values - jnp.mean(values, axis=-1, keepdims=True)
        variance = jnp.mean(centred * centred, axis=-1, keepdims=True)
        out_ref[at, :] = (centred * lax.rsqrt(variance + EPSILON) * gain + shift).astype(BF16)
        return carry

    lax.fori_loop(0, x_ref.shape[0] // STEP, body, 0, unroll=UNROLL)


def norm_back(x_ref, grad_ref, base_ref, out_ref, low_ref, gain, images):
    rows = x_ref.shape[0] // images
    width = x_ref.shape[1]
    sums = []
    for image in range(images):

        def body(index, carry, image=image):
            at = pl.ds(pl.multiple_of(image * rows + index * STEP, STEP), STEP)
            values = x_ref[at, :].astype(F32)
            grad = grad_ref[at, :]
            centred = values - jnp.mean(values, axis=-1, keepdims=True)
            variance = jnp.mean(centred * centred, axis=-1, keepdims=True)
            inverse = lax.rsqrt(variance + EPSILON)
            unit = centred * inverse
            scaled = grad * gain
            mean_one = jnp.mean(scaled, axis=-1, keepdims=True)
            mean_two = jnp.mean(scaled * unit, axis=-1, keepdims=True)
            out = base_ref[at, :] + inverse * (scaled - mean_one - unit * mean_two)
            out_ref[at, :] = out.astype(out_ref.dtype)
            if low_ref is not None:
                low_ref[at, :] = out.astype(BF16)
            return (
                carry[0] + fold_rows(grad * unit),
                carry[1] + fold_rows(grad),
                carry[2] + fold_rows(out),
            )

        zero = jnp.zeros((8, width), F32)
        sums.append(lax.fori_loop(0, rows // STEP, body, (zero, zero, zero), unroll=UNROLL))
    return sums


def weigh(sums, share):
    total = sums[0]
    for more in sums[1:]:
        total = total + more * share
    return jnp.sum(total, axis=0, keepdims=True)


def as_square(ref, part):
    rows, width = ref.shape[1:]
    per = width // rows
    return ref[pl.ds(part * per, per)].reshape(width, width)


def forward_attention(x_ref, bias_ref, vec_ref, attn_ref, keep, mid_ref):
    n1_ref, proj_ref, p_ref, att_ref = keep
    images = bias_ref.shape[0]
    rows = x_ref.shape[0] // images
    width = x_ref.shape[1]
    pairs = width // (2 * HD)
    scale = HD**-0.5

    norm_rows(x_ref, n1_ref, vec_ref[0:1, :], vec_ref[1:2, :])
    for part, bias_row in enumerate((4, None, 5)):
        value = dot_nt(n1_ref[...], as_square(attn_ref, part))
        if bias_row is not None:
            value = value + vec_ref[bias_row : bias_row + 1, :]
        proj_ref[part] = value.astype(BF16)

    def image_body(image, carry):
        at = block_rows(image, rows)
        for pair in range(pairs):
            lanes = slice(pair * 2 * HD, (pair + 1) * 2 * HD)
            query = stack_heads(proj_ref[0, at, lanes])
            scores = dot_nt(query, proj_ref[1, at, lanes]) * scale + bias_ref[image]
            top = jnp.max(scores, axis=-1, keepdims=True)
            powers = jnp.exp(scores - top)
            total = jnp.sum(powers, axis=-1, keepdims=True)
            probs = (powers * (1.0 / total)).astype(BF16)
            p_ref[image, pair] = probs
            att_ref[at, lanes] = unstack_heads(dot_nn(probs, proj_ref[2, at, lanes])).astype(BF16)
        return carry

    lax.fori_loop(0, images, image_body, 0)
    mid_ref[...] = x_ref[...].astype(F32) + dot_nt(att_ref[...], as_square(attn_ref, 3)) + vec_ref[6:7, :]


def forward_hidden(mid_ref, vec_ref, up_ref, down_ref, keep, scratch, out_ref):
    n2_ref, a_ref, gp_ref = keep
    h_ref, acc_ref = scratch
    norm_rows(mid_ref, n2_ref, vec_ref[2:3, :], vec_ref[3:4, :])
    acc_ref[...] = mid_ref[...] + vec_ref[11:12, :]

    def part_body(part, carry):
        h_ref[...] = dot_nn(n2_ref[...], as_square(up_ref, part))
        bias = vec_ref[pl.ds(7 + part, 1), :]

        def gelu_body(index, inner):
            at = block_rows(index, STEP)
            hidden = h_ref[at, :] + bias
            share = 0.5 + 0.5 * lax.erf(hidden * 0.7071067811865476)
            a_ref[part, at, :] = (hidden * share).astype(BF16)
            bell = jnp.exp(-0.5 * hidden * hidden) * 0.3989422804014327
            gp_ref[part, at, :] = (share + hidden * bell).astype(gp_ref.dtype)
            return inner

        lax.fori_loop(0, h_ref.shape[0] // STEP, gelu_body, 0, unroll=UNROLL)
        acc_ref[...] += dot_nt(a_ref[part], as_square(down_ref, part))
        return carry

    lax.fori_loop(0, a_ref.shape[0], part_body, 0)
    out_ref[...] = acc_ref[...].astype(out_ref.dtype)


def drop_shared(refs):
    @pl.when(jnp.logical_not(counts_shared()))
    def _():
        for ref in refs:
            rows = ref.shape[-2] // 2
            ref[..., rows:, :] = jnp.zeros((*ref.shape[:-2], rows, ref.shape[-1]), ref.dtype)


def backward_hidden(g_ref, mid_ref, vec_ref, up_ref, down_ref, share, keep, scratch, gm_ref, gvec_ref, store):
    n2_ref, a_ref, gp_ref = keep
    go_ref, gh_ref, acc_ref, h_ref, got_ref, n2t_ref = scratch
    images = 2
    rows = mid_ref.shape[0] // images
    width = mid_ref.shape[1]
    zero = jnp.zeros((8, width), F32)
    sums = []
    for image in range(images):

        def low_body(index, carry, image=image):
            at = pl.ds(pl.multiple_of(image * rows + index * STEP, STEP), STEP)
            grad = g_ref[at, :]
            go_ref[at, :] = grad.astype(BF16)
            return carry + fold_rows(grad)

        sums.append(lax.fori_loop(0, rows // STEP, low_body, zero, unroll=UNROLL))
    gvec_ref[11:12, :] = weigh(sums, share)
    acc_ref[...] = jnp.zeros_like(acc_ref)
    got_ref[...] = go_ref[...].T
    n2t_ref[...] = n2_ref[...].T

    def part_body(part, carry):
        store(2, part, dot_nn(got_ref[...], a_ref[part]))
        h_ref[...] = dot_nn(go_ref[...], as_square(down_ref, part))
        inner_sums = []
        for image in range(images):

            def hidden_body(index, inner, image=image):
                at = pl.ds(pl.multiple_of(image * rows + index * STEP, STEP), STEP)
                grad = (h_ref[at, :] * gp_ref[part, at, :].astype(F32)).astype(BF16)
                gh_ref[at, :] = grad
                return inner + fold_rows(grad.astype(F32))

            inner_sums.append(lax.fori_loop(0, rows // STEP, hidden_body, zero, unroll=UNROLL))
        gvec_ref[pl.ds(7 + part, 1), :] = weigh(inner_sums, share)
        store(1, part, dot_nn(n2t_ref[...], gh_ref[...]))
        acc_ref[...] += dot_nt(gh_ref[...], as_square(up_ref, part))
        return carry

    lax.fori_loop(0, a_ref.shape[0], part_body, 0)
    sums = norm_back(mid_ref, acc_ref, g_ref, gm_ref, None, vec_ref[2:3, :], images)
    for place, row in enumerate((2, 3, 6)):
        gvec_ref[row : row + 1, :] = weigh([one[place] for one in sums], share)


def backward_attention(gm_ref, x_ref, vec_ref, attn_ref, share, keep, scratch, gx_ref, gvec_ref, store):
    n1_ref, proj_ref, p_ref, att_ref = keep
    go_ref, acc_ref, ga_ref, dproj_ref = scratch
    images = p_ref.shape[0]
    rows = x_ref.shape[0] // images
    width = x_ref.shape[1]
    pairs = width // (2 * HD)
    scale = HD**-0.5
    go_ref[...] = gm_ref[...].astype(BF16)
    store(0, 3, dot_tn(go_ref[...], att_ref[...]))
    ga_ref[...] = dot_nn(go_ref[...], as_square(attn_ref, 3)).astype(BF16)

    def image_body(image, carry):
        at = block_rows(image, rows)
        for pair in range(pairs):
            lanes = slice(pair * 2 * HD, (pair + 1) * 2 * HD)
            query = stack_heads(proj_ref[0, at, lanes])
            keys = proj_ref[1, at, lanes]
            grad_out = stack_heads(ga_ref[at, lanes])
            probs = p_ref[image, pair]
            grad_probs = dot_nt(grad_out, proj_ref[2, at, lanes])
            dproj_ref[2, at, lanes] = dot_tn(probs, grad_out).astype(BF16)
            wide = probs.astype(F32)
            inner = jnp.sum(grad_probs * wide, axis=-1, keepdims=True)
            grad_scores = (wide * (grad_probs - inner)).astype(BF16)
            dproj_ref[0, at, lanes] = (unstack_heads(dot_nn(grad_scores, keys)) * scale).astype(BF16)
            dproj_ref[1, at, lanes] = (dot_tn(grad_scores, query) * scale).astype(BF16)
        return carry

    lax.fori_loop(0, images, image_body, 0)
    for part, row in enumerate((4, None, 5)):
        store(0, part, dot_tn(dproj_ref[part], n1_ref[...]))
        value = dot_nn(dproj_ref[part], as_square(attn_ref, part))
        if part == 0:
            acc_ref[...] = value
        else:
            acc_ref[...] += value
        if row is not None:
            sums = [
                fold_rows(dproj_ref[part, image * rows : (image + 1) * rows, :].astype(F32))
                for image in range(images)
            ]
            gvec_ref[row : row + 1, :] = weigh(sums, share)
    sums = norm_back(x_ref, acc_ref, gm_ref, gx_ref, None, vec_ref[0:1, :], images)
    for place, row in enumerate((0, 1)):
        gvec_ref[row : row + 1, :] = weigh([one[place] for one in sums], share)
    store(3, 0, gvec_ref[...])


def load_weights(plan, source, weights, tiles_ref, sems):
    attn_ref, up_ref, down_ref = weights
    thin, tile = plan.thin, plan.tile
    copies = []

    def copy(src, dst):
        copies.append(pltpu.make_async_copy(src, dst, sems.at[len(copies)]))

    for i in range(plan.outer):
        to = pl.ds(i * plan.inner, plan.inner)
        copy(source.at[i, :, pl.ds(0, thin)], attn_ref.at[to])
        copy(source.at[i, :, pl.ds(3 * thin, tile)], tiles_ref.at[to])
    first = len(copies)
    for m in range(plan.inner):
        to = pl.ds(m * plan.outer, plan.outer)
        copy(source.at[:, m, pl.ds(thin, thin)], up_ref.at[to])
        copy(source.at[:, m, pl.ds(2 * thin, thin)], down_ref.at[to])
    for one in copies:
        one.start()
    return copies[:first], copies[first:]


def wait_all(copies):
    for one in copies:
        one.wait()


def sum_tiles(tiles_ref, vec_ref):
    vec_ref[...] = jnp.sum(tiles_ref[...].astype(F32), axis=0)


def coordinates(plan):
    outer, inner = lax.axis_index("dp"), lax.axis_index("mp")
    here = (inner // 2, inner % 2)
    return (outer // 2, outer % 2, *here) if plan.direct else (0, 0, *here)


def counts_shared():
    return lax.axis_index("mp") == 0


def place_blocks(plan, pieces, put):
    if not plan.direct:
        for owner in range(plan.inner):
            put(owner, pieces[0][owner])
        return
    at = coordinates(plan)
    for i, piece in enumerate(pieces):
        c, x, y = i % 2, i // 2 % 2, i // 4
        low = ((at[1] ^ y) * 2 + (at[2] ^ x)) * 2 + (at[3] ^ c)
        for k in range(piece.shape[0]):
            put((at[0] ^ k) * 8 + low, piece[k])


def storer(plan, packed_ref, places, relative=True):
    thin, width = plan.thin, plan.width
    per = width // thin
    here = coordinates(plan)
    if not relative:
        here = (0, 0, 0, here[3])

    def put(owner, row, block):
        c, x, y = owner % 2, owner // 2 % 2, owner // 4 % 2
        z = owner // 8
        packed_ref[c ^ here[3], y ^ here[1], x ^ here[2], z ^ here[0], row : row + block.shape[0], :] = block

    def store(kind, part, value):
        low = value.astype(BF16)
        if kind == 3:
            for owner in range(plan.outer * plan.inner):
                put(owner, places[3], low)
            return
        blocks = low.reshape(per, thin, width)
        for i in range(per):
            owner = part * per + i if kind == 0 else i * plan.inner + part
            put(owner, places[kind], blocks[i])

    return store


def send_out(packed_ref, outs, sems):
    copies = [pltpu.make_async_copy(packed_ref.at[i], outs[i], sems.at[i]) for i in range(2)]
    for one in copies:
        one.start()
    wait_all(copies)


def prepare_kernel(plan, attn_ref, up_ref, down_ref, vec_ref, keep_ref, first_ref, last_ref, line_ref):
    thin, tile, width = plan.thin, plan.tile, plan.width
    count = vec_ref.shape[1]
    device = lax.axis_index("dp") * plan.inner + lax.axis_index("mp")
    row_at = device * count // width
    offset = device * count - row_at * width
    kept = jnp.sum(keep_ref[...]) + 2 * keep_ref.shape[0]
    kept = jnp.where(counts_shared(), kept, 0)
    row = lax.broadcasted_iota(jnp.int32, (tile, width), 0)
    here = lax.broadcasted_iota(jnp.int32, (tile, width), 1) == lax.axis_index("dp")
    for layer, out_ref in enumerate((first_ref, last_ref)):
        out_ref[0:thin, :] = attn_ref[layer]
        out_ref[thin : 2 * thin, :] = up_ref[layer]
        out_ref[2 * thin : 3 * thin, :] = down_ref[layer]
        line_ref[...] = jnp.zeros_like(line_ref)
        line_ref[0:1, 0:count] = vec_ref[layer : layer + 1, :].astype(F32)
        moved = pltpu.roll(line_ref[...], offset, 1)[0:1]
        piece = jnp.where(row == row_at, moved[:, :width], 0.0)
        piece = jnp.where(row == row_at + 1, moved[:, width:], piece)
        if layer == 1:
            piece = jnp.where(here & (row == 12), (kept >> 5).astype(F32), piece)
            piece = jnp.where(here & (row == 13), (kept & 31).astype(F32), piece)
        out_ref[3 * thin :, :] = piece.astype(BF16)


def first_kernel(plan, pieces, x_ref, bias_ref, *refs):
    sources, refs = refs[:pieces], refs[pieces:]
    attn_ref, up_ref, down_ref, vec_ref, mid_ref, out_ref, *refs = refs
    attn_keep, hidden_keep, (h_ref, acc_ref) = refs[:4], refs[4:7], refs[7:]
    thin = plan.thin
    vec_ref[...] = jnp.zeros_like(vec_ref)

    def put(owner, block):
        at = owner % plan.inner * plan.outer + owner // plan.inner
        attn_ref[owner] = block[:thin]
        up_ref[at] = block[thin : 2 * thin]
        down_ref[at] = block[2 * thin : 3 * thin]
        vec_ref[...] += block[3 * thin : 3 * thin + plan.tile].astype(F32)

    place_blocks(plan, sources, put)
    forward_attention(x_ref, bias_ref, vec_ref, attn_ref, attn_keep, mid_ref)
    forward_hidden(mid_ref, vec_ref, up_ref, down_ref, hidden_keep, (h_ref, acc_ref), out_ref)
    drop_shared((attn_keep[0], attn_keep[3], hidden_keep[0], hidden_keep[1]))


def last_kernel(plan, x_ref, bias_ref, goal_ref, source, *refs):
    out_ref, gx_ref, outs, refs = refs[0], refs[1], refs[2:4], refs[4:]
    attn_keep, hidden_keep, refs = refs[0:4], refs[4:7], refs[7:]
    mid_ref, g_ref, gm_ref, gvec_ref, go_ref, gh_ref, ga_ref, acc_ref, h_ref, got_ref, n2t_ref, dproj_ref = refs[:12]
    packed_ref, vec_ref, tiles_ref, attn_ref, up_ref, down_ref, sems = refs[12:]
    early, late = load_weights(plan, source, (attn_ref, up_ref, down_ref), tiles_ref, sems)
    wait_all(early)
    sum_tiles(tiles_ref, vec_ref)
    forward_attention(x_ref, bias_ref, vec_ref, attn_ref, attn_keep, mid_ref)
    wait_all(late)
    forward_hidden(mid_ref, vec_ref, up_ref, down_ref, hidden_keep, (h_ref, acc_ref), out_ref)
    drop_shared((attn_keep[0], attn_keep[3], hidden_keep[0], hidden_keep[1]))
    high = jnp.sum(vec_ref[12:13, :], axis=-1, keepdims=True)
    rest = jnp.sum(vec_ref[13:14, :], axis=-1, keepdims=True)
    loss_scale = float(plan.slots) / (high * 32.0 + rest)
    g_ref[...] = goal_ref[...].astype(F32) * loss_scale
    gvec_ref[...] = jnp.zeros_like(gvec_ref)
    share = counts_shared().astype(F32)
    thin = plan.thin
    store = storer(plan, packed_ref, (0, thin, 2 * thin, 3 * thin))
    scratch = (go_ref, gh_ref, acc_ref, h_ref, got_ref, n2t_ref)
    backward_hidden(g_ref, mid_ref, vec_ref, up_ref, down_ref, share, hidden_keep, scratch, gm_ref, gvec_ref, store)
    scratch = (go_ref, acc_ref, ga_ref, dproj_ref)
    backward_attention(gm_ref, x_ref, vec_ref, attn_ref, share, attn_keep, scratch, gx_ref, gvec_ref, store)
    send_out(packed_ref, outs, sems)


def back_hidden_kernel(plan, g_ref, mid_ref, vec_ref, up_ref, down_ref, *refs):
    keep, gm_ref, gvec_ref, outs, scratch, (packed_ref, sems) = refs[:3], refs[3], refs[4], refs[5:7], refs[7:13], refs[13:]
    gvec_ref[...] = jnp.zeros_like(gvec_ref)
    share = counts_shared().astype(F32)
    store = storer(plan, packed_ref, (None, 0, plan.thin, None))
    backward_hidden(g_ref, mid_ref, vec_ref, up_ref, down_ref, share, keep, scratch, gm_ref, gvec_ref, store)
    send_out(packed_ref, outs, sems)


def back_attend_kernel(plan, gm_ref, x_ref, vec_ref, attn_ref, early_ref, *refs):
    keep, gx_ref, outs, scratch, (gvec_ref, packed_ref, sems) = refs[:4], refs[4], refs[5:7], refs[7:11], refs[11:]
    gvec_ref[...] = early_ref[...]
    share = counts_shared().astype(F32)
    store = storer(plan, packed_ref, (0, None, None, plan.thin), not plan.direct)
    backward_attention(gm_ref, x_ref, vec_ref, attn_ref, share, keep, scratch, gx_ref, gvec_ref, store)
    send_out(packed_ref, outs, sems)


def finish_kernel(plan, counts, *refs):
    sources, (attn_out, vec_out, up_out, down_out, *tiles) = refs[: sum(counts)], refs[sum(counts) :]
    thin, tile, width = plan.thin, plan.tile, plan.width

    def total(which, start, count):
        value = None
        first = sum(counts[:which])
        for ref in sources[first : first + counts[which]]:
            blocks = [ref[start : start + count, :]] if len(ref.shape) == 2 else [
                ref[k, start : start + count, :] for k in range(ref.shape[0])
            ]
            for block in blocks:
                term = block.astype(F32)
                value = term if value is None else value + term
        return value

    count = vec_out.shape[1]
    device = lax.axis_index("dp") * plan.inner + lax.axis_index("mp")
    row = device * count // width
    offset = device * count - row * width
    for layer, (attn, hidden) in enumerate((((2, 0), (1, 0)), ((0, 0), (0, thin)))):
        tile_at = thin if layer == 0 else 3 * thin
        attn_out[layer] = total(attn[0], attn[1], thin)
        up_out[layer] = total(hidden[0], hidden[1], thin)
        down_out[layer] = total(hidden[0], hidden[1] + thin, thin)
        tiles[layer][...] = total(attn[0], tile_at, tile)
        both = jnp.concatenate(
            [tiles[layer][pl.ds(row, 1), :], tiles[layer][pl.ds(row + 1, 1), :]], axis=1
        )
        both = jnp.broadcast_to(both, (8, 2 * width))
        moved = pltpu.roll(both, 2 * width - offset, 1)
        vec_out[layer : layer + 1, :] = moved[0:1, :count]


def place_kernel(own_ref, *refs):
    others, out_ref = refs[:-1], refs[-1]
    rows = own_ref.shape[0] // 2
    kept = out_ref.shape[1]
    mine = lax.axis_index("mp")
    out_ref[mine] = own_ref[0:rows, :].astype(F32)[:kept]
    for i, ref in enumerate(others):
        out_ref[mine ^ (i + 1)] = ref[...].astype(F32)[:kept]
    out_ref[out_ref.shape[0] - 1] = own_ref[rows : 2 * rows, :].astype(F32)[:kept]


def pack_kernel(slot_ref, own_ref, *refs):
    others, out_ref = refs[:-1], refs[-1]
    rows = own_ref.shape[0] // 2
    sources = [own_ref[0:rows, :]] + [ref[...] for ref in others] + [own_ref[rows : 2 * rows, :]]
    step = 256

    def body(index, carry):
        slots = lax.broadcasted_iota(jnp.int32, (step, rows), 0) + index * step
        total = None
        for i, values in enumerate(sources):
            picks = jnp.where(slots == slot_ref[i], 1.0, 0.0).astype(BF16)
            term = dot_nn(picks, values)
            total = term if total is None else total + term
        out_ref[block_rows(index, step), :] = total
        return carry

    lax.fori_loop(0, out_ref.shape[0] // step, body, 0)


VMEM = pl.BlockSpec(memory_space=pltpu.VMEM)
ANY = pl.BlockSpec(memory_space=pl.ANY)


def call(kernel, operands, specs, outs, out_specs, scratch, flops):
    return pl.pallas_call(
        kernel,
        out_shape=[jax.ShapeDtypeStruct(shape, dtype) for shape, dtype in outs],
        in_specs=specs,
        out_specs=out_specs,
        scratch_shapes=scratch,
        compiler_params=pltpu.CompilerParams(vmem_limit_bytes=56 * 1024 * 1024),
        cost_estimate=pl.CostEstimate(flops=flops, bytes_accessed=8 << 20, transcendentals=0),
    )(*operands)


@dataclasses.dataclass(frozen=True)
class Plan:
    outer: int
    inner: int
    thin: int
    tile: int
    width: int
    slots: int
    direct: bool


def flip(array, mask, devices):
    return lax.ppermute(array, ("dp", "mp"), [(d, d ^ mask) for d in range(devices)])


def gather_column(block, devices):
    column = [block] + [flip(block, 8 * k, devices) for k in range(1, devices // 8)]
    column = jnp.stack(column)
    return column


def gather_plane(column, devices):
    plane = [column] + [flip(column, mask, devices) for mask in (2, 4, 6)]
    pieces = []
    for piece in plane:
        pieces += [piece, flip(piece, 1, devices)]
    return pieces


PLANE = ((0, 0), (0, 1), (1, 0), (1, 1))


def sum_cores(halves, devices):
    kept, sent = halves
    got = flip(sent, 1, devices)
    sums = [kept[at].astype(F32) + got[at].astype(F32) for at in PLANE]
    return [sums[0]] + [one.astype(BF16) for one in sums[1:]]


def sum_plane(sums, devices):
    total = sums[0]
    for one, mask in zip(sums[1:], (2, 4, 6)):
        total = total + flip(one, mask, devices).astype(F32)
    return total


def sum_column(total, devices):
    return [total[0]] + [
        flip(total[k].astype(BF16), 8 * k, devices) for k in range(1, total.shape[0])
    ]


def sum_by_groups(halves, devices):
    kept, sent = halves
    total = kept.astype(F32) + flip(sent, 1, devices).astype(F32)
    zs = total.shape[2]
    planes = [[8 * z + 2 * at + c for at in range(4)] for z in range(zs) for c in range(2)]
    columns = [[8 * z + at for z in range(zs)] for at in range(8)]
    total = total.reshape(4, *total.shape[2:]).astype(BF16)
    got = lax.all_to_all(total, ("dp", "mp"), 0, 0, axis_index_groups=planes, tiled=True)
    total = sum(got[k].astype(F32) for k in range(4)).astype(BF16)
    if zs == 1:
        return [total]
    return [lax.all_to_all(total, ("dp", "mp"), 0, 0, axis_index_groups=columns, tiled=True)]


def shards(patches, targets, keep_mask, attn_weights, vectors, up_weights, down_weights):
    image_count, patch_rows, width = patches.shape
    layers = attn_weights.shape[0]
    dp_size, mp_size = lax.axis_size("dp"), lax.axis_size("mp")
    devices = dp_size * mp_size
    rank = lax.axis_index("mp")
    lane_rank = lax.axis_index("dp")
    device = lane_rank * mp_size + rank
    thin = attn_weights.shape[2]
    vec_rows = vectors.shape[1]
    parts = thin * devices // width
    assert image_count == mp_size + 1 and layers == 2 and parts == mp_size == 4
    direct = thin % 16 == 0
    images, tile = 2, 16
    rows = -(-patch_rows // 16) * 16
    total = images * rows

    keep_rows = jnp.concatenate([jnp.ones((image_count, 2), jnp.int32), keep_mask], axis=1)
    keep_rows = jnp.pad(keep_rows, ((0, 0), (0, rows - patch_rows)))

    attn_turned = attn_weights.transpose(0, 2, 1)
    down_turned = down_weights.transpose(0, 2, 1)
    packing = Plan(dp_size, mp_size, thin, tile, width, SLOTS * dp_size, direct)
    block_shape = ((3 * thin + tile, width), BF16)
    first_block, last_block = call(
        functools.partial(prepare_kernel, packing),
        (attn_turned, up_weights, down_turned, vectors, keep_mask),
        [VMEM] * 5,
        [block_shape, block_shape],
        [VMEM, VMEM],
        [pltpu.VMEM((8, 2 * width), F32)],
        1 << 20,
    )
    if direct:
        plan = packing
        first_pieces = gather_plane(gather_column(first_block, devices), devices)
        source = lax.all_gather(last_block, ("dp", "mp"))
        source = source.reshape(dp_size, mp_size, 3 * thin + tile, width)
    else:
        plan = Plan(1, parts, width, tile, width, SLOTS * dp_size, False)

        def squares(array):
            return array.reshape(parts, width, width)

        def by_part(array):
            split = array.reshape(dp_size, mp_size, thin, width).transpose(1, 0, 2, 3)
            return squares(split)

        def one_tile(array):
            summed = jnp.sum(array.astype(F32), axis=0).astype(BF16)
            return jnp.pad(summed[None], ((0, parts - 1), (0, 0), (0, 0)))

        def normal(block):
            every = lax.all_gather(block, ("dp", "mp"))
            return jnp.concatenate(
                [
                    squares(every[:, :thin]),
                    by_part(every[:, thin : 2 * thin]),
                    by_part(every[:, 2 * thin : 3 * thin]),
                    one_tile(every[:, 3 * thin :]),
                ],
                axis=1,
            )

        first_pieces = [normal(first_block)]
        source = normal(last_block)[None]

    flat = keep_rows.reshape(-1)
    slot = jnp.where(flat == 1, jnp.cumsum(flat) - flat, SLOTS).reshape(image_count, 1, rows)

    def mine(array):
        return jnp.concatenate(
            [lax.dynamic_slice_in_dim(array, rank, 1, 0), array[mp_size:]], axis=0
        )

    def padded(array):
        return jnp.pad(mine(array), ((0, 0), (0, rows - patch_rows), (0, 0)))

    kept = mine(keep_rows)
    stream = padded(patches).reshape(total, width)
    bias = jnp.where(kept == 1, 0.0, MASKED).astype(F32)[:, None, :]
    goal = jnp.where((kept == 1)[:, :, None], padded(targets), 0).reshape(total, width)
    slots = jnp.concatenate(
        [lax.dynamic_slice_in_dim(slot, rank ^ k, 1, 0) for k in range(mp_size)] + [slot[mp_size:]],
        axis=0,
    )

    pairs = width // (2 * HD)
    stream_shape = ((total, width), F32)
    low_shape = ((total, width), BF16)
    three_shape = ((3, total, width), BF16)
    turned_shape = ((width, total), BF16)
    vec_shape = ((tile, width), F32)
    attn_keep = [low_shape, three_shape, ((images, pairs, 2 * rows, rows), BF16), low_shape]
    hidden_keep = [low_shape, ((parts, total, width), BF16), ((parts, total, width), F32)]
    blocks = plan.outer * plan.inner
    weight_shape = ((blocks, plan.thin, width), BF16)
    zs = max(blocks // 8, 1)

    def half(count):
        return ((2, 2, zs, count, width), BF16)

    def both(count):
        return ((2, 2, 2, zs, count, width), BF16)

    sems = [pltpu.SemaphoreType.DMA((2 * (plan.outer + plan.inner),))]

    def vmem(shapes):
        return [pltpu.VMEM(shape, dtype) for shape, dtype in shapes]

    layer_flops = 8 * total * parts * width * width
    attn_rows, hidden_rows = plan.thin + tile, 2 * plan.thin
    last_rows = attn_rows + hidden_rows

    first = call(
        functools.partial(first_kernel, plan, len(first_pieces)),
        (stream, bias, *first_pieces),
        [VMEM] * (2 + len(first_pieces)),
        [weight_shape, weight_shape, weight_shape, vec_shape, stream_shape, stream_shape]
        + attn_keep
        + hidden_keep,
        [VMEM] * 13,
        vmem([stream_shape, stream_shape]),
        layer_flops,
    )
    attn_full, up_full, down_full, vec, mid, middle = first[:6]
    attn_kept, hidden_kept = first[6:10], first[10:]
    output, grad_middle, *last_halves = call(
        functools.partial(last_kernel, plan),
        (middle, bias, goal, source),
        [VMEM, VMEM, VMEM, ANY],
        [low_shape, stream_shape, half(last_rows), half(last_rows)],
        [VMEM, VMEM, ANY, ANY],
        vmem(
            attn_keep
            + hidden_keep
            + [stream_shape, stream_shape, stream_shape, vec_shape, low_shape, low_shape, low_shape]
            + [stream_shape, stream_shape, turned_shape, turned_shape, three_shape]
            + [both(last_rows), vec_shape, ((blocks, tile, width), BF16)]
            + [weight_shape] * 3
        )
        + sems,
        3 * layer_flops,
    )
    grad_mid, early_vec, *hidden_halves = call(
        functools.partial(back_hidden_kernel, plan),
        (grad_middle, mid, vec, up_full, down_full, *hidden_kept),
        [VMEM] * 8,
        [stream_shape, vec_shape, half(hidden_rows), half(hidden_rows)],
        [VMEM, VMEM, ANY, ANY],
        vmem(
            [low_shape, low_shape, stream_shape, stream_shape, turned_shape, turned_shape]
            + [both(hidden_rows)]
        )
        + sems,
        2 * layer_flops,
    )
    if direct:
        last_sums = sum_cores(last_halves, devices)
        grad_mid, early_vec, hidden_halves, last_sums = lax.optimization_barrier(
            (grad_mid, early_vec, hidden_halves, last_sums)
        )
    grad_first, *attn_halves = call(
        functools.partial(back_attend_kernel, plan),
        (grad_mid, stream, vec, attn_full, early_vec, *attn_kept),
        [VMEM] * 9,
        [low_shape, half(attn_rows), half(attn_rows)],
        [VMEM, ANY, ANY],
        vmem([low_shape, stream_shape, low_shape, three_shape, vec_shape, both(attn_rows)]) + sems,
        layer_flops,
    )

    if direct:
        hidden_sums = sum_cores(hidden_halves, devices)
        attn_halves, hidden_sums, grad_first = lax.optimization_barrier(
            (attn_halves, hidden_sums, grad_first)
        )
        last_total = sum_plane(last_sums, devices)
        hidden_total = sum_plane(hidden_sums, devices)
        last_terms = sum_column(last_total, devices)
        hidden_terms = sum_column(hidden_total, devices)
        attn_terms = sum_by_groups(attn_halves, devices)
        terms = (*last_terms, *hidden_terms, *attn_terms)
        turned = (layers, thin, width)
        attn_grads, vector_grads, up_grads, down_grads = call(
            functools.partial(
                finish_kernel, plan, (len(last_terms), len(hidden_terms), len(attn_terms))
            ),
            terms,
            [VMEM] * len(terms),
            [(turned, F32), (vectors.shape, F32), (turned, F32), (turned, F32)],
            [VMEM] * 4,
            vmem([vec_shape, vec_shape]),
            1 << 20,
        )
        attn_grads, down_grads = attn_grads.transpose(0, 2, 1), down_grads.transpose(0, 2, 1)
    else:

        def square_blocks(halves):
            stacked = jnp.stack(halves)[:, 0, :, 0]
            stacked = jnp.stack([stacked[k % 2, k // 2] for k in range(parts)])
            return jnp.stack(
                [lax.dynamic_index_in_dim(stacked, rank ^ k, 0, False) for k in range(parts)]
            )

        def outputs_of(attn, up, down, tail):
            def by_owner(array):
                split = array.reshape(mp_size, dp_size, thin, width).transpose(1, 0, 2, 3)
                return split.reshape(devices, thin, width)

            pieces = [
                attn.reshape(devices, thin, width),
                by_owner(up),
                by_owner(down),
                jnp.broadcast_to(tail[0], (devices, tile, width)),
            ]
            owned = lax.psum_scatter(
                jnp.concatenate(pieces, axis=1), ("dp", "mp"), scatter_dimension=0, tiled=False
            ).astype(F32)
            own_vec = lax.dynamic_slice_in_dim(
                owned[3 * thin :].reshape(-1), device * vec_rows, vec_rows
            )
            return owned[:thin].T, own_vec, owned[thin : 2 * thin], owned[2 * thin : 3 * thin].T

        last_all = square_blocks(last_halves)
        attn_all, hidden_all = square_blocks(attn_halves), square_blocks(hidden_halves)
        late = outputs_of(
            last_all[:, :width],
            last_all[:, width : 2 * width],
            last_all[:, 2 * width : 3 * width],
            last_all[:, 3 * width :],
        )
        early = outputs_of(
            attn_all[:, :width], hidden_all[:, :width], hidden_all[:, width:], attn_all[:, width:]
        )
        attn_grads, vector_grads, up_grads, down_grads = (
            jnp.stack([one, two]) for one, two in zip(early, late)
        )

    def others(array):
        return [flip(array[:rows], k, devices) for k in range(1, mp_size)]

    (activations,) = call(
        pack_kernel,
        (slots, output, *others(output)),
        [VMEM] * (mp_size + 1),
        [((SLOTS, width), F32)],
        [VMEM],
        [],
        2 * SLOTS * image_count * rows * width,
    )
    (input_grads,) = call(
        place_kernel,
        (grad_first, *others(grad_first)),
        [VMEM] * mp_size,
        [((image_count, patch_rows, width), F32)],
        [VMEM],
        [],
        image_count * patch_rows * width,
    )
    return (activations, input_grads, attn_grads, vector_grads, up_grads, down_grads)


def solution(mesh):
    in_specs = (
        P("dp", None, None),
        P("dp", None, None),
        P("dp", None),
        P(None, None, ("dp", "mp")),
        P(None, ("dp", "mp")),
        P(None, "dp", "mp"),
        P(None, "mp", "dp"),
    )
    out_specs = (
        P("dp", None),
        P("dp", None, None),
        P(None, None, ("dp", "mp")),
        P(None, ("dp", "mp")),
        P(None, "dp", "mp"),
        P(None, "mp", "dp"),
    )
    return jax.shard_map(shards, mesh=mesh, in_specs=in_specs, out_specs=out_specs, check_vma=False)
```

```python
import dataclasses
import functools

import jax
import jax.numpy as jnp
from jax import lax
from jax.experimental import pallas as pl
from jax.experimental.pallas import tpu as pltpu
from jax.sharding import PartitionSpec as P

HD = 64
SLOTS = 1024
EPSILON = 1e-06
MASKED = -1e30
STEP = 16
UNROLL = 13

F32 = jnp.float32
BF16 = jnp.bfloat16


def dot_nn(left, right):
    return lax.dot_general(left, right, (((1,), (0,)), ((), ())), preferred_element_type=F32)


def dot_nt(left, right):
    return lax.dot_general(left, right, (((1,), (1,)), ((), ())), preferred_element_type=F32)


def dot_tn(left, right):
    return lax.dot_general(left, right, (((0,), (0,)), ((), ())), preferred_element_type=F32)


def block_rows(index, step):
    return pl.ds(pl.multiple_of(index * step, step), step)


def fold_rows(values):
    return jnp.sum(values.reshape(values.shape[0] // 8, 8, values.shape[1]), axis=0)


def low_halves(rows):
    lane = lax.broadcasted_iota(jnp.int32, (rows, 2 * HD), 1)
    return lane < HD


def stack_heads(pair):
    low = low_halves(pair.shape[0])
    zero = jnp.zeros_like(pair)
    return jnp.concatenate([jnp.where(low, pair, zero), jnp.where(low, zero, pair)], axis=0)


def unstack_heads(stacked):
    rows = stacked.shape[0] // 2
    return jnp.where(low_halves(rows), stacked[:rows], stacked[rows:])


def norm_rows(x_ref, out_ref, gain, shift):
    def body(index, carry):
        at = block_rows(index, STEP)
        values = x_ref[at, :].astype(F32)
        centred = values - jnp.mean(values, axis=-1, keepdims=True)
        variance = jnp.mean(centred * centred, axis=-1, keepdims=True)
        out_ref[at, :] = (centred * lax.rsqrt(variance + EPSILON) * gain + shift).astype(BF16)
        return carry

    lax.fori_loop(0, x_ref.shape[0] // STEP, body, 0, unroll=UNROLL)


def norm_back(x_ref, grad_ref, base_ref, out_ref, low_ref, gain, images):
    rows = x_ref.shape[0] // images
    width = x_ref.shape[1]
    sums = []
    for image in range(images):

        def body(index, carry, image=image):
            at = pl.ds(pl.multiple_of(image * rows + index * STEP, STEP), STEP)
            values = x_ref[at, :].astype(F32)
            grad = grad_ref[at, :]
            centred = values - jnp.mean(values, axis=-1, keepdims=True)
            variance = jnp.mean(centred * centred, axis=-1, keepdims=True)
            inverse = lax.rsqrt(variance + EPSILON)
            unit = centred * inverse
            scaled = grad * gain
            mean_one = jnp.mean(scaled, axis=-1, keepdims=True)
            mean_two = jnp.mean(scaled * unit, axis=-1, keepdims=True)
            out = base_ref[at, :] + inverse * (scaled - mean_one - unit * mean_two)
            out_ref[at, :] = out.astype(out_ref.dtype)
            if low_ref is not None:
                low_ref[at, :] = out.astype(BF16)
            return (
                carry[0] + fold_rows(grad * unit),
                carry[1] + fold_rows(grad),
                carry[2] + fold_rows(out),
            )

        zero = jnp.zeros((8, width), F32)
        sums.append(lax.fori_loop(0, rows // STEP, body, (zero, zero, zero), unroll=UNROLL))
    return sums


def weigh(sums, share):
    total = sums[0]
    for more in sums[1:]:
        total = total + more * share
    return jnp.sum(total, axis=0, keepdims=True)


def as_square(ref, part):
    rows, width = ref.shape[1:]
    per = width // rows
    return ref[pl.ds(part * per, per)].reshape(width, width)


def forward_attention(x_ref, bias_ref, vec_ref, attn_ref, keep, mid_ref):
    n1_ref, proj_ref, p_ref, att_ref = keep
    images = bias_ref.shape[0]
    rows = x_ref.shape[0] // images
    width = x_ref.shape[1]
    pairs = width // (2 * HD)
    scale = HD**-0.5

    norm_rows(x_ref, n1_ref, vec_ref[0:1, :], vec_ref[1:2, :])
    for part, bias_row in enumerate((4, None, 5)):
        value = dot_nt(n1_ref[...], as_square(attn_ref, part))
        if bias_row is not None:
            value = value + vec_ref[bias_row : bias_row + 1, :]
        proj_ref[part] = value.astype(BF16)

    def image_body(image, carry):
        at = block_rows(image, rows)
        for pair in range(pairs):
            lanes = slice(pair * 2 * HD, (pair + 1) * 2 * HD)
            query = stack_heads(proj_ref[0, at, lanes])
            scores = dot_nt(query, proj_ref[1, at, lanes]) * scale + bias_ref[image]
            top = jnp.max(scores, axis=-1, keepdims=True)
            powers = jnp.exp(scores - top)
            total = jnp.sum(powers, axis=-1, keepdims=True)
            probs = (powers * (1.0 / total)).astype(BF16)
            p_ref[image, pair] = probs
            att_ref[at, lanes] = unstack_heads(dot_nn(probs, proj_ref[2, at, lanes])).astype(BF16)
        return carry

    lax.fori_loop(0, images, image_body, 0)
    mid_ref[...] = x_ref[...].astype(F32) + dot_nt(att_ref[...], as_square(attn_ref, 3)) + vec_ref[6:7, :]


def forward_hidden(mid_ref, vec_ref, up_ref, down_ref, keep, scratch, out_ref):
    n2_ref, a_ref, gp_ref = keep
    h_ref, acc_ref = scratch
    norm_rows(mid_ref, n2_ref, vec_ref[2:3, :], vec_ref[3:4, :])
    acc_ref[...] = mid_ref[...] + vec_ref[11:12, :]

    def part_body(part, carry):
        h_ref[...] = dot_nn(n2_ref[...], as_square(up_ref, part))
        bias = vec_ref[pl.ds(7 + part, 1), :]

        def gelu_body(index, inner):
            at = block_rows(index, STEP)
            hidden = h_ref[at, :] + bias
            share = 0.5 + 0.5 * lax.erf(hidden * 0.7071067811865476)
            a_ref[part, at, :] = (hidden * share).astype(BF16)
            bell = jnp.exp(-0.5 * hidden * hidden) * 0.3989422804014327
            gp_ref[part, at, :] = (share + hidden * bell).astype(gp_ref.dtype)
            return inner

        lax.fori_loop(0, h_ref.shape[0] // STEP, gelu_body, 0, unroll=UNROLL)
        acc_ref[...] += dot_nt(a_ref[part], as_square(down_ref, part))
        return carry

    lax.fori_loop(0, a_ref.shape[0], part_body, 0)
    out_ref[...] = acc_ref[...].astype(out_ref.dtype)


def drop_shared(refs):
    @pl.when(jnp.logical_not(counts_shared()))
    def _():
        for ref in refs:
            rows = ref.shape[-2] // 2
            ref[..., rows:, :] = jnp.zeros((*ref.shape[:-2], rows, ref.shape[-1]), ref.dtype)


def backward_hidden(g_ref, mid_ref, vec_ref, up_ref, down_ref, share, keep, scratch, gm_ref, gvec_ref, store):
    n2_ref, a_ref, gp_ref = keep
    go_ref, gh_ref, acc_ref, h_ref, got_ref, n2t_ref = scratch
    images = 2
    rows = mid_ref.shape[0] // images
    width = mid_ref.shape[1]
    zero = jnp.zeros((8, width), F32)
    sums = []
    for image in range(images):

        def low_body(index, carry, image=image):
            at = pl.ds(pl.multiple_of(image * rows + index * STEP, STEP), STEP)
            grad = g_ref[at, :]
            go_ref[at, :] = grad.astype(BF16)
            return carry + fold_rows(grad)

        sums.append(lax.fori_loop(0, rows // STEP, low_body, zero, unroll=UNROLL))
    gvec_ref[11:12, :] = weigh(sums, share)
    acc_ref[...] = jnp.zeros_like(acc_ref)
    got_ref[...] = go_ref[...].T
    n2t_ref[...] = n2_ref[...].T

    def part_body(part, carry):
        store(2, part, dot_nn(got_ref[...], a_ref[part]))
        h_ref[...] = dot_nn(go_ref[...], as_square(down_ref, part))
        inner_sums = []
        for image in range(images):

            def hidden_body(index, inner, image=image):
                at = pl.ds(pl.multiple_of(image * rows + index * STEP, STEP), STEP)
                grad = (h_ref[at, :] * gp_ref[part, at, :].astype(F32)).astype(BF16)
                gh_ref[at, :] = grad
                return inner + fold_rows(grad.astype(F32))

            inner_sums.append(lax.fori_loop(0, rows // STEP, hidden_body, zero, unroll=UNROLL))
        gvec_ref[pl.ds(7 + part, 1), :] = weigh(inner_sums, share)
        store(1, part, dot_nn(n2t_ref[...], gh_ref[...]))
        acc_ref[...] += dot_nt(gh_ref[...], as_square(up_ref, part))
        return carry

    lax.fori_loop(0, a_ref.shape[0], part_body, 0)
    sums = norm_back(mid_ref, acc_ref, g_ref, gm_ref, None, vec_ref[2:3, :], images)
    for place, row in enumerate((2, 3, 6)):
        gvec_ref[row : row + 1, :] = weigh([one[place] for one in sums], share)


def backward_attention(gm_ref, x_ref, vec_ref, attn_ref, share, keep, scratch, gx_ref, gvec_ref, store):
    n1_ref, proj_ref, p_ref, att_ref = keep
    go_ref, acc_ref, ga_ref, dproj_ref = scratch
    images = p_ref.shape[0]
    rows = x_ref.shape[0] // images
    width = x_ref.shape[1]
    pairs = width // (2 * HD)
    scale = HD**-0.5
    go_ref[...] = gm_ref[...].astype(BF16)
    store(0, 3, dot_tn(go_ref[...], att_ref[...]))
    ga_ref[...] = dot_nn(go_ref[...], as_square(attn_ref, 3)).astype(BF16)

    def image_body(image, carry):
        at = block_rows(image, rows)
        for pair in range(pairs):
            lanes = slice(pair * 2 * HD, (pair + 1) * 2 * HD)
            query = stack_heads(proj_ref[0, at, lanes])
            keys = proj_ref[1, at, lanes]
            grad_out = stack_heads(ga_ref[at, lanes])
            probs = p_ref[image, pair]
            grad_probs = dot_nt(grad_out, proj_ref[2, at, lanes])
            dproj_ref[2, at, lanes] = dot_tn(probs, grad_out).astype(BF16)
            wide = probs.astype(F32)
            inner = jnp.sum(grad_probs * wide, axis=-1, keepdims=True)
            grad_scores = (wide * (grad_probs - inner)).astype(BF16)
            dproj_ref[0, at, lanes] = (unstack_heads(dot_nn(grad_scores, keys)) * scale).astype(BF16)
            dproj_ref[1, at, lanes] = (dot_tn(grad_scores, query) * scale).astype(BF16)
        return carry

    lax.fori_loop(0, images, image_body, 0)
    for part, row in enumerate((4, None, 5)):
        store(0, part, dot_tn(dproj_ref[part], n1_ref[...]))
        value = dot_nn(dproj_ref[part], as_square(attn_ref, part))
        if part == 0:
            acc_ref[...] = value
        else:
            acc_ref[...] += value
        if row is not None:
            sums = [
                fold_rows(dproj_ref[part, image * rows : (image + 1) * rows, :].astype(F32))
                for image in range(images)
            ]
            gvec_ref[row : row + 1, :] = weigh(sums, share)
    sums = norm_back(x_ref, acc_ref, gm_ref, gx_ref, None, vec_ref[0:1, :], images)
    for place, row in enumerate((0, 1)):
        gvec_ref[row : row + 1, :] = weigh([one[place] for one in sums], share)
    store(3, 0, gvec_ref[...])


def wait_all(copies):
    for one in copies:
        one.wait()


def coordinates(plan):
    outer, inner = lax.axis_index("dp"), lax.axis_index("mp")
    here = (inner // 2, inner % 2)
    return (outer // 2, outer % 2, *here) if plan.direct else (0, 0, *here)


def counts_shared():
    return lax.axis_index("mp") == 0


def place_blocks(plan, pieces, put):
    if not plan.direct:
        for owner in range(plan.inner):
            put(owner, pieces[0][owner])
        return
    at = coordinates(plan)
    for i, piece in enumerate(pieces):
        c, x, y = i % 2, i // 2 % 2, i // 4
        low = ((at[1] ^ y) * 2 + (at[2] ^ x)) * 2 + (at[3] ^ c)
        for k in range(piece.shape[0]):
            put((at[0] ^ k) * 8 + low, piece[k])


def storer(plan, packed_ref):
    thin, width = plan.thin, plan.width
    per = width // thin
    here = coordinates(plan)

    def put(owner, row, block):
        c, x, y = owner % 2, owner // 2 % 2, owner // 4 % 2
        z = owner // 8
        packed_ref[c ^ here[3], y ^ here[1], x ^ here[2], z, row : row + block.shape[0], :] = block

    def store(kind, part, value):
        low = value.astype(BF16)
        if kind == 3:
            for owner in range(plan.outer * plan.inner):
                put(owner, 3 * thin, low)
            return
        blocks = low.reshape(per, thin, width)
        for i in range(per):
            owner = part * per + i if kind == 0 else i * plan.inner + part
            put(owner, kind * thin, blocks[i])

    return store


def send_out(packed_ref, outs, sems):
    copies = [pltpu.make_async_copy(packed_ref.at[i], outs[i], sems.at[i]) for i in range(2)]
    for one in copies:
        one.start()
    wait_all(copies)


def prepare_kernel(plan, attn_ref, up_ref, down_ref, vec_ref, keep_ref, first_ref, last_ref, line_ref):
    thin, tile, width = plan.thin, plan.tile, plan.width
    count = vec_ref.shape[1]
    device = lax.axis_index("dp") * plan.inner + lax.axis_index("mp")
    row_at = device * count // width
    offset = device * count - row_at * width
    kept = jnp.sum(keep_ref[...]) + 2 * keep_ref.shape[0]
    kept = jnp.where(counts_shared(), kept, 0)
    row = lax.broadcasted_iota(jnp.int32, (tile, width), 0)
    here = lax.broadcasted_iota(jnp.int32, (tile, width), 1) == lax.axis_index("dp")
    for layer, out_ref in enumerate((first_ref, last_ref)):
        out_ref[0:thin, :] = attn_ref[layer]
        out_ref[thin : 2 * thin, :] = up_ref[layer]
        out_ref[2 * thin : 3 * thin, :] = down_ref[layer]
        line_ref[...] = jnp.zeros_like(line_ref)
        line_ref[0:1, 0:count] = vec_ref[layer : layer + 1, :].astype(F32)
        moved = pltpu.roll(line_ref[...], offset, 1)[0:1]
        piece = jnp.where(row == row_at, moved[:, :width], 0.0)
        piece = jnp.where(row == row_at + 1, moved[:, width:], piece)
        if layer == 1:
            piece = jnp.where(here & (row == 12), (kept >> 5).astype(F32), piece)
            piece = jnp.where(here & (row == 13), (kept & 31).astype(F32), piece)
        out_ref[3 * thin :, :] = piece.astype(BF16)


def place_weights(plan, sources, attn_ref, up_ref, down_ref, vec_ref):
    thin = plan.thin
    vec_ref[...] = jnp.zeros_like(vec_ref)

    def put(owner, block):
        at = owner % plan.inner * plan.outer + owner // plan.inner
        attn_ref[owner] = block[:thin]
        up_ref[at] = block[thin : 2 * thin]
        down_ref[at] = block[2 * thin : 3 * thin]
        vec_ref[...] += block[3 * thin : 3 * thin + plan.tile].astype(F32)

    place_blocks(plan, sources, put)


def first_kernel(plan, pieces, x_ref, bias_ref, *refs):
    sources, refs = refs[:pieces], refs[pieces:]
    attn_ref, up_ref, down_ref, vec_ref, mid_ref, out_ref, *refs = refs
    attn_keep, hidden_keep, (h_ref, acc_ref) = refs[:4], refs[4:7], refs[7:]
    place_weights(plan, sources, attn_ref, up_ref, down_ref, vec_ref)
    forward_attention(x_ref, bias_ref, vec_ref, attn_ref, attn_keep, mid_ref)
    forward_hidden(mid_ref, vec_ref, up_ref, down_ref, hidden_keep, (h_ref, acc_ref), out_ref)
    drop_shared((attn_keep[0], attn_keep[3], hidden_keep[0], hidden_keep[1]))


def last_kernel(plan, pieces, x_ref, bias_ref, goal_ref, *refs):
    sources, refs = refs[:pieces], refs[pieces:]
    out_ref, gx_ref, outs, refs = refs[0], refs[1], refs[2:4], refs[4:]
    attn_keep, hidden_keep, refs = refs[0:4], refs[4:7], refs[7:]
    mid_ref, g_ref, gm_ref, gvec_ref, go_ref, gh_ref, ga_ref, acc_ref, h_ref, got_ref, n2t_ref, dproj_ref = refs[:12]
    packed_ref, vec_ref, attn_ref, up_ref, down_ref, sems = refs[12:]
    place_weights(plan, sources, attn_ref, up_ref, down_ref, vec_ref)
    forward_attention(x_ref, bias_ref, vec_ref, attn_ref, attn_keep, mid_ref)
    forward_hidden(mid_ref, vec_ref, up_ref, down_ref, hidden_keep, (h_ref, acc_ref), out_ref)
    drop_shared((attn_keep[0], attn_keep[3], hidden_keep[0], hidden_keep[1]))
    high = jnp.sum(vec_ref[12:13, :], axis=-1, keepdims=True)
    rest = jnp.sum(vec_ref[13:14, :], axis=-1, keepdims=True)
    loss_scale = float(plan.slots) / (high * 32.0 + rest)
    g_ref[...] = goal_ref[...].astype(F32) * loss_scale
    gvec_ref[...] = jnp.zeros_like(gvec_ref)
    share = counts_shared().astype(F32)
    store = storer(plan, packed_ref)
    scratch = (go_ref, gh_ref, acc_ref, h_ref, got_ref, n2t_ref)
    backward_hidden(g_ref, mid_ref, vec_ref, up_ref, down_ref, share, hidden_keep, scratch, gm_ref, gvec_ref, store)
    scratch = (go_ref, acc_ref, ga_ref, dproj_ref)
    backward_attention(gm_ref, x_ref, vec_ref, attn_ref, share, attn_keep, scratch, gx_ref, gvec_ref, store)
    send_out(packed_ref, outs, sems)


def back_kernel(plan, g_ref, x_ref, mid_ref, vec_ref, attn_ref, up_ref, down_ref, *refs):
    attn_keep, hidden_keep, gx_ref, outs, refs = refs[:4], refs[4:7], refs[7], refs[8:10], refs[10:]
    gm_ref, gvec_ref, go_ref, gh_ref, ga_ref, acc_ref, h_ref, got_ref, n2t_ref, dproj_ref, packed_ref, sems = refs
    gvec_ref[...] = jnp.zeros_like(gvec_ref)
    share = counts_shared().astype(F32)
    store = storer(plan, packed_ref)
    scratch = (go_ref, gh_ref, acc_ref, h_ref, got_ref, n2t_ref)
    backward_hidden(g_ref, mid_ref, vec_ref, up_ref, down_ref, share, hidden_keep, scratch, gm_ref, gvec_ref, store)
    scratch = (go_ref, acc_ref, ga_ref, dproj_ref)
    backward_attention(gm_ref, x_ref, vec_ref, attn_ref, share, attn_keep, scratch, gx_ref, gvec_ref, store)
    send_out(packed_ref, outs, sems)


def finish_kernel(plan, *refs):
    sources, (attn_out, vec_out, up_out, down_out, *tiles) = refs[:2], refs[2:]
    thin, tile, width = plan.thin, plan.tile, plan.width

    count = vec_out.shape[1]
    device = lax.axis_index("dp") * plan.inner + lax.axis_index("mp")
    row = device * count // width
    offset = device * count - row * width
    for layer, ref in enumerate(sources):

        def total(start, count, ref=ref):
            value = ref[0, start : start + count, :].astype(F32)
            for k in range(1, ref.shape[0]):
                value = value + ref[k, start : start + count, :].astype(F32)
            return value

        attn_out[layer] = total(0, thin)
        up_out[layer] = total(thin, thin)
        down_out[layer] = total(2 * thin, thin)
        tiles[layer][...] = total(3 * thin, tile)
        both = jnp.concatenate(
            [tiles[layer][pl.ds(row, 1), :], tiles[layer][pl.ds(row + 1, 1), :]], axis=1
        )
        both = jnp.broadcast_to(both, (8, 2 * width))
        moved = pltpu.roll(both, 2 * width - offset, 1)
        vec_out[layer : layer + 1, :] = moved[0:1, :count]


def place_kernel(own_ref, *refs):
    others, out_ref = refs[:-1], refs[-1]
    rows = own_ref.shape[0] // 2
    kept = out_ref.shape[1]
    mine = lax.axis_index("mp")
    out_ref[mine] = own_ref[0:rows, :].astype(F32)[:kept]
    for i, ref in enumerate(others):
        out_ref[mine ^ (i + 1)] = ref[...].astype(F32)[:kept]
    out_ref[out_ref.shape[0] - 1] = own_ref[rows : 2 * rows, :].astype(F32)[:kept]


def pack_kernel(slot_ref, own_ref, *refs):
    others, out_ref = refs[:-1], refs[-1]
    rows = own_ref.shape[0] // 2
    sources = [own_ref[0:rows, :]] + [ref[...] for ref in others] + [own_ref[rows : 2 * rows, :]]
    step = 256

    def body(index, carry):
        slots = lax.broadcasted_iota(jnp.int32, (step, rows), 0) + index * step
        total = None
        for i, values in enumerate(sources):
            picks = jnp.where(slots == slot_ref[i], 1.0, 0.0).astype(BF16)
            term = dot_nn(picks, values)
            total = term if total is None else total + term
        out_ref[block_rows(index, step), :] = total
        return carry

    lax.fori_loop(0, out_ref.shape[0] // step, body, 0)


VMEM = pl.BlockSpec(memory_space=pltpu.VMEM)
ANY = pl.BlockSpec(memory_space=pl.ANY)


def call(kernel, operands, specs, outs, out_specs, scratch, flops):
    return pl.pallas_call(
        kernel,
        out_shape=[jax.ShapeDtypeStruct(shape, dtype) for shape, dtype in outs],
        in_specs=specs,
        out_specs=out_specs,
        scratch_shapes=scratch,
        compiler_params=pltpu.CompilerParams(vmem_limit_bytes=56 * 1024 * 1024),
        cost_estimate=pl.CostEstimate(flops=flops, bytes_accessed=8 << 20, transcendentals=0),
    )(*operands)


@dataclasses.dataclass(frozen=True)
class Plan:
    outer: int
    inner: int
    thin: int
    tile: int
    width: int
    slots: int
    direct: bool


def flip(array, mask, devices):
    return lax.ppermute(array, ("dp", "mp"), [(d, d ^ mask) for d in range(devices)])


def gather_column(block, devices):
    return jnp.stack([block] + [flip(block, 8 * k, devices) for k in range(1, devices // 8)])


def gather_plane(column, devices):
    return [column] + [flip(column, mask, devices) for mask in (2, 4, 6)]


def gather_cores(plane, devices):
    pieces = []
    for piece in plane:
        pieces += [piece, flip(piece, 1, devices)]
    return pieces


def spread(rows, devices):
    across = flip(rows, 2, devices)
    return [flip(rows, 1, devices), across, flip(across, 1, devices)]


PLANE = ((0, 0), (0, 1), (1, 0), (1, 1))


def sum_cores(halves, devices):
    kept, sent = halves
    got = flip(sent, 1, devices)
    sums = [kept[at].astype(F32) + got[at].astype(F32) for at in PLANE]
    return [sums[0]] + [one.astype(BF16) for one in sums[1:]]


def sum_plane(sums, devices):
    total = sums[0]
    for one, mask in zip(sums[1:], (2, 4, 6)):
        total = total + flip(one, mask, devices).astype(F32)
    return total.astype(BF16)


def sum_column(total, devices):
    zs = total.shape[0]
    if zs == 1:
        return total
    columns = [[8 * z + at for z in range(zs)] for at in range(8)]
    return lax.all_to_all(total, ("dp", "mp"), 0, 0, axis_index_groups=columns, tiled=True)


def shards(patches, targets, keep_mask, attn_weights, vectors, up_weights, down_weights):
    image_count, patch_rows, width = patches.shape
    layers = attn_weights.shape[0]
    dp_size, mp_size = lax.axis_size("dp"), lax.axis_size("mp")
    devices = dp_size * mp_size
    rank = lax.axis_index("mp")
    lane_rank = lax.axis_index("dp")
    device = lane_rank * mp_size + rank
    thin = attn_weights.shape[2]
    vec_rows = vectors.shape[1]
    parts = thin * devices // width
    assert image_count == mp_size + 1 and layers == 2 and parts == mp_size == 4
    direct = thin % 16 == 0
    images, tile = 2, 16
    rows = -(-patch_rows // 16) * 16
    total = images * rows

    keep_rows = jnp.concatenate([jnp.ones((image_count, 2), jnp.int32), keep_mask], axis=1)
    keep_rows = jnp.pad(keep_rows, ((0, 0), (0, rows - patch_rows)))

    attn_turned = attn_weights.transpose(0, 2, 1)
    down_turned = down_weights.transpose(0, 2, 1)
    packing = Plan(dp_size, mp_size, thin, tile, width, SLOTS * dp_size, direct)
    block_shape = ((3 * thin + tile, width), BF16)
    first_block, last_block = call(
        functools.partial(prepare_kernel, packing),
        (attn_turned, up_weights, down_turned, vectors, keep_mask),
        [VMEM] * 5,
        [block_shape, block_shape],
        [VMEM, VMEM],
        [pltpu.VMEM((8, 2 * width), F32)],
        1 << 20,
    )
    if direct:
        plan = packing
        first_column = gather_column(first_block, devices)
        first_column, last_block = lax.optimization_barrier((first_column, last_block))
        first_plane = gather_plane(first_column, devices)
        last_column = gather_column(last_block, devices)
        first_plane, last_column = lax.optimization_barrier((first_plane, last_column))
        first_pieces = gather_cores(first_plane, devices)
        last_plane = gather_plane(last_column, devices)
    else:
        plan = Plan(1, parts, width, tile, width, SLOTS * dp_size, False)

        def squares(array):
            return array.reshape(parts, width, width)

        def by_part(array):
            split = array.reshape(dp_size, mp_size, thin, width).transpose(1, 0, 2, 3)
            return squares(split)

        def one_tile(array):
            summed = jnp.sum(array.astype(F32), axis=0).astype(BF16)
            return jnp.pad(summed[None], ((0, parts - 1), (0, 0), (0, 0)))

        def normal(block):
            every = lax.all_gather(block, ("dp", "mp"))
            return jnp.concatenate(
                [
                    squares(every[:, :thin]),
                    by_part(every[:, thin : 2 * thin]),
                    by_part(every[:, 2 * thin : 3 * thin]),
                    one_tile(every[:, 3 * thin :]),
                ],
                axis=1,
            )

        first_pieces, last_pieces = [normal(first_block)], [normal(last_block)]

    flat = keep_rows.reshape(-1)
    slot = jnp.where(flat == 1, jnp.cumsum(flat) - flat, SLOTS).reshape(image_count, 1, rows)

    def mine(array):
        return jnp.concatenate(
            [lax.dynamic_slice_in_dim(array, rank, 1, 0), array[mp_size:]], axis=0
        )

    def padded(array):
        return jnp.pad(mine(array), ((0, 0), (0, rows - patch_rows), (0, 0)))

    kept = mine(keep_rows)
    stream = padded(patches).reshape(total, width)
    bias = jnp.where(kept == 1, 0.0, MASKED).astype(F32)[:, None, :]
    goal = jnp.where((kept == 1)[:, :, None], padded(targets), 0).reshape(total, width)
    slots = jnp.concatenate(
        [lax.dynamic_slice_in_dim(slot, rank ^ k, 1, 0) for k in range(mp_size)] + [slot[mp_size:]],
        axis=0,
    )

    stream, slots, goal = lax.optimization_barrier((stream, slots, goal))

    pairs = width // (2 * HD)
    stream_shape = ((total, width), F32)
    low_shape = ((total, width), BF16)
    three_shape = ((3, total, width), BF16)
    turned_shape = ((width, total), BF16)
    vec_shape = ((tile, width), F32)
    attn_keep = [low_shape, three_shape, ((images, pairs, 2 * rows, rows), BF16), low_shape]
    hidden_keep = [low_shape, ((parts, total, width), BF16), ((parts, total, width), F32)]
    blocks = plan.outer * plan.inner
    weight_shape = ((blocks, plan.thin, width), BF16)
    zs = max(blocks // 8, 1)

    def vmem(shapes):
        return [pltpu.VMEM(shape, dtype) for shape, dtype in shapes]

    layer_flops = 8 * total * parts * width * width
    block_rows_of = 3 * plan.thin + tile

    first = call(
        functools.partial(first_kernel, plan, len(first_pieces)),
        (stream, bias, *first_pieces),
        [VMEM] * (2 + len(first_pieces)),
        [weight_shape, weight_shape, weight_shape, vec_shape, stream_shape, stream_shape]
        + attn_keep
        + hidden_keep,
        [VMEM] * 13,
        vmem([stream_shape, stream_shape]),
        layer_flops,
    )
    attn_full, up_full, down_full, vec, mid, middle = first[:6]
    attn_kept, hidden_kept = first[6:10], first[10:]
    if direct:
        middle, last_plane = lax.optimization_barrier((middle, last_plane))
        last_pieces = gather_cores(last_plane, devices)
    back_scratch = [
        stream_shape,
        vec_shape,
        low_shape,
        low_shape,
        low_shape,
        stream_shape,
        stream_shape,
        turned_shape,
        turned_shape,
        three_shape,
        ((2, 2, 2, zs, block_rows_of, width), BF16),
    ]
    half_shape = ((2, 2, zs, block_rows_of, width), BF16)
    sems = [pltpu.SemaphoreType.DMA((2,))]
    output, grad_middle, *last_halves = call(
        functools.partial(last_kernel, plan, len(last_pieces)),
        (middle, bias, goal, *last_pieces),
        [VMEM] * (3 + len(last_pieces)),
        [low_shape, stream_shape, half_shape, half_shape],
        [VMEM, VMEM, ANY, ANY],
        vmem(
            attn_keep
            + hidden_keep
            + [stream_shape, stream_shape]
            + back_scratch
            + [vec_shape]
            + [weight_shape] * 3
        )
        + sems,
        3 * layer_flops,
    )
    output_pieces = spread(output[:rows], devices)
    if direct:
        last_sums = sum_cores(last_halves, devices)
        grad_middle, last_sums, output_pieces = lax.optimization_barrier(
            (grad_middle, last_sums, output_pieces)
        )
    grad_first, *first_halves = call(
        functools.partial(back_kernel, plan),
        (grad_middle, stream, mid, vec, attn_full, up_full, down_full, *attn_kept, *hidden_kept),
        [VMEM] * 14,
        [low_shape, half_shape, half_shape],
        [VMEM, ANY, ANY],
        vmem(back_scratch) + sems,
        3 * layer_flops,
    )

    if direct:
        last_total = sum_plane(last_sums, devices)
        last_total, first_halves, grad_first = lax.optimization_barrier(
            (last_total, first_halves, grad_first)
        )
        first_sums = sum_cores(first_halves, devices)
        first_sums, output = lax.optimization_barrier((first_sums, output))
        last_terms = sum_column(last_total, devices)
        first_total = sum_plane(first_sums, devices)
        first_terms = sum_column(first_total, devices)
        turned = (layers, thin, width)
        attn_grads, vector_grads, up_grads, down_grads = call(
            functools.partial(finish_kernel, plan),
            (first_terms, last_terms),
            [VMEM] * 2,
            [(turned, F32), (vectors.shape, F32), (turned, F32), (turned, F32)],
            [VMEM] * 4,
            vmem([vec_shape, vec_shape]),
            1 << 20,
        )
        attn_grads, down_grads = attn_grads.transpose(0, 2, 1), down_grads.transpose(0, 2, 1)
    else:

        def square_blocks(halves):
            stacked = jnp.stack(halves)[:, 0, :, 0]
            stacked = jnp.stack([stacked[k % 2, k // 2] for k in range(parts)])
            return jnp.stack(
                [lax.dynamic_index_in_dim(stacked, rank ^ k, 0, False) for k in range(parts)]
            )

        def outputs_of(halves):
            def by_owner(array):
                split = array.reshape(mp_size, dp_size, thin, width).transpose(1, 0, 2, 3)
                return split.reshape(devices, thin, width)

            every = square_blocks(halves)
            pieces = [
                every[:, :width].reshape(devices, thin, width),
                by_owner(every[:, width : 2 * width]),
                by_owner(every[:, 2 * width : 3 * width]),
                jnp.broadcast_to(every[0, 3 * width :], (devices, tile, width)),
            ]
            owned = lax.psum_scatter(
                jnp.concatenate(pieces, axis=1), ("dp", "mp"), scatter_dimension=0, tiled=False
            ).astype(F32)
            own_vec = lax.dynamic_slice_in_dim(
                owned[3 * thin :].reshape(-1), device * vec_rows, vec_rows
            )
            return owned[:thin].T, own_vec, owned[thin : 2 * thin], owned[2 * thin : 3 * thin].T

        attn_grads, vector_grads, up_grads, down_grads = (
            jnp.stack([one, two]) for one, two in zip(outputs_of(first_halves), outputs_of(last_halves))
        )

    (activations,) = call(
        pack_kernel,
        (slots, output, *output_pieces),
        [VMEM] * (mp_size + 1),
        [((SLOTS, width), F32)],
        [VMEM],
        [],
        2 * SLOTS * image_count * rows * width,
    )
    (input_grads,) = call(
        place_kernel,
        (grad_first, *spread(grad_first[:rows], devices)),
        [VMEM] * mp_size,
        [((image_count, patch_rows, width), F32)],
        [VMEM],
        [],
        image_count * patch_rows * width,
    )
    return (activations, input_grads, attn_grads, vector_grads, up_grads, down_grads)


def solution(mesh):
    in_specs = (
        P("dp", None, None),
        P("dp", None, None),
        P("dp", None),
        P(None, None, ("dp", "mp")),
        P(None, ("dp", "mp")),
        P(None, "dp", "mp"),
        P(None, "mp", "dp"),
    )
    out_specs = (
        P("dp", None),
        P("dp", None, None),
        P(None, None, ("dp", "mp")),
        P(None, ("dp", "mp")),
        P(None, "dp", "mp"),
        P(None, "mp", "dp"),
    )
    return jax.shard_map(shards, mesh=mesh, in_specs=in_specs, out_specs=out_specs, check_vma=False)
```

```python
import dataclasses
import functools

import jax
import jax.numpy as jnp
from jax import lax
from jax.experimental import pallas as pl
from jax.experimental.pallas import tpu as pltpu
from jax.sharding import PartitionSpec as P

HD = 64
SLOTS = 1024
EPSILON = 1e-06
MASKED = -1e30
STEP = 16
UNROLL = 13

F32 = jnp.float32
BF16 = jnp.bfloat16


def dot_nn(left, right):
    return lax.dot_general(left, right, (((1,), (0,)), ((), ())), preferred_element_type=F32)


def dot_nt(left, right):
    return lax.dot_general(left, right, (((1,), (1,)), ((), ())), preferred_element_type=F32)


def dot_tn(left, right):
    return lax.dot_general(left, right, (((0,), (0,)), ((), ())), preferred_element_type=F32)


def block_rows(index, step):
    return pl.ds(pl.multiple_of(index * step, step), step)


def fold_rows(values):
    return jnp.sum(values.reshape(values.shape[0] // 8, 8, values.shape[1]), axis=0)


def low_halves(rows):
    lane = lax.broadcasted_iota(jnp.int32, (rows, 2 * HD), 1)
    return lane < HD


def stack_heads(pair):
    low = low_halves(pair.shape[0])
    zero = jnp.zeros_like(pair)
    return jnp.concatenate([jnp.where(low, pair, zero), jnp.where(low, zero, pair)], axis=0)


def unstack_heads(stacked):
    rows = stacked.shape[0] // 2
    return jnp.where(low_halves(rows), stacked[:rows], stacked[rows:])


def norm_rows(x_ref, out_ref, gain, shift):
    def body(index, carry):
        at = block_rows(index, STEP)
        values = x_ref[at, :].astype(F32)
        centred = values - jnp.mean(values, axis=-1, keepdims=True)
        variance = jnp.mean(centred * centred, axis=-1, keepdims=True)
        out_ref[at, :] = (centred * lax.rsqrt(variance + EPSILON) * gain + shift).astype(BF16)
        return carry

    lax.fori_loop(0, x_ref.shape[0] // STEP, body, 0, unroll=UNROLL)


def norm_back(x_ref, grad_ref, base_ref, out_ref, low_ref, gain, images):
    rows = x_ref.shape[0] // images
    width = x_ref.shape[1]
    sums = []
    for image in range(images):

        def body(index, carry, image=image):
            at = pl.ds(pl.multiple_of(image * rows + index * STEP, STEP), STEP)
            values = x_ref[at, :].astype(F32)
            grad = grad_ref[at, :]
            centred = values - jnp.mean(values, axis=-1, keepdims=True)
            variance = jnp.mean(centred * centred, axis=-1, keepdims=True)
            inverse = lax.rsqrt(variance + EPSILON)
            unit = centred * inverse
            scaled = grad * gain
            mean_one = jnp.mean(scaled, axis=-1, keepdims=True)
            mean_two = jnp.mean(scaled * unit, axis=-1, keepdims=True)
            out = base_ref[at, :] + inverse * (scaled - mean_one - unit * mean_two)
            out_ref[at, :] = out.astype(out_ref.dtype)
            if low_ref is not None:
                low_ref[at, :] = out.astype(BF16)
            return (
                carry[0] + fold_rows(grad * unit),
                carry[1] + fold_rows(grad),
                carry[2] + fold_rows(out),
            )

        zero = jnp.zeros((8, width), F32)
        sums.append(lax.fori_loop(0, rows // STEP, body, (zero, zero, zero), unroll=UNROLL))
    return sums


def weigh(sums, share):
    total = sums[0]
    for more in sums[1:]:
        total = total + more * share
    return jnp.sum(total, axis=0, keepdims=True)


def as_square(ref, part):
    rows, width = ref.shape[1:]
    per = width // rows
    return ref[pl.ds(part * per, per)].reshape(width, width)


def forward_attention(x_ref, bias_ref, vec_ref, attn_ref, keep, mid_ref):
    n1_ref, proj_ref, p_ref, att_ref = keep
    images = bias_ref.shape[0]
    rows = x_ref.shape[0] // images
    width = x_ref.shape[1]
    pairs = width // (2 * HD)
    scale = HD**-0.5

    norm_rows(x_ref, n1_ref, vec_ref[0:1, :], vec_ref[1:2, :])
    for part, bias_row in enumerate((4, None, 5)):
        value = dot_nt(n1_ref[...], as_square(attn_ref, part))
        if bias_row is not None:
            value = value + vec_ref[bias_row : bias_row + 1, :]
        proj_ref[part] = value.astype(BF16)

    def image_body(image, carry):
        at = block_rows(image, rows)
        for pair in range(pairs):
            lanes = slice(pair * 2 * HD, (pair + 1) * 2 * HD)
            query = stack_heads(proj_ref[0, at, lanes])
            scores = dot_nt(query, proj_ref[1, at, lanes]) * scale + bias_ref[image]
            top = jnp.max(scores, axis=-1, keepdims=True)
            powers = jnp.exp(scores - top)
            total = jnp.sum(powers, axis=-1, keepdims=True)
            probs = (powers * (1.0 / total)).astype(BF16)
            p_ref[image, pair] = probs
            att_ref[at, lanes] = unstack_heads(dot_nn(probs, proj_ref[2, at, lanes])).astype(BF16)
        return carry

    lax.fori_loop(0, images, image_body, 0)
    mid_ref[...] = x_ref[...].astype(F32) + dot_nt(att_ref[...], as_square(attn_ref, 3)) + vec_ref[6:7, :]


def forward_hidden(mid_ref, vec_ref, up_ref, down_ref, keep, scratch, out_ref):
    n2_ref, a_ref, gp_ref = keep
    h_ref, acc_ref = scratch
    norm_rows(mid_ref, n2_ref, vec_ref[2:3, :], vec_ref[3:4, :])
    acc_ref[...] = mid_ref[...] + vec_ref[11:12, :]

    def part_body(part, carry):
        h_ref[...] = dot_nn(n2_ref[...], as_square(up_ref, part))
        bias = vec_ref[pl.ds(7 + part, 1), :]

        def gelu_body(index, inner):
            at = block_rows(index, STEP)
            hidden = h_ref[at, :] + bias
            share = 0.5 + 0.5 * lax.erf(hidden * 0.7071067811865476)
            a_ref[part, at, :] = (hidden * share).astype(BF16)
            bell = jnp.exp(-0.5 * hidden * hidden) * 0.3989422804014327
            gp_ref[part, at, :] = (share + hidden * bell).astype(gp_ref.dtype)
            return inner

        lax.fori_loop(0, h_ref.shape[0] // STEP, gelu_body, 0, unroll=UNROLL)
        acc_ref[...] += dot_nt(a_ref[part], as_square(down_ref, part))
        return carry

    lax.fori_loop(0, a_ref.shape[0], part_body, 0)
    out_ref[...] = acc_ref[...].astype(out_ref.dtype)


def drop_shared(refs):
    @pl.when(jnp.logical_not(counts_shared()))
    def _():
        for ref in refs:
            rows = ref.shape[-2] // 2
            ref[..., rows:, :] = jnp.zeros((*ref.shape[:-2], rows, ref.shape[-1]), ref.dtype)


def backward_hidden(g_ref, mid_ref, vec_ref, up_ref, down_ref, share, keep, scratch, gm_ref, gvec_ref, store):
    n2_ref, a_ref, gp_ref = keep
    go_ref, gh_ref, acc_ref, h_ref, got_ref, n2t_ref = scratch
    images = 2
    rows = mid_ref.shape[0] // images
    width = mid_ref.shape[1]
    zero = jnp.zeros((8, width), F32)
    sums = []
    for image in range(images):

        def low_body(index, carry, image=image):
            at = pl.ds(pl.multiple_of(image * rows + index * STEP, STEP), STEP)
            grad = g_ref[at, :]
            go_ref[at, :] = grad.astype(BF16)
            return carry + fold_rows(grad)

        sums.append(lax.fori_loop(0, rows // STEP, low_body, zero, unroll=UNROLL))
    gvec_ref[11:12, :] = weigh(sums, share)
    acc_ref[...] = jnp.zeros_like(acc_ref)
    got_ref[...] = go_ref[...].T
    n2t_ref[...] = n2_ref[...].T

    def part_body(part, carry):
        store(2, part, dot_nn(got_ref[...], a_ref[part]))
        h_ref[...] = dot_nn(go_ref[...], as_square(down_ref, part))
        inner_sums = []
        for image in range(images):

            def hidden_body(index, inner, image=image):
                at = pl.ds(pl.multiple_of(image * rows + index * STEP, STEP), STEP)
                grad = (h_ref[at, :] * gp_ref[part, at, :].astype(F32)).astype(BF16)
                gh_ref[at, :] = grad
                return inner + fold_rows(grad.astype(F32))

            inner_sums.append(lax.fori_loop(0, rows // STEP, hidden_body, zero, unroll=UNROLL))
        gvec_ref[pl.ds(7 + part, 1), :] = weigh(inner_sums, share)
        store(1, part, dot_nn(n2t_ref[...], gh_ref[...]))
        acc_ref[...] += dot_nt(gh_ref[...], as_square(up_ref, part))
        return carry

    lax.fori_loop(0, a_ref.shape[0], part_body, 0)
    sums = norm_back(mid_ref, acc_ref, g_ref, gm_ref, None, vec_ref[2:3, :], images)
    for place, row in enumerate((2, 3, 6)):
        gvec_ref[row : row + 1, :] = weigh([one[place] for one in sums], share)


def backward_attention(gm_ref, x_ref, vec_ref, attn_ref, share, keep, scratch, gx_ref, gvec_ref, store):
    n1_ref, proj_ref, p_ref, att_ref = keep
    go_ref, acc_ref, ga_ref, dproj_ref = scratch
    images = p_ref.shape[0]
    rows = x_ref.shape[0] // images
    width = x_ref.shape[1]
    pairs = width // (2 * HD)
    scale = HD**-0.5
    go_ref[...] = gm_ref[...].astype(BF16)
    store(0, 3, dot_tn(go_ref[...], att_ref[...]))
    ga_ref[...] = dot_nn(go_ref[...], as_square(attn_ref, 3)).astype(BF16)

    def image_body(image, carry):
        at = block_rows(image, rows)
        for pair in range(pairs):
            lanes = slice(pair * 2 * HD, (pair + 1) * 2 * HD)
            query = stack_heads(proj_ref[0, at, lanes])
            keys = proj_ref[1, at, lanes]
            grad_out = stack_heads(ga_ref[at, lanes])
            probs = p_ref[image, pair]
            grad_probs = dot_nt(grad_out, proj_ref[2, at, lanes])
            dproj_ref[2, at, lanes] = dot_tn(probs, grad_out).astype(BF16)
            wide = probs.astype(F32)
            inner = jnp.sum(grad_probs * wide, axis=-1, keepdims=True)
            grad_scores = (wide * (grad_probs - inner)).astype(BF16)
            dproj_ref[0, at, lanes] = (unstack_heads(dot_nn(grad_scores, keys)) * scale).astype(BF16)
            dproj_ref[1, at, lanes] = (dot_tn(grad_scores, query) * scale).astype(BF16)
        return carry

    lax.fori_loop(0, images, image_body, 0)
    for part, row in enumerate((4, None, 5)):
        store(0, part, dot_tn(dproj_ref[part], n1_ref[...]))
        value = dot_nn(dproj_ref[part], as_square(attn_ref, part))
        if part == 0:
            acc_ref[...] = value
        else:
            acc_ref[...] += value
        if row is not None:
            sums = [
                fold_rows(dproj_ref[part, image * rows : (image + 1) * rows, :].astype(F32))
                for image in range(images)
            ]
            gvec_ref[row : row + 1, :] = weigh(sums, share)
    sums = norm_back(x_ref, acc_ref, gm_ref, gx_ref, None, vec_ref[0:1, :], images)
    for place, row in enumerate((0, 1)):
        gvec_ref[row : row + 1, :] = weigh([one[place] for one in sums], share)
    store(3, 0, gvec_ref[...])


def coordinates(plan):
    outer, inner = lax.axis_index("dp"), lax.axis_index("mp")
    here = (inner // 2, inner % 2)
    return (outer // 2, outer % 2, *here) if plan.direct else (0, 0, *here)


def counts_shared():
    return lax.axis_index("mp") == 0


def place_weights(plan, pieces, attn_ref, up_ref, down_ref, vec_ref):
    thin, rows = plan.thin, 3 * plan.thin

    def put(owner, block):
        at = owner % plan.inner * plan.outer + owner // plan.inner
        attn_ref[owner] = block[:thin]
        up_ref[at] = block[thin : 2 * thin]
        down_ref[at] = block[2 * thin : 3 * thin]

    if not plan.direct:
        for owner in range(plan.inner):
            put(owner, pieces[0][owner, :rows])
        vec_ref[...] = pieces[0][0, rows:].astype(F32)
        return
    at = coordinates(plan)
    vec = None
    for i, piece in enumerate(pieces):
        c, x, y = i % 2, i // 2 % 2, i // 4
        low = ((at[1] ^ y) * 2 + (at[2] ^ x)) * 2 + (at[3] ^ c)
        count = piece.shape[0] // rows
        for k in range(count):
            put((at[0] ^ k) * 8 + low, piece[k * rows : (k + 1) * rows])
        tail = piece[count * rows :].astype(F32)
        vec = tail if vec is None else vec + tail
    vec_ref[...] = vec


def storer(plan, packed_ref):
    thin, width = plan.thin, plan.width
    per = width // thin
    here = coordinates(plan)

    def put(owner, kind, block):
        c, x, y = owner % 2, owner // 2 % 2, owner // 4 % 2
        row = pl.multiple_of((owner // 8 * 3 + kind) * thin, thin)
        packed_ref[c ^ here[3], y ^ here[1], x ^ here[2], pl.ds(row, thin), :] = block

    def store(kind, part, value):
        low = value.astype(BF16)
        if kind == 3:
            for i in range(8):
                packed_ref[i % 2, i // 4, i // 2 % 2, packed_ref.shape[3] - plan.tile :, :] = low
            return
        blocks = low.reshape(per, thin, width)
        for i in range(per):
            owner = part * per + i if kind == 0 else i * plan.inner + part
            put(owner, kind, blocks[i])

    return store


def send_hidden(plan, packed_ref, outs, sems):
    thin = plan.thin
    copies = []
    for z in range((packed_ref.shape[3] - plan.tile) // (3 * thin)):
        at = pl.ds((3 * z + 1) * thin, 2 * thin)
        for i in range(2):
            source, target = packed_ref.at[i, :, :, at], outs[i].at[:, :, at]
            copies.append(pltpu.make_async_copy(source, target, sems.at[len(copies)]))
    for one in copies:
        one.start()
    return copies


def send_rest(plan, packed_ref, outs, sems, copies):
    thin, tile = plan.thin, plan.tile
    more = list(copies)
    last = packed_ref.shape[3] - tile
    places = [pl.ds(3 * z * thin, thin) for z in range(last // (3 * thin))] + [pl.ds(last, tile)]
    for at in places:
        for i in range(2):
            source, target = packed_ref.at[i, :, :, at], outs[i].at[:, :, at]
            more.append(pltpu.make_async_copy(source, target, sems.at[len(more)]))
    for one in more[len(copies) :]:
        one.start()
    for one in more:
        one.wait()


def prepare_kernel(plan, attn_ref, up_ref, down_ref, vec_ref, keep_ref, first_ref, last_ref, line_ref):
    thin, tile, width = plan.thin, plan.tile, plan.width
    count = vec_ref.shape[1]
    device = lax.axis_index("dp") * plan.inner + lax.axis_index("mp")
    row_at = device * count // width
    offset = device * count - row_at * width
    kept = jnp.sum(keep_ref[...]) + 2 * keep_ref.shape[0]
    kept = jnp.where(counts_shared(), kept, 0)
    row = lax.broadcasted_iota(jnp.int32, (tile, width), 0)
    here = lax.broadcasted_iota(jnp.int32, (tile, width), 1) == lax.axis_index("dp")
    for layer, out_ref in enumerate((first_ref, last_ref)):
        out_ref[0:thin, :] = attn_ref[layer]
        out_ref[thin : 2 * thin, :] = up_ref[layer]
        out_ref[2 * thin : 3 * thin, :] = down_ref[layer]
        line_ref[...] = jnp.zeros_like(line_ref)
        line_ref[0:1, 0:count] = vec_ref[layer : layer + 1, :].astype(F32)
        moved = pltpu.roll(line_ref[...], offset, 1)[0:1]
        piece = jnp.where(row == row_at, moved[:, :width], 0.0)
        piece = jnp.where(row == row_at + 1, moved[:, width:], piece)
        if layer == 1:
            piece = jnp.where(here & (row == 12), (kept >> 5).astype(F32), piece)
            piece = jnp.where(here & (row == 13), (kept & 31).astype(F32), piece)
        out_ref[3 * thin :, :] = piece.astype(BF16)


def first_kernel(plan, pieces, x_ref, bias_ref, *refs):
    sources, refs = refs[:pieces], refs[pieces:]
    attn_ref, up_ref, down_ref, vec_ref, mid_ref, out_ref, *refs = refs
    attn_keep, hidden_keep, (h_ref, acc_ref) = refs[:4], refs[4:7], refs[7:]
    place_weights(plan, sources, attn_ref, up_ref, down_ref, vec_ref)
    forward_attention(x_ref, bias_ref, vec_ref, attn_ref, attn_keep, mid_ref)
    forward_hidden(mid_ref, vec_ref, up_ref, down_ref, hidden_keep, (h_ref, acc_ref), out_ref)
    drop_shared((attn_keep[0], attn_keep[3], hidden_keep[0], hidden_keep[1]))


def last_kernel(plan, pieces, x_ref, bias_ref, goal_ref, *refs):
    sources, refs = refs[:pieces], refs[pieces:]
    out_ref, gx_ref, outs, refs = refs[0], refs[1], refs[2:4], refs[4:]
    attn_keep, hidden_keep, refs = refs[0:4], refs[4:7], refs[7:]
    mid_ref, g_ref, gm_ref, gvec_ref, go_ref, gh_ref, ga_ref, acc_ref, h_ref, got_ref, n2t_ref, dproj_ref = refs[:12]
    packed_ref, vec_ref, attn_ref, up_ref, down_ref, sems = refs[12:]
    place_weights(plan, sources, attn_ref, up_ref, down_ref, vec_ref)
    forward_attention(x_ref, bias_ref, vec_ref, attn_ref, attn_keep, mid_ref)
    forward_hidden(mid_ref, vec_ref, up_ref, down_ref, hidden_keep, (h_ref, acc_ref), out_ref)
    drop_shared((attn_keep[0], attn_keep[3], hidden_keep[0], hidden_keep[1]))
    high = jnp.sum(vec_ref[12:13, :], axis=-1, keepdims=True)
    rest = jnp.sum(vec_ref[13:14, :], axis=-1, keepdims=True)
    loss_scale = float(plan.slots) / (high * 32.0 + rest)
    g_ref[...] = goal_ref[...].astype(F32) * loss_scale
    gvec_ref[...] = jnp.zeros_like(gvec_ref)
    share = counts_shared().astype(F32)
    store = storer(plan, packed_ref)
    scratch = (go_ref, gh_ref, acc_ref, h_ref, got_ref, n2t_ref)
    backward_hidden(g_ref, mid_ref, vec_ref, up_ref, down_ref, share, hidden_keep, scratch, gm_ref, gvec_ref, store)
    copies = send_hidden(plan, packed_ref, outs, sems)
    scratch = (go_ref, acc_ref, ga_ref, dproj_ref)
    backward_attention(gm_ref, x_ref, vec_ref, attn_ref, share, attn_keep, scratch, gx_ref, gvec_ref, store)
    send_rest(plan, packed_ref, outs, sems, copies)


def back_kernel(plan, g_ref, x_ref, mid_ref, vec_ref, attn_ref, up_ref, down_ref, *refs):
    attn_keep, hidden_keep, gx_ref, outs, refs = refs[:4], refs[4:7], refs[7], refs[8:10], refs[10:]
    gm_ref, gvec_ref, go_ref, gh_ref, ga_ref, acc_ref, h_ref, got_ref, n2t_ref, dproj_ref, packed_ref, sems = refs
    gvec_ref[...] = jnp.zeros_like(gvec_ref)
    share = counts_shared().astype(F32)
    store = storer(plan, packed_ref)
    scratch = (go_ref, gh_ref, acc_ref, h_ref, got_ref, n2t_ref)
    backward_hidden(g_ref, mid_ref, vec_ref, up_ref, down_ref, share, hidden_keep, scratch, gm_ref, gvec_ref, store)
    copies = send_hidden(plan, packed_ref, outs, sems)
    scratch = (go_ref, acc_ref, ga_ref, dproj_ref)
    backward_attention(gm_ref, x_ref, vec_ref, attn_ref, share, attn_keep, scratch, gx_ref, gvec_ref, store)
    send_rest(plan, packed_ref, outs, sems, copies)


def finish_kernel(plan, *refs):
    sources, (attn_out, vec_out, up_out, down_out, *tiles) = refs[:2], refs[2:]
    thin, tile, width = plan.thin, plan.tile, plan.width

    count = vec_out.shape[1]
    device = lax.axis_index("dp") * plan.inner + lax.axis_index("mp")
    row = device * count // width
    offset = device * count - row * width
    for layer, ref in enumerate(sources):

        def total(start, count, ref=ref):
            value = ref[0, start : start + count, :].astype(F32)
            for k in range(1, ref.shape[0]):
                value = value + ref[k, start : start + count, :].astype(F32)
            return value

        attn_out[layer] = total(0, thin)
        up_out[layer] = total(thin, thin)
        down_out[layer] = total(2 * thin, thin)
        tiles[layer][...] = total(3 * thin, tile)
        both = jnp.concatenate(
            [tiles[layer][pl.ds(row, 1), :], tiles[layer][pl.ds(row + 1, 1), :]], axis=1
        )
        both = jnp.broadcast_to(both, (8, 2 * width))
        moved = pltpu.roll(both, 2 * width - offset, 1)
        vec_out[layer : layer + 1, :] = moved[0:1, :count]


def place_kernel(own_ref, *refs):
    others, out_ref = refs[:-1], refs[-1]
    rows = own_ref.shape[0] // 2
    kept = out_ref.shape[1]
    mine = lax.axis_index("mp")
    out_ref[mine] = own_ref[0:rows, :].astype(F32)[:kept]
    for i, ref in enumerate(others):
        out_ref[mine ^ (i + 1)] = ref[...].astype(F32)[:kept]
    out_ref[out_ref.shape[0] - 1] = own_ref[rows : 2 * rows, :].astype(F32)[:kept]


def pack_kernel(slot_ref, own_ref, *refs):
    others, out_ref = refs[:-1], refs[-1]
    rows = own_ref.shape[0] // 2
    sources = [own_ref[0:rows, :]] + [ref[...] for ref in others] + [own_ref[rows : 2 * rows, :]]
    step = 256

    def body(index, carry):
        slots = lax.broadcasted_iota(jnp.int32, (step, rows), 0) + index * step
        total = None
        for i, values in enumerate(sources):
            picks = jnp.where(slots == slot_ref[i], 1.0, 0.0).astype(BF16)
            term = dot_nn(picks, values)
            total = term if total is None else total + term
        out_ref[block_rows(index, step), :] = total
        return carry

    lax.fori_loop(0, out_ref.shape[0] // step, body, 0)


VMEM = pl.BlockSpec(memory_space=pltpu.VMEM)
ANY = pl.BlockSpec(memory_space=pl.ANY)


def call(kernel, operands, specs, outs, out_specs, scratch, flops):
    return pl.pallas_call(
        kernel,
        out_shape=[jax.ShapeDtypeStruct(shape, dtype) for shape, dtype in outs],
        in_specs=specs,
        out_specs=out_specs,
        scratch_shapes=scratch,
        compiler_params=pltpu.CompilerParams(vmem_limit_bytes=26 * 1024 * 1024),
        cost_estimate=pl.CostEstimate(flops=flops, bytes_accessed=8 << 20, transcendentals=0),
    )(*operands)


@dataclasses.dataclass(frozen=True)
class Plan:
    outer: int
    inner: int
    thin: int
    tile: int
    width: int
    slots: int
    direct: bool


def flip(array, mask, devices):
    return lax.ppermute(array, ("dp", "mp"), [(d, d ^ mask) for d in range(devices)])


def gather_column(block, tile, devices):
    column = [block] + [flip(block, 8 * k, devices) for k in range(1, devices // 8)]
    rows = block.shape[0] - tile
    summed = sum(one[rows:].astype(F32) for one in column).astype(BF16)
    return jnp.concatenate([one[:rows] for one in column] + [summed], axis=0)


def gather_plane(column, devices):
    return [column] + [flip(column, mask, devices) for mask in (2, 4, 6)]


def gather_cores(plane, devices):
    pieces = []
    for piece in plane:
        pieces += [piece, flip(piece, 1, devices)]
    return pieces


def spread(rows, devices):
    across = flip(rows, 2, devices)
    return [flip(rows, 1, devices), across, flip(across, 1, devices)]


PLANE = ((0, 0), (0, 1), (1, 0), (1, 1))


def sum_cores(halves, devices):
    kept, sent = halves
    got = flip(sent, 1, devices)
    sums = [kept[at].astype(F32) + got[at].astype(F32) for at in PLANE]
    return [sums[0]] + [one.astype(BF16) for one in sums[1:]]


def plane_kernel(plan, *refs):
    terms, out_ref = refs[:-1], refs[-1]
    rows, zs = 3 * plan.thin, out_ref.shape[0]

    def added(start, count):
        return sum(ref[start : start + count, :].astype(F32) for ref in terms).astype(BF16)

    tail = added(zs * rows, plan.tile)
    for z in range(zs):
        out_ref[z, 0:rows, :] = added(z * rows, rows)
        out_ref[z, rows:, :] = tail


def sum_plane(plan, sums, devices):
    terms = [sums[0]] + [flip(one, mask, devices) for one, mask in zip(sums[1:], (2, 4, 6))]
    shape = (devices // 8, 3 * plan.thin + plan.tile, plan.width)
    (blocks,) = call(
        functools.partial(plane_kernel, plan), terms, [VMEM] * 4, [(shape, BF16)], [VMEM], [], 1 << 20
    )
    return blocks


def sum_column(blocks, devices):
    zs = devices // 8
    if zs == 1:
        return blocks
    columns = [[8 * z + at for z in range(zs)] for at in range(8)]
    return lax.all_to_all(blocks, ("dp", "mp"), 0, 0, axis_index_groups=columns, tiled=True)


def shards(patches, targets, keep_mask, attn_weights, vectors, up_weights, down_weights):
    image_count, patch_rows, width = patches.shape
    layers = attn_weights.shape[0]
    dp_size, mp_size = lax.axis_size("dp"), lax.axis_size("mp")
    devices = dp_size * mp_size
    rank = lax.axis_index("mp")
    lane_rank = lax.axis_index("dp")
    device = lane_rank * mp_size + rank
    thin = attn_weights.shape[2]
    vec_rows = vectors.shape[1]
    parts = thin * devices // width
    assert image_count == mp_size + 1 and layers == 2 and parts == mp_size == 4
    direct = thin % 16 == 0
    images, tile = 2, 16
    rows = -(-patch_rows // 16) * 16
    total = images * rows

    keep_rows = jnp.concatenate([jnp.ones((image_count, 2), jnp.int32), keep_mask], axis=1)
    keep_rows = jnp.pad(keep_rows, ((0, 0), (0, rows - patch_rows)))

    attn_turned = attn_weights.transpose(0, 2, 1)
    down_turned = down_weights.transpose(0, 2, 1)
    packing = Plan(dp_size, mp_size, thin, tile, width, SLOTS * dp_size, direct)
    block_shape = ((3 * thin + tile, width), BF16)
    first_block, last_block = call(
        functools.partial(prepare_kernel, packing),
        (attn_turned, up_weights, down_turned, vectors, keep_mask),
        [VMEM] * 5,
        [block_shape, block_shape],
        [VMEM, VMEM],
        [pltpu.VMEM((8, 2 * width), F32)],
        1 << 20,
    )
    if direct:
        plan = packing
        first_column = gather_column(first_block, tile, devices)
        first_column, last_block = lax.optimization_barrier((first_column, last_block))
        first_plane = gather_plane(first_column, devices)
        last_column = gather_column(last_block, tile, devices)
        first_plane, last_column = lax.optimization_barrier((first_plane, last_column))
        first_pieces = gather_cores(first_plane, devices)
        last_plane = gather_plane(last_column, devices)
    else:
        plan = Plan(1, parts, width, tile, width, SLOTS * dp_size, False)

        def squares(array):
            return array.reshape(parts, width, width)

        def by_part(array):
            split = array.reshape(dp_size, mp_size, thin, width).transpose(1, 0, 2, 3)
            return squares(split)

        def one_tile(array):
            summed = jnp.sum(array.astype(F32), axis=0).astype(BF16)
            return jnp.pad(summed[None], ((0, parts - 1), (0, 0), (0, 0)))

        def normal(block):
            every = lax.all_gather(block, ("dp", "mp"))
            return jnp.concatenate(
                [
                    squares(every[:, :thin]),
                    by_part(every[:, thin : 2 * thin]),
                    by_part(every[:, 2 * thin : 3 * thin]),
                    one_tile(every[:, 3 * thin :]),
                ],
                axis=1,
            )

        first_pieces, last_pieces = [normal(first_block)], [normal(last_block)]

    flat = keep_rows.reshape(-1)
    slot = jnp.where(flat == 1, jnp.cumsum(flat) - flat, SLOTS).reshape(image_count, 1, rows)

    def mine(array):
        return jnp.concatenate(
            [lax.dynamic_slice_in_dim(array, rank, 1, 0), array[mp_size:]], axis=0
        )

    def padded(array):
        return jnp.pad(mine(array), ((0, 0), (0, rows - patch_rows), (0, 0)))

    kept = mine(keep_rows)
    stream = padded(patches).reshape(total, width)
    bias = jnp.where(kept == 1, 0.0, MASKED).astype(F32)[:, None, :]
    goal = jnp.where((kept == 1)[:, :, None], padded(targets), 0).reshape(total, width)
    slots = jnp.concatenate(
        [lax.dynamic_slice_in_dim(slot, rank ^ k, 1, 0) for k in range(mp_size)] + [slot[mp_size:]],
        axis=0,
    )

    stream, slots, goal = lax.optimization_barrier((stream, slots, goal))

    pairs = width // (2 * HD)
    stream_shape = ((total, width), F32)
    low_shape = ((total, width), BF16)
    three_shape = ((3, total, width), BF16)
    turned_shape = ((width, total), BF16)
    vec_shape = ((tile, width), F32)
    attn_keep = [low_shape, three_shape, ((images, pairs, 2 * rows, rows), BF16), low_shape]
    hidden_keep = [low_shape, ((parts, total, width), BF16), ((parts, total, width), F32)]
    blocks = plan.outer * plan.inner
    weight_shape = ((blocks, plan.thin, width), BF16)
    zs = max(blocks // 8, 1)

    def vmem(shapes):
        return [pltpu.VMEM(shape, dtype) for shape, dtype in shapes]

    layer_flops = 8 * total * parts * width * width
    half_rows = 3 * plan.thin * zs + tile

    first = call(
        functools.partial(first_kernel, plan, len(first_pieces)),
        (stream, bias, *first_pieces),
        [VMEM] * (2 + len(first_pieces)),
        [weight_shape, weight_shape, weight_shape, vec_shape, stream_shape, stream_shape]
        + attn_keep
        + hidden_keep,
        [VMEM] * 13,
        vmem([stream_shape, stream_shape]),
        layer_flops,
    )
    attn_full, up_full, down_full, vec, mid, middle = first[:6]
    attn_kept, hidden_kept = first[6:10], first[10:]
    if direct:
        middle, last_plane = lax.optimization_barrier((middle, last_plane))
        last_pieces = gather_cores(last_plane, devices)
    back_scratch = [
        stream_shape,
        vec_shape,
        low_shape,
        low_shape,
        low_shape,
        stream_shape,
        stream_shape,
        turned_shape,
        turned_shape,
        three_shape,
        ((2, 2, 2, half_rows, width), BF16),
    ]
    half_shape = ((2, 2, half_rows, width), BF16)
    sems = [pltpu.SemaphoreType.DMA((4 * zs + 2,))]
    output, grad_middle, *last_halves = call(
        functools.partial(last_kernel, plan, len(last_pieces)),
        (middle, bias, goal, *last_pieces),
        [VMEM] * (3 + len(last_pieces)),
        [low_shape, stream_shape, half_shape, half_shape],
        [VMEM, VMEM, ANY, ANY],
        vmem(
            attn_keep
            + hidden_keep
            + [stream_shape, stream_shape]
            + back_scratch
            + [vec_shape]
            + [weight_shape] * 3
        )
        + sems,
        3 * layer_flops,
    )
    output_pieces = spread(output[:rows], devices)
    if direct:
        last_sums = sum_cores(last_halves, devices)
        grad_middle, last_sums, output_pieces = lax.optimization_barrier(
            (grad_middle, last_sums, output_pieces)
        )
    grad_first, *first_halves = call(
        functools.partial(back_kernel, plan),
        (grad_middle, stream, mid, vec, attn_full, up_full, down_full, *attn_kept, *hidden_kept),
        [VMEM] * 14,
        [low_shape, half_shape, half_shape],
        [VMEM, ANY, ANY],
        vmem(back_scratch) + sems,
        3 * layer_flops,
    )

    def place_images(output, output_pieces, grad_first):
        (activations,) = call(
            pack_kernel,
            (slots, output, *output_pieces),
            [VMEM] * (mp_size + 1),
            [((SLOTS, width), F32)],
            [VMEM],
            [],
            2 * SLOTS * image_count * rows * width,
        )
        (input_grads,) = call(
            place_kernel,
            (grad_first, *spread(grad_first[:rows], devices)),
            [VMEM] * mp_size,
            [((image_count, patch_rows, width), F32)],
            [VMEM],
            [],
            image_count * patch_rows * width,
        )
        return activations, input_grads

    if direct:
        last_total = sum_plane(plan, last_sums, devices)
        last_total, first_halves, grad_first = lax.optimization_barrier(
            (last_total, first_halves, grad_first)
        )
        first_sums = sum_cores(first_halves, devices)
        first_sums, output = lax.optimization_barrier((first_sums, output))
        last_terms = sum_column(last_total, devices)
        first_total = sum_plane(plan, first_sums, devices)
        images_out = place_images(output, output_pieces, grad_first)
        first_total, images_out = lax.optimization_barrier((first_total, images_out))
        first_terms = sum_column(first_total, devices)
        turned = (layers, thin, width)
        attn_grads, vector_grads, up_grads, down_grads = call(
            functools.partial(finish_kernel, plan),
            (first_terms, last_terms),
            [VMEM] * 2,
            [(turned, F32), (vectors.shape, F32), (turned, F32), (turned, F32)],
            [VMEM] * 4,
            vmem([vec_shape, vec_shape]),
            1 << 20,
        )
        attn_grads, down_grads = attn_grads.transpose(0, 2, 1), down_grads.transpose(0, 2, 1)
    else:

        def square_blocks(halves):
            stacked = jnp.stack(halves)[:, 0]
            stacked = jnp.stack([stacked[k % 2, k // 2] for k in range(parts)])
            return jnp.stack(
                [lax.dynamic_index_in_dim(stacked, rank ^ k, 0, False) for k in range(parts)]
            )

        def outputs_of(halves):
            def by_owner(array):
                split = array.reshape(mp_size, dp_size, thin, width).transpose(1, 0, 2, 3)
                return split.reshape(devices, thin, width)

            every = square_blocks(halves)
            pieces = [
                every[:, :width].reshape(devices, thin, width),
                by_owner(every[:, width : 2 * width]),
                by_owner(every[:, 2 * width : 3 * width]),
                jnp.broadcast_to(every[0, 3 * width :], (devices, tile, width)),
            ]
            owned = lax.psum_scatter(
                jnp.concatenate(pieces, axis=1), ("dp", "mp"), scatter_dimension=0, tiled=False
            ).astype(F32)
            own_vec = lax.dynamic_slice_in_dim(
                owned[3 * thin :].reshape(-1), device * vec_rows, vec_rows
            )
            return owned[:thin].T, own_vec, owned[thin : 2 * thin], owned[2 * thin : 3 * thin].T

        attn_grads, vector_grads, up_grads, down_grads = (
            jnp.stack([one, two]) for one, two in zip(outputs_of(first_halves), outputs_of(last_halves))
        )
        images_out = place_images(output, output_pieces, grad_first)

    activations, input_grads = images_out
    return (activations, input_grads, attn_grads, vector_grads, up_grads, down_grads)


def solution(mesh):
    in_specs = (
        P("dp", None, None),
        P("dp", None, None),
        P("dp", None),
        P(None, None, ("dp", "mp")),
        P(None, ("dp", "mp")),
        P(None, "dp", "mp"),
        P(None, "mp", "dp"),
    )
    out_specs = (
        P("dp", None),
        P("dp", None, None),
        P(None, None, ("dp", "mp")),
        P(None, ("dp", "mp")),
        P(None, "dp", "mp"),
        P(None, "mp", "dp"),
    )
    return jax.shard_map(shards, mesh=mesh, in_specs=in_specs, out_specs=out_specs, check_vma=False)
```

```python
import dataclasses
import functools

import jax
import jax.numpy as jnp
from jax import lax
from jax.experimental import pallas as pl
from jax.experimental.pallas import tpu as pltpu
from jax.sharding import PartitionSpec as P

HD = 64
SLOTS = 1024
EPSILON = 1e-06
MASKED = -1e30
STEP = 16
UNROLL = 13

F32 = jnp.float32
BF16 = jnp.bfloat16


def dot_nn(left, right):
    return lax.dot_general(left, right, (((1,), (0,)), ((), ())), preferred_element_type=F32)


def dot_nt(left, right):
    return lax.dot_general(left, right, (((1,), (1,)), ((), ())), preferred_element_type=F32)


def dot_tn(left, right):
    return lax.dot_general(left, right, (((0,), (0,)), ((), ())), preferred_element_type=F32)


def block_rows(index, step):
    return pl.ds(pl.multiple_of(index * step, step), step)


def fold_rows(values):
    return jnp.sum(values.reshape(values.shape[0] // 8, 8, values.shape[1]), axis=0)


def low_halves(rows):
    lane = lax.broadcasted_iota(jnp.int32, (rows, 2 * HD), 1)
    return lane < HD


def stack_heads(pair):
    low = low_halves(pair.shape[0])
    zero = jnp.zeros_like(pair)
    return jnp.concatenate([jnp.where(low, pair, zero), jnp.where(low, zero, pair)], axis=0)


def unstack_heads(stacked):
    rows = stacked.shape[0] // 2
    return jnp.where(low_halves(rows), stacked[:rows], stacked[rows:])


def norm_rows(x_ref, out_ref, gain, shift):
    def body(index, carry):
        at = block_rows(index, STEP)
        values = x_ref[at, :].astype(F32)
        centred = values - jnp.mean(values, axis=-1, keepdims=True)
        variance = jnp.mean(centred * centred, axis=-1, keepdims=True)
        out_ref[at, :] = (centred * lax.rsqrt(variance + EPSILON) * gain + shift).astype(BF16)
        return carry

    lax.fori_loop(0, x_ref.shape[0] // STEP, body, 0, unroll=UNROLL)


def norm_back(x_ref, grad_ref, base_ref, out_ref, low_ref, gain, images):
    rows = x_ref.shape[0] // images
    width = x_ref.shape[1]
    sums = []
    for image in range(images):

        def body(index, carry, image=image):
            at = pl.ds(pl.multiple_of(image * rows + index * STEP, STEP), STEP)
            values = x_ref[at, :].astype(F32)
            grad = grad_ref[at, :]
            centred = values - jnp.mean(values, axis=-1, keepdims=True)
            variance = jnp.mean(centred * centred, axis=-1, keepdims=True)
            inverse = lax.rsqrt(variance + EPSILON)
            unit = centred * inverse
            scaled = grad * gain
            mean_one = jnp.mean(scaled, axis=-1, keepdims=True)
            mean_two = jnp.mean(scaled * unit, axis=-1, keepdims=True)
            out = base_ref[at, :] + inverse * (scaled - mean_one - unit * mean_two)
            out_ref[at, :] = out.astype(out_ref.dtype)
            if low_ref is not None:
                low_ref[at, :] = out.astype(BF16)
            return (
                carry[0] + fold_rows(grad * unit),
                carry[1] + fold_rows(grad),
                carry[2] + fold_rows(out),
            )

        zero = jnp.zeros((8, width), F32)
        sums.append(lax.fori_loop(0, rows // STEP, body, (zero, zero, zero), unroll=UNROLL))
    return sums


def weigh(sums, share):
    total = sums[0]
    for more in sums[1:]:
        total = total + more * share
    return jnp.sum(total, axis=0, keepdims=True)


def as_square(ref, part):
    rows, width = ref.shape[1:]
    per = width // rows
    return ref[pl.ds(part * per, per)].reshape(width, width)


def forward_attention(x_ref, bias_ref, vec_ref, attn_ref, keep, mid_ref):
    n1_ref, proj_ref, p_ref, att_ref = keep
    images = bias_ref.shape[0]
    rows = x_ref.shape[0] // images
    width = x_ref.shape[1]
    pairs = width // (2 * HD)
    scale = HD**-0.5

    norm_rows(x_ref, n1_ref, vec_ref[0:1, :], vec_ref[1:2, :])
    for part, bias_row in enumerate((4, None, 5)):
        value = dot_nt(n1_ref[...], as_square(attn_ref, part))
        if bias_row is not None:
            value = value + vec_ref[bias_row : bias_row + 1, :]
        proj_ref[part] = value.astype(BF16)

    def image_body(image, carry):
        at = block_rows(image, rows)
        for pair in range(pairs):
            lanes = slice(pair * 2 * HD, (pair + 1) * 2 * HD)
            query = stack_heads(proj_ref[0, at, lanes])
            scores = dot_nt(query, proj_ref[1, at, lanes]) * scale + bias_ref[image]
            top = jnp.max(scores, axis=-1, keepdims=True)
            powers = jnp.exp(scores - top)
            total = jnp.sum(powers, axis=-1, keepdims=True)
            probs = (powers * (1.0 / total)).astype(BF16)
            p_ref[image, pair] = probs
            att_ref[at, lanes] = unstack_heads(dot_nn(probs, proj_ref[2, at, lanes])).astype(BF16)
        return carry

    lax.fori_loop(0, images, image_body, 0)
    mid_ref[...] = x_ref[...].astype(F32) + dot_nt(att_ref[...], as_square(attn_ref, 3)) + vec_ref[6:7, :]


def forward_hidden(mid_ref, vec_ref, up_ref, down_ref, keep, scratch, out_ref):
    n2_ref, a_ref, gp_ref = keep
    h_ref, acc_ref = scratch
    norm_rows(mid_ref, n2_ref, vec_ref[2:3, :], vec_ref[3:4, :])
    acc_ref[...] = mid_ref[...] + vec_ref[11:12, :]

    def part_body(part, carry):
        h_ref[...] = dot_nn(n2_ref[...], as_square(up_ref, part))
        bias = vec_ref[pl.ds(7 + part, 1), :]

        def gelu_body(index, inner):
            at = block_rows(index, STEP)
            hidden = h_ref[at, :] + bias
            share = 0.5 + 0.5 * lax.erf(hidden * 0.7071067811865476)
            a_ref[part, at, :] = (hidden * share).astype(BF16)
            bell = jnp.exp(-0.5 * hidden * hidden) * 0.3989422804014327
            gp_ref[part, at, :] = (share + hidden * bell).astype(gp_ref.dtype)
            return inner

        lax.fori_loop(0, h_ref.shape[0] // STEP, gelu_body, 0, unroll=UNROLL)
        acc_ref[...] += dot_nt(a_ref[part], as_square(down_ref, part))
        return carry

    lax.fori_loop(0, a_ref.shape[0], part_body, 0)
    out_ref[...] = acc_ref[...].astype(out_ref.dtype)


def drop_shared(refs):
    @pl.when(jnp.logical_not(counts_shared()))
    def _():
        for ref in refs:
            rows = ref.shape[-2] // 2
            ref[..., rows:, :] = jnp.zeros((*ref.shape[:-2], rows, ref.shape[-1]), ref.dtype)


def backward_hidden(g_ref, mid_ref, vec_ref, up_ref, down_ref, share, keep, scratch, gm_ref, gvec_ref, store):
    n2_ref, a_ref, gp_ref = keep
    go_ref, gh_ref, acc_ref, h_ref, got_ref, n2t_ref = scratch
    images = 2
    rows = mid_ref.shape[0] // images
    width = mid_ref.shape[1]
    zero = jnp.zeros((8, width), F32)
    sums = []
    for image in range(images):

        def low_body(index, carry, image=image):
            at = pl.ds(pl.multiple_of(image * rows + index * STEP, STEP), STEP)
            grad = g_ref[at, :]
            go_ref[at, :] = grad.astype(BF16)
            return carry + fold_rows(grad)

        sums.append(lax.fori_loop(0, rows // STEP, low_body, zero, unroll=UNROLL))
    gvec_ref[11:12, :] = weigh(sums, share)
    acc_ref[...] = jnp.zeros_like(acc_ref)
    got_ref[...] = go_ref[...].T
    n2t_ref[...] = n2_ref[...].T

    def part_body(part, carry):
        store(2, part, dot_nn(got_ref[...], a_ref[part]))
        h_ref[...] = dot_nn(go_ref[...], as_square(down_ref, part))
        inner_sums = []
        for image in range(images):

            def hidden_body(index, inner, image=image):
                at = pl.ds(pl.multiple_of(image * rows + index * STEP, STEP), STEP)
                grad = (h_ref[at, :] * gp_ref[part, at, :].astype(F32)).astype(BF16)
                gh_ref[at, :] = grad
                return inner + fold_rows(grad.astype(F32))

            inner_sums.append(lax.fori_loop(0, rows // STEP, hidden_body, zero, unroll=UNROLL))
        gvec_ref[pl.ds(7 + part, 1), :] = weigh(inner_sums, share)
        store(1, part, dot_nn(n2t_ref[...], gh_ref[...]))
        acc_ref[...] += dot_nt(gh_ref[...], as_square(up_ref, part))
        return carry

    lax.fori_loop(0, a_ref.shape[0], part_body, 0)
    sums = norm_back(mid_ref, acc_ref, g_ref, gm_ref, None, vec_ref[2:3, :], images)
    for place, row in enumerate((2, 3, 6)):
        gvec_ref[row : row + 1, :] = weigh([one[place] for one in sums], share)


def backward_attention(gm_ref, x_ref, vec_ref, attn_ref, share, keep, scratch, gx_ref, gvec_ref, store):
    n1_ref, proj_ref, p_ref, att_ref = keep
    go_ref, acc_ref, ga_ref, dproj_ref = scratch
    images = p_ref.shape[0]
    rows = x_ref.shape[0] // images
    width = x_ref.shape[1]
    pairs = width // (2 * HD)
    scale = HD**-0.5
    go_ref[...] = gm_ref[...].astype(BF16)
    store(0, 3, dot_tn(go_ref[...], att_ref[...]))
    ga_ref[...] = dot_nn(go_ref[...], as_square(attn_ref, 3)).astype(BF16)

    def image_body(image, carry):
        at = block_rows(image, rows)
        for pair in range(pairs):
            lanes = slice(pair * 2 * HD, (pair + 1) * 2 * HD)
            query = stack_heads(proj_ref[0, at, lanes])
            keys = proj_ref[1, at, lanes]
            grad_out = stack_heads(ga_ref[at, lanes])
            probs = p_ref[image, pair]
            grad_probs = dot_nt(grad_out, proj_ref[2, at, lanes])
            dproj_ref[2, at, lanes] = dot_tn(probs, grad_out).astype(BF16)
            wide = probs.astype(F32)
            inner = jnp.sum(grad_probs * wide, axis=-1, keepdims=True)
            grad_scores = (wide * (grad_probs - inner)).astype(BF16)
            dproj_ref[0, at, lanes] = (unstack_heads(dot_nn(grad_scores, keys)) * scale).astype(BF16)
            dproj_ref[1, at, lanes] = (dot_tn(grad_scores, query) * scale).astype(BF16)
        return carry

    lax.fori_loop(0, images, image_body, 0)
    for part, row in enumerate((4, None, 5)):
        store(0, part, dot_tn(dproj_ref[part], n1_ref[...]))
        value = dot_nn(dproj_ref[part], as_square(attn_ref, part))
        if part == 0:
            acc_ref[...] = value
        else:
            acc_ref[...] += value
        if row is not None:
            sums = [
                fold_rows(dproj_ref[part, image * rows : (image + 1) * rows, :].astype(F32))
                for image in range(images)
            ]
            gvec_ref[row : row + 1, :] = weigh(sums, share)
    sums = norm_back(x_ref, acc_ref, gm_ref, gx_ref, None, vec_ref[0:1, :], images)
    for place, row in enumerate((0, 1)):
        gvec_ref[row : row + 1, :] = weigh([one[place] for one in sums], share)
    store(3, 0, gvec_ref[...])


def coordinates(plan):
    outer, inner = lax.axis_index("dp"), lax.axis_index("mp")
    here = (inner // 2, inner % 2)
    return (outer // 2, outer % 2, *here) if plan.direct else (0, 0, *here)


def counts_shared():
    return lax.axis_index("mp") == 0


def place_weights(plan, pieces, by_distance, attn_ref, up_ref, down_ref, vec_ref):
    thin, rows = plan.thin, 3 * plan.thin

    def put(owner, block):
        at = owner % plan.inner * plan.outer + owner // plan.inner
        attn_ref[owner] = block[:thin]
        up_ref[at] = block[thin : 2 * thin]
        down_ref[at] = block[2 * thin : 3 * thin]

    if not plan.direct:
        for owner in range(plan.inner):
            put(owner, pieces[0][owner, :rows])
        vec_ref[...] = pieces[0][0, rows:].astype(F32)
        return
    at = coordinates(plan)
    vec = None
    for i, piece in enumerate(pieces):
        c, x, y = i % 2, i // 2 % 2, i // 4
        low = ((at[1] ^ y) * 2 + (at[2] ^ x)) * 2 + (at[3] ^ c)
        count = piece.shape[0] // rows
        for k in range(count):
            put(((at[0] ^ k) if by_distance else k) * 8 + low, piece[k * rows : (k + 1) * rows])
        tail = piece[count * rows :].astype(F32)
        vec = tail if vec is None else vec + tail
    vec_ref[...] = vec


def storer(plan, packed_ref):
    thin, width = plan.thin, plan.width
    per = width // thin
    core = lax.axis_index("mp") % 2

    def put(owner, kind, block):
        c, x, y = owner % 2, owner // 2 % 2, owner // 4 % 2
        row = pl.multiple_of((owner // 8 * 3 + kind) * thin, thin)
        packed_ref[c ^ core, y, x, pl.ds(row, thin), :] = block

    def store(kind, part, value):
        low = value.astype(BF16)
        if kind == 3:
            for i in range(8):
                packed_ref[i % 2, i // 4, i // 2 % 2, packed_ref.shape[3] - plan.tile :, :] = low
            return
        blocks = low.reshape(per, thin, width)
        for i in range(per):
            owner = part * per + i if kind == 0 else i * plan.inner + part
            put(owner, kind, blocks[i])

    return store


def send_hidden(plan, packed_ref, outs, sems):
    thin = plan.thin
    copies = []
    for z in range((packed_ref.shape[3] - plan.tile) // (3 * thin)):
        at = pl.ds((3 * z + 1) * thin, 2 * thin)
        for i in range(2):
            source, target = packed_ref.at[i, :, :, at], outs[i].at[:, :, at]
            copies.append(pltpu.make_async_copy(source, target, sems.at[len(copies)]))
    for one in copies:
        one.start()
    return copies


def send_rest(plan, packed_ref, outs, sems, copies):
    thin, tile = plan.thin, plan.tile
    more = list(copies)
    last = packed_ref.shape[3] - tile
    places = [pl.ds(3 * z * thin, thin) for z in range(last // (3 * thin))] + [pl.ds(last, tile)]
    for at in places:
        for i in range(2):
            source, target = packed_ref.at[i, :, :, at], outs[i].at[:, :, at]
            more.append(pltpu.make_async_copy(source, target, sems.at[len(more)]))
    for one in more[len(copies) :]:
        one.start()
    for one in more:
        one.wait()


def prepare_kernel(plan, attn_ref, up_ref, down_ref, vec_in, keep_in, first_ref, last_ref, line_ref, vec_ref, keep_ref, sems):
    thin, tile, width = plan.thin, plan.tile, plan.width
    outs = (first_ref, last_ref)
    copies = [
        pltpu.make_async_copy(vec_in, vec_ref, sems.at[0]),
        pltpu.make_async_copy(keep_in, keep_ref, sems.at[1]),
    ]
    for kind, ref in enumerate((attn_ref, up_ref, down_ref)):
        for layer, out_ref in enumerate(outs):
            if plan.direct:
                target = out_ref.at[pl.ds(kind * thin, thin)]
                copies.append(pltpu.make_async_copy(ref.at[layer], target, sems.at[len(copies)]))
            else:
                out_ref[kind * thin : (kind + 1) * thin, :] = ref[layer]
    for one in copies:
        one.start()
    count = vec_ref.shape[1]
    device = lax.axis_index("dp") * plan.inner + lax.axis_index("mp")
    row_at = device * count // width
    offset = device * count - row_at * width
    copies[0].wait()
    copies[1].wait()
    kept = jnp.sum(keep_ref[...]) + 2 * keep_ref.shape[0]
    kept = jnp.where(counts_shared(), kept, 0)
    row = lax.broadcasted_iota(jnp.int32, (tile, width), 0)
    here = lax.broadcasted_iota(jnp.int32, (tile, width), 1) == lax.axis_index("dp")
    for layer, out_ref in enumerate(outs):
        line_ref[...] = jnp.zeros_like(line_ref)
        line_ref[0:1, 0:count] = vec_ref[layer : layer + 1, :].astype(F32)
        moved = pltpu.roll(line_ref[...], offset, 1)[0:1]
        piece = jnp.where(row == row_at, moved[:, :width], 0.0)
        piece = jnp.where(row == row_at + 1, moved[:, width:], piece)
        if layer == 1:
            piece = jnp.where(here & (row == 12), (kept >> 5).astype(F32), piece)
            piece = jnp.where(here & (row == 13), (kept & 31).astype(F32), piece)
        out_ref[3 * thin :, :] = piece.astype(BF16)
    for one in copies[2:]:
        one.wait()


def first_kernel(plan, pieces, x_ref, bias_ref, *refs):
    sources, refs = refs[:pieces], refs[pieces:]
    attn_ref, up_ref, down_ref, vec_ref, mid_ref, out_ref, *refs = refs
    attn_keep, hidden_keep, (h_ref, acc_ref) = refs[:4], refs[4:7], refs[7:]
    place_weights(plan, sources, True, attn_ref, up_ref, down_ref, vec_ref)
    forward_attention(x_ref, bias_ref, vec_ref, attn_ref, attn_keep, mid_ref)
    forward_hidden(mid_ref, vec_ref, up_ref, down_ref, hidden_keep, (h_ref, acc_ref), out_ref)
    drop_shared((attn_keep[0], attn_keep[3], hidden_keep[0], hidden_keep[1]))


def last_kernel(plan, pieces, x_ref, bias_ref, goal_ref, *refs):
    sources, refs = refs[:pieces], refs[pieces:]
    out_ref, gx_ref, outs, refs = refs[0], refs[1], refs[2:4], refs[4:]
    attn_keep, hidden_keep, refs = refs[0:4], refs[4:7], refs[7:]
    mid_ref, g_ref, gm_ref, gvec_ref, go_ref, gh_ref, ga_ref, acc_ref, h_ref, got_ref, n2t_ref, dproj_ref = refs[:12]
    packed_ref, vec_ref, attn_ref, up_ref, down_ref, sems = refs[12:]
    place_weights(plan, sources, False, attn_ref, up_ref, down_ref, vec_ref)
    forward_attention(x_ref, bias_ref, vec_ref, attn_ref, attn_keep, mid_ref)
    forward_hidden(mid_ref, vec_ref, up_ref, down_ref, hidden_keep, (h_ref, acc_ref), out_ref)
    drop_shared((attn_keep[0], attn_keep[3], hidden_keep[0], hidden_keep[1]))
    high = jnp.sum(vec_ref[12:13, :], axis=-1, keepdims=True)
    rest = jnp.sum(vec_ref[13:14, :], axis=-1, keepdims=True)
    loss_scale = float(plan.slots) / (high * 32.0 + rest)
    g_ref[...] = goal_ref[...].astype(F32) * loss_scale
    gvec_ref[...] = jnp.zeros_like(gvec_ref)
    share = counts_shared().astype(F32)
    store = storer(plan, packed_ref)
    scratch = (go_ref, gh_ref, acc_ref, h_ref, got_ref, n2t_ref)
    backward_hidden(g_ref, mid_ref, vec_ref, up_ref, down_ref, share, hidden_keep, scratch, gm_ref, gvec_ref, store)
    copies = send_hidden(plan, packed_ref, outs, sems)
    scratch = (go_ref, acc_ref, ga_ref, dproj_ref)
    backward_attention(gm_ref, x_ref, vec_ref, attn_ref, share, attn_keep, scratch, gx_ref, gvec_ref, store)
    send_rest(plan, packed_ref, outs, sems, copies)


def back_kernel(plan, g_ref, x_ref, mid_ref, vec_ref, attn_ref, up_ref, down_ref, *refs):
    attn_keep, hidden_keep, gx_ref, outs, refs = refs[:4], refs[4:7], refs[7], refs[8:10], refs[10:]
    gm_ref, gvec_ref, go_ref, gh_ref, ga_ref, acc_ref, h_ref, got_ref, n2t_ref, dproj_ref, packed_ref, sems = refs
    gvec_ref[...] = jnp.zeros_like(gvec_ref)
    share = counts_shared().astype(F32)
    store = storer(plan, packed_ref)
    scratch = (go_ref, gh_ref, acc_ref, h_ref, got_ref, n2t_ref)
    backward_hidden(g_ref, mid_ref, vec_ref, up_ref, down_ref, share, hidden_keep, scratch, gm_ref, gvec_ref, store)
    copies = send_hidden(plan, packed_ref, outs, sems)
    scratch = (go_ref, acc_ref, ga_ref, dproj_ref)
    backward_attention(gm_ref, x_ref, vec_ref, attn_ref, share, attn_keep, scratch, gx_ref, gvec_ref, store)
    send_rest(plan, packed_ref, outs, sems, copies)


def finish_kernel(plan, terms, *refs):
    (late, *early), (attn_out, vec_out, up_out, down_out, *tiles) = refs[:terms], refs[terms:]
    thin, tile, width = plan.thin, plan.tile, plan.width

    count = vec_out.shape[1]
    device = lax.axis_index("dp") * plan.inner + lax.axis_index("mp")
    row = device * count // width
    offset = device * count - row * width
    for layer in range(2):

        def total(start, count, layer=layer):
            at = slice(start, start + count)
            blocks = [ref[at, :] for ref in early] if layer == 0 else [late[k, at, :] for k in range(late.shape[0])]
            return sum(block.astype(F32) for block in blocks)

        attn_out[layer] = total(0, thin)
        up_out[layer] = total(thin, thin)
        down_out[layer] = total(2 * thin, thin)
        tiles[layer][...] = total(3 * thin, tile)
        both = jnp.concatenate(
            [tiles[layer][pl.ds(row, 1), :], tiles[layer][pl.ds(row + 1, 1), :]], axis=1
        )
        both = jnp.broadcast_to(both, (8, 2 * width))
        moved = pltpu.roll(both, 2 * width - offset, 1)
        vec_out[layer : layer + 1, :] = moved[0:1, :count]


def place_kernel(own_ref, *refs):
    others, out_ref = refs[:-1], refs[-1]
    rows = own_ref.shape[0] // 2
    kept = out_ref.shape[1]
    mine = lax.axis_index("mp")
    out_ref[mine] = own_ref[0:rows, :].astype(F32)[:kept]
    for i, ref in enumerate(others):
        out_ref[mine ^ (i + 1)] = ref[...].astype(F32)[:kept]
    out_ref[out_ref.shape[0] - 1] = own_ref[rows : 2 * rows, :].astype(F32)[:kept]


def pack_kernel(slot_ref, own_ref, *refs):
    others, out_ref = refs[:-1], refs[-1]
    rows = own_ref.shape[0] // 2
    sources = [own_ref[0:rows, :]] + [ref[...] for ref in others] + [own_ref[rows : 2 * rows, :]]
    step = 256

    def body(index, carry):
        slots = lax.broadcasted_iota(jnp.int32, (step, rows), 0) + index * step
        total = None
        for i, values in enumerate(sources):
            picks = jnp.where(slots == slot_ref[i], 1.0, 0.0).astype(BF16)
            term = dot_nn(picks, values)
            total = term if total is None else total + term
        out_ref[block_rows(index, step), :] = total
        return carry

    lax.fori_loop(0, out_ref.shape[0] // step, body, 0)


VMEM = pl.BlockSpec(memory_space=pltpu.VMEM)
ANY = pl.BlockSpec(memory_space=pl.ANY)


def call(kernel, operands, specs, outs, out_specs, scratch, flops):
    return pl.pallas_call(
        kernel,
        out_shape=[jax.ShapeDtypeStruct(shape, dtype) for shape, dtype in outs],
        in_specs=specs,
        out_specs=out_specs,
        scratch_shapes=scratch,
        compiler_params=pltpu.CompilerParams(vmem_limit_bytes=26 * 1024 * 1024),
        cost_estimate=pl.CostEstimate(flops=flops, bytes_accessed=8 << 20, transcendentals=0),
    )(*operands)


@dataclasses.dataclass(frozen=True)
class Plan:
    outer: int
    inner: int
    thin: int
    tile: int
    width: int
    slots: int
    direct: bool


def flip(array, mask, devices):
    return lax.ppermute(array, ("dp", "mp"), [(d, d ^ mask) for d in range(devices)])


def gather_column(block, tile, devices, by_permutes):
    zs = devices // 8
    if by_permutes:
        column = [block] + [flip(block, 8 * k, devices) for k in range(1, zs)]
    else:
        column = exchange(jnp.broadcast_to(block, (zs, *block.shape)), column_groups(devices))
        column = [column[k] for k in range(zs)]
    rows = block.shape[0] - tile
    summed = sum(one[rows:].astype(F32) for one in column).astype(BF16)
    return jnp.concatenate([one[:rows] for one in column] + [summed], axis=0)


def gather_plane(column, devices):
    return [column] + [flip(column, mask, devices) for mask in (2, 4, 6)]


def gather_cores(plane, devices):
    pieces = []
    for piece in plane:
        pieces += [piece, flip(piece, 1, devices)]
    return pieces


def spread(rows, devices):
    across = flip(rows, 2, devices)
    return [flip(rows, 1, devices), across, flip(across, 1, devices)]


def sum_cores(halves, devices):
    kept, sent = halves
    total = kept.astype(F32) + flip(sent, 1, devices).astype(F32)
    return total.astype(BF16).reshape(4, *kept.shape[2:])


def plane_kernel(plan, terms_ref, *out_refs):
    rows, tile = 3 * plan.thin, plan.tile
    zs = (terms_ref.shape[1] - tile) // rows

    def added(start, count):
        terms = [terms_ref[k, pl.ds(start, count), :].astype(F32) for k in range(4)]
        return sum(terms).astype(BF16)

    tail = added(zs * rows, tile)
    for z in range(zs):
        if len(out_refs) == 1:
            out_refs[0][z, 0:rows, :] = added(z * rows, rows)
            out_refs[0][z, rows:, :] = tail
        else:
            at = pl.multiple_of((coordinates(plan)[0] ^ z) * rows, rows)
            out_refs[z][0:rows, :] = added(at, rows)
            out_refs[z][rows:, :] = tail


def exchange(blocks, groups):
    return lax.all_to_all(blocks, ("dp", "mp"), 0, 0, axis_index_groups=groups, tiled=True)


def column_groups(devices):
    return [[8 * z + at for z in range(devices // 8)] for at in range(8)]


def sum_plane(plan, sums, devices, apart):
    zs = devices // 8
    planes = [[8 * z + 2 * at + c for at in range(4)] for z in range(zs) for c in range(2)]
    terms = exchange(sums, planes)
    shape = (3 * plan.thin + plan.tile, plan.width)
    outs = [(shape, BF16)] * zs if apart else [((zs, *shape), BF16)]
    return call(
        functools.partial(plane_kernel, plan), (terms,), [VMEM], outs, [VMEM] * len(outs), [], 1 << 20
    )


def shards(patches, targets, keep_mask, attn_weights, vectors, up_weights, down_weights):
    image_count, patch_rows, width = patches.shape
    layers = attn_weights.shape[0]
    dp_size, mp_size = lax.axis_size("dp"), lax.axis_size("mp")
    devices = dp_size * mp_size
    rank = lax.axis_index("mp")
    lane_rank = lax.axis_index("dp")
    device = lane_rank * mp_size + rank
    thin = attn_weights.shape[2]
    vec_rows = vectors.shape[1]
    parts = thin * devices // width
    assert image_count == mp_size + 1 and layers == 2 and parts == mp_size == 4
    direct = thin % 16 == 0
    images, tile = 2, 16
    rows = -(-patch_rows // 16) * 16
    total = images * rows

    keep_rows = jnp.concatenate([jnp.ones((image_count, 2), jnp.int32), keep_mask], axis=1)
    keep_rows = jnp.pad(keep_rows, ((0, 0), (0, rows - patch_rows)))

    attn_turned = attn_weights.transpose(0, 2, 1)
    down_turned = down_weights.transpose(0, 2, 1)
    packing = Plan(dp_size, mp_size, thin, tile, width, SLOTS * dp_size, direct)
    block_shape = ((3 * thin + tile, width), BF16)
    first_block, last_block = call(
        functools.partial(prepare_kernel, packing),
        (attn_turned, up_weights, down_turned, vectors, keep_mask),
        [ANY if direct else VMEM] * 3 + [ANY] * 2,
        [block_shape, block_shape],
        [VMEM, VMEM],
        [
            pltpu.VMEM((8, 2 * width), F32),
            pltpu.VMEM(vectors.shape, BF16),
            pltpu.VMEM(keep_mask.shape, jnp.int32),
            pltpu.SemaphoreType.DMA((8,)),
        ],
        1 << 20,
    )
    if direct:
        plan = packing
        first_column = gather_column(first_block, tile, devices, True)
        first_column, last_block = lax.optimization_barrier((first_column, last_block))
        first_plane = gather_plane(first_column, devices)
        last_column = gather_column(last_block, tile, devices, False)
        first_plane, last_column = lax.optimization_barrier((first_plane, last_column))
        first_pieces = gather_cores(first_plane, devices)
        last_plane = gather_plane(last_column, devices)
    else:
        plan = Plan(1, parts, width, tile, width, SLOTS * dp_size, False)

        def squares(array):
            return array.reshape(parts, width, width)

        def by_part(array):
            split = array.reshape(dp_size, mp_size, thin, width).transpose(1, 0, 2, 3)
            return squares(split)

        def one_tile(array):
            summed = jnp.sum(array.astype(F32), axis=0).astype(BF16)
            return jnp.pad(summed[None], ((0, parts - 1), (0, 0), (0, 0)))

        def normal(block):
            every = lax.all_gather(block, ("dp", "mp"))
            return jnp.concatenate(
                [
                    squares(every[:, :thin]),
                    by_part(every[:, thin : 2 * thin]),
                    by_part(every[:, 2 * thin : 3 * thin]),
                    one_tile(every[:, 3 * thin :]),
                ],
                axis=1,
            )

        first_pieces, last_pieces = [normal(first_block)], [normal(last_block)]

    flat = keep_rows.reshape(-1)
    slot = jnp.where(flat == 1, jnp.cumsum(flat) - flat, SLOTS).reshape(image_count, 1, rows)

    def mine(array):
        return jnp.concatenate(
            [lax.dynamic_slice_in_dim(array, rank, 1, 0), array[mp_size:]], axis=0
        )

    def padded(array):
        return jnp.pad(mine(array), ((0, 0), (0, rows - patch_rows), (0, 0)))

    kept = mine(keep_rows)
    stream = padded(patches).reshape(total, width)
    bias = jnp.where(kept == 1, 0.0, MASKED).astype(F32)[:, None, :]
    goal = jnp.where((kept == 1)[:, :, None], padded(targets), 0).reshape(total, width)
    slots = jnp.concatenate(
        [lax.dynamic_slice_in_dim(slot, rank ^ k, 1, 0) for k in range(mp_size)] + [slot[mp_size:]],
        axis=0,
    )

    stream, slots, goal = lax.optimization_barrier((stream, slots, goal))

    pairs = width // (2 * HD)
    stream_shape = ((total, width), F32)
    low_shape = ((total, width), BF16)
    three_shape = ((3, total, width), BF16)
    turned_shape = ((width, total), BF16)
    vec_shape = ((tile, width), F32)
    attn_keep = [low_shape, three_shape, ((images, pairs, 2 * rows, rows), BF16), low_shape]
    hidden_keep = [low_shape, ((parts, total, width), BF16), ((parts, total, width), F32)]
    blocks = plan.outer * plan.inner
    weight_shape = ((blocks, plan.thin, width), BF16)
    zs = max(blocks // 8, 1)

    def vmem(shapes):
        return [pltpu.VMEM(shape, dtype) for shape, dtype in shapes]

    layer_flops = 8 * total * parts * width * width
    half_rows = 3 * plan.thin * zs + tile

    first = call(
        functools.partial(first_kernel, plan, len(first_pieces)),
        (stream, bias, *first_pieces),
        [VMEM] * (2 + len(first_pieces)),
        [weight_shape, weight_shape, weight_shape, vec_shape, stream_shape, stream_shape]
        + attn_keep
        + hidden_keep,
        [VMEM] * 13,
        vmem([stream_shape, stream_shape]),
        layer_flops,
    )
    attn_full, up_full, down_full, vec, mid, middle = first[:6]
    attn_kept, hidden_kept = first[6:10], first[10:]
    if direct:
        middle, last_plane = lax.optimization_barrier((middle, last_plane))
        last_pieces = gather_cores(last_plane, devices)
    back_scratch = [
        stream_shape,
        vec_shape,
        low_shape,
        low_shape,
        low_shape,
        stream_shape,
        stream_shape,
        turned_shape,
        turned_shape,
        three_shape,
        ((2, 2, 2, half_rows, width), BF16),
    ]
    half_shape = ((2, 2, half_rows, width), BF16)
    sems = [pltpu.SemaphoreType.DMA((4 * zs + 2,))]
    output, grad_middle, *last_halves = call(
        functools.partial(last_kernel, plan, len(last_pieces)),
        (middle, bias, goal, *last_pieces),
        [VMEM] * (3 + len(last_pieces)),
        [low_shape, stream_shape, half_shape, half_shape],
        [VMEM, VMEM, ANY, ANY],
        vmem(
            attn_keep
            + hidden_keep
            + [stream_shape, stream_shape]
            + back_scratch
            + [vec_shape]
            + [weight_shape] * 3
        )
        + sems,
        3 * layer_flops,
    )
    output_pieces = spread(output[:rows], devices)
    if direct:
        last_sums = sum_cores(last_halves, devices)
        grad_middle, last_sums, output_pieces = lax.optimization_barrier(
            (grad_middle, last_sums, output_pieces)
        )
    grad_first, *first_halves = call(
        functools.partial(back_kernel, plan),
        (grad_middle, stream, mid, vec, attn_full, up_full, down_full, *attn_kept, *hidden_kept),
        [VMEM] * 14,
        [low_shape, half_shape, half_shape],
        [VMEM, ANY, ANY],
        vmem(back_scratch) + sems,
        3 * layer_flops,
    )

    def place_images(output, output_pieces, grad_first):
        (activations,) = call(
            pack_kernel,
            (slots, output, *output_pieces),
            [VMEM] * (mp_size + 1),
            [((SLOTS, width), F32)],
            [VMEM],
            [],
            2 * SLOTS * image_count * rows * width,
        )
        (input_grads,) = call(
            place_kernel,
            (grad_first, *spread(grad_first[:rows], devices)),
            [VMEM] * mp_size,
            [((image_count, patch_rows, width), F32)],
            [VMEM],
            [],
            image_count * patch_rows * width,
        )
        return activations, input_grads

    if direct:
        (last_total,) = sum_plane(plan, last_sums, devices, False)
        first_sums = sum_cores(first_halves, devices)
        first_sums, last_total, output, grad_first = lax.optimization_barrier(
            (first_sums, last_total, output, grad_first)
        )
        last_terms = last_total
        if devices > 8:
            last_terms = exchange(last_total, column_groups(devices))
        first_total = sum_plane(plan, first_sums, devices, True)
        images_out = place_images(output, output_pieces, grad_first)
        first_total, images_out = lax.optimization_barrier((first_total, images_out))
        first_terms = [one if k == 0 else flip(one, 8 * k, devices) for k, one in enumerate(first_total)]
        terms = (last_terms, *first_terms)
        turned = (layers, thin, width)
        attn_grads, vector_grads, up_grads, down_grads = call(
            functools.partial(finish_kernel, plan, len(terms)),
            terms,
            [VMEM] * len(terms),
            [(turned, F32), (vectors.shape, F32), (turned, F32), (turned, F32)],
            [VMEM] * 4,
            vmem([vec_shape, vec_shape]),
            1 << 20,
        )
        attn_grads, down_grads = attn_grads.transpose(0, 2, 1), down_grads.transpose(0, 2, 1)
    else:

        def square_blocks(halves):
            stacked = jnp.stack(halves)[:, 0]
            return jnp.stack(
                [
                    lax.dynamic_index_in_dim(stacked[:, k // 2], k % 2 ^ rank % 2, 0, False)
                    for k in range(parts)
                ]
            )

        def outputs_of(halves):
            def by_owner(array):
                split = array.reshape(mp_size, dp_size, thin, width).transpose(1, 0, 2, 3)
                return split.reshape(devices, thin, width)

            every = square_blocks(halves)
            pieces = [
                every[:, :width].reshape(devices, thin, width),
                by_owner(every[:, width : 2 * width]),
                by_owner(every[:, 2 * width : 3 * width]),
                jnp.broadcast_to(every[0, 3 * width :], (devices, tile, width)),
            ]
            owned = lax.psum_scatter(
                jnp.concatenate(pieces, axis=1), ("dp", "mp"), scatter_dimension=0, tiled=False
            ).astype(F32)
            own_vec = lax.dynamic_slice_in_dim(
                owned[3 * thin :].reshape(-1), device * vec_rows, vec_rows
            )
            return owned[:thin].T, own_vec, owned[thin : 2 * thin], owned[2 * thin : 3 * thin].T

        attn_grads, vector_grads, up_grads, down_grads = (
            jnp.stack([one, two]) for one, two in zip(outputs_of(first_halves), outputs_of(last_halves))
        )
        images_out = place_images(output, output_pieces, grad_first)

    activations, input_grads = images_out
    return (activations, input_grads, attn_grads, vector_grads, up_grads, down_grads)


def solution(mesh):
    in_specs = (
        P("dp", None, None),
        P("dp", None, None),
        P("dp", None),
        P(None, None, ("dp", "mp")),
        P(None, ("dp", "mp")),
        P(None, "dp", "mp"),
        P(None, "mp", "dp"),
    )
    out_specs = (
        P("dp", None),
        P("dp", None, None),
        P(None, None, ("dp", "mp")),
        P(None, ("dp", "mp")),
        P(None, "dp", "mp"),
        P(None, "mp", "dp"),
    )
    return jax.shard_map(shards, mesh=mesh, in_specs=in_specs, out_specs=out_specs, check_vma=False)
```

```python
import dataclasses
import functools

import jax
import jax.numpy as jnp
from jax import lax
from jax.experimental import pallas as pl
from jax.experimental.pallas import tpu as pltpu
from jax.sharding import PartitionSpec as P

HD = 64
SLOTS = 1024
EPSILON = 1e-06
MASKED = -1e30
STEP = 16
UNROLL = 13

F32 = jnp.float32
BF16 = jnp.bfloat16


def dot_nn(left, right):
    return lax.dot_general(left, right, (((1,), (0,)), ((), ())), preferred_element_type=F32)


def dot_nt(left, right):
    return lax.dot_general(left, right, (((1,), (1,)), ((), ())), preferred_element_type=F32)


def dot_tn(left, right):
    return lax.dot_general(left, right, (((0,), (0,)), ((), ())), preferred_element_type=F32)


def block_rows(index, step):
    return pl.ds(pl.multiple_of(index * step, step), step)


def fold_rows(values):
    return jnp.sum(values.reshape(values.shape[0] // 8, 8, values.shape[1]), axis=0)


def low_halves(rows):
    lane = lax.broadcasted_iota(jnp.int32, (rows, 2 * HD), 1)
    return lane < HD


def stack_heads(pair):
    low = low_halves(pair.shape[0])
    zero = jnp.zeros_like(pair)
    return jnp.concatenate([jnp.where(low, pair, zero), jnp.where(low, zero, pair)], axis=0)


def unstack_heads(stacked):
    rows = stacked.shape[0] // 2
    return jnp.where(low_halves(rows), stacked[:rows], stacked[rows:])


def norm_rows(x_ref, out_ref, gain, shift):
    def body(index, carry):
        at = block_rows(index, STEP)
        values = x_ref[at, :].astype(F32)
        centred = values - jnp.mean(values, axis=-1, keepdims=True)
        variance = jnp.mean(centred * centred, axis=-1, keepdims=True)
        out_ref[at, :] = (centred * lax.rsqrt(variance + EPSILON) * gain + shift).astype(BF16)
        return carry

    lax.fori_loop(0, x_ref.shape[0] // STEP, body, 0, unroll=UNROLL)


def norm_back(x_ref, grad_ref, base_ref, out_ref, low_ref, gain, images):
    rows = x_ref.shape[0] // images
    width = x_ref.shape[1]
    sums = []
    for image in range(images):

        def body(index, carry, image=image):
            at = pl.ds(pl.multiple_of(image * rows + index * STEP, STEP), STEP)
            values = x_ref[at, :].astype(F32)
            grad = grad_ref[at, :]
            centred = values - jnp.mean(values, axis=-1, keepdims=True)
            variance = jnp.mean(centred * centred, axis=-1, keepdims=True)
            inverse = lax.rsqrt(variance + EPSILON)
            unit = centred * inverse
            scaled = grad * gain
            mean_one = jnp.mean(scaled, axis=-1, keepdims=True)
            mean_two = jnp.mean(scaled * unit, axis=-1, keepdims=True)
            out = base_ref[at, :] + inverse * (scaled - mean_one - unit * mean_two)
            out_ref[at, :] = out.astype(out_ref.dtype)
            if low_ref is not None:
                low_ref[at, :] = out.astype(BF16)
            return (
                carry[0] + fold_rows(grad * unit),
                carry[1] + fold_rows(grad),
                carry[2] + fold_rows(out),
            )

        zero = jnp.zeros((8, width), F32)
        sums.append(lax.fori_loop(0, rows // STEP, body, (zero, zero, zero), unroll=UNROLL))
    return sums


def weigh(sums, share):
    total = sums[0]
    for more in sums[1:]:
        total = total + more * share
    return jnp.sum(total, axis=0, keepdims=True)


def as_square(ref, part):
    rows, width = ref.shape[1:]
    per = width // rows
    return ref[pl.ds(part * per, per)].reshape(width, width)


def forward_attention(x_ref, bias_ref, vec_ref, attn_ref, keep, mid_ref):
    n1_ref, proj_ref, p_ref, att_ref = keep
    images = bias_ref.shape[0]
    rows = x_ref.shape[0] // images
    width = x_ref.shape[1]
    pairs = width // (2 * HD)
    scale = HD**-0.5

    norm_rows(x_ref, n1_ref, vec_ref[0:1, :], vec_ref[1:2, :])
    for part, bias_row in enumerate((4, None, 5)):
        value = dot_nt(n1_ref[...], as_square(attn_ref, part))
        if bias_row is not None:
            value = value + vec_ref[bias_row : bias_row + 1, :]
        proj_ref[part] = value.astype(BF16)

    def image_body(image, carry):
        at = block_rows(image, rows)
        for pair in range(pairs):
            lanes = slice(pair * 2 * HD, (pair + 1) * 2 * HD)
            query = stack_heads(proj_ref[0, at, lanes])
            scores = dot_nt(query, proj_ref[1, at, lanes]) * scale + bias_ref[image]
            top = jnp.max(scores, axis=-1, keepdims=True)
            powers = jnp.exp(scores - top)
            total = jnp.sum(powers, axis=-1, keepdims=True)
            probs = (powers * (1.0 / total)).astype(BF16)
            p_ref[image, pair] = probs
            att_ref[at, lanes] = unstack_heads(dot_nn(probs, proj_ref[2, at, lanes])).astype(BF16)
        return carry

    lax.fori_loop(0, images, image_body, 0)
    mid_ref[...] = x_ref[...].astype(F32) + dot_nt(att_ref[...], as_square(attn_ref, 3)) + vec_ref[6:7, :]


def forward_hidden(mid_ref, vec_ref, up_ref, down_ref, keep, scratch, out_ref):
    n2_ref, a_ref, gp_ref = keep
    h_ref, acc_ref = scratch
    norm_rows(mid_ref, n2_ref, vec_ref[2:3, :], vec_ref[3:4, :])
    acc_ref[...] = mid_ref[...] + vec_ref[11:12, :]

    def part_body(part, carry):
        h_ref[...] = dot_nn(n2_ref[...], as_square(up_ref, part))
        bias = vec_ref[pl.ds(7 + part, 1), :]

        def gelu_body(index, inner):
            at = block_rows(index, STEP)
            hidden = h_ref[at, :] + bias
            share = 0.5 + 0.5 * lax.erf(hidden * 0.7071067811865476)
            a_ref[part, at, :] = (hidden * share).astype(BF16)
            bell = jnp.exp(-0.5 * hidden * hidden) * 0.3989422804014327
            gp_ref[part, at, :] = (share + hidden * bell).astype(gp_ref.dtype)
            return inner

        lax.fori_loop(0, h_ref.shape[0] // STEP, gelu_body, 0, unroll=UNROLL)
        acc_ref[...] += dot_nt(a_ref[part], as_square(down_ref, part))
        return carry

    lax.fori_loop(0, a_ref.shape[0], part_body, 0)
    out_ref[...] = acc_ref[...].astype(out_ref.dtype)


def drop_shared(refs):
    @pl.when(jnp.logical_not(counts_shared()))
    def _():
        for ref in refs:
            rows = ref.shape[-2] // 2
            ref[..., rows:, :] = jnp.zeros((*ref.shape[:-2], rows, ref.shape[-1]), ref.dtype)


def backward_hidden(g_ref, mid_ref, vec_ref, up_ref, down_ref, share, keep, scratch, gm_ref, gvec_ref, store):
    n2_ref, a_ref, gp_ref = keep
    go_ref, gh_ref, acc_ref, h_ref, got_ref, n2t_ref = scratch
    images = 2
    rows = mid_ref.shape[0] // images
    width = mid_ref.shape[1]
    zero = jnp.zeros((8, width), F32)
    sums = []
    for image in range(images):

        def low_body(index, carry, image=image):
            at = pl.ds(pl.multiple_of(image * rows + index * STEP, STEP), STEP)
            grad = g_ref[at, :]
            go_ref[at, :] = grad.astype(BF16)
            return carry + fold_rows(grad)

        sums.append(lax.fori_loop(0, rows // STEP, low_body, zero, unroll=UNROLL))
    gvec_ref[11:12, :] = weigh(sums, share)
    acc_ref[...] = jnp.zeros_like(acc_ref)
    got_ref[...] = go_ref[...].T
    n2t_ref[...] = n2_ref[...].T

    def part_body(part, carry):
        store(2, part, dot_nn(got_ref[...], a_ref[part]))
        h_ref[...] = dot_nn(go_ref[...], as_square(down_ref, part))
        inner_sums = []
        for image in range(images):

            def hidden_body(index, inner, image=image):
                at = pl.ds(pl.multiple_of(image * rows + index * STEP, STEP), STEP)
                grad = (h_ref[at, :] * gp_ref[part, at, :].astype(F32)).astype(BF16)
                gh_ref[at, :] = grad
                return inner + fold_rows(grad.astype(F32))

            inner_sums.append(lax.fori_loop(0, rows // STEP, hidden_body, zero, unroll=UNROLL))
        gvec_ref[pl.ds(7 + part, 1), :] = weigh(inner_sums, share)
        store(1, part, dot_nn(n2t_ref[...], gh_ref[...]))
        acc_ref[...] += dot_nt(gh_ref[...], as_square(up_ref, part))
        return carry

    lax.fori_loop(0, a_ref.shape[0], part_body, 0)
    sums = norm_back(mid_ref, acc_ref, g_ref, gm_ref, None, vec_ref[2:3, :], images)
    for place, row in enumerate((2, 3, 6)):
        gvec_ref[row : row + 1, :] = weigh([one[place] for one in sums], share)


def backward_attention(gm_ref, x_ref, vec_ref, attn_ref, share, keep, scratch, gx_ref, gvec_ref, store):
    n1_ref, proj_ref, p_ref, att_ref = keep
    go_ref, acc_ref, ga_ref, dproj_ref = scratch
    images = p_ref.shape[0]
    rows = x_ref.shape[0] // images
    width = x_ref.shape[1]
    pairs = width // (2 * HD)
    scale = HD**-0.5
    go_ref[...] = gm_ref[...].astype(BF16)
    store(0, 3, dot_tn(go_ref[...], att_ref[...]))
    ga_ref[...] = dot_nn(go_ref[...], as_square(attn_ref, 3)).astype(BF16)

    def image_body(image, carry):
        at = block_rows(image, rows)
        for pair in range(pairs):
            lanes = slice(pair * 2 * HD, (pair + 1) * 2 * HD)
            query = stack_heads(proj_ref[0, at, lanes])
            keys = proj_ref[1, at, lanes]
            grad_out = stack_heads(ga_ref[at, lanes])
            probs = p_ref[image, pair]
            grad_probs = dot_nt(grad_out, proj_ref[2, at, lanes])
            dproj_ref[2, at, lanes] = dot_tn(probs, grad_out).astype(BF16)
            wide = probs.astype(F32)
            inner = jnp.sum(grad_probs * wide, axis=-1, keepdims=True)
            grad_scores = (wide * (grad_probs - inner)).astype(BF16)
            dproj_ref[0, at, lanes] = (unstack_heads(dot_nn(grad_scores, keys)) * scale).astype(BF16)
            dproj_ref[1, at, lanes] = (dot_tn(grad_scores, query) * scale).astype(BF16)
        return carry

    lax.fori_loop(0, images, image_body, 0)
    for part, row in enumerate((4, None, 5)):
        store(0, part, dot_tn(dproj_ref[part], n1_ref[...]))
        value = dot_nn(dproj_ref[part], as_square(attn_ref, part))
        if part == 0:
            acc_ref[...] = value
        else:
            acc_ref[...] += value
        if row is not None:
            sums = [
                fold_rows(dproj_ref[part, image * rows : (image + 1) * rows, :].astype(F32))
                for image in range(images)
            ]
            gvec_ref[row : row + 1, :] = weigh(sums, share)
    sums = norm_back(x_ref, acc_ref, gm_ref, gx_ref, None, vec_ref[0:1, :], images)
    for place, row in enumerate((0, 1)):
        gvec_ref[row : row + 1, :] = weigh([one[place] for one in sums], share)
    store(3, 0, gvec_ref[...])


def coordinates(plan):
    outer, inner = lax.axis_index("dp"), lax.axis_index("mp")
    here = (inner // 2, inner % 2)
    return (outer // 2, outer % 2, *here) if plan.direct else (0, 0, *here)


def counts_shared():
    return lax.axis_index("mp") == 0


def place_weights(plan, pieces, attn_ref, up_ref, down_ref, vec_ref):
    thin, rows = plan.thin, 3 * plan.thin

    def put(owner, block):
        at = owner % plan.inner * plan.outer + owner // plan.inner
        attn_ref[owner] = block[:thin]
        up_ref[at] = block[thin : 2 * thin]
        down_ref[at] = block[2 * thin : 3 * thin]

    if not plan.direct:
        for owner in range(plan.inner):
            put(owner, pieces[0][owner, :rows])
        vec_ref[...] = pieces[0][0, rows:].astype(F32)
        return
    at = coordinates(plan)
    vec = None
    for i, piece in enumerate(pieces):
        c, x, y = i % 2, i // 2 % 2, i // 4
        low = ((at[1] ^ y) * 2 + (at[2] ^ x)) * 2 + (at[3] ^ c)
        count = piece.shape[0] // rows
        for k in range(count):
            put((at[0] ^ k) * 8 + low, piece[k * rows : (k + 1) * rows])
        tail = piece[count * rows :].astype(F32)
        vec = tail if vec is None else vec + tail
    vec_ref[...] = vec


def storer(plan, packed_ref):
    thin, width = plan.thin, plan.width
    per = width // thin
    here = coordinates(plan)
    zs = (packed_ref.shape[3] - plan.tile) // (3 * thin)

    def put(owner, kind, block):
        c, x, y = owner % 2, owner // 2 % 2, owner // 4 % 2
        row = pl.multiple_of((kind * zs + owner // 8) * thin, thin)
        packed_ref[c ^ here[3], y ^ here[1], x ^ here[2], pl.ds(row, thin), :] = block

    def store(kind, part, value):
        low = value.astype(BF16)
        if kind == 3:
            for i in range(8):
                packed_ref[i % 2, i // 4, i // 2 % 2, 3 * zs * thin :, :] = low
            return
        blocks = low.reshape(per, thin, width)
        for i in range(per):
            owner = part * per + i if kind == 0 else i * plan.inner + part
            put(owner, kind, blocks[i])

    return store


def start_copies(packed_ref, outs, sems, start, count, before=()):
    at = pl.ds(start, count)
    pairs = [(packed_ref.at[0, :, :, at], outs[0].at[:, :, at])]
    for i in range(4):
        pairs.append((packed_ref.at[1, i // 2, i % 2, at], outs[1 + i].at[at]))
    copies = list(before)
    for source, target in pairs:
        copies.append(pltpu.make_async_copy(source, target, sems.at[len(copies)]))
        copies[-1].start()
    return copies


def send_rest(plan, packed_ref, outs, sems, copies):
    last = packed_ref.shape[3] - plan.tile
    copies = start_copies(packed_ref, outs, sems, 0, last // 3, copies)
    copies = start_copies(packed_ref, outs, sems, last, plan.tile, copies)
    for one in copies:
        one.wait()


def send_hidden(plan, packed_ref, outs, sems):
    third = (packed_ref.shape[3] - plan.tile) // 3
    return start_copies(packed_ref, outs, sems, third, 2 * third)


def prepare_kernel(plan, attn_ref, up_ref, down_ref, vec_in, keep_in, first_ref, last_ref, line_ref, vec_ref, keep_ref, sems):
    thin, tile, width = plan.thin, plan.tile, plan.width
    outs = (first_ref, last_ref)
    copies = [
        pltpu.make_async_copy(vec_in, vec_ref, sems.at[0]),
        pltpu.make_async_copy(keep_in, keep_ref, sems.at[1]),
    ]
    for kind, ref in enumerate((attn_ref, up_ref, down_ref)):
        for layer, out_ref in enumerate(outs):
            if plan.direct:
                target = out_ref.at[pl.ds(kind * thin, thin)]
                copies.append(pltpu.make_async_copy(ref.at[layer], target, sems.at[len(copies)]))
            else:
                out_ref[kind * thin : (kind + 1) * thin, :] = ref[layer]
    for one in copies:
        one.start()
    count = vec_ref.shape[1]
    device = lax.axis_index("dp") * plan.inner + lax.axis_index("mp")
    row_at = device * count // width
    offset = device * count - row_at * width
    copies[0].wait()
    copies[1].wait()
    kept = jnp.sum(keep_ref[...]) + 2 * keep_ref.shape[0]
    kept = jnp.where(counts_shared(), kept, 0)
    row = lax.broadcasted_iota(jnp.int32, (tile, width), 0)
    here = lax.broadcasted_iota(jnp.int32, (tile, width), 1) == lax.axis_index("dp")
    for layer, out_ref in enumerate(outs):
        line_ref[...] = jnp.zeros_like(line_ref)
        line_ref[0:1, 0:count] = vec_ref[layer : layer + 1, :].astype(F32)
        moved = pltpu.roll(line_ref[...], offset, 1)[0:1]
        piece = jnp.where(row == row_at, moved[:, :width], 0.0)
        piece = jnp.where(row == row_at + 1, moved[:, width:], piece)
        if layer == 1:
            piece = jnp.where(here & (row == 12), (kept >> 5).astype(F32), piece)
            piece = jnp.where(here & (row == 13), (kept & 31).astype(F32), piece)
        out_ref[3 * thin :, :] = piece.astype(BF16)
    for one in copies[2:]:
        one.wait()


def first_kernel(plan, pieces, x_ref, bias_ref, *refs):
    sources, refs = refs[:pieces], refs[pieces:]
    attn_ref, up_ref, down_ref, vec_ref, mid_ref, out_ref, *refs = refs
    attn_keep, hidden_keep, (h_ref, acc_ref) = refs[:4], refs[4:7], refs[7:]
    place_weights(plan, sources, attn_ref, up_ref, down_ref, vec_ref)
    forward_attention(x_ref, bias_ref, vec_ref, attn_ref, attn_keep, mid_ref)
    forward_hidden(mid_ref, vec_ref, up_ref, down_ref, hidden_keep, (h_ref, acc_ref), out_ref)
    drop_shared((attn_keep[0], attn_keep[3], hidden_keep[0], hidden_keep[1]))


def last_kernel(plan, pieces, x_ref, bias_ref, goal_ref, *refs):
    sources, refs = refs[:pieces], refs[pieces:]
    out_ref, gx_ref, outs, refs = refs[0], refs[1], refs[2:7], refs[7:]
    attn_keep, hidden_keep, refs = refs[0:4], refs[4:7], refs[7:]
    mid_ref, g_ref, gm_ref, gvec_ref, go_ref, gh_ref, ga_ref, acc_ref, h_ref, got_ref, n2t_ref, dproj_ref = refs[:12]
    packed_ref, vec_ref, attn_ref, up_ref, down_ref, sems = refs[12:]
    place_weights(plan, sources, attn_ref, up_ref, down_ref, vec_ref)
    forward_attention(x_ref, bias_ref, vec_ref, attn_ref, attn_keep, mid_ref)
    forward_hidden(mid_ref, vec_ref, up_ref, down_ref, hidden_keep, (h_ref, acc_ref), out_ref)
    drop_shared((attn_keep[0], attn_keep[3], hidden_keep[0], hidden_keep[1]))
    high = jnp.sum(vec_ref[12:13, :], axis=-1, keepdims=True)
    rest = jnp.sum(vec_ref[13:14, :], axis=-1, keepdims=True)
    loss_scale = float(plan.slots) / (high * 32.0 + rest)
    g_ref[...] = goal_ref[...].astype(F32) * loss_scale
    gvec_ref[...] = jnp.zeros_like(gvec_ref)
    share = counts_shared().astype(F32)
    store = storer(plan, packed_ref)
    scratch = (go_ref, gh_ref, acc_ref, h_ref, got_ref, n2t_ref)
    backward_hidden(g_ref, mid_ref, vec_ref, up_ref, down_ref, share, hidden_keep, scratch, gm_ref, gvec_ref, store)
    copies = send_hidden(plan, packed_ref, outs, sems)
    scratch = (go_ref, acc_ref, ga_ref, dproj_ref)
    backward_attention(gm_ref, x_ref, vec_ref, attn_ref, share, attn_keep, scratch, gx_ref, gvec_ref, store)
    send_rest(plan, packed_ref, outs, sems, copies)


def back_kernel(plan, g_ref, x_ref, mid_ref, vec_ref, attn_ref, up_ref, down_ref, *refs):
    attn_keep, hidden_keep, gx_ref, outs, refs = refs[:4], refs[4:7], refs[7], refs[8:13], refs[13:]
    gm_ref, gvec_ref, go_ref, gh_ref, ga_ref, acc_ref, h_ref, got_ref, n2t_ref, dproj_ref, packed_ref, sems = refs
    gvec_ref[...] = jnp.zeros_like(gvec_ref)
    share = counts_shared().astype(F32)
    store = storer(plan, packed_ref)
    scratch = (go_ref, gh_ref, acc_ref, h_ref, got_ref, n2t_ref)
    backward_hidden(g_ref, mid_ref, vec_ref, up_ref, down_ref, share, hidden_keep, scratch, gm_ref, gvec_ref, store)
    copies = send_hidden(plan, packed_ref, outs, sems)
    scratch = (go_ref, acc_ref, ga_ref, dproj_ref)
    backward_attention(gm_ref, x_ref, vec_ref, attn_ref, share, attn_keep, scratch, gx_ref, gvec_ref, store)
    send_rest(plan, packed_ref, outs, sems, copies)


def finish_kernel(plan, terms, *refs):
    (late, *early), (attn_out, vec_out, up_out, down_out, *tiles) = refs[:terms], refs[terms:]
    thin, tile, width = plan.thin, plan.tile, plan.width

    count = vec_out.shape[1]
    device = lax.axis_index("dp") * plan.inner + lax.axis_index("mp")
    row = device * count // width
    offset = device * count - row * width
    for layer in range(2):

        def total(start, count, layer=layer):
            at = slice(start, start + count)
            blocks = [ref[at, :] for ref in early] if layer == 0 else [late[k, at, :] for k in range(late.shape[0])]
            return sum(block.astype(F32) for block in blocks)

        attn_out[layer] = total(0, thin)
        up_out[layer] = total(thin, thin)
        down_out[layer] = total(2 * thin, thin)
        tiles[layer][...] = total(3 * thin, tile)
        both = jnp.concatenate(
            [tiles[layer][pl.ds(row, 1), :], tiles[layer][pl.ds(row + 1, 1), :]], axis=1
        )
        both = jnp.broadcast_to(both, (8, 2 * width))
        moved = pltpu.roll(both, 2 * width - offset, 1)
        vec_out[layer : layer + 1, :] = moved[0:1, :count]


def place_kernel(own_ref, *refs):
    others, out_ref = refs[:-1], refs[-1]
    rows = own_ref.shape[0] // 2
    kept = out_ref.shape[1]
    mine = lax.axis_index("mp")
    out_ref[mine] = own_ref[0:rows, :].astype(F32)[:kept]
    for i, ref in enumerate(others):
        out_ref[mine ^ (i + 1)] = ref[...].astype(F32)[:kept]
    out_ref[out_ref.shape[0] - 1] = own_ref[rows : 2 * rows, :].astype(F32)[:kept]


def pack_kernel(slot_ref, own_ref, *refs):
    others, out_ref = refs[:-1], refs[-1]
    rows = own_ref.shape[0] // 2
    sources = [own_ref[0:rows, :]] + [ref[...] for ref in others] + [own_ref[rows : 2 * rows, :]]
    step = 256

    def body(index, carry):
        slots = lax.broadcasted_iota(jnp.int32, (step, rows), 0) + index * step
        total = None
        for i, values in enumerate(sources):
            picks = jnp.where(slots == slot_ref[i], 1.0, 0.0).astype(BF16)
            term = dot_nn(picks, values)
            total = term if total is None else total + term
        out_ref[block_rows(index, step), :] = total
        return carry

    lax.fori_loop(0, out_ref.shape[0] // step, body, 0)


VMEM = pl.BlockSpec(memory_space=pltpu.VMEM)
ANY = pl.BlockSpec(memory_space=pl.ANY)


def call(kernel, operands, specs, outs, out_specs, scratch, flops, limit=26):
    return pl.pallas_call(
        kernel,
        out_shape=[jax.ShapeDtypeStruct(shape, dtype) for shape, dtype in outs],
        in_specs=specs,
        out_specs=out_specs,
        scratch_shapes=scratch,
        compiler_params=pltpu.CompilerParams(vmem_limit_bytes=limit << 20),
        cost_estimate=pl.CostEstimate(flops=flops, bytes_accessed=8 << 20, transcendentals=0),
    )(*operands)


@dataclasses.dataclass(frozen=True)
class Plan:
    outer: int
    inner: int
    thin: int
    tile: int
    width: int
    slots: int
    direct: bool


def flip(array, mask, devices):
    return lax.ppermute(array, ("dp", "mp"), [(d, d ^ mask) for d in range(devices)])


def column_kernel(plan, *refs):
    blocks, out_ref = refs[:-1], refs[-1]
    rows = 3 * plan.thin
    for k, ref in enumerate(blocks):
        out_ref[k * rows : (k + 1) * rows, :] = ref[0:rows, :]
    tail = sum(ref[rows:, :].astype(F32) for ref in blocks)
    out_ref[len(blocks) * rows :, :] = tail.astype(BF16)


def gather_column(plan, block, devices):
    blocks = [block] + [flip(block, 8 * k, devices) for k in range(1, devices // 8)]
    shape = (len(blocks) * 3 * plan.thin + plan.tile, plan.width)
    (column,) = call(
        functools.partial(column_kernel, plan), blocks, [VMEM] * len(blocks), [(shape, BF16)], [VMEM], [], 1 << 20
    )
    return column


def gather_plane(column, devices):
    return [column] + [flip(column, mask, devices) for mask in (2, 4, 6)]


def gather_cores(plane, devices):
    pieces = []
    for piece in plane:
        pieces += [piece, flip(piece, 1, devices)]
    return pieces


def spread(rows, devices):
    across = flip(rows, 2, devices)
    return [flip(rows, 1, devices), across, flip(across, 1, devices)]


def sum_cores(kept, messages, devices):
    sums = []
    for i, message in enumerate(messages):
        total = kept[i // 2, i % 2].astype(F32) + flip(message, 1, devices).astype(F32)
        sums.append(total.astype(BF16))
    return sums


def plane_kernel(plan, *refs):
    terms, out_refs = refs[:4], refs[4:]
    thin, tile = plan.thin, plan.tile
    zs = (terms[0].shape[0] - tile) // (3 * thin)

    def added(start, count):
        return sum(ref[pl.ds(start, count), :].astype(F32) for ref in terms).astype(BF16)

    tail = added(3 * zs * thin, tile)
    for z in range(zs):
        for kind in range(3):
            to = slice(kind * thin, (kind + 1) * thin)
            if len(out_refs) == 1:
                out_refs[0][z, to, :] = added((kind * zs + z) * thin, thin)
            else:
                row = (kind * zs + (coordinates(plan)[0] ^ z)) * thin
                out_refs[z][to, :] = added(pl.multiple_of(row, thin), thin)
        if len(out_refs) == 1:
            out_refs[0][z, 3 * thin :, :] = tail
        else:
            out_refs[z][3 * thin :, :] = tail


def exchange(blocks, groups):
    return lax.all_to_all(blocks, ("dp", "mp"), 0, 0, axis_index_groups=groups, tiled=True)


def column_groups(devices):
    return [[8 * z + at for z in range(devices // 8)] for at in range(8)]


def sum_plane(plan, sums, devices, apart):
    zs = devices // 8
    terms = [sums[0]] + [flip(one, mask, devices) for one, mask in zip(sums[1:], (2, 4, 6))]
    shape = (3 * plan.thin + plan.tile, plan.width)
    outs = [(shape, BF16)] * zs if apart else [((zs, *shape), BF16)]
    return call(
        functools.partial(plane_kernel, plan), terms, [VMEM] * 4, outs, [VMEM] * len(outs), [], 1 << 20
    )


def shards(patches, targets, keep_mask, attn_weights, vectors, up_weights, down_weights):
    image_count, patch_rows, width = patches.shape
    layers = attn_weights.shape[0]
    dp_size, mp_size = lax.axis_size("dp"), lax.axis_size("mp")
    devices = dp_size * mp_size
    rank = lax.axis_index("mp")
    lane_rank = lax.axis_index("dp")
    device = lane_rank * mp_size + rank
    thin = attn_weights.shape[2]
    vec_rows = vectors.shape[1]
    parts = thin * devices // width
    assert image_count == mp_size + 1 and layers == 2 and parts == mp_size == 4
    direct = thin % 16 == 0
    images, tile = 2, 16
    rows = -(-patch_rows // 16) * 16
    total = images * rows

    keep_rows = jnp.concatenate([jnp.ones((image_count, 2), jnp.int32), keep_mask], axis=1)
    keep_rows = jnp.pad(keep_rows, ((0, 0), (0, rows - patch_rows)))

    attn_turned = attn_weights.transpose(0, 2, 1)
    down_turned = down_weights.transpose(0, 2, 1)
    packing = Plan(dp_size, mp_size, thin, tile, width, SLOTS * dp_size, direct)
    block_shape = ((3 * thin + tile, width), BF16)
    first_block, last_block = call(
        functools.partial(prepare_kernel, packing),
        (attn_turned, up_weights, down_turned, vectors, keep_mask),
        [ANY if direct else VMEM] * 3 + [ANY] * 2,
        [block_shape, block_shape],
        [VMEM, VMEM],
        [
            pltpu.VMEM((8, 2 * width), F32),
            pltpu.VMEM(vectors.shape, BF16),
            pltpu.VMEM(keep_mask.shape, jnp.int32),
            pltpu.SemaphoreType.DMA((8,)),
        ],
        1 << 20,
        60,
    )
    if direct:
        plan = packing
        first_column = gather_column(plan, first_block, devices)
        first_column, last_block = lax.optimization_barrier((first_column, last_block))
        first_plane = gather_plane(first_column, devices)
        last_column = gather_column(plan, last_block, devices)
        first_plane, last_column = lax.optimization_barrier((first_plane, last_column))
        first_pieces = gather_cores(first_plane, devices)
        last_plane = gather_plane(last_column, devices)
    else:
        plan = Plan(1, parts, width, tile, width, SLOTS * dp_size, False)

        def squares(array):
            return array.reshape(parts, width, width)

        def by_part(array):
            split = array.reshape(dp_size, mp_size, thin, width).transpose(1, 0, 2, 3)
            return squares(split)

        def one_tile(array):
            summed = jnp.sum(array.astype(F32), axis=0).astype(BF16)
            return jnp.pad(summed[None], ((0, parts - 1), (0, 0), (0, 0)))

        def normal(block):
            every = lax.all_gather(block, ("dp", "mp"))
            return jnp.concatenate(
                [
                    squares(every[:, :thin]),
                    by_part(every[:, thin : 2 * thin]),
                    by_part(every[:, 2 * thin : 3 * thin]),
                    one_tile(every[:, 3 * thin :]),
                ],
                axis=1,
            )

        first_pieces, last_pieces = [normal(first_block)], [normal(last_block)]

    flat = keep_rows.reshape(-1)
    slot = jnp.where(flat == 1, jnp.cumsum(flat) - flat, SLOTS).reshape(image_count, 1, rows)

    def mine(array):
        return jnp.concatenate(
            [lax.dynamic_slice_in_dim(array, rank, 1, 0), array[mp_size:]], axis=0
        )

    def padded(array):
        return jnp.pad(mine(array), ((0, 0), (0, rows - patch_rows), (0, 0)))

    kept = mine(keep_rows)
    stream = padded(patches).reshape(total, width)
    bias = jnp.where(kept == 1, 0.0, MASKED).astype(F32)[:, None, :]
    goal = jnp.where((kept == 1)[:, :, None], padded(targets), 0).reshape(total, width)
    slots = jnp.concatenate(
        [lax.dynamic_slice_in_dim(slot, rank ^ k, 1, 0) for k in range(mp_size)] + [slot[mp_size:]],
        axis=0,
    )

    stream, slots, goal = lax.optimization_barrier((stream, slots, goal))

    pairs = width // (2 * HD)
    stream_shape = ((total, width), F32)
    low_shape = ((total, width), BF16)
    three_shape = ((3, total, width), BF16)
    turned_shape = ((width, total), BF16)
    vec_shape = ((tile, width), F32)
    attn_keep = [low_shape, three_shape, ((images, pairs, 2 * rows, rows), BF16), low_shape]
    hidden_keep = [low_shape, ((parts, total, width), BF16), ((parts, total, width), F32)]
    blocks = plan.outer * plan.inner
    weight_shape = ((blocks, plan.thin, width), BF16)
    zs = max(blocks // 8, 1)

    def vmem(shapes):
        return [pltpu.VMEM(shape, dtype) for shape, dtype in shapes]

    layer_flops = 8 * total * parts * width * width
    half_rows = 3 * plan.thin * zs + tile

    first = call(
        functools.partial(first_kernel, plan, len(first_pieces)),
        (stream, bias, *first_pieces),
        [VMEM] * (2 + len(first_pieces)),
        [weight_shape, weight_shape, weight_shape, vec_shape, stream_shape, stream_shape]
        + attn_keep
        + hidden_keep,
        [VMEM] * 13,
        vmem([stream_shape, stream_shape]),
        layer_flops,
    )
    attn_full, up_full, down_full, vec, mid, middle = first[:6]
    attn_kept, hidden_kept = first[6:10], first[10:]
    if direct:
        middle, last_plane = lax.optimization_barrier((middle, last_plane))
        last_pieces = gather_cores(last_plane, devices)
    back_scratch = [
        stream_shape,
        vec_shape,
        low_shape,
        low_shape,
        low_shape,
        stream_shape,
        stream_shape,
        turned_shape,
        turned_shape,
        three_shape,
        ((2, 2, 2, half_rows, width), BF16),
    ]
    half_shape = ((2, 2, half_rows, width), BF16)
    message_shape = ((half_rows, width), BF16)
    sems = [pltpu.SemaphoreType.DMA((15,))]
    output, grad_middle, *last_halves = call(
        functools.partial(last_kernel, plan, len(last_pieces)),
        (middle, bias, goal, *last_pieces),
        [VMEM] * (3 + len(last_pieces)),
        [low_shape, stream_shape, half_shape] + [message_shape] * 4,
        [VMEM] * 2 + [ANY] * 5,
        vmem(
            attn_keep
            + hidden_keep
            + [stream_shape, stream_shape]
            + back_scratch
            + [vec_shape]
            + [weight_shape] * 3
        )
        + sems,
        3 * layer_flops,
    )
    output_pieces = spread(output[:rows], devices)
    if direct:
        last_sums = sum_cores(last_halves[0], last_halves[1:], devices)
        grad_middle, last_sums, output_pieces = lax.optimization_barrier(
            (grad_middle, last_sums, output_pieces)
        )
    grad_first, *first_halves = call(
        functools.partial(back_kernel, plan),
        (grad_middle, stream, mid, vec, attn_full, up_full, down_full, *attn_kept, *hidden_kept),
        [VMEM] * 14,
        [low_shape, half_shape] + [message_shape] * 4,
        [VMEM] + [ANY] * 5,
        vmem(back_scratch) + sems,
        3 * layer_flops,
    )

    def pack_output(output, output_pieces):
        (activations,) = call(
            pack_kernel,
            (slots, output, *output_pieces),
            [VMEM] * (mp_size + 1),
            [((SLOTS, width), F32)],
            [VMEM],
            [],
            2 * SLOTS * image_count * rows * width,
        )
        return activations

    def place_grads(grad_first, grad_pieces):
        (input_grads,) = call(
            place_kernel,
            (grad_first, *grad_pieces),
            [VMEM] * mp_size,
            [((image_count, patch_rows, width), F32)],
            [VMEM],
            [],
            image_count * patch_rows * width,
        )
        return input_grads

    if direct:
        (last_total,) = sum_plane(plan, last_sums, devices, False)
        last_total, first_halves, grad_first = lax.optimization_barrier(
            (last_total, first_halves, grad_first)
        )
        first_sums = sum_cores(first_halves[0], first_halves[1:], devices)
        first_sums, last_total, output = lax.optimization_barrier((first_sums, last_total, output))
        first_total = sum_plane(plan, first_sums, devices, True)
        activations = pack_output(output, output_pieces)
        last_total, activations = lax.optimization_barrier((last_total, activations))
        last_terms = last_total
        if devices > 8:
            last_terms = exchange(last_total, column_groups(devices))
        first_total, grad_first, last_terms, activations = lax.optimization_barrier(
            (first_total, grad_first, last_terms, activations)
        )
        input_grads = place_grads(grad_first, spread(grad_first[:rows], devices))
        first_terms = [one if k == 0 else flip(one, 8 * k, devices) for k, one in enumerate(first_total)]
        terms = (last_terms, *first_terms)
        turned = (layers, thin, width)
        attn_grads, vector_grads, up_grads, down_grads = call(
            functools.partial(finish_kernel, plan, len(terms)),
            terms,
            [VMEM] * len(terms),
            [(turned, F32), (vectors.shape, F32), (turned, F32), (turned, F32)],
            [VMEM] * 4,
            vmem([vec_shape, vec_shape]),
            1 << 20,
        )
        attn_grads, down_grads = attn_grads.transpose(0, 2, 1), down_grads.transpose(0, 2, 1)
    else:

        def square_blocks(halves):
            stacked = jnp.stack([halves[0][0], jnp.stack(halves[1:3])])
            stacked = jnp.stack([stacked[k % 2, k // 2] for k in range(parts)])
            return jnp.stack(
                [lax.dynamic_index_in_dim(stacked, rank ^ k, 0, False) for k in range(parts)]
            )

        def outputs_of(halves):
            def by_owner(array):
                split = array.reshape(mp_size, dp_size, thin, width).transpose(1, 0, 2, 3)
                return split.reshape(devices, thin, width)

            every = square_blocks(halves)
            pieces = [
                every[:, :width].reshape(devices, thin, width),
                by_owner(every[:, width : 2 * width]),
                by_owner(every[:, 2 * width : 3 * width]),
                jnp.broadcast_to(every[0, 3 * width :], (devices, tile, width)),
            ]
            owned = lax.psum_scatter(
                jnp.concatenate(pieces, axis=1), ("dp", "mp"), scatter_dimension=0, tiled=False
            ).astype(F32)
            own_vec = lax.dynamic_slice_in_dim(
                owned[3 * thin :].reshape(-1), device * vec_rows, vec_rows
            )
            return owned[:thin].T, own_vec, owned[thin : 2 * thin], owned[2 * thin : 3 * thin].T

        attn_grads, vector_grads, up_grads, down_grads = (
            jnp.stack([one, two]) for one, two in zip(outputs_of(first_halves), outputs_of(last_halves))
        )
        activations = pack_output(output, output_pieces)
        input_grads = place_grads(grad_first, spread(grad_first[:rows], devices))

    return (activations, input_grads, attn_grads, vector_grads, up_grads, down_grads)


def solution(mesh):
    in_specs = (
        P("dp", None, None),
        P("dp", None, None),
        P("dp", None),
        P(None, None, ("dp", "mp")),
        P(None, ("dp", "mp")),
        P(None, "dp", "mp"),
        P(None, "mp", "dp"),
    )
    out_specs = (
        P("dp", None),
        P("dp", None, None),
        P(None, None, ("dp", "mp")),
        P(None, ("dp", "mp")),
        P(None, "dp", "mp"),
        P(None, "mp", "dp"),
    )
    return jax.shard_map(shards, mesh=mesh, in_specs=in_specs, out_specs=out_specs, check_vma=False)
```

```python
import dataclasses
import functools

import jax
import jax.numpy as jnp
from jax import lax
from jax.experimental import pallas as pl
from jax.experimental.pallas import tpu as pltpu
from jax.sharding import PartitionSpec as P

HD = 64
SLOTS = 1024
EPSILON = 1e-06
MASKED = -1e30
STEP = 16
UNROLL = 13

F32 = jnp.float32
BF16 = jnp.bfloat16


def dot_nn(left, right):
    return lax.dot_general(left, right, (((1,), (0,)), ((), ())), preferred_element_type=F32)


def dot_nt(left, right):
    return lax.dot_general(left, right, (((1,), (1,)), ((), ())), preferred_element_type=F32)


def dot_tn(left, right):
    return lax.dot_general(left, right, (((0,), (0,)), ((), ())), preferred_element_type=F32)


def block_rows(index, step):
    return pl.ds(pl.multiple_of(index * step, step), step)


def fold_rows(values):
    return jnp.sum(values.reshape(values.shape[0] // 8, 8, values.shape[1]), axis=0)


def low_halves(rows):
    lane = lax.broadcasted_iota(jnp.int32, (rows, 2 * HD), 1)
    return lane < HD


def stack_heads(pair):
    low = low_halves(pair.shape[0])
    zero = jnp.zeros_like(pair)
    return jnp.concatenate([jnp.where(low, pair, zero), jnp.where(low, zero, pair)], axis=0)


def unstack_heads(stacked):
    rows = stacked.shape[0] // 2
    return jnp.where(low_halves(rows), stacked[:rows], stacked[rows:])


def norm_rows(x_ref, out_ref, gain, shift):
    def body(index, carry):
        at = block_rows(index, STEP)
        values = x_ref[at, :].astype(F32)
        centred = values - jnp.mean(values, axis=-1, keepdims=True)
        variance = jnp.mean(centred * centred, axis=-1, keepdims=True)
        out_ref[at, :] = (centred * lax.rsqrt(variance + EPSILON) * gain + shift).astype(BF16)
        return carry

    lax.fori_loop(0, x_ref.shape[0] // STEP, body, 0, unroll=UNROLL)


def norm_back(x_ref, grad_ref, base_ref, out_ref, low_ref, gain, images):
    rows = x_ref.shape[0] // images
    width = x_ref.shape[1]
    sums = []
    for image in range(images):

        def body(index, carry, image=image):
            at = pl.ds(pl.multiple_of(image * rows + index * STEP, STEP), STEP)
            values = x_ref[at, :].astype(F32)
            grad = grad_ref[at, :]
            centred = values - jnp.mean(values, axis=-1, keepdims=True)
            variance = jnp.mean(centred * centred, axis=-1, keepdims=True)
            inverse = lax.rsqrt(variance + EPSILON)
            unit = centred * inverse
            scaled = grad * gain
            mean_one = jnp.mean(scaled, axis=-1, keepdims=True)
            mean_two = jnp.mean(scaled * unit, axis=-1, keepdims=True)
            out = base_ref[at, :] + inverse * (scaled - mean_one - unit * mean_two)
            out_ref[at, :] = out.astype(out_ref.dtype)
            if low_ref is not None:
                low_ref[at, :] = out.astype(BF16)
            return (
                carry[0] + fold_rows(grad * unit),
                carry[1] + fold_rows(grad),
                carry[2] + fold_rows(out),
            )

        zero = jnp.zeros((8, width), F32)
        sums.append(lax.fori_loop(0, rows // STEP, body, (zero, zero, zero), unroll=UNROLL))
    return sums


def weigh(sums, share):
    total = sums[0]
    for more in sums[1:]:
        total = total + more * share
    return jnp.sum(total, axis=0, keepdims=True)


def as_square(ref, part):
    rows, width = ref.shape[1:]
    per = width // rows
    return ref[pl.ds(part * per, per)].reshape(width, width)


def forward_attention(x_ref, bias_ref, vec_ref, attn_ref, keep, mid_ref):
    n1_ref, proj_ref, p_ref, att_ref = keep
    images = bias_ref.shape[0]
    rows = x_ref.shape[0] // images
    width = x_ref.shape[1]
    pairs = width // (2 * HD)
    scale = HD**-0.5

    norm_rows(x_ref, n1_ref, vec_ref[0:1, :], vec_ref[1:2, :])
    for part, bias_row in enumerate((4, None, 5)):
        value = dot_nt(n1_ref[...], as_square(attn_ref, part))
        if bias_row is not None:
            value = value + vec_ref[bias_row : bias_row + 1, :]
        proj_ref[part] = value.astype(BF16)

    def image_body(image, carry):
        at = block_rows(image, rows)
        for pair in range(pairs):
            lanes = slice(pair * 2 * HD, (pair + 1) * 2 * HD)
            query = stack_heads(proj_ref[0, at, lanes])
            scores = dot_nt(query, proj_ref[1, at, lanes]) * scale + bias_ref[image]
            top = jnp.max(scores, axis=-1, keepdims=True)
            powers = jnp.exp(scores - top)
            total = jnp.sum(powers, axis=-1, keepdims=True)
            probs = (powers * (1.0 / total)).astype(BF16)
            p_ref[image, pair] = probs
            att_ref[at, lanes] = unstack_heads(dot_nn(probs, proj_ref[2, at, lanes])).astype(BF16)
        return carry

    lax.fori_loop(0, images, image_body, 0)
    mid_ref[...] = x_ref[...].astype(F32) + dot_nt(att_ref[...], as_square(attn_ref, 3)) + vec_ref[6:7, :]


def forward_hidden(mid_ref, vec_ref, up_ref, down_ref, keep, scratch, out_ref):
    n2_ref, a_ref, gp_ref = keep
    h_ref, acc_ref = scratch
    norm_rows(mid_ref, n2_ref, vec_ref[2:3, :], vec_ref[3:4, :])
    acc_ref[...] = mid_ref[...] + vec_ref[11:12, :]

    def part_body(part, carry):
        h_ref[...] = dot_nn(n2_ref[...], as_square(up_ref, part))
        bias = vec_ref[pl.ds(7 + part, 1), :]

        def gelu_body(index, inner):
            at = block_rows(index, STEP)
            hidden = h_ref[at, :] + bias
            share = 0.5 + 0.5 * lax.erf(hidden * 0.7071067811865476)
            a_ref[part, at, :] = (hidden * share).astype(BF16)
            bell = jnp.exp(-0.5 * hidden * hidden) * 0.3989422804014327
            gp_ref[part, at, :] = (share + hidden * bell).astype(gp_ref.dtype)
            return inner

        lax.fori_loop(0, h_ref.shape[0] // STEP, gelu_body, 0, unroll=UNROLL)
        acc_ref[...] += dot_nt(a_ref[part], as_square(down_ref, part))
        return carry

    lax.fori_loop(0, a_ref.shape[0], part_body, 0)
    out_ref[...] = acc_ref[...].astype(out_ref.dtype)


def drop_shared(refs):
    @pl.when(jnp.logical_not(counts_shared()))
    def _():
        for ref in refs:
            rows = ref.shape[-2] // 2
            ref[..., rows:, :] = jnp.zeros((*ref.shape[:-2], rows, ref.shape[-1]), ref.dtype)


def backward_hidden(g_ref, mid_ref, vec_ref, up_ref, down_ref, share, keep, scratch, gm_ref, gvec_ref, store):
    n2_ref, a_ref, gp_ref = keep
    go_ref, gh_ref, acc_ref, h_ref, got_ref, n2t_ref = scratch
    images = 2
    rows = mid_ref.shape[0] // images
    width = mid_ref.shape[1]
    zero = jnp.zeros((8, width), F32)
    sums = []
    for image in range(images):

        def low_body(index, carry, image=image):
            at = pl.ds(pl.multiple_of(image * rows + index * STEP, STEP), STEP)
            grad = g_ref[at, :]
            go_ref[at, :] = grad.astype(BF16)
            return carry + fold_rows(grad)

        sums.append(lax.fori_loop(0, rows // STEP, low_body, zero, unroll=UNROLL))
    gvec_ref[11:12, :] = weigh(sums, share)
    acc_ref[...] = jnp.zeros_like(acc_ref)
    got_ref[...] = go_ref[...].T
    n2t_ref[...] = n2_ref[...].T

    def part_body(part, carry):
        store(2, part, dot_nn(got_ref[...], a_ref[part]))
        h_ref[...] = dot_nn(go_ref[...], as_square(down_ref, part))
        inner_sums = []
        for image in range(images):

            def hidden_body(index, inner, image=image):
                at = pl.ds(pl.multiple_of(image * rows + index * STEP, STEP), STEP)
                grad = (h_ref[at, :] * gp_ref[part, at, :].astype(F32)).astype(BF16)
                gh_ref[at, :] = grad
                return inner + fold_rows(grad.astype(F32))

            inner_sums.append(lax.fori_loop(0, rows // STEP, hidden_body, zero, unroll=UNROLL))
        gvec_ref[pl.ds(7 + part, 1), :] = weigh(inner_sums, share)
        store(1, part, dot_nn(n2t_ref[...], gh_ref[...]))
        acc_ref[...] += dot_nt(gh_ref[...], as_square(up_ref, part))
        return carry

    lax.fori_loop(0, a_ref.shape[0], part_body, 0)
    sums = norm_back(mid_ref, acc_ref, g_ref, gm_ref, None, vec_ref[2:3, :], images)
    for place, row in enumerate((2, 3, 6)):
        gvec_ref[row : row + 1, :] = weigh([one[place] for one in sums], share)


def backward_attention(gm_ref, x_ref, vec_ref, attn_ref, share, keep, scratch, gx_ref, gvec_ref, store):
    n1_ref, proj_ref, p_ref, att_ref = keep
    go_ref, acc_ref, ga_ref, dproj_ref = scratch
    images = p_ref.shape[0]
    rows = x_ref.shape[0] // images
    width = x_ref.shape[1]
    pairs = width // (2 * HD)
    scale = HD**-0.5
    go_ref[...] = gm_ref[...].astype(BF16)
    store(0, 3, dot_tn(go_ref[...], att_ref[...]))
    ga_ref[...] = dot_nn(go_ref[...], as_square(attn_ref, 3)).astype(BF16)

    def image_body(image, carry):
        at = block_rows(image, rows)
        for pair in range(pairs):
            lanes = slice(pair * 2 * HD, (pair + 1) * 2 * HD)
            query = stack_heads(proj_ref[0, at, lanes])
            keys = proj_ref[1, at, lanes]
            grad_out = stack_heads(ga_ref[at, lanes])
            probs = p_ref[image, pair]
            grad_probs = dot_nt(grad_out, proj_ref[2, at, lanes])
            dproj_ref[2, at, lanes] = dot_tn(probs, grad_out).astype(BF16)
            wide = probs.astype(F32)
            inner = jnp.sum(grad_probs * wide, axis=-1, keepdims=True)
            grad_scores = (wide * (grad_probs - inner)).astype(BF16)
            dproj_ref[0, at, lanes] = (unstack_heads(dot_nn(grad_scores, keys)) * scale).astype(BF16)
            dproj_ref[1, at, lanes] = (dot_tn(grad_scores, query) * scale).astype(BF16)
        return carry

    lax.fori_loop(0, images, image_body, 0)
    for part, row in enumerate((4, None, 5)):
        store(0, part, dot_tn(dproj_ref[part], n1_ref[...]))
        value = dot_nn(dproj_ref[part], as_square(attn_ref, part))
        if part == 0:
            acc_ref[...] = value
        else:
            acc_ref[...] += value
        if row is not None:
            sums = [
                fold_rows(dproj_ref[part, image * rows : (image + 1) * rows, :].astype(F32))
                for image in range(images)
            ]
            gvec_ref[row : row + 1, :] = weigh(sums, share)
    sums = norm_back(x_ref, acc_ref, gm_ref, gx_ref, None, vec_ref[0:1, :], images)
    for place, row in enumerate((0, 1)):
        gvec_ref[row : row + 1, :] = weigh([one[place] for one in sums], share)
    store(3, 0, gvec_ref[...])


def coordinates(plan):
    outer, inner = lax.axis_index("dp"), lax.axis_index("mp")
    here = (inner // 2, inner % 2)
    return (outer // 2, outer % 2, *here) if plan.direct else (0, 0, *here)


def counts_shared():
    return lax.axis_index("mp") == 0


def place_weights(plan, pieces, attn_ref, up_ref, down_ref, vec_ref):
    thin, rows = plan.thin, 3 * plan.thin

    def put(owner, block):
        at = owner % plan.inner * plan.outer + owner // plan.inner
        attn_ref[owner] = block[:thin]
        up_ref[at] = block[thin : 2 * thin]
        down_ref[at] = block[2 * thin : 3 * thin]

    if not plan.direct:
        for owner in range(plan.inner):
            put(owner, pieces[0][owner, :rows])
        vec_ref[...] = pieces[0][0, rows:].astype(F32)
        return
    at = coordinates(plan)
    vec = None
    for i, piece in enumerate(pieces):
        c, x, y = i % 2, i // 2 % 2, i // 4
        low = ((at[1] ^ y) * 2 + (at[2] ^ x)) * 2 + (at[3] ^ c)
        count = piece.shape[0] // rows
        for k in range(count):
            put((at[0] ^ k) * 8 + low, piece[k * rows : (k + 1) * rows])
        tail = piece[count * rows :].astype(F32)
        vec = tail if vec is None else vec + tail
    vec_ref[...] = vec


def storer(plan, packed_ref):
    thin, width = plan.thin, plan.width
    per = width // thin
    here = coordinates(plan)
    zs = (packed_ref.shape[3] - plan.tile) // (3 * thin)

    def put(owner, kind, block):
        c, x, y = owner % 2, owner // 2 % 2, owner // 4 % 2
        row = pl.multiple_of((kind * zs + owner // 8) * thin, thin)
        packed_ref[c ^ here[3], y ^ here[1], x ^ here[2], pl.ds(row, thin), :] = block

    def store(kind, part, value):
        low = value.astype(BF16)
        if kind == 3:
            for i in range(8):
                packed_ref[i % 2, i // 4, i // 2 % 2, 3 * zs * thin :, :] = low
            return
        blocks = low.reshape(per, thin, width)
        for i in range(per):
            owner = part * per + i if kind == 0 else i * plan.inner + part
            put(owner, kind, blocks[i])

    return store


def start_copies(packed_ref, outs, sems, start, count, before=()):
    at = pl.ds(start, count)
    pairs = [(packed_ref.at[0, :, :, at], outs[0].at[:, :, at])]
    for i in range(4):
        pairs.append((packed_ref.at[1, i // 2, i % 2, at], outs[1 + i].at[at]))
    copies = list(before)
    for source, target in pairs:
        copies.append(pltpu.make_async_copy(source, target, sems.at[len(copies)]))
        copies[-1].start()
    return copies


def send_rest(plan, packed_ref, outs, sems, copies):
    last = packed_ref.shape[3] - plan.tile
    copies = start_copies(packed_ref, outs, sems, 0, last // 3, copies)
    copies = start_copies(packed_ref, outs, sems, last, plan.tile, copies)
    for one in copies:
        one.wait()


def send_hidden(plan, packed_ref, outs, sems):
    third = (packed_ref.shape[3] - plan.tile) // 3
    return start_copies(packed_ref, outs, sems, third, 2 * third)


def prepare_kernel(plan, attn_ref, up_ref, down_ref, vec_in, keep_in, first_ref, last_ref, line_ref, vec_ref, keep_ref, sems):
    thin, tile, width = plan.thin, plan.tile, plan.width
    outs = (first_ref, last_ref)
    copies = [
        pltpu.make_async_copy(vec_in, vec_ref, sems.at[0]),
        pltpu.make_async_copy(keep_in, keep_ref, sems.at[1]),
    ]
    for kind, ref in enumerate((attn_ref, up_ref, down_ref)):
        for layer, out_ref in enumerate(outs):
            if plan.direct:
                target = out_ref.at[pl.ds(kind * thin, thin)]
                copies.append(pltpu.make_async_copy(ref.at[layer], target, sems.at[len(copies)]))
            else:
                out_ref[kind * thin : (kind + 1) * thin, :] = ref[layer]
    for one in copies:
        one.start()
    count = vec_ref.shape[1]
    device = lax.axis_index("dp") * plan.inner + lax.axis_index("mp")
    row_at = device * count // width
    offset = device * count - row_at * width
    copies[0].wait()
    copies[1].wait()
    kept = jnp.sum(keep_ref[...]) + 2 * keep_ref.shape[0]
    kept = jnp.where(counts_shared(), kept, 0)
    row = lax.broadcasted_iota(jnp.int32, (tile, width), 0)
    here = lax.broadcasted_iota(jnp.int32, (tile, width), 1) == lax.axis_index("dp")
    for layer, out_ref in enumerate(outs):
        line_ref[...] = jnp.zeros_like(line_ref)
        line_ref[0:1, 0:count] = vec_ref[layer : layer + 1, :].astype(F32)
        moved = pltpu.roll(line_ref[...], offset, 1)[0:1]
        piece = jnp.where(row == row_at, moved[:, :width], 0.0)
        piece = jnp.where(row == row_at + 1, moved[:, width:], piece)
        if layer == 1:
            piece = jnp.where(here & (row == 12), (kept >> 5).astype(F32), piece)
            piece = jnp.where(here & (row == 13), (kept & 31).astype(F32), piece)
        out_ref[3 * thin :, :] = piece.astype(BF16)
    for one in copies[2:]:
        one.wait()


def first_kernel(plan, pieces, x_ref, bias_ref, *refs):
    sources, refs = refs[:pieces], refs[pieces:]
    attn_ref, up_ref, down_ref, vec_ref, mid_ref, out_ref, *refs = refs
    attn_keep, hidden_keep, (h_ref, acc_ref) = refs[:4], refs[4:7], refs[7:]
    place_weights(plan, sources, attn_ref, up_ref, down_ref, vec_ref)
    forward_attention(x_ref, bias_ref, vec_ref, attn_ref, attn_keep, mid_ref)
    forward_hidden(mid_ref, vec_ref, up_ref, down_ref, hidden_keep, (h_ref, acc_ref), out_ref)
    drop_shared((attn_keep[0], attn_keep[3], hidden_keep[0], hidden_keep[1]))


def last_kernel(plan, pieces, x_ref, bias_ref, goal_ref, *refs):
    sources, refs = refs[:pieces], refs[pieces:]
    out_ref, gx_ref, outs, refs = refs[0], refs[1], refs[2:7], refs[7:]
    attn_keep, hidden_keep, refs = refs[0:4], refs[4:7], refs[7:]
    mid_ref, g_ref, gm_ref, gvec_ref, go_ref, gh_ref, ga_ref, acc_ref, h_ref, got_ref, n2t_ref, dproj_ref = refs[:12]
    packed_ref, vec_ref, attn_ref, up_ref, down_ref, sems = refs[12:]
    place_weights(plan, sources, attn_ref, up_ref, down_ref, vec_ref)
    forward_attention(x_ref, bias_ref, vec_ref, attn_ref, attn_keep, mid_ref)
    forward_hidden(mid_ref, vec_ref, up_ref, down_ref, hidden_keep, (h_ref, acc_ref), out_ref)
    drop_shared((attn_keep[0], attn_keep[3], hidden_keep[0], hidden_keep[1]))
    high = jnp.sum(vec_ref[12:13, :], axis=-1, keepdims=True)
    rest = jnp.sum(vec_ref[13:14, :], axis=-1, keepdims=True)
    loss_scale = float(plan.slots) / (high * 32.0 + rest)
    g_ref[...] = goal_ref[...].astype(F32) * loss_scale
    gvec_ref[...] = jnp.zeros_like(gvec_ref)
    share = counts_shared().astype(F32)
    store = storer(plan, packed_ref)
    scratch = (go_ref, gh_ref, acc_ref, h_ref, got_ref, n2t_ref)
    backward_hidden(g_ref, mid_ref, vec_ref, up_ref, down_ref, share, hidden_keep, scratch, gm_ref, gvec_ref, store)
    copies = send_hidden(plan, packed_ref, outs, sems)
    scratch = (go_ref, acc_ref, ga_ref, dproj_ref)
    backward_attention(gm_ref, x_ref, vec_ref, attn_ref, share, attn_keep, scratch, gx_ref, gvec_ref, store)
    send_rest(plan, packed_ref, outs, sems, copies)


def back_kernel(plan, g_ref, x_ref, mid_ref, vec_ref, attn_ref, up_ref, down_ref, *refs):
    attn_keep, hidden_keep, gx_ref, outs, refs = refs[:4], refs[4:7], refs[7], refs[8:13], refs[13:]
    gm_ref, gvec_ref, go_ref, gh_ref, ga_ref, acc_ref, h_ref, got_ref, n2t_ref, dproj_ref, packed_ref, sems = refs
    gvec_ref[...] = jnp.zeros_like(gvec_ref)
    share = counts_shared().astype(F32)
    store = storer(plan, packed_ref)
    scratch = (go_ref, gh_ref, acc_ref, h_ref, got_ref, n2t_ref)
    backward_hidden(g_ref, mid_ref, vec_ref, up_ref, down_ref, share, hidden_keep, scratch, gm_ref, gvec_ref, store)
    copies = send_hidden(plan, packed_ref, outs, sems)
    scratch = (go_ref, acc_ref, ga_ref, dproj_ref)
    backward_attention(gm_ref, x_ref, vec_ref, attn_ref, share, attn_keep, scratch, gx_ref, gvec_ref, store)
    send_rest(plan, packed_ref, outs, sems, copies)


def finish_kernel(plan, terms, *refs):
    (late, *early), (attn_out, vec_out, up_out, down_out, *tiles) = refs[:terms], refs[terms:]
    thin, tile, width = plan.thin, plan.tile, plan.width

    count = vec_out.shape[1]
    device = lax.axis_index("dp") * plan.inner + lax.axis_index("mp")
    row = device * count // width
    offset = device * count - row * width
    for layer in range(2):

        def total(start, count, layer=layer):
            at = slice(start, start + count)
            blocks = [ref[at, :] for ref in early] if layer == 0 else [late[k, at, :] for k in range(late.shape[0])]
            return sum(block.astype(F32) for block in blocks)

        attn_out[layer] = total(0, thin)
        up_out[layer] = total(thin, thin)
        down_out[layer] = total(2 * thin, thin)
        tiles[layer][...] = total(3 * thin, tile)
        both = jnp.concatenate(
            [tiles[layer][pl.ds(row, 1), :], tiles[layer][pl.ds(row + 1, 1), :]], axis=1
        )
        both = jnp.broadcast_to(both, (8, 2 * width))
        moved = pltpu.roll(both, 2 * width - offset, 1)
        vec_out[layer : layer + 1, :] = moved[0:1, :count]


def place_kernel(own_ref, *refs):
    others, out_ref = refs[:-1], refs[-1]
    rows = own_ref.shape[0] // 2
    kept = out_ref.shape[1]
    mine = lax.axis_index("mp")
    out_ref[mine] = own_ref[0:rows, :].astype(F32)[:kept]
    for i, ref in enumerate(others):
        out_ref[mine ^ (i + 1)] = ref[...].astype(F32)[:kept]
    out_ref[out_ref.shape[0] - 1] = own_ref[rows : 2 * rows, :].astype(F32)[:kept]


def pack_kernel(slot_ref, own_ref, *refs):
    others, out_ref = refs[:-1], refs[-1]
    rows = own_ref.shape[0] // 2
    sources = [own_ref[0:rows, :]] + [ref[...] for ref in others] + [own_ref[rows : 2 * rows, :]]
    step = 256

    def body(index, carry):
        slots = lax.broadcasted_iota(jnp.int32, (step, rows), 0) + index * step
        total = None
        for i, values in enumerate(sources):
            picks = jnp.where(slots == slot_ref[i], 1.0, 0.0).astype(BF16)
            term = dot_nn(picks, values)
            total = term if total is None else total + term
        out_ref[block_rows(index, step), :] = total
        return carry

    lax.fori_loop(0, out_ref.shape[0] // step, body, 0)


VMEM = pl.BlockSpec(memory_space=pltpu.VMEM)
ANY = pl.BlockSpec(memory_space=pl.ANY)


def call(kernel, operands, specs, outs, out_specs, scratch, flops, limit=26):
    return pl.pallas_call(
        kernel,
        out_shape=[jax.ShapeDtypeStruct(shape, dtype) for shape, dtype in outs],
        in_specs=specs,
        out_specs=out_specs,
        scratch_shapes=scratch,
        compiler_params=pltpu.CompilerParams(vmem_limit_bytes=limit << 20),
        cost_estimate=pl.CostEstimate(flops=flops, bytes_accessed=8 << 20, transcendentals=0),
    )(*operands)


@dataclasses.dataclass(frozen=True)
class Plan:
    outer: int
    inner: int
    thin: int
    tile: int
    width: int
    slots: int
    direct: bool


def flip(array, mask, devices):
    return lax.ppermute(array, ("dp", "mp"), [(d, d ^ mask) for d in range(devices)])


def column_kernel(plan, *refs):
    blocks, out_ref = refs[:-1], refs[-1]
    rows = 3 * plan.thin
    for k, ref in enumerate(blocks):
        out_ref[k * rows : (k + 1) * rows, :] = ref[0:rows, :]
    tail = sum(ref[rows:, :].astype(F32) for ref in blocks)
    out_ref[len(blocks) * rows :, :] = tail.astype(BF16)


def gather_column(plan, block, devices):
    blocks = [block] + [flip(block, 8 * k, devices) for k in range(1, devices // 8)]
    shape = (len(blocks) * 3 * plan.thin + plan.tile, plan.width)
    (column,) = call(
        functools.partial(column_kernel, plan), blocks, [VMEM] * len(blocks), [(shape, BF16)], [VMEM], [], 1 << 20
    )
    return column


def gather_plane(column, devices):
    return [column] + [flip(column, mask, devices) for mask in (2, 4, 6)]


def gather_cores(plane, devices):
    pieces = []
    for piece in plane:
        pieces += [piece, flip(piece, 1, devices)]
    return pieces


def spread(rows, devices):
    across = flip(rows, 2, devices)
    return [flip(rows, 1, devices), across, flip(across, 1, devices)]


def sum_cores(kept, messages, devices):
    sums = []
    for i, message in enumerate(messages):
        total = kept[i // 2, i % 2].astype(F32) + flip(message, 1, devices).astype(F32)
        sums.append(total.astype(BF16))
    return sums


def plane_kernel(plan, *refs):
    terms, out_refs = refs[:4], refs[4:]
    thin, tile = plan.thin, plan.tile
    zs = (terms[0].shape[0] - tile) // (3 * thin)

    def added(start, count):
        return sum(ref[pl.ds(start, count), :].astype(F32) for ref in terms).astype(BF16)

    tail = added(3 * zs * thin, tile)
    for z in range(zs):
        for kind in range(3):
            to = slice(kind * thin, (kind + 1) * thin)
            if len(out_refs) == 1:
                out_refs[0][z, to, :] = added((kind * zs + z) * thin, thin)
            else:
                row = (kind * zs + (coordinates(plan)[0] ^ z)) * thin
                out_refs[z][to, :] = added(pl.multiple_of(row, thin), thin)
        if len(out_refs) == 1:
            out_refs[0][z, 3 * thin :, :] = tail
        else:
            out_refs[z][3 * thin :, :] = tail


def exchange(blocks, groups):
    return lax.all_to_all(blocks, ("dp", "mp"), 0, 0, axis_index_groups=groups, tiled=True)


def column_groups(devices):
    return [[8 * z + at for z in range(devices // 8)] for at in range(8)]


def sum_plane(plan, sums, devices, apart):
    zs = devices // 8
    terms = [sums[0]] + [flip(one, mask, devices) for one, mask in zip(sums[1:], (2, 4, 6))]
    shape = (3 * plan.thin + plan.tile, plan.width)
    outs = [(shape, BF16)] * zs if apart else [((zs, *shape), BF16)]
    return call(
        functools.partial(plane_kernel, plan), terms, [VMEM] * 4, outs, [VMEM] * len(outs), [], 1 << 20
    )


def shards(patches, targets, keep_mask, attn_weights, vectors, up_weights, down_weights):
    image_count, patch_rows, width = patches.shape
    layers = attn_weights.shape[0]
    dp_size, mp_size = lax.axis_size("dp"), lax.axis_size("mp")
    devices = dp_size * mp_size
    rank = lax.axis_index("mp")
    lane_rank = lax.axis_index("dp")
    device = lane_rank * mp_size + rank
    thin = attn_weights.shape[2]
    vec_rows = vectors.shape[1]
    parts = thin * devices // width
    assert image_count == mp_size + 1 and layers == 2 and parts == mp_size == 4
    direct = thin % 16 == 0
    images, tile = 2, 16
    rows = -(-patch_rows // 16) * 16
    total = images * rows

    keep_rows = jnp.concatenate([jnp.ones((image_count, 2), jnp.int32), keep_mask], axis=1)
    keep_rows = jnp.pad(keep_rows, ((0, 0), (0, rows - patch_rows)))

    attn_turned = attn_weights.transpose(0, 2, 1)
    down_turned = down_weights.transpose(0, 2, 1)
    packing = Plan(dp_size, mp_size, thin, tile, width, SLOTS * dp_size, direct)
    block_shape = ((3 * thin + tile, width), BF16)
    first_block, last_block = call(
        functools.partial(prepare_kernel, packing),
        (attn_turned, up_weights, down_turned, vectors, keep_mask),
        [ANY if direct else VMEM] * 3 + [ANY] * 2,
        [block_shape, block_shape],
        [VMEM, VMEM],
        [
            pltpu.VMEM((8, 2 * width), F32),
            pltpu.VMEM(vectors.shape, BF16),
            pltpu.VMEM(keep_mask.shape, jnp.int32),
            pltpu.SemaphoreType.DMA((8,)),
        ],
        1 << 20,
        60,
    )
    if direct:
        plan = packing
        first_column = gather_column(plan, first_block, devices)
        first_column, last_block = lax.optimization_barrier((first_column, last_block))
        first_plane = gather_plane(first_column, devices)
        last_column = gather_column(plan, last_block, devices)
        first_plane, last_column = lax.optimization_barrier((first_plane, last_column))
        first_pieces = gather_cores(first_plane, devices)
        last_plane = gather_plane(last_column, devices)
    else:
        plan = Plan(1, parts, width, tile, width, SLOTS * dp_size, False)

        def squares(array):
            return array.reshape(parts, width, width)

        def by_part(array):
            split = array.reshape(dp_size, mp_size, thin, width).transpose(1, 0, 2, 3)
            return squares(split)

        def one_tile(array):
            summed = jnp.sum(array.astype(F32), axis=0).astype(BF16)
            return jnp.pad(summed[None], ((0, parts - 1), (0, 0), (0, 0)))

        def normal(block):
            every = lax.all_gather(block, ("dp", "mp"))
            return jnp.concatenate(
                [
                    squares(every[:, :thin]),
                    by_part(every[:, thin : 2 * thin]),
                    by_part(every[:, 2 * thin : 3 * thin]),
                    one_tile(every[:, 3 * thin :]),
                ],
                axis=1,
            )

        first_pieces, last_pieces = [normal(first_block)], [normal(last_block)]

    flat = keep_rows.reshape(-1)
    slot = jnp.where(flat == 1, jnp.cumsum(flat) - flat, SLOTS).reshape(image_count, 1, rows)

    def mine(array):
        return jnp.concatenate(
            [lax.dynamic_slice_in_dim(array, rank, 1, 0), array[mp_size:]], axis=0
        )

    def padded(array):
        return jnp.pad(mine(array), ((0, 0), (0, rows - patch_rows), (0, 0)))

    kept = mine(keep_rows)
    stream = padded(patches).reshape(total, width)
    bias = jnp.where(kept == 1, 0.0, MASKED).astype(F32)[:, None, :]
    goal = jnp.where((kept == 1)[:, :, None], padded(targets), 0).reshape(total, width)
    slots = jnp.concatenate(
        [lax.dynamic_slice_in_dim(slot, rank ^ k, 1, 0) for k in range(mp_size)] + [slot[mp_size:]],
        axis=0,
    )

    stream, slots, goal = lax.optimization_barrier((stream, slots, goal))

    pairs = width // (2 * HD)
    stream_shape = ((total, width), F32)
    low_shape = ((total, width), BF16)
    three_shape = ((3, total, width), BF16)
    turned_shape = ((width, total), BF16)
    vec_shape = ((tile, width), F32)
    attn_keep = [low_shape, three_shape, ((images, pairs, 2 * rows, rows), BF16), low_shape]
    hidden_keep = [low_shape, ((parts, total, width), BF16), ((parts, total, width), F32)]
    blocks = plan.outer * plan.inner
    weight_shape = ((blocks, plan.thin, width), BF16)
    zs = max(blocks // 8, 1)

    def vmem(shapes):
        return [pltpu.VMEM(shape, dtype) for shape, dtype in shapes]

    layer_flops = 8 * total * parts * width * width
    half_rows = 3 * plan.thin * zs + tile

    first = call(
        functools.partial(first_kernel, plan, len(first_pieces)),
        (stream, bias, *first_pieces),
        [VMEM] * (2 + len(first_pieces)),
        [weight_shape, weight_shape, weight_shape, vec_shape, stream_shape, stream_shape]
        + attn_keep
        + hidden_keep,
        [VMEM] * 13,
        vmem([stream_shape, stream_shape]),
        layer_flops,
    )
    attn_full, up_full, down_full, vec, mid, middle = first[:6]
    attn_kept, hidden_kept = first[6:10], first[10:]
    if direct:
        middle, last_plane = lax.optimization_barrier((middle, last_plane))
        last_pieces = gather_cores(last_plane, devices)
    back_scratch = [
        stream_shape,
        vec_shape,
        low_shape,
        low_shape,
        low_shape,
        stream_shape,
        stream_shape,
        turned_shape,
        turned_shape,
        three_shape,
        ((2, 2, 2, half_rows, width), BF16),
    ]
    half_shape = ((2, 2, half_rows, width), BF16)
    message_shape = ((half_rows, width), BF16)
    sems = [pltpu.SemaphoreType.DMA((15,))]
    output, grad_middle, *last_halves = call(
        functools.partial(last_kernel, plan, len(last_pieces)),
        (middle, bias, goal, *last_pieces),
        [VMEM] * (3 + len(last_pieces)),
        [low_shape, stream_shape, half_shape] + [message_shape] * 4,
        [VMEM] * 2 + [ANY] * 5,
        vmem(
            attn_keep
            + hidden_keep
            + [stream_shape, stream_shape]
            + back_scratch
            + [vec_shape]
            + [weight_shape] * 3
        )
        + sems,
        3 * layer_flops,
    )
    output_pieces = spread(output[:rows], devices)
    if direct:
        last_sums = sum_cores(last_halves[0], last_halves[1:], devices)
        grad_middle, last_sums, output_pieces = lax.optimization_barrier(
            (grad_middle, last_sums, output_pieces)
        )
    grad_first, *first_halves = call(
        functools.partial(back_kernel, plan),
        (grad_middle, stream, mid, vec, attn_full, up_full, down_full, *attn_kept, *hidden_kept),
        [VMEM] * 14,
        [low_shape, half_shape] + [message_shape] * 4,
        [VMEM] + [ANY] * 5,
        vmem(back_scratch) + sems,
        3 * layer_flops,
    )

    def pack_output(output, output_pieces):
        (activations,) = call(
            pack_kernel,
            (slots, output, *output_pieces),
            [VMEM] * (mp_size + 1),
            [((SLOTS, width), F32)],
            [VMEM],
            [],
            2 * SLOTS * image_count * rows * width,
        )
        return activations

    def place_grads(grad_first, grad_pieces):
        (input_grads,) = call(
            place_kernel,
            (grad_first, *grad_pieces),
            [VMEM] * mp_size,
            [((image_count, patch_rows, width), F32)],
            [VMEM],
            [],
            image_count * patch_rows * width,
        )
        return input_grads

    if direct:
        (last_total,) = sum_plane(plan, last_sums, devices, False)
        activations = pack_output(output, output_pieces)
        last_total, first_halves, grad_first, activations = lax.optimization_barrier(
            (last_total, first_halves, grad_first, activations)
        )
        last_terms = last_total
        if devices > 8:
            last_terms = exchange(last_total, column_groups(devices))
        across = flip(grad_first[:rows], 2, devices)
        first_sums = sum_cores(first_halves[0], first_halves[1:], devices)
        first_sums, across, grad_first = lax.optimization_barrier((first_sums, across, grad_first))
        first_total = sum_plane(plan, first_sums, devices, True)
        beside = flip(grad_first[:rows], 1, devices)
        input_grads = place_grads(grad_first, [beside, across, flip(across, 1, devices)])
        first_total, last_terms, input_grads = lax.optimization_barrier(
            (first_total, last_terms, input_grads)
        )
        first_terms = [one if k == 0 else flip(one, 8 * k, devices) for k, one in enumerate(first_total)]
        terms = (last_terms, *first_terms)
        turned = (layers, thin, width)
        attn_grads, vector_grads, up_grads, down_grads = call(
            functools.partial(finish_kernel, plan, len(terms)),
            terms,
            [VMEM] * len(terms),
            [(turned, F32), (vectors.shape, F32), (turned, F32), (turned, F32)],
            [VMEM] * 4,
            vmem([vec_shape, vec_shape]),
            1 << 20,
        )
        attn_grads, down_grads = attn_grads.transpose(0, 2, 1), down_grads.transpose(0, 2, 1)
    else:

        def square_blocks(halves):
            stacked = jnp.stack([halves[0][0], jnp.stack(halves[1:3])])
            stacked = jnp.stack([stacked[k % 2, k // 2] for k in range(parts)])
            return jnp.stack(
                [lax.dynamic_index_in_dim(stacked, rank ^ k, 0, False) for k in range(parts)]
            )

        def outputs_of(halves):
            def by_owner(array):
                split = array.reshape(mp_size, dp_size, thin, width).transpose(1, 0, 2, 3)
                return split.reshape(devices, thin, width)

            every = square_blocks(halves)
            pieces = [
                every[:, :width].reshape(devices, thin, width),
                by_owner(every[:, width : 2 * width]),
                by_owner(every[:, 2 * width : 3 * width]),
                jnp.broadcast_to(every[0, 3 * width :], (devices, tile, width)),
            ]
            owned = lax.psum_scatter(
                jnp.concatenate(pieces, axis=1), ("dp", "mp"), scatter_dimension=0, tiled=False
            ).astype(F32)
            own_vec = lax.dynamic_slice_in_dim(
                owned[3 * thin :].reshape(-1), device * vec_rows, vec_rows
            )
            return owned[:thin].T, own_vec, owned[thin : 2 * thin], owned[2 * thin : 3 * thin].T

        attn_grads, vector_grads, up_grads, down_grads = (
            jnp.stack([one, two]) for one, two in zip(outputs_of(first_halves), outputs_of(last_halves))
        )
        activations = pack_output(output, output_pieces)
        input_grads = place_grads(grad_first, spread(grad_first[:rows], devices))

    return (activations, input_grads, attn_grads, vector_grads, up_grads, down_grads)


def solution(mesh):
    in_specs = (
        P("dp", None, None),
        P("dp", None, None),
        P("dp", None),
        P(None, None, ("dp", "mp")),
        P(None, ("dp", "mp")),
        P(None, "dp", "mp"),
        P(None, "mp", "dp"),
    )
    out_specs = (
        P("dp", None),
        P("dp", None, None),
        P(None, None, ("dp", "mp")),
        P(None, ("dp", "mp")),
        P(None, "dp", "mp"),
        P(None, "mp", "dp"),
    )
    return jax.shard_map(shards, mesh=mesh, in_specs=in_specs, out_specs=out_specs, check_vma=False)
```

```python
import dataclasses
import functools

import jax
import jax.numpy as jnp
from jax import lax
from jax.experimental import pallas as pl
from jax.experimental.pallas import tpu as pltpu
from jax.sharding import PartitionSpec as P

HD = 64
SLOTS = 1024
EPSILON = 1e-06
MASKED = -1e30
STEP = 16
UNROLL = 13

F32 = jnp.float32
BF16 = jnp.bfloat16


def dot_nn(left, right):
    return lax.dot_general(left, right, (((1,), (0,)), ((), ())), preferred_element_type=F32)


def dot_nt(left, right):
    return lax.dot_general(left, right, (((1,), (1,)), ((), ())), preferred_element_type=F32)


def dot_tn(left, right):
    return lax.dot_general(left, right, (((0,), (0,)), ((), ())), preferred_element_type=F32)


def block_rows(index, step):
    return pl.ds(pl.multiple_of(index * step, step), step)


def fold_rows(values):
    return jnp.sum(values.reshape(values.shape[0] // 8, 8, values.shape[1]), axis=0)


def low_halves(rows):
    lane = lax.broadcasted_iota(jnp.int32, (rows, 2 * HD), 1)
    return lane < HD


def stack_heads(pair):
    low = low_halves(pair.shape[0])
    zero = jnp.zeros_like(pair)
    return jnp.concatenate([jnp.where(low, pair, zero), jnp.where(low, zero, pair)], axis=0)


def unstack_heads(stacked):
    rows = stacked.shape[0] // 2
    return jnp.where(low_halves(rows), stacked[:rows], stacked[rows:])


def norm_rows(x_ref, out_ref, gain, shift):
    def body(index, carry):
        at = block_rows(index, STEP)
        values = x_ref[at, :].astype(F32)
        centred = values - jnp.mean(values, axis=-1, keepdims=True)
        variance = jnp.mean(centred * centred, axis=-1, keepdims=True)
        out_ref[at, :] = (centred * lax.rsqrt(variance + EPSILON) * gain + shift).astype(BF16)
        return carry

    lax.fori_loop(0, x_ref.shape[0] // STEP, body, 0, unroll=UNROLL)


def norm_back(x_ref, grad_ref, base_ref, out_ref, low_ref, gain, images):
    rows = x_ref.shape[0] // images
    width = x_ref.shape[1]
    sums = []
    for image in range(images):

        def body(index, carry, image=image):
            at = pl.ds(pl.multiple_of(image * rows + index * STEP, STEP), STEP)
            values = x_ref[at, :].astype(F32)
            grad = grad_ref[at, :]
            centred = values - jnp.mean(values, axis=-1, keepdims=True)
            variance = jnp.mean(centred * centred, axis=-1, keepdims=True)
            inverse = lax.rsqrt(variance + EPSILON)
            unit = centred * inverse
            scaled = grad * gain
            mean_one = jnp.mean(scaled, axis=-1, keepdims=True)
            mean_two = jnp.mean(scaled * unit, axis=-1, keepdims=True)
            out = base_ref[at, :] + inverse * (scaled - mean_one - unit * mean_two)
            out_ref[at, :] = out.astype(out_ref.dtype)
            if low_ref is not None:
                low_ref[at, :] = out.astype(BF16)
            return (
                carry[0] + fold_rows(grad * unit),
                carry[1] + fold_rows(grad),
                carry[2] + fold_rows(out),
            )

        zero = jnp.zeros((8, width), F32)
        sums.append(lax.fori_loop(0, rows // STEP, body, (zero, zero, zero), unroll=UNROLL))
    return sums


def weigh(sums, share):
    total = sums[0]
    for more in sums[1:]:
        total = total + more * share
    return jnp.sum(total, axis=0, keepdims=True)


def as_square(ref, part):
    rows, width = ref.shape[1:]
    per = width // rows
    return ref[pl.ds(part * per, per)].reshape(width, width)


def forward_attention(x_ref, bias_ref, vec_ref, attn_ref, keep, mid_ref):
    n1_ref, proj_ref, p_ref, att_ref = keep
    images = bias_ref.shape[0]
    rows = x_ref.shape[0] // images
    width = x_ref.shape[1]
    pairs = width // (2 * HD)
    scale = HD**-0.5

    norm_rows(x_ref, n1_ref, vec_ref[0:1, :], vec_ref[1:2, :])
    for part, bias_row in enumerate((4, None, 5)):
        value = dot_nt(n1_ref[...], as_square(attn_ref, part))
        if bias_row is not None:
            value = value + vec_ref[bias_row : bias_row + 1, :]
        proj_ref[part] = value.astype(BF16)

    def image_body(image, carry):
        at = block_rows(image, rows)
        for pair in range(pairs):
            lanes = slice(pair * 2 * HD, (pair + 1) * 2 * HD)
            query = stack_heads(proj_ref[0, at, lanes])
            scores = dot_nt(query, proj_ref[1, at, lanes]) * scale + bias_ref[image]
            top = jnp.max(scores, axis=-1, keepdims=True)
            powers = jnp.exp(scores - top)
            total = jnp.sum(powers, axis=-1, keepdims=True)
            probs = (powers * (1.0 / total)).astype(BF16)
            p_ref[image, pair] = probs
            att_ref[at, lanes] = unstack_heads(dot_nn(probs, proj_ref[2, at, lanes])).astype(BF16)
        return carry

    lax.fori_loop(0, images, image_body, 0)
    mid_ref[...] = x_ref[...].astype(F32) + dot_nt(att_ref[...], as_square(attn_ref, 3)) + vec_ref[6:7, :]


def forward_hidden(mid_ref, vec_ref, up_ref, down_ref, keep, scratch, out_ref):
    n2_ref, a_ref, gp_ref = keep
    h_ref, acc_ref = scratch
    norm_rows(mid_ref, n2_ref, vec_ref[2:3, :], vec_ref[3:4, :])
    acc_ref[...] = mid_ref[...] + vec_ref[11:12, :]

    def part_body(part, carry):
        h_ref[...] = dot_nn(n2_ref[...], as_square(up_ref, part))
        bias = vec_ref[pl.ds(7 + part, 1), :]

        def gelu_body(index, inner):
            at = block_rows(index, STEP)
            hidden = h_ref[at, :] + bias
            share = 0.5 + 0.5 * lax.erf(hidden * 0.7071067811865476)
            a_ref[part, at, :] = (hidden * share).astype(BF16)
            bell = jnp.exp(-0.5 * hidden * hidden) * 0.3989422804014327
            gp_ref[part, at, :] = (share + hidden * bell).astype(gp_ref.dtype)
            return inner

        lax.fori_loop(0, h_ref.shape[0] // STEP, gelu_body, 0, unroll=UNROLL)
        acc_ref[...] += dot_nt(a_ref[part], as_square(down_ref, part))
        return carry

    lax.fori_loop(0, a_ref.shape[0], part_body, 0)
    out_ref[...] = acc_ref[...].astype(out_ref.dtype)


def drop_shared(refs):
    @pl.when(jnp.logical_not(counts_shared()))
    def _():
        for ref in refs:
            rows = ref.shape[-2] // 2
            ref[..., rows:, :] = jnp.zeros((*ref.shape[:-2], rows, ref.shape[-1]), ref.dtype)


def backward_hidden(g_ref, mid_ref, vec_ref, up_ref, down_ref, share, keep, scratch, gm_ref, gvec_ref, store):
    n2_ref, a_ref, gp_ref = keep
    go_ref, gh_ref, acc_ref, h_ref, got_ref, n2t_ref = scratch
    images = 2
    rows = mid_ref.shape[0] // images
    width = mid_ref.shape[1]
    zero = jnp.zeros((8, width), F32)
    sums = []
    for image in range(images):

        def low_body(index, carry, image=image):
            at = pl.ds(pl.multiple_of(image * rows + index * STEP, STEP), STEP)
            grad = g_ref[at, :]
            go_ref[at, :] = grad.astype(BF16)
            return carry + fold_rows(grad)

        sums.append(lax.fori_loop(0, rows // STEP, low_body, zero, unroll=UNROLL))
    gvec_ref[11:12, :] = weigh(sums, share)
    acc_ref[...] = jnp.zeros_like(acc_ref)
    got_ref[...] = go_ref[...].T
    n2t_ref[...] = n2_ref[...].T

    def part_body(part, carry):
        store(2, part, dot_nn(got_ref[...], a_ref[part]))
        h_ref[...] = dot_nn(go_ref[...], as_square(down_ref, part))
        inner_sums = []
        for image in range(images):

            def hidden_body(index, inner, image=image):
                at = pl.ds(pl.multiple_of(image * rows + index * STEP, STEP), STEP)
                grad = (h_ref[at, :] * gp_ref[part, at, :].astype(F32)).astype(BF16)
                gh_ref[at, :] = grad
                return inner + fold_rows(grad.astype(F32))

            inner_sums.append(lax.fori_loop(0, rows // STEP, hidden_body, zero, unroll=UNROLL))
        gvec_ref[pl.ds(7 + part, 1), :] = weigh(inner_sums, share)
        store(1, part, dot_nn(n2t_ref[...], gh_ref[...]))
        acc_ref[...] += dot_nt(gh_ref[...], as_square(up_ref, part))
        return carry

    lax.fori_loop(0, a_ref.shape[0], part_body, 0)
    sums = norm_back(mid_ref, acc_ref, g_ref, gm_ref, None, vec_ref[2:3, :], images)
    for place, row in enumerate((2, 3, 6)):
        gvec_ref[row : row + 1, :] = weigh([one[place] for one in sums], share)


def backward_attention(gm_ref, x_ref, vec_ref, attn_ref, share, keep, scratch, gx_ref, gvec_ref, store):
    n1_ref, proj_ref, p_ref, att_ref = keep
    go_ref, acc_ref, ga_ref, dproj_ref = scratch
    images = p_ref.shape[0]
    rows = x_ref.shape[0] // images
    width = x_ref.shape[1]
    pairs = width // (2 * HD)
    scale = HD**-0.5
    go_ref[...] = gm_ref[...].astype(BF16)
    store(0, 3, dot_tn(go_ref[...], att_ref[...]))
    ga_ref[...] = dot_nn(go_ref[...], as_square(attn_ref, 3)).astype(BF16)

    def image_body(image, carry):
        at = block_rows(image, rows)
        for pair in range(pairs):
            lanes = slice(pair * 2 * HD, (pair + 1) * 2 * HD)
            query = stack_heads(proj_ref[0, at, lanes])
            keys = proj_ref[1, at, lanes]
            grad_out = stack_heads(ga_ref[at, lanes])
            probs = p_ref[image, pair]
            grad_probs = dot_nt(grad_out, proj_ref[2, at, lanes])
            dproj_ref[2, at, lanes] = dot_tn(probs, grad_out).astype(BF16)
            wide = probs.astype(F32)
            inner = jnp.sum(grad_probs * wide, axis=-1, keepdims=True)
            grad_scores = (wide * (grad_probs - inner)).astype(BF16)
            dproj_ref[0, at, lanes] = (unstack_heads(dot_nn(grad_scores, keys)) * scale).astype(BF16)
            dproj_ref[1, at, lanes] = (dot_tn(grad_scores, query) * scale).astype(BF16)
        return carry

    lax.fori_loop(0, images, image_body, 0)
    for part, row in enumerate((4, None, 5)):
        store(0, part, dot_tn(dproj_ref[part], n1_ref[...]))
        value = dot_nn(dproj_ref[part], as_square(attn_ref, part))
        if part == 0:
            acc_ref[...] = value
        else:
            acc_ref[...] += value
        if row is not None:
            sums = [
                fold_rows(dproj_ref[part, image * rows : (image + 1) * rows, :].astype(F32))
                for image in range(images)
            ]
            gvec_ref[row : row + 1, :] = weigh(sums, share)
    sums = norm_back(x_ref, acc_ref, gm_ref, gx_ref, None, vec_ref[0:1, :], images)
    for place, row in enumerate((0, 1)):
        gvec_ref[row : row + 1, :] = weigh([one[place] for one in sums], share)
    store(3, 0, gvec_ref[...])


def coordinates(plan):
    outer, inner = lax.axis_index("dp"), lax.axis_index("mp")
    here = (inner // 2, inner % 2)
    return (outer // 2, outer % 2, *here) if plan.direct else (0, 0, *here)


def counts_shared():
    return lax.axis_index("mp") == 0


def place_weights(plan, pieces, attn_ref, up_ref, down_ref, vec_ref):
    thin, rows = plan.thin, 3 * plan.thin

    def put(owner, block):
        at = owner % plan.inner * plan.outer + owner // plan.inner
        attn_ref[owner] = block[:thin]
        up_ref[at] = block[thin : 2 * thin]
        down_ref[at] = block[2 * thin : 3 * thin]

    if not plan.direct:
        for owner in range(plan.inner):
            put(owner, pieces[0][owner, :rows])
        vec_ref[...] = pieces[0][0, rows:].astype(F32)
        return
    at = coordinates(plan)
    vec = None
    for i, piece in enumerate(pieces):
        c, x, y = i % 2, i // 2 % 2, i // 4
        low = ((at[1] ^ y) * 2 + (at[2] ^ x)) * 2 + (at[3] ^ c)
        count = piece.shape[0] // rows
        for k in range(count):
            put((at[0] ^ k) * 8 + low, piece[k * rows : (k + 1) * rows])
        tail = piece[count * rows :].astype(F32)
        vec = tail if vec is None else vec + tail
    vec_ref[...] = vec


def storer(plan, packed_ref, kinds):
    thin, width = plan.thin, plan.width
    per = width // thin
    here = coordinates(plan)

    def put(owner, kind, block):
        c, x, y = owner % 2, owner // 2 % 2, owner // 4 % 2
        row = pl.multiple_of((kinds.index(kind) * plan.zs + owner // 8) * thin, thin)
        packed_ref[c ^ here[3], y ^ here[1], x ^ here[2], pl.ds(row, thin), :] = block

    def store(kind, part, value):
        low = value.astype(BF16)
        if kind == 3:
            for i in range(8):
                packed_ref[i % 2, i // 4, i // 2 % 2, len(kinds) * plan.zs * thin :, :] = low
            return
        blocks = low.reshape(per, thin, width)
        for i in range(per):
            owner = part * per + i if kind == 0 else i * plan.inner + part
            put(owner, kind, blocks[i])

    return store


def start_copies(packed_ref, outs, sems, start, count, before=()):
    at = pl.ds(start, count)
    copies = list(before)
    for i in range(2):
        source, target = packed_ref.at[i, :, :, at], outs[i].at[:, :, at]
        copies.append(pltpu.make_async_copy(source, target, sems.at[len(copies)]))
        copies[-1].start()
    return copies


def wait_all(copies):
    for one in copies:
        one.wait()


def prepare_kernel(plan, attn_ref, up_ref, down_ref, vec_in, keep_in, first_ref, last_ref, line_ref, vec_ref, keep_ref, sems):
    thin, tile, width = plan.thin, plan.tile, plan.width
    outs = (first_ref, last_ref)
    copies = [
        pltpu.make_async_copy(vec_in, vec_ref, sems.at[0]),
        pltpu.make_async_copy(keep_in, keep_ref, sems.at[1]),
    ]
    for kind, ref in enumerate((attn_ref, up_ref, down_ref)):
        for layer, out_ref in enumerate(outs):
            if plan.direct:
                target = out_ref.at[pl.ds(kind * thin, thin)]
                copies.append(pltpu.make_async_copy(ref.at[layer], target, sems.at[len(copies)]))
            else:
                out_ref[kind * thin : (kind + 1) * thin, :] = ref[layer]
    for one in copies:
        one.start()
    count = vec_ref.shape[1]
    device = lax.axis_index("dp") * plan.inner + lax.axis_index("mp")
    row_at = device * count // width
    offset = device * count - row_at * width
    copies[0].wait()
    copies[1].wait()
    kept = jnp.sum(keep_ref[...]) + 2 * keep_ref.shape[0]
    kept = jnp.where(counts_shared(), kept, 0)
    row = lax.broadcasted_iota(jnp.int32, (tile, width), 0)
    here = lax.broadcasted_iota(jnp.int32, (tile, width), 1) == lax.axis_index("dp")
    for layer, out_ref in enumerate(outs):
        line_ref[...] = jnp.zeros_like(line_ref)
        line_ref[0:1, 0:count] = vec_ref[layer : layer + 1, :].astype(F32)
        moved = pltpu.roll(line_ref[...], offset, 1)[0:1]
        piece = jnp.where(row == row_at, moved[:, :width], 0.0)
        piece = jnp.where(row == row_at + 1, moved[:, width:], piece)
        if layer == 1:
            piece = jnp.where(here & (row == 12), (kept >> 5).astype(F32), piece)
            piece = jnp.where(here & (row == 13), (kept & 31).astype(F32), piece)
        out_ref[3 * thin :, :] = piece.astype(BF16)
    for one in copies[2:]:
        one.wait()


def first_kernel(plan, pieces, x_ref, bias_ref, *refs):
    sources, refs = refs[:pieces], refs[pieces:]
    attn_ref, up_ref, down_ref, vec_ref, mid_ref, out_ref, *refs = refs
    attn_keep, hidden_keep, (h_ref, acc_ref) = refs[:4], refs[4:7], refs[7:]
    place_weights(plan, sources, attn_ref, up_ref, down_ref, vec_ref)
    forward_attention(x_ref, bias_ref, vec_ref, attn_ref, attn_keep, mid_ref)
    forward_hidden(mid_ref, vec_ref, up_ref, down_ref, hidden_keep, (h_ref, acc_ref), out_ref)
    drop_shared((attn_keep[0], attn_keep[3], hidden_keep[0], hidden_keep[1]))


HIDDEN_KINDS, ATTENTION_KINDS, ALL_KINDS = (1, 2), (0,), (1, 2, 0)


def last_hidden_kernel(plan, pieces, x_ref, bias_ref, goal_ref, *refs):
    sources, refs = refs[:pieces], refs[pieces:]
    out_ref, gm_ref, gvec_ref, vec_ref, attn_ref, *refs = refs
    attn_keep, outs, hidden_keep, refs = refs[0:4], refs[4:6], refs[6:9], refs[9:]
    mid_ref, g_ref, go_ref, gh_ref, acc_ref, h_ref, got_ref, n2t_ref, up_ref, down_ref, packed_ref, sems = refs
    place_weights(plan, sources, attn_ref, up_ref, down_ref, vec_ref)
    forward_attention(x_ref, bias_ref, vec_ref, attn_ref, attn_keep, mid_ref)
    forward_hidden(mid_ref, vec_ref, up_ref, down_ref, hidden_keep, (h_ref, acc_ref), out_ref)
    drop_shared((attn_keep[0], attn_keep[3], hidden_keep[0], hidden_keep[1]))
    high = jnp.sum(vec_ref[12:13, :], axis=-1, keepdims=True)
    rest = jnp.sum(vec_ref[13:14, :], axis=-1, keepdims=True)
    loss_scale = float(plan.slots) / (high * 32.0 + rest)
    g_ref[...] = goal_ref[...].astype(F32) * loss_scale
    gvec_ref[...] = jnp.zeros_like(gvec_ref)
    share = counts_shared().astype(F32)
    store = storer(plan, packed_ref, HIDDEN_KINDS)
    scratch = (go_ref, gh_ref, acc_ref, h_ref, got_ref, n2t_ref)
    backward_hidden(g_ref, mid_ref, vec_ref, up_ref, down_ref, share, hidden_keep, scratch, gm_ref, gvec_ref, store)
    wait_all(start_copies(packed_ref, outs, sems, 0, packed_ref.shape[3]))


def last_attention_kernel(plan, gm_ref, x_ref, vec_ref, attn_ref, early_ref, *refs):
    keep, gx_ref, outs, refs = refs[:4], refs[4], refs[5:7], refs[7:]
    gvec_ref, go_ref, acc_ref, ga_ref, dproj_ref, packed_ref, sems = refs
    gvec_ref[...] = early_ref[...]
    share = counts_shared().astype(F32)
    store = storer(plan, packed_ref, ATTENTION_KINDS)
    scratch = (go_ref, acc_ref, ga_ref, dproj_ref)
    backward_attention(gm_ref, x_ref, vec_ref, attn_ref, share, keep, scratch, gx_ref, gvec_ref, store)
    wait_all(start_copies(packed_ref, outs, sems, 0, packed_ref.shape[3]))


def back_kernel(plan, g_ref, x_ref, mid_ref, vec_ref, attn_ref, up_ref, down_ref, *refs):
    attn_keep, hidden_keep, gx_ref, outs, refs = refs[:4], refs[4:7], refs[7], refs[8:10], refs[10:]
    gm_ref, gvec_ref, go_ref, gh_ref, ga_ref, acc_ref, h_ref, got_ref, n2t_ref, dproj_ref, packed_ref, sems = refs
    gvec_ref[...] = jnp.zeros_like(gvec_ref)
    share = counts_shared().astype(F32)
    store = storer(plan, packed_ref, ALL_KINDS)
    scratch = (go_ref, gh_ref, acc_ref, h_ref, got_ref, n2t_ref)
    backward_hidden(g_ref, mid_ref, vec_ref, up_ref, down_ref, share, hidden_keep, scratch, gm_ref, gvec_ref, store)
    hidden_rows = 2 * plan.zs * plan.thin
    copies = start_copies(packed_ref, outs, sems, 0, hidden_rows)
    scratch = (go_ref, acc_ref, ga_ref, dproj_ref)
    backward_attention(gm_ref, x_ref, vec_ref, attn_ref, share, attn_keep, scratch, gx_ref, gvec_ref, store)
    rest = packed_ref.shape[3] - hidden_rows
    wait_all(start_copies(packed_ref, outs, sems, hidden_rows, rest, copies))


def add_kernel(kept_hidden, got_hidden, kept_attn, got_attn, *out_refs):
    count = kept_hidden.shape[2]
    for i, out_ref in enumerate(out_refs):
        at = (i // 2, i % 2)
        total = kept_hidden[at].astype(F32) + got_hidden[at].astype(F32)
        out_ref[0:count, :] = total.astype(BF16)
        total = kept_attn[at].astype(F32) + got_attn[at].astype(F32)
        out_ref[count:, :] = total.astype(BF16)


def finish_kernel(plan, count_of, *refs):
    layers = (refs[:count_of], refs[count_of : 2 * count_of])
    attn_out, vec_out, up_out, down_out, *tiles = refs[2 * count_of :]
    thin, tile, width = plan.thin, plan.tile, plan.width

    count = vec_out.shape[1]
    device = lax.axis_index("dp") * plan.inner + lax.axis_index("mp")
    row = device * count // width
    offset = device * count - row * width
    for layer in range(2):

        def total(start, count, layer=layer):
            return sum(ref[start : start + count, :].astype(F32) for ref in layers[layer])

        attn_out[layer] = total(0, thin)
        up_out[layer] = total(thin, thin)
        down_out[layer] = total(2 * thin, thin)
        tiles[layer][...] = total(3 * thin, tile)
        both = jnp.concatenate(
            [tiles[layer][pl.ds(row, 1), :], tiles[layer][pl.ds(row + 1, 1), :]], axis=1
        )
        both = jnp.broadcast_to(both, (8, 2 * width))
        moved = pltpu.roll(both, 2 * width - offset, 1)
        vec_out[layer : layer + 1, :] = moved[0:1, :count]


def place_kernel(own_ref, *refs):
    others, out_ref = refs[:-1], refs[-1]
    rows = own_ref.shape[0] // 2
    kept = out_ref.shape[1]
    mine = lax.axis_index("mp")
    out_ref[mine] = own_ref[0:rows, :].astype(F32)[:kept]
    for i, ref in enumerate(others):
        out_ref[mine ^ (i + 1)] = ref[...].astype(F32)[:kept]
    out_ref[out_ref.shape[0] - 1] = own_ref[rows : 2 * rows, :].astype(F32)[:kept]


def pack_kernel(slot_ref, own_ref, *refs):
    others, out_ref = refs[:-1], refs[-1]
    rows = own_ref.shape[0] // 2
    sources = [own_ref[0:rows, :]] + [ref[...] for ref in others] + [own_ref[rows : 2 * rows, :]]
    step = 256

    def body(index, carry):
        slots = lax.broadcasted_iota(jnp.int32, (step, rows), 0) + index * step
        total = None
        for i, values in enumerate(sources):
            picks = jnp.where(slots == slot_ref[i], 1.0, 0.0).astype(BF16)
            term = dot_nn(picks, values)
            total = term if total is None else total + term
        out_ref[block_rows(index, step), :] = total
        return carry

    lax.fori_loop(0, out_ref.shape[0] // step, body, 0)


VMEM = pl.BlockSpec(memory_space=pltpu.VMEM)
ANY = pl.BlockSpec(memory_space=pl.ANY)


def call(kernel, operands, specs, outs, out_specs, scratch, flops, limit=26):
    return pl.pallas_call(
        kernel,
        out_shape=[jax.ShapeDtypeStruct(shape, dtype) for shape, dtype in outs],
        in_specs=specs,
        out_specs=out_specs,
        scratch_shapes=scratch,
        compiler_params=pltpu.CompilerParams(vmem_limit_bytes=limit << 20),
        cost_estimate=pl.CostEstimate(flops=flops, bytes_accessed=8 << 20, transcendentals=0),
    )(*operands)


@dataclasses.dataclass(frozen=True)
class Plan:
    outer: int
    inner: int
    thin: int
    tile: int
    width: int
    slots: int
    direct: bool

    @property
    def zs(self):
        return self.outer // 2 if self.direct else 1


def flip(array, mask, devices):
    return lax.ppermute(array, ("dp", "mp"), [(d, d ^ mask) for d in range(devices)])


def column_kernel(plan, *refs):
    blocks, out_ref = refs[:-1], refs[-1]
    rows = 3 * plan.thin
    for k, ref in enumerate(blocks):
        out_ref[k * rows : (k + 1) * rows, :] = ref[0:rows, :]
    tail = sum(ref[rows:, :].astype(F32) for ref in blocks)
    out_ref[len(blocks) * rows :, :] = tail.astype(BF16)


def gather_column(plan, block, devices):
    blocks = [block] + [flip(block, 8 * k, devices) for k in range(1, devices // 8)]
    shape = (len(blocks) * 3 * plan.thin + plan.tile, plan.width)
    (column,) = call(
        functools.partial(column_kernel, plan), blocks, [VMEM] * len(blocks), [(shape, BF16)], [VMEM], [], 1 << 20
    )
    return column


def gather_plane(column, devices):
    return [column] + [flip(column, mask, devices) for mask in (2, 4, 6)]


def gather_cores(plane, devices):
    pieces = []
    for piece in plane:
        pieces += [piece, flip(piece, 1, devices)]
    return pieces


def spread(rows, devices):
    across = flip(rows, 2, devices)
    return [flip(rows, 1, devices), across, flip(across, 1, devices)]


def sum_cores(kept, sent, devices):
    got = flip(sent, 1, devices)
    return [(kept[i // 2, i % 2].astype(F32) + got[i // 2, i % 2].astype(F32)).astype(BF16) for i in range(4)]


def plane_kernel(plan, *refs):
    terms, out_refs = refs[:4], refs[4:]
    thin, tile = plan.thin, plan.tile
    zs = len(out_refs)

    def added(start, count):
        return sum(ref[pl.ds(start, count), :].astype(F32) for ref in terms).astype(BF16)

    tail = added(3 * zs * thin, tile)
    for z, out_ref in enumerate(out_refs):
        for kind in range(3):
            row = (ALL_KINDS.index(kind) * zs + (coordinates(plan)[0] ^ z)) * thin
            out_ref[kind * thin : (kind + 1) * thin, :] = added(pl.multiple_of(row, thin), thin)
        out_ref[3 * thin :, :] = tail


def sum_plane(plan, sums, devices):
    zs = devices // 8
    terms = [sums[0]] + [flip(one, mask, devices) for one, mask in zip(sums[1:], (2, 4, 6))]
    outs = [((3 * plan.thin + plan.tile, plan.width), BF16)] * zs
    return call(
        functools.partial(plane_kernel, plan), terms, [VMEM] * 4, outs, [VMEM] * zs, [], 1 << 20
    )


def sum_column(blocks, devices):
    return [one if k == 0 else flip(one, 8 * k, devices) for k, one in enumerate(blocks)]


def shards(patches, targets, keep_mask, attn_weights, vectors, up_weights, down_weights):
    image_count, patch_rows, width = patches.shape
    layers = attn_weights.shape[0]
    dp_size, mp_size = lax.axis_size("dp"), lax.axis_size("mp")
    devices = dp_size * mp_size
    rank = lax.axis_index("mp")
    lane_rank = lax.axis_index("dp")
    device = lane_rank * mp_size + rank
    thin = attn_weights.shape[2]
    vec_rows = vectors.shape[1]
    parts = thin * devices // width
    assert image_count == mp_size + 1 and layers == 2 and parts == mp_size == 4
    direct = thin % 16 == 0
    images, tile = 2, 16
    rows = -(-patch_rows // 16) * 16
    total = images * rows

    keep_rows = jnp.concatenate([jnp.ones((image_count, 2), jnp.int32), keep_mask], axis=1)
    keep_rows = jnp.pad(keep_rows, ((0, 0), (0, rows - patch_rows)))

    attn_turned = attn_weights.transpose(0, 2, 1)
    down_turned = down_weights.transpose(0, 2, 1)
    packing = Plan(dp_size, mp_size, thin, tile, width, SLOTS * dp_size, direct)
    block_shape = ((3 * thin + tile, width), BF16)
    first_block, last_block = call(
        functools.partial(prepare_kernel, packing),
        (attn_turned, up_weights, down_turned, vectors, keep_mask),
        [ANY if direct else VMEM] * 3 + [ANY] * 2,
        [block_shape, block_shape],
        [VMEM, VMEM],
        [
            pltpu.VMEM((8, 2 * width), F32),
            pltpu.VMEM(vectors.shape, BF16),
            pltpu.VMEM(keep_mask.shape, jnp.int32),
            pltpu.SemaphoreType.DMA((8,)),
        ],
        1 << 20,
        60,
    )
    if direct:
        plan = packing
        first_column = gather_column(plan, first_block, devices)
        first_column, last_block = lax.optimization_barrier((first_column, last_block))
        first_plane = gather_plane(first_column, devices)
        last_column = gather_column(plan, last_block, devices)
        first_plane, last_column = lax.optimization_barrier((first_plane, last_column))
        first_pieces = gather_cores(first_plane, devices)
        last_plane = gather_plane(last_column, devices)
    else:
        plan = Plan(1, parts, width, tile, width, SLOTS * dp_size, False)

        def squares(array):
            return array.reshape(parts, width, width)

        def by_part(array):
            split = array.reshape(dp_size, mp_size, thin, width).transpose(1, 0, 2, 3)
            return squares(split)

        def one_tile(array):
            summed = jnp.sum(array.astype(F32), axis=0).astype(BF16)
            return jnp.pad(summed[None], ((0, parts - 1), (0, 0), (0, 0)))

        def normal(block):
            every = lax.all_gather(block, ("dp", "mp"))
            return jnp.concatenate(
                [
                    squares(every[:, :thin]),
                    by_part(every[:, thin : 2 * thin]),
                    by_part(every[:, 2 * thin : 3 * thin]),
                    one_tile(every[:, 3 * thin :]),
                ],
                axis=1,
            )

        first_pieces, last_pieces = [normal(first_block)], [normal(last_block)]

    flat = keep_rows.reshape(-1)
    slot = jnp.where(flat == 1, jnp.cumsum(flat) - flat, SLOTS).reshape(image_count, 1, rows)

    def mine(array):
        return jnp.concatenate(
            [lax.dynamic_slice_in_dim(array, rank, 1, 0), array[mp_size:]], axis=0
        )

    def padded(array):
        return jnp.pad(mine(array), ((0, 0), (0, rows - patch_rows), (0, 0)))

    kept = mine(keep_rows)
    stream = padded(patches).reshape(total, width)
    bias = jnp.where(kept == 1, 0.0, MASKED).astype(F32)[:, None, :]
    goal = jnp.where((kept == 1)[:, :, None], padded(targets), 0).reshape(total, width)
    slots = jnp.concatenate(
        [lax.dynamic_slice_in_dim(slot, rank ^ k, 1, 0) for k in range(mp_size)] + [slot[mp_size:]],
        axis=0,
    )

    stream, slots, goal = lax.optimization_barrier((stream, slots, goal))

    pairs = width // (2 * HD)
    stream_shape = ((total, width), F32)
    low_shape = ((total, width), BF16)
    three_shape = ((3, total, width), BF16)
    turned_shape = ((width, total), BF16)
    vec_shape = ((tile, width), F32)
    attn_keep = [low_shape, three_shape, ((images, pairs, 2 * rows, rows), BF16), low_shape]
    hidden_keep = [low_shape, ((parts, total, width), BF16), ((parts, total, width), F32)]
    blocks = plan.outer * plan.inner
    weight_shape = ((blocks, plan.thin, width), BF16)
    zs = max(blocks // 8, 1)

    def vmem(shapes):
        return [pltpu.VMEM(shape, dtype) for shape, dtype in shapes]

    layer_flops = 8 * total * parts * width * width
    hidden_rows, attn_rows = 2 * plan.thin * zs, plan.thin * zs + tile

    def half(count):
        return ((2, 2, count, width), BF16)

    def both(count):
        return ((2, 2, 2, count, width), BF16)


    first = call(
        functools.partial(first_kernel, plan, len(first_pieces)),
        (stream, bias, *first_pieces),
        [VMEM] * (2 + len(first_pieces)),
        [weight_shape, weight_shape, weight_shape, vec_shape, stream_shape, stream_shape]
        + attn_keep
        + hidden_keep,
        [VMEM] * 13,
        vmem([stream_shape, stream_shape]),
        layer_flops,
    )
    attn_full, up_full, down_full, vec, mid, middle = first[:6]
    attn_kept, hidden_kept = first[6:10], first[10:]
    if direct:
        middle, last_plane = lax.optimization_barrier((middle, last_plane))
        last_pieces = gather_cores(last_plane, devices)
    sems = [pltpu.SemaphoreType.DMA((4,))]
    output, last_mid_grad, last_gvec, last_vec, last_attn, *refs = call(
        functools.partial(last_hidden_kernel, plan, len(last_pieces)),
        (middle, bias, goal, *last_pieces),
        [VMEM] * (3 + len(last_pieces)),
        [low_shape, stream_shape, vec_shape, vec_shape, weight_shape]
        + attn_keep
        + [half(hidden_rows), half(hidden_rows)],
        [VMEM] * 9 + [ANY] * 2,
        vmem(
            hidden_keep
            + [stream_shape, stream_shape, low_shape, low_shape, stream_shape, stream_shape]
            + [turned_shape, turned_shape, weight_shape, weight_shape, both(hidden_rows)]
        )
        + sems,
        2 * layer_flops,
    )
    last_kept, last_hidden = refs[:4], refs[4:]
    grad_middle, *last_attention = call(
        functools.partial(last_attention_kernel, plan),
        (last_mid_grad, middle, last_vec, last_attn, last_gvec, *last_kept),
        [VMEM] * 9,
        [stream_shape, half(attn_rows), half(attn_rows)],
        [VMEM, ANY, ANY],
        vmem([vec_shape, low_shape, stream_shape, low_shape, three_shape, both(attn_rows)]) + sems,
        layer_flops,
    )
    output_pieces = spread(output[:rows], devices)
    if direct:
        terms = []
        for kept_half, sent_half in (last_hidden, last_attention):
            terms += [kept_half, flip(sent_half, 1, devices)]
        message = ((hidden_rows + attn_rows, width), BF16)
        last_sums = call(add_kernel, terms, [VMEM] * 4, [message] * 4, [VMEM] * 4, [], 1 << 20)
        grad_middle, last_sums, output_pieces = lax.optimization_barrier(
            (grad_middle, last_sums, output_pieces)
        )
    grad_first, *first_halves = call(
        functools.partial(back_kernel, plan),
        (grad_middle, stream, mid, vec, attn_full, up_full, down_full, *attn_kept, *hidden_kept),
        [VMEM] * 14,
        [low_shape, half(hidden_rows + attn_rows), half(hidden_rows + attn_rows)],
        [VMEM, ANY, ANY],
        vmem(
            [stream_shape, vec_shape, low_shape, low_shape, low_shape, stream_shape, stream_shape]
            + [turned_shape, turned_shape, three_shape, both(hidden_rows + attn_rows)]
        )
        + sems,
        3 * layer_flops,
    )

    def pack_output(output, output_pieces):
        (activations,) = call(
            pack_kernel,
            (slots, output, *output_pieces),
            [VMEM] * (mp_size + 1),
            [((SLOTS, width), F32)],
            [VMEM],
            [],
            2 * SLOTS * image_count * rows * width,
        )
        return activations

    def place_grads(grad_first, grad_pieces):
        (input_grads,) = call(
            place_kernel,
            (grad_first, *grad_pieces),
            [VMEM] * mp_size,
            [((image_count, patch_rows, width), F32)],
            [VMEM],
            [],
            image_count * patch_rows * width,
        )
        return input_grads

    if direct:
        last_total = sum_plane(plan, last_sums, devices)
        activations = pack_output(output, output_pieces)
        last_total, first_halves, grad_first, activations = lax.optimization_barrier(
            (last_total, first_halves, grad_first, activations)
        )
        across = flip(grad_first[:rows], 2, devices)
        first_sums = sum_cores(*first_halves, devices)
        first_sums, last_total, across, grad_first = lax.optimization_barrier(
            (first_sums, last_total, across, grad_first)
        )
        first_total = sum_plane(plan, first_sums, devices)
        last_terms = sum_column(last_total, devices)
        beside = flip(grad_first[:rows], 1, devices)
        input_grads = place_grads(grad_first, [beside, across, flip(across, 1, devices)])
        first_total, last_terms, input_grads = lax.optimization_barrier(
            (first_total, last_terms, input_grads)
        )
        first_terms = sum_column(first_total, devices)
        terms = (*first_terms, *last_terms)
        turned = (layers, thin, width)
        attn_grads, vector_grads, up_grads, down_grads = call(
            functools.partial(finish_kernel, plan, len(first_terms)),
            terms,
            [VMEM] * len(terms),
            [(turned, F32), (vectors.shape, F32), (turned, F32), (turned, F32)],
            [VMEM] * 4,
            vmem([vec_shape, vec_shape]),
            1 << 20,
        )
        attn_grads, down_grads = attn_grads.transpose(0, 2, 1), down_grads.transpose(0, 2, 1)
    else:
        last_halves = [
            jnp.concatenate(halves, axis=2) for halves in zip(last_hidden, last_attention)
        ]

        def square_blocks(halves):
            stacked = jnp.stack(halves)[:, 0]
            stacked = jnp.stack([stacked[k % 2, k // 2] for k in range(parts)])
            return jnp.stack(
                [lax.dynamic_index_in_dim(stacked, rank ^ k, 0, False) for k in range(parts)]
            )

        def outputs_of(halves):
            def by_owner(array):
                split = array.reshape(mp_size, dp_size, thin, width).transpose(1, 0, 2, 3)
                return split.reshape(devices, thin, width)

            every = square_blocks(halves)
            pieces = [
                every[:, 2 * width : 3 * width].reshape(devices, thin, width),
                by_owner(every[:, :width]),
                by_owner(every[:, width : 2 * width]),
                jnp.broadcast_to(every[0, 3 * width :], (devices, tile, width)),
            ]
            owned = lax.psum_scatter(
                jnp.concatenate(pieces, axis=1), ("dp", "mp"), scatter_dimension=0, tiled=False
            ).astype(F32)
            own_vec = lax.dynamic_slice_in_dim(
                owned[3 * thin :].reshape(-1), device * vec_rows, vec_rows
            )
            return owned[:thin].T, own_vec, owned[thin : 2 * thin], owned[2 * thin : 3 * thin].T

        attn_grads, vector_grads, up_grads, down_grads = (
            jnp.stack([one, two]) for one, two in zip(outputs_of(first_halves), outputs_of(last_halves))
        )
        activations = pack_output(output, output_pieces)
        input_grads = place_grads(grad_first, spread(grad_first[:rows], devices))

    return (activations, input_grads, attn_grads, vector_grads, up_grads, down_grads)


def solution(mesh):
    in_specs = (
        P("dp", None, None),
        P("dp", None, None),
        P("dp", None),
        P(None, None, ("dp", "mp")),
        P(None, ("dp", "mp")),
        P(None, "dp", "mp"),
        P(None, "mp", "dp"),
    )
    out_specs = (
        P("dp", None),
        P("dp", None, None),
        P(None, None, ("dp", "mp")),
        P(None, ("dp", "mp")),
        P(None, "dp", "mp"),
        P(None, "mp", "dp"),
    )
    return jax.shard_map(shards, mesh=mesh, in_specs=in_specs, out_specs=out_specs, check_vma=False)
```

```python
import dataclasses
import functools

import jax
import jax.numpy as jnp
from jax import lax
from jax.experimental import pallas as pl
from jax.experimental.pallas import tpu as pltpu
from jax.sharding import PartitionSpec as P

HD = 64
SLOTS = 1024
EPSILON = 1e-06
MASKED = -1e30
STEP = 16
UNROLL = 13

F32 = jnp.float32
BF16 = jnp.bfloat16


def dot_nn(left, right):
    return lax.dot_general(left, right, (((1,), (0,)), ((), ())), preferred_element_type=F32)


def dot_nt(left, right):
    return lax.dot_general(left, right, (((1,), (1,)), ((), ())), preferred_element_type=F32)


def dot_tn(left, right):
    return lax.dot_general(left, right, (((0,), (0,)), ((), ())), preferred_element_type=F32)


def block_rows(index, step):
    return pl.ds(pl.multiple_of(index * step, step), step)


def fold_rows(values):
    return jnp.sum(values.reshape(values.shape[0] // 8, 8, values.shape[1]), axis=0)


def low_halves(rows):
    lane = lax.broadcasted_iota(jnp.int32, (rows, 2 * HD), 1)
    return lane < HD


def stack_heads(pair):
    low = low_halves(pair.shape[0])
    zero = jnp.zeros_like(pair)
    return jnp.concatenate([jnp.where(low, pair, zero), jnp.where(low, zero, pair)], axis=0)


def unstack_heads(stacked):
    rows = stacked.shape[0] // 2
    return jnp.where(low_halves(rows), stacked[:rows], stacked[rows:])


def norm_rows(x_ref, out_ref, gain, shift):
    def body(index, carry):
        at = block_rows(index, STEP)
        values = x_ref[at, :].astype(F32)
        centred = values - jnp.mean(values, axis=-1, keepdims=True)
        variance = jnp.mean(centred * centred, axis=-1, keepdims=True)
        out_ref[at, :] = (centred * lax.rsqrt(variance + EPSILON) * gain + shift).astype(BF16)
        return carry

    lax.fori_loop(0, x_ref.shape[0] // STEP, body, 0, unroll=UNROLL)


def norm_back(x_ref, grad_ref, base_ref, out_ref, low_ref, gain, images):
    rows = x_ref.shape[0] // images
    width = x_ref.shape[1]
    sums = []
    for image in range(images):

        def body(index, carry, image=image):
            at = pl.ds(pl.multiple_of(image * rows + index * STEP, STEP), STEP)
            values = x_ref[at, :].astype(F32)
            grad = grad_ref[at, :]
            centred = values - jnp.mean(values, axis=-1, keepdims=True)
            variance = jnp.mean(centred * centred, axis=-1, keepdims=True)
            inverse = lax.rsqrt(variance + EPSILON)
            unit = centred * inverse
            scaled = grad * gain
            mean_one = jnp.mean(scaled, axis=-1, keepdims=True)
            mean_two = jnp.mean(scaled * unit, axis=-1, keepdims=True)
            out = base_ref[at, :] + inverse * (scaled - mean_one - unit * mean_two)
            out_ref[at, :] = out.astype(out_ref.dtype)
            if low_ref is not None:
                low_ref[at, :] = out.astype(BF16)
            return (
                carry[0] + fold_rows(grad * unit),
                carry[1] + fold_rows(grad),
                carry[2] + fold_rows(out),
            )

        zero = jnp.zeros((8, width), F32)
        sums.append(lax.fori_loop(0, rows // STEP, body, (zero, zero, zero), unroll=UNROLL))
    return sums


def weigh(sums, share):
    total = sums[0]
    for more in sums[1:]:
        total = total + more * share
    return jnp.sum(total, axis=0, keepdims=True)


def as_square(ref, part):
    rows, width = ref.shape[1:]
    per = width // rows
    return ref[pl.ds(part * per, per)].reshape(width, width)


def forward_attention(x_ref, bias_ref, vec_ref, attn_ref, keep, mid_ref):
    n1_ref, proj_ref, p_ref, att_ref = keep
    images = bias_ref.shape[0]
    rows = x_ref.shape[0] // images
    width = x_ref.shape[1]
    pairs = width // (2 * HD)
    scale = HD**-0.5

    norm_rows(x_ref, n1_ref, vec_ref[0:1, :], vec_ref[1:2, :])
    for part, bias_row in enumerate((4, None, 5)):
        value = dot_nt(n1_ref[...], as_square(attn_ref, part))
        if bias_row is not None:
            value = value + vec_ref[bias_row : bias_row + 1, :]
        proj_ref[part] = value.astype(BF16)

    def image_body(image, carry):
        at = block_rows(image, rows)
        for pair in range(pairs):
            lanes = slice(pair * 2 * HD, (pair + 1) * 2 * HD)
            query = stack_heads(proj_ref[0, at, lanes])
            scores = dot_nt(query, proj_ref[1, at, lanes]) * scale + bias_ref[image]
            top = jnp.max(scores, axis=-1, keepdims=True)
            powers = jnp.exp(scores - top)
            total = jnp.sum(powers, axis=-1, keepdims=True)
            probs = (powers * (1.0 / total)).astype(BF16)
            p_ref[image, pair] = probs
            att_ref[at, lanes] = unstack_heads(dot_nn(probs, proj_ref[2, at, lanes])).astype(BF16)
        return carry

    lax.fori_loop(0, images, image_body, 0)
    mid_ref[...] = x_ref[...].astype(F32) + dot_nt(att_ref[...], as_square(attn_ref, 3)) + vec_ref[6:7, :]


def forward_hidden(mid_ref, vec_ref, up_ref, down_ref, keep, scratch, out_ref):
    n2_ref, a_ref, gp_ref = keep
    h_ref, acc_ref = scratch
    norm_rows(mid_ref, n2_ref, vec_ref[2:3, :], vec_ref[3:4, :])
    acc_ref[...] = mid_ref[...] + vec_ref[11:12, :]

    def part_body(part, carry):
        h_ref[part % 2] = dot_nn(n2_ref[...], as_square(up_ref, part))
        bias = vec_ref[pl.ds(7 + part, 1), :]

        def gelu_body(index, inner):
            at = block_rows(index, STEP)
            hidden = h_ref[part % 2, at, :] + bias
            share = 0.5 + 0.5 * lax.erf(hidden * 0.7071067811865476)
            a_ref[part, at, :] = (hidden * share).astype(BF16)
            bell = jnp.exp(-0.5 * hidden * hidden) * 0.3989422804014327
            gp_ref[part, at, :] = (share + hidden * bell).astype(gp_ref.dtype)
            return inner

        lax.fori_loop(0, h_ref.shape[1] // STEP, gelu_body, 0, unroll=True)
        acc_ref[...] += dot_nt(a_ref[part], as_square(down_ref, part))
        return carry

    for part in range(a_ref.shape[0]):
        part_body(part, 0)
    out_ref[...] = acc_ref[...].astype(out_ref.dtype)


def drop_shared(refs):
    @pl.when(jnp.logical_not(counts_shared()))
    def _():
        for ref in refs:
            rows = ref.shape[-2] // 2
            ref[..., rows:, :] = jnp.zeros((*ref.shape[:-2], rows, ref.shape[-1]), ref.dtype)


def backward_hidden(g_ref, mid_ref, vec_ref, up_ref, down_ref, share, keep, scratch, gm_ref, gvec_ref, store):
    n2_ref, a_ref, gp_ref = keep
    go_ref, gh_ref, acc_ref, h_ref, got_ref, n2t_ref = scratch
    images = 2
    rows = mid_ref.shape[0] // images
    width = mid_ref.shape[1]
    zero = jnp.zeros((8, width), F32)
    sums = []
    for image in range(images):

        def low_body(index, carry, image=image):
            at = pl.ds(pl.multiple_of(image * rows + index * STEP, STEP), STEP)
            grad = g_ref[at, :]
            go_ref[at, :] = grad.astype(BF16)
            return carry + fold_rows(grad)

        sums.append(lax.fori_loop(0, rows // STEP, low_body, zero, unroll=UNROLL))
    gvec_ref[11:12, :] = weigh(sums, share)
    acc_ref[...] = jnp.zeros_like(acc_ref)
    got_ref[...] = go_ref[...].T
    n2t_ref[...] = n2_ref[...].T

    def part_body(part, carry):
        store(2, part, dot_nn(got_ref[...], a_ref[part]))
        h_ref[part % 2] = dot_nn(go_ref[...], as_square(down_ref, part))
        inner_sums = []
        for image in range(images):

            def hidden_body(index, inner, image=image):
                at = pl.ds(pl.multiple_of(image * rows + index * STEP, STEP), STEP)
                grad = (h_ref[part % 2, at, :] * gp_ref[part, at, :].astype(F32)).astype(BF16)
                gh_ref[part % 2, at, :] = grad
                return inner + fold_rows(grad.astype(F32))

            inner_sums.append(lax.fori_loop(0, rows // STEP, hidden_body, zero, unroll=UNROLL))
        gvec_ref[pl.ds(7 + part, 1), :] = weigh(inner_sums, share)
        store(1, part, dot_nn(n2t_ref[...], gh_ref[part % 2]))
        acc_ref[...] += dot_nt(gh_ref[part % 2], as_square(up_ref, part))
        return carry

    for part in range(a_ref.shape[0]):
        part_body(part, 0)
    sums = norm_back(mid_ref, acc_ref, g_ref, gm_ref, None, vec_ref[2:3, :], images)
    for place, row in enumerate((2, 3, 6)):
        gvec_ref[row : row + 1, :] = weigh([one[place] for one in sums], share)


def backward_attention(gm_ref, x_ref, vec_ref, attn_ref, share, keep, scratch, gx_ref, gvec_ref, store):
    n1_ref, proj_ref, p_ref, att_ref = keep
    go_ref, acc_ref, ga_ref, dproj_ref = scratch
    images = p_ref.shape[0]
    rows = x_ref.shape[0] // images
    width = x_ref.shape[1]
    pairs = width // (2 * HD)
    scale = HD**-0.5
    go_ref[...] = gm_ref[...].astype(BF16)
    store(0, 3, dot_tn(go_ref[...], att_ref[...]))
    ga_ref[...] = dot_nn(go_ref[...], as_square(attn_ref, 3)).astype(BF16)

    def image_body(image, carry):
        at = block_rows(image, rows)
        for pair in range(pairs):
            lanes = slice(pair * 2 * HD, (pair + 1) * 2 * HD)
            query = stack_heads(proj_ref[0, at, lanes])
            keys = proj_ref[1, at, lanes]
            grad_out = stack_heads(ga_ref[at, lanes])
            probs = p_ref[image, pair]
            grad_probs = dot_nt(grad_out, proj_ref[2, at, lanes])
            dproj_ref[2, at, lanes] = dot_tn(probs, grad_out).astype(BF16)
            wide = probs.astype(F32)
            inner = jnp.sum(grad_probs * wide, axis=-1, keepdims=True)
            grad_scores = (wide * (grad_probs - inner)).astype(BF16)
            dproj_ref[0, at, lanes] = (unstack_heads(dot_nn(grad_scores, keys)) * scale).astype(BF16)
            dproj_ref[1, at, lanes] = (dot_tn(grad_scores, query) * scale).astype(BF16)
        return carry

    lax.fori_loop(0, images, image_body, 0)
    for part, row in enumerate((4, None, 5)):
        store(0, part, dot_tn(dproj_ref[part], n1_ref[...]))
        value = dot_nn(dproj_ref[part], as_square(attn_ref, part))
        if part == 0:
            acc_ref[...] = value
        else:
            acc_ref[...] += value
        if row is not None:
            sums = [
                fold_rows(dproj_ref[part, image * rows : (image + 1) * rows, :].astype(F32))
                for image in range(images)
            ]
            gvec_ref[row : row + 1, :] = weigh(sums, share)
    sums = norm_back(x_ref, acc_ref, gm_ref, gx_ref, None, vec_ref[0:1, :], images)
    for place, row in enumerate((0, 1)):
        gvec_ref[row : row + 1, :] = weigh([one[place] for one in sums], share)
    store(3, 0, gvec_ref[...])


def coordinates(plan):
    outer, inner = lax.axis_index("dp"), lax.axis_index("mp")
    here = (inner // 2, inner % 2)
    return (outer // 2, outer % 2, *here) if plan.direct else (0, 0, *here)


def counts_shared():
    return lax.axis_index("mp") == 0


def place_weights(plan, pieces, attn_ref, up_ref, down_ref, vec_ref):
    thin, rows = plan.thin, 3 * plan.thin

    def put(owner, block):
        at = owner % plan.inner * plan.outer + owner // plan.inner
        attn_ref[owner] = block[:thin]
        up_ref[at] = block[thin : 2 * thin]
        down_ref[at] = block[2 * thin : 3 * thin]

    if not plan.direct:
        for owner in range(plan.inner):
            put(owner, pieces[0][owner, :rows])
        vec_ref[...] = pieces[0][0, rows:].astype(F32)
        return
    at = coordinates(plan)
    vec = None
    for i, piece in enumerate(pieces):
        c, x, y = i % 2, i // 2 % 2, i // 4
        low = ((at[1] ^ y) * 2 + (at[2] ^ x)) * 2 + (at[3] ^ c)
        count = piece.shape[0] // rows
        for k in range(count):
            put((at[0] ^ k) * 8 + low, piece[k * rows : (k + 1) * rows])
        tail = piece[count * rows :].astype(F32)
        vec = tail if vec is None else vec + tail
    vec_ref[...] = vec


def storer(plan, packed_ref, kinds):
    thin, width = plan.thin, plan.width
    per = width // thin
    here = coordinates(plan)

    def put(owner, kind, block):
        c, x, y = owner % 2, owner // 2 % 2, owner // 4 % 2
        row = pl.multiple_of((kinds.index(kind) * plan.zs + owner // 8) * thin, thin)
        packed_ref[c ^ here[3], y ^ here[1], x ^ here[2], pl.ds(row, thin), :] = block

    def store(kind, part, value):
        low = value.astype(BF16)
        if kind == 3:
            for i in range(8):
                packed_ref[i % 2, i // 4, i // 2 % 2, len(kinds) * plan.zs * thin :, :] = low
            return
        blocks = low.reshape(per, thin, width)
        for i in range(per):
            owner = part * per + i if kind == 0 else i * plan.inner + part
            put(owner, kind, blocks[i])

    return store


def start_copies(packed_ref, outs, sems, start, count, before=()):
    at = pl.ds(start, count)
    copies = list(before)
    for i in range(2):
        source, target = packed_ref.at[i, :, :, at], outs[i].at[:, :, at]
        copies.append(pltpu.make_async_copy(source, target, sems.at[len(copies)]))
        copies[-1].start()
    return copies


def wait_all(copies):
    for one in copies:
        one.wait()


def prepare_kernel(plan, attn_ref, up_ref, down_ref, vec_in, keep_in, first_ref, last_ref, line_ref, vec_ref, keep_ref, sems):
    thin, tile, width = plan.thin, plan.tile, plan.width
    outs = (first_ref, last_ref)
    copies = [
        pltpu.make_async_copy(vec_in, vec_ref, sems.at[0]),
        pltpu.make_async_copy(keep_in, keep_ref, sems.at[1]),
    ]
    for kind, ref in enumerate((attn_ref, up_ref, down_ref)):
        for layer, out_ref in enumerate(outs):
            if plan.direct:
                target = out_ref.at[pl.ds(kind * thin, thin)]
                copies.append(pltpu.make_async_copy(ref.at[layer], target, sems.at[len(copies)]))
            else:
                out_ref[kind * thin : (kind + 1) * thin, :] = ref[layer]
    for one in copies:
        one.start()
    count = vec_ref.shape[1]
    device = lax.axis_index("dp") * plan.inner + lax.axis_index("mp")
    row_at = device * count // width
    offset = device * count - row_at * width
    copies[0].wait()
    copies[1].wait()
    kept = jnp.sum(keep_ref[...]) + 2 * keep_ref.shape[0]
    kept = jnp.where(counts_shared(), kept, 0)
    row = lax.broadcasted_iota(jnp.int32, (tile, width), 0)
    here = lax.broadcasted_iota(jnp.int32, (tile, width), 1) == lax.axis_index("dp")
    for layer, out_ref in enumerate(outs):
        line_ref[...] = jnp.zeros_like(line_ref)
        line_ref[0:1, 0:count] = vec_ref[layer : layer + 1, :].astype(F32)
        moved = pltpu.roll(line_ref[...], offset, 1)[0:1]
        piece = jnp.where(row == row_at, moved[:, :width], 0.0)
        piece = jnp.where(row == row_at + 1, moved[:, width:], piece)
        if layer == 1:
            piece = jnp.where(here & (row == 12), (kept >> 5).astype(F32), piece)
            piece = jnp.where(here & (row == 13), (kept & 31).astype(F32), piece)
        out_ref[3 * thin :, :] = piece.astype(BF16)
    for one in copies[2:]:
        one.wait()


def forward_kernel(plan, pieces, x_ref, bias_ref, *refs):
    sources, refs = refs[:pieces], refs[pieces:]
    attn_ref, up_ref, down_ref, vec_ref, mid_ref, out_ref, *refs = refs
    attn_keep, hidden_keep, (h_ref, acc_ref) = refs[:4], refs[4:7], refs[7:]
    place_weights(plan, sources, attn_ref, up_ref, down_ref, vec_ref)
    forward_attention(x_ref, bias_ref, vec_ref, attn_ref, attn_keep, mid_ref)
    forward_hidden(mid_ref, vec_ref, up_ref, down_ref, hidden_keep, (h_ref, acc_ref), out_ref)
    drop_shared((attn_keep[0], attn_keep[3], hidden_keep[0], hidden_keep[1]))


HIDDEN_KINDS, ATTENTION_KINDS, ALL_KINDS = (1, 2), (0,), (1, 2, 0)


def last_hidden_kernel(plan, goal_ref, mid_ref, vec_ref, up_ref, down_ref, *refs):
    keep, gm_ref, gvec_ref, outs, refs = refs[:3], refs[3], refs[4], refs[5:7], refs[7:]
    g_ref, go_ref, gh_ref, acc_ref, h_ref, got_ref, n2t_ref, packed_ref, sems = refs
    high = jnp.sum(vec_ref[12:13, :], axis=-1, keepdims=True)
    rest = jnp.sum(vec_ref[13:14, :], axis=-1, keepdims=True)
    loss_scale = float(plan.slots) / (high * 32.0 + rest)
    g_ref[...] = goal_ref[...].astype(F32) * loss_scale
    gvec_ref[...] = jnp.zeros_like(gvec_ref)
    share = counts_shared().astype(F32)
    store = storer(plan, packed_ref, HIDDEN_KINDS)
    scratch = (go_ref, gh_ref, acc_ref, h_ref, got_ref, n2t_ref)
    backward_hidden(g_ref, mid_ref, vec_ref, up_ref, down_ref, share, keep, scratch, gm_ref, gvec_ref, store)
    wait_all(start_copies(packed_ref, outs, sems, 0, packed_ref.shape[3]))


def last_attention_kernel(plan, gm_ref, x_ref, vec_ref, attn_ref, early_ref, *refs):
    keep, gx_ref, outs, refs = refs[:4], refs[4], refs[5:7], refs[7:]
    gvec_ref, go_ref, acc_ref, ga_ref, dproj_ref, packed_ref, sems = refs
    gvec_ref[...] = early_ref[...]
    share = counts_shared().astype(F32)
    store = storer(plan, packed_ref, ATTENTION_KINDS)
    scratch = (go_ref, acc_ref, ga_ref, dproj_ref)
    backward_attention(gm_ref, x_ref, vec_ref, attn_ref, share, keep, scratch, gx_ref, gvec_ref, store)
    wait_all(start_copies(packed_ref, outs, sems, 0, packed_ref.shape[3]))


def back_kernel(plan, g_ref, x_ref, mid_ref, vec_ref, attn_ref, up_ref, down_ref, *refs):
    attn_keep, hidden_keep, gx_ref, outs, refs = refs[:4], refs[4:7], refs[7], refs[8:10], refs[10:]
    gm_ref, gvec_ref, go_ref, gh_ref, ga_ref, acc_ref, h_ref, got_ref, n2t_ref, dproj_ref, packed_ref, sems = refs
    gvec_ref[...] = jnp.zeros_like(gvec_ref)
    share = counts_shared().astype(F32)
    store = storer(plan, packed_ref, ALL_KINDS)
    scratch = (go_ref, gh_ref, acc_ref, h_ref, got_ref, n2t_ref)
    backward_hidden(g_ref, mid_ref, vec_ref, up_ref, down_ref, share, hidden_keep, scratch, gm_ref, gvec_ref, store)
    hidden_rows = 2 * plan.zs * plan.thin
    copies = start_copies(packed_ref, outs, sems, 0, hidden_rows)
    scratch = (go_ref, acc_ref, ga_ref, dproj_ref)
    backward_attention(gm_ref, x_ref, vec_ref, attn_ref, share, attn_keep, scratch, gx_ref, gvec_ref, store)
    rest = packed_ref.shape[3] - hidden_rows
    wait_all(start_copies(packed_ref, outs, sems, hidden_rows, rest, copies))


def add_kernel(kept_hidden, got_hidden, kept_attn, got_attn, *out_refs):
    count = kept_hidden.shape[2]
    for i, out_ref in enumerate(out_refs):
        at = (i // 2, i % 2)
        total = kept_hidden[at].astype(F32) + got_hidden[at].astype(F32)
        out_ref[0:count, :] = total.astype(BF16)
        total = kept_attn[at].astype(F32) + got_attn[at].astype(F32)
        out_ref[count:, :] = total.astype(BF16)


def finish_kernel(plan, count_of, *refs):
    layers = (refs[:count_of], refs[count_of : 2 * count_of])
    attn_out, vec_out, up_out, down_out, *tiles = refs[2 * count_of :]
    thin, tile, width = plan.thin, plan.tile, plan.width

    count = vec_out.shape[1]
    device = lax.axis_index("dp") * plan.inner + lax.axis_index("mp")
    row = device * count // width
    offset = device * count - row * width
    for layer in range(2):

        def total(start, count, layer=layer):
            return sum(ref[start : start + count, :].astype(F32) for ref in layers[layer])

        attn_out[layer] = total(0, thin)
        up_out[layer] = total(thin, thin)
        down_out[layer] = total(2 * thin, thin)
        tiles[layer][...] = total(3 * thin, tile)
        both = jnp.concatenate(
            [tiles[layer][pl.ds(row, 1), :], tiles[layer][pl.ds(row + 1, 1), :]], axis=1
        )
        both = jnp.broadcast_to(both, (8, 2 * width))
        moved = pltpu.roll(both, 2 * width - offset, 1)
        vec_out[layer : layer + 1, :] = moved[0:1, :count]


def place_kernel(own_ref, *refs):
    others, out_ref = refs[:-1], refs[-1]
    rows = own_ref.shape[0] // 2
    kept = out_ref.shape[1]
    mine = lax.axis_index("mp")
    out_ref[mine] = own_ref[0:rows, :].astype(F32)[:kept]
    for i, ref in enumerate(others):
        out_ref[mine ^ (i + 1)] = ref[...].astype(F32)[:kept]
    out_ref[out_ref.shape[0] - 1] = own_ref[rows : 2 * rows, :].astype(F32)[:kept]


def pack_kernel(slot_ref, own_ref, *refs):
    others, out_ref = refs[:-1], refs[-1]
    rows = own_ref.shape[0] // 2
    sources = [own_ref[0:rows, :]] + [ref[...] for ref in others] + [own_ref[rows : 2 * rows, :]]
    step = 256

    def body(index, carry):
        slots = lax.broadcasted_iota(jnp.int32, (step, rows), 0) + index * step
        total = None
        for i, values in enumerate(sources):
            picks = jnp.where(slots == slot_ref[i], 1.0, 0.0).astype(BF16)
            term = dot_nn(picks, values)
            total = term if total is None else total + term
        out_ref[block_rows(index, step), :] = total
        return carry

    lax.fori_loop(0, out_ref.shape[0] // step, body, 0)


VMEM = pl.BlockSpec(memory_space=pltpu.VMEM)
ANY = pl.BlockSpec(memory_space=pl.ANY)


def call(kernel, operands, specs, outs, out_specs, scratch, flops, limit=26):
    return pl.pallas_call(
        kernel,
        out_shape=[jax.ShapeDtypeStruct(shape, dtype) for shape, dtype in outs],
        in_specs=specs,
        out_specs=out_specs,
        scratch_shapes=scratch,
        compiler_params=pltpu.CompilerParams(vmem_limit_bytes=limit << 20),
        cost_estimate=pl.CostEstimate(flops=flops, bytes_accessed=8 << 20, transcendentals=0),
    )(*operands)


@dataclasses.dataclass(frozen=True)
class Plan:
    outer: int
    inner: int
    thin: int
    tile: int
    width: int
    slots: int
    direct: bool

    @property
    def zs(self):
        return self.outer // 2 if self.direct else 1


def flip(array, mask, devices):
    return lax.ppermute(array, ("dp", "mp"), [(d, d ^ mask) for d in range(devices)])


def column_kernel(plan, *refs):
    blocks, out_ref = refs[:-1], refs[-1]
    rows = 3 * plan.thin
    for k, ref in enumerate(blocks):
        out_ref[k * rows : (k + 1) * rows, :] = ref[0:rows, :]
    tail = sum(ref[rows:, :].astype(F32) for ref in blocks)
    out_ref[len(blocks) * rows :, :] = tail.astype(BF16)


def gather_column(plan, block, devices):
    blocks = [block] + [flip(block, 8 * k, devices) for k in range(1, devices // 8)]
    shape = (len(blocks) * 3 * plan.thin + plan.tile, plan.width)
    (column,) = call(
        functools.partial(column_kernel, plan), blocks, [VMEM] * len(blocks), [(shape, BF16)], [VMEM], [], 1 << 20
    )
    return column


def gather_plane(column, devices):
    return [column] + [flip(column, mask, devices) for mask in (2, 4, 6)]


def gather_cores(plane, devices):
    pieces = []
    for piece in plane:
        pieces += [piece, flip(piece, 1, devices)]
    return pieces


def spread(rows, devices):
    across = flip(rows, 2, devices)
    return [flip(rows, 1, devices), across, flip(across, 1, devices)]


def sum_cores(kept, sent, devices):
    got = flip(sent, 1, devices)
    return [(kept[i // 2, i % 2].astype(F32) + got[i // 2, i % 2].astype(F32)).astype(BF16) for i in range(4)]


def plane_kernel(plan, *refs):
    terms, out_refs = refs[:4], refs[4:]
    thin, tile = plan.thin, plan.tile
    zs = len(out_refs)

    def added(start, count):
        return sum(ref[pl.ds(start, count), :].astype(F32) for ref in terms).astype(BF16)

    tail = added(3 * zs * thin, tile)
    for z, out_ref in enumerate(out_refs):
        for kind in range(3):
            row = (ALL_KINDS.index(kind) * zs + (coordinates(plan)[0] ^ z)) * thin
            out_ref[kind * thin : (kind + 1) * thin, :] = added(pl.multiple_of(row, thin), thin)
        out_ref[3 * thin :, :] = tail


def sum_plane(plan, sums, devices):
    zs = devices // 8
    terms = [sums[0]] + [flip(one, mask, devices) for one, mask in zip(sums[1:], (2, 4, 6))]
    outs = [((3 * plan.thin + plan.tile, plan.width), BF16)] * zs
    return call(
        functools.partial(plane_kernel, plan), terms, [VMEM] * 4, outs, [VMEM] * zs, [], 1 << 20
    )


def sum_column(blocks, devices):
    return [one if k == 0 else flip(one, 8 * k, devices) for k, one in enumerate(blocks)]


def shards(patches, targets, keep_mask, attn_weights, vectors, up_weights, down_weights):
    image_count, patch_rows, width = patches.shape
    layers = attn_weights.shape[0]
    dp_size, mp_size = lax.axis_size("dp"), lax.axis_size("mp")
    devices = dp_size * mp_size
    rank = lax.axis_index("mp")
    lane_rank = lax.axis_index("dp")
    device = lane_rank * mp_size + rank
    thin = attn_weights.shape[2]
    vec_rows = vectors.shape[1]
    parts = thin * devices // width
    assert image_count == mp_size + 1 and layers == 2 and parts == mp_size == 4
    direct = thin % 16 == 0
    images, tile = 2, 16
    rows = -(-patch_rows // 16) * 16
    total = images * rows

    keep_rows = jnp.concatenate([jnp.ones((image_count, 2), jnp.int32), keep_mask], axis=1)
    keep_rows = jnp.pad(keep_rows, ((0, 0), (0, rows - patch_rows)))

    attn_turned = attn_weights.transpose(0, 2, 1)
    down_turned = down_weights.transpose(0, 2, 1)
    packing = Plan(dp_size, mp_size, thin, tile, width, SLOTS * dp_size, direct)
    block_shape = ((3 * thin + tile, width), BF16)
    first_block, last_block = call(
        functools.partial(prepare_kernel, packing),
        (attn_turned, up_weights, down_turned, vectors, keep_mask),
        [ANY if direct else VMEM] * 3 + [ANY] * 2,
        [block_shape, block_shape],
        [VMEM, VMEM],
        [
            pltpu.VMEM((8, 2 * width), F32),
            pltpu.VMEM(vectors.shape, BF16),
            pltpu.VMEM(keep_mask.shape, jnp.int32),
            pltpu.SemaphoreType.DMA((8,)),
        ],
        1 << 20,
        60,
    )
    if direct:
        plan = packing
        first_column = gather_column(plan, first_block, devices)
        first_column, last_block = lax.optimization_barrier((first_column, last_block))
        first_plane = gather_plane(first_column, devices)
        last_column = gather_column(plan, last_block, devices)
        first_plane, last_column = lax.optimization_barrier((first_plane, last_column))
        first_pieces = gather_cores(first_plane, devices)
        last_plane = gather_plane(last_column, devices)
    else:
        plan = Plan(1, parts, width, tile, width, SLOTS * dp_size, False)

        def squares(array):
            return array.reshape(parts, width, width)

        def by_part(array):
            split = array.reshape(dp_size, mp_size, thin, width).transpose(1, 0, 2, 3)
            return squares(split)

        def one_tile(array):
            summed = jnp.sum(array.astype(F32), axis=0).astype(BF16)
            return jnp.pad(summed[None], ((0, parts - 1), (0, 0), (0, 0)))

        def normal(block):
            every = lax.all_gather(block, ("dp", "mp"))
            return jnp.concatenate(
                [
                    squares(every[:, :thin]),
                    by_part(every[:, thin : 2 * thin]),
                    by_part(every[:, 2 * thin : 3 * thin]),
                    one_tile(every[:, 3 * thin :]),
                ],
                axis=1,
            )

        first_pieces, last_pieces = [normal(first_block)], [normal(last_block)]

    flat = keep_rows.reshape(-1)
    slot = jnp.where(flat == 1, jnp.cumsum(flat) - flat, SLOTS).reshape(image_count, 1, rows)

    def mine(array):
        return jnp.concatenate(
            [lax.dynamic_slice_in_dim(array, rank, 1, 0), array[mp_size:]], axis=0
        )

    def padded(array):
        return jnp.pad(mine(array), ((0, 0), (0, rows - patch_rows), (0, 0)))

    kept = mine(keep_rows)
    stream = padded(patches).reshape(total, width)
    bias = jnp.where(kept == 1, 0.0, MASKED).astype(F32)[:, None, :]
    goal = jnp.where((kept == 1)[:, :, None], padded(targets), 0).reshape(total, width)
    slots = jnp.concatenate(
        [lax.dynamic_slice_in_dim(slot, rank ^ k, 1, 0) for k in range(mp_size)] + [slot[mp_size:]],
        axis=0,
    )

    stream, slots, goal = lax.optimization_barrier((stream, slots, goal))

    pairs = width // (2 * HD)
    stream_shape = ((total, width), F32)
    low_shape = ((total, width), BF16)
    pair_shape, low_pair_shape = ((2, total, width), F32), ((2, total, width), BF16)
    three_shape = ((3, total, width), BF16)
    turned_shape = ((width, total), BF16)
    vec_shape = ((tile, width), F32)
    attn_keep = [low_shape, three_shape, ((images, pairs, 2 * rows, rows), BF16), low_shape]
    hidden_keep = [low_shape, ((parts, total, width), BF16), ((parts, total, width), F32)]
    blocks = plan.outer * plan.inner
    weight_shape = ((blocks, plan.thin, width), BF16)
    zs = max(blocks // 8, 1)

    def vmem(shapes):
        return [pltpu.VMEM(shape, dtype) for shape, dtype in shapes]

    layer_flops = 8 * total * parts * width * width
    hidden_rows, attn_rows = 2 * plan.thin * zs, plan.thin * zs + tile

    def half(count):
        return ((2, 2, count, width), BF16)

    def both(count):
        return ((2, 2, 2, count, width), BF16)


    def forward(rows_in, pieces, out_shape):
        results = call(
            functools.partial(forward_kernel, plan, len(pieces)),
            (rows_in, bias, *pieces),
            [VMEM] * (2 + len(pieces)),
            [weight_shape, weight_shape, weight_shape, vec_shape, stream_shape, out_shape]
            + attn_keep
            + hidden_keep,
            [VMEM] * 13,
            vmem([pair_shape, stream_shape]),
            layer_flops,
        )
        return (*results[:6], results[6:10], results[10:])

    attn_full, up_full, down_full, vec, mid, middle, attn_kept, hidden_kept = forward(
        stream, first_pieces, stream_shape
    )
    if direct:
        middle, last_plane = lax.optimization_barrier((middle, last_plane))
        last_pieces = gather_cores(last_plane, devices)
    sems = [pltpu.SemaphoreType.DMA((4,))]
    last_attn, last_up, last_down, last_vec, last_mid, output, last_kept, last_hidden_kept = forward(
        middle, last_pieces, low_shape
    )
    last_mid_grad, last_gvec, *last_hidden = call(
        functools.partial(last_hidden_kernel, plan),
        (goal, last_mid, last_vec, last_up, last_down, *last_hidden_kept),
        [VMEM] * 8,
        [stream_shape, vec_shape, half(hidden_rows), half(hidden_rows)],
        [VMEM] * 2 + [ANY] * 2,
        vmem(
            [stream_shape, low_shape, low_pair_shape, stream_shape, pair_shape]
            + [turned_shape, turned_shape, both(hidden_rows)]
        )
        + sems,
        layer_flops,
    )
    across = flip(output[:rows], 2, devices)
    last_mid_grad, last_gvec, last_hidden, across, output = lax.optimization_barrier(
        (last_mid_grad, last_gvec, last_hidden, across, output)
    )
    grad_middle, *last_attention = call(
        functools.partial(last_attention_kernel, plan),
        (last_mid_grad, middle, last_vec, last_attn, last_gvec, *last_kept),
        [VMEM] * 9,
        [stream_shape, half(attn_rows), half(attn_rows)],
        [VMEM, ANY, ANY],
        vmem([vec_shape, low_shape, stream_shape, low_shape, three_shape, both(attn_rows)]) + sems,
        layer_flops,
    )
    output_pieces = [flip(output[:rows], 1, devices), across, flip(across, 1, devices)]
    if direct:
        terms = []
        for kept_half, sent_half in (last_hidden, last_attention):
            terms += [kept_half, flip(sent_half, 1, devices)]
        message = ((hidden_rows + attn_rows, width), BF16)
        last_sums = call(add_kernel, terms, [VMEM] * 4, [message] * 4, [VMEM] * 4, [], 1 << 20)
        grad_middle, last_sums, output_pieces = lax.optimization_barrier(
            (grad_middle, last_sums, output_pieces)
        )
    grad_first, *first_halves = call(
        functools.partial(back_kernel, plan),
        (grad_middle, stream, mid, vec, attn_full, up_full, down_full, *attn_kept, *hidden_kept),
        [VMEM] * 14,
        [low_shape, half(hidden_rows + attn_rows), half(hidden_rows + attn_rows)],
        [VMEM, ANY, ANY],
        vmem(
            [stream_shape, vec_shape, low_shape, low_pair_shape, low_shape, stream_shape, pair_shape]
            + [turned_shape, turned_shape, three_shape, both(hidden_rows + attn_rows)]
        )
        + sems,
        3 * layer_flops,
    )

    def pack_output(output, output_pieces):
        (activations,) = call(
            pack_kernel,
            (slots, output, *output_pieces),
            [VMEM] * (mp_size + 1),
            [((SLOTS, width), F32)],
            [VMEM],
            [],
            2 * SLOTS * image_count * rows * width,
        )
        return activations

    def place_grads(grad_first, grad_pieces):
        (input_grads,) = call(
            place_kernel,
            (grad_first, *grad_pieces),
            [VMEM] * mp_size,
            [((image_count, patch_rows, width), F32)],
            [VMEM],
            [],
            image_count * patch_rows * width,
        )
        return input_grads

    if direct:
        last_total = sum_plane(plan, last_sums, devices)
        activations = pack_output(output, output_pieces)
        last_total, first_halves, grad_first, activations = lax.optimization_barrier(
            (last_total, first_halves, grad_first, activations)
        )
        across = flip(grad_first[:rows], 2, devices)
        first_sums = sum_cores(*first_halves, devices)
        first_sums, last_total, across, grad_first = lax.optimization_barrier(
            (first_sums, last_total, across, grad_first)
        )
        first_total = sum_plane(plan, first_sums, devices)
        last_terms = sum_column(last_total, devices)
        beside = flip(grad_first[:rows], 1, devices)
        input_grads = place_grads(grad_first, [beside, across, flip(across, 1, devices)])
        first_total, last_terms, input_grads = lax.optimization_barrier(
            (first_total, last_terms, input_grads)
        )
        first_terms = sum_column(first_total, devices)
        terms = (*first_terms, *last_terms)
        turned = (layers, thin, width)
        attn_grads, vector_grads, up_grads, down_grads = call(
            functools.partial(finish_kernel, plan, len(first_terms)),
            terms,
            [VMEM] * len(terms),
            [(turned, F32), (vectors.shape, F32), (turned, F32), (turned, F32)],
            [VMEM] * 4,
            vmem([vec_shape, vec_shape]),
            1 << 20,
        )
        attn_grads, down_grads = attn_grads.transpose(0, 2, 1), down_grads.transpose(0, 2, 1)
    else:
        last_halves = [
            jnp.concatenate(halves, axis=2) for halves in zip(last_hidden, last_attention)
        ]

        def square_blocks(halves):
            stacked = jnp.stack(halves)[:, 0]
            stacked = jnp.stack([stacked[k % 2, k // 2] for k in range(parts)])
            return jnp.stack(
                [lax.dynamic_index_in_dim(stacked, rank ^ k, 0, False) for k in range(parts)]
            )

        def outputs_of(halves):
            def by_owner(array):
                split = array.reshape(mp_size, dp_size, thin, width).transpose(1, 0, 2, 3)
                return split.reshape(devices, thin, width)

            every = square_blocks(halves)
            pieces = [
                every[:, 2 * width : 3 * width].reshape(devices, thin, width),
                by_owner(every[:, :width]),
                by_owner(every[:, width : 2 * width]),
                jnp.broadcast_to(every[0, 3 * width :], (devices, tile, width)),
            ]
            owned = lax.psum_scatter(
                jnp.concatenate(pieces, axis=1), ("dp", "mp"), scatter_dimension=0, tiled=False
            ).astype(F32)
            own_vec = lax.dynamic_slice_in_dim(
                owned[3 * thin :].reshape(-1), device * vec_rows, vec_rows
            )
            return owned[:thin].T, own_vec, owned[thin : 2 * thin], owned[2 * thin : 3 * thin].T

        attn_grads, vector_grads, up_grads, down_grads = (
            jnp.stack([one, two]) for one, two in zip(outputs_of(first_halves), outputs_of(last_halves))
        )
        activations = pack_output(output, output_pieces)
        input_grads = place_grads(grad_first, spread(grad_first[:rows], devices))

    return (activations, input_grads, attn_grads, vector_grads, up_grads, down_grads)


def solution(mesh):
    in_specs = (
        P("dp", None, None),
        P("dp", None, None),
        P("dp", None),
        P(None, None, ("dp", "mp")),
        P(None, ("dp", "mp")),
        P(None, "dp", "mp"),
        P(None, "mp", "dp"),
    )
    out_specs = (
        P("dp", None),
        P("dp", None, None),
        P(None, None, ("dp", "mp")),
        P(None, ("dp", "mp")),
        P(None, "dp", "mp"),
        P(None, "mp", "dp"),
    )
    return jax.shard_map(shards, mesh=mesh, in_specs=in_specs, out_specs=out_specs, check_vma=False)
```

```python
import dataclasses
import functools

import jax
import jax.numpy as jnp
from jax import lax
from jax.experimental import pallas as pl
from jax.experimental.pallas import tpu as pltpu
from jax.sharding import PartitionSpec as P

HD = 64
SLOTS = 1024
EPSILON = 1e-06
MASKED = -1e30
STEP = 16

F32 = jnp.float32
BF16 = jnp.bfloat16


def dot_nn(left, right):
    return lax.dot_general(left, right, (((1,), (0,)), ((), ())), preferred_element_type=F32)


def dot_nt(left, right):
    return lax.dot_general(left, right, (((1,), (1,)), ((), ())), preferred_element_type=F32)


def dot_tn(left, right):
    return lax.dot_general(left, right, (((0,), (0,)), ((), ())), preferred_element_type=F32)


def block_rows(index, step):
    return pl.ds(pl.multiple_of(index * step, step), step)


def fold_rows(values):
    return jnp.sum(values.reshape(values.shape[0] // 8, 8, values.shape[1]), axis=0)


def low_halves(rows):
    lane = lax.broadcasted_iota(jnp.int32, (rows, 2 * HD), 1)
    return lane < HD


def stack_heads(pair):
    low = low_halves(pair.shape[0])
    zero = jnp.zeros_like(pair)
    return jnp.concatenate([jnp.where(low, pair, zero), jnp.where(low, zero, pair)], axis=0)


def unstack_heads(stacked):
    rows = stacked.shape[0] // 2
    return jnp.where(low_halves(rows), stacked[:rows], stacked[rows:])


def norm_rows(x_ref, out_ref, gain, shift):
    def body(index, carry):
        at = block_rows(index, STEP)
        values = x_ref[at, :].astype(F32)
        centred = values - jnp.mean(values, axis=-1, keepdims=True)
        variance = jnp.mean(centred * centred, axis=-1, keepdims=True)
        out_ref[at, :] = (centred * lax.rsqrt(variance + EPSILON) * gain + shift).astype(BF16)
        return carry

    lax.fori_loop(0, x_ref.shape[0] // STEP, body, 0, unroll=True)


def norm_back(x_ref, grad_ref, base_ref, out_ref, low_ref, gain, images):
    rows = x_ref.shape[0] // images
    width = x_ref.shape[1]
    sums = []
    for image in range(images):

        def body(index, carry, image=image):
            at = pl.ds(pl.multiple_of(image * rows + index * STEP, STEP), STEP)
            values = x_ref[at, :].astype(F32)
            grad = grad_ref[at, :]
            centred = values - jnp.mean(values, axis=-1, keepdims=True)
            variance = jnp.mean(centred * centred, axis=-1, keepdims=True)
            inverse = lax.rsqrt(variance + EPSILON)
            unit = centred * inverse
            scaled = grad * gain
            mean_one = jnp.mean(scaled, axis=-1, keepdims=True)
            mean_two = jnp.mean(scaled * unit, axis=-1, keepdims=True)
            out = base_ref[at, :] + inverse * (scaled - mean_one - unit * mean_two)
            out_ref[at, :] = out.astype(out_ref.dtype)
            if low_ref is not None:
                low_ref[at, :] = out.astype(BF16)
            return (
                carry[0] + fold_rows(grad * unit),
                carry[1] + fold_rows(grad),
                carry[2] + fold_rows(out),
            )

        zero = jnp.zeros((8, width), F32)
        sums.append(lax.fori_loop(0, rows // STEP, body, (zero, zero, zero), unroll=True))
    return sums


def weigh(sums, share):
    total = sums[0]
    for more in sums[1:]:
        total = total + more * share
    return jnp.sum(total, axis=0, keepdims=True)


def as_square(ref, part):
    rows, width = ref.shape[1:]
    per = width // rows
    return ref[pl.ds(part * per, per)].reshape(width, width)


def forward_attention(x_ref, bias_ref, vec_ref, attn_ref, keep, mid_ref):
    n1_ref, proj_ref, p_ref, att_ref = keep
    images = bias_ref.shape[0]
    rows = x_ref.shape[0] // images
    width = x_ref.shape[1]
    pairs = width // (2 * HD)
    scale = HD**-0.5

    norm_rows(x_ref, n1_ref, vec_ref[0:1, :], vec_ref[1:2, :])
    for part, bias_row in enumerate((4, None, 5)):
        value = dot_nt(n1_ref[...], as_square(attn_ref, part))
        if bias_row is not None:
            value = value + vec_ref[bias_row : bias_row + 1, :]
        proj_ref[part] = value.astype(BF16)

    def image_body(image, carry):
        at = block_rows(image, rows)
        for pair in range(pairs):
            lanes = slice(pair * 2 * HD, (pair + 1) * 2 * HD)
            query = stack_heads(proj_ref[0, at, lanes])
            scores = dot_nt(query, proj_ref[1, at, lanes]) * scale + bias_ref[image]
            top = jnp.max(scores, axis=-1, keepdims=True)
            powers = jnp.exp(scores - top)
            total = jnp.sum(powers, axis=-1, keepdims=True)
            probs = (powers * (1.0 / total)).astype(BF16)
            p_ref[image, pair] = probs
            att_ref[at, lanes] = unstack_heads(dot_nn(probs, proj_ref[2, at, lanes])).astype(BF16)
        return carry

    for image in range(images):
        image_body(image, 0)
    mid_ref[...] = x_ref[...].astype(F32) + dot_nt(att_ref[...], as_square(attn_ref, 3)) + vec_ref[6:7, :]


def forward_hidden(mid_ref, vec_ref, up_ref, down_ref, keep, scratch, out_ref):
    n2_ref, a_ref, gp_ref = keep
    h_ref, acc_ref = scratch
    norm_rows(mid_ref, n2_ref, vec_ref[2:3, :], vec_ref[3:4, :])
    acc_ref[...] = mid_ref[...] + vec_ref[11:12, :]

    def part_body(part, carry):
        h_ref[part % 2] = dot_nn(n2_ref[...], as_square(up_ref, part))
        bias = vec_ref[pl.ds(7 + part, 1), :]

        def gelu_body(index, inner):
            at = block_rows(index, STEP)
            hidden = h_ref[part % 2, at, :] + bias
            share = 0.5 + 0.5 * lax.erf(hidden * 0.7071067811865476)
            a_ref[part, at, :] = (hidden * share).astype(BF16)
            bell = jnp.exp(-0.5 * hidden * hidden) * 0.3989422804014327
            gp_ref[part, at, :] = (share + hidden * bell).astype(gp_ref.dtype)
            return inner

        lax.fori_loop(0, h_ref.shape[1] // STEP, gelu_body, 0, unroll=True)
        acc_ref[...] += dot_nt(a_ref[part], as_square(down_ref, part))
        return carry

    for part in range(a_ref.shape[0]):
        part_body(part, 0)
    out_ref[...] = acc_ref[...].astype(out_ref.dtype)


def drop_shared(refs):
    @pl.when(jnp.logical_not(counts_shared()))
    def _():
        for ref in refs:
            rows = ref.shape[-2] // 2
            ref[..., rows:, :] = jnp.zeros((*ref.shape[:-2], rows, ref.shape[-1]), ref.dtype)


def backward_hidden(g_ref, mid_ref, vec_ref, up_ref, down_ref, share, keep, scratch, gm_ref, gvec_ref, store):
    n2_ref, a_ref, gp_ref = keep
    go_ref, gh_ref, acc_ref, h_ref, got_ref, n2t_ref = scratch
    images = 2
    rows = mid_ref.shape[0] // images
    width = mid_ref.shape[1]
    zero = jnp.zeros((8, width), F32)
    sums = []
    for image in range(images):

        def low_body(index, carry, image=image):
            at = pl.ds(pl.multiple_of(image * rows + index * STEP, STEP), STEP)
            grad = g_ref[at, :]
            go_ref[at, :] = grad.astype(BF16)
            return carry + fold_rows(grad)

        sums.append(lax.fori_loop(0, rows // STEP, low_body, zero, unroll=True))
    gvec_ref[11:12, :] = weigh(sums, share)
    acc_ref[...] = jnp.zeros_like(acc_ref)
    got_ref[...] = go_ref[...].T
    n2t_ref[...] = n2_ref[...].T

    def part_body(part, carry):
        store(2, part, dot_nn(got_ref[...], a_ref[part]))
        h_ref[part % 2] = dot_nn(go_ref[...], as_square(down_ref, part))
        inner_sums = []
        for image in range(images):

            def hidden_body(index, inner, image=image):
                at = pl.ds(pl.multiple_of(image * rows + index * STEP, STEP), STEP)
                grad = (h_ref[part % 2, at, :] * gp_ref[part, at, :].astype(F32)).astype(BF16)
                gh_ref[part % 2, at, :] = grad
                return inner + fold_rows(grad.astype(F32))

            inner_sums.append(lax.fori_loop(0, rows // STEP, hidden_body, zero, unroll=True))
        gvec_ref[pl.ds(7 + part, 1), :] = weigh(inner_sums, share)
        store(1, part, dot_nn(n2t_ref[...], gh_ref[part % 2]))
        acc_ref[...] += dot_nt(gh_ref[part % 2], as_square(up_ref, part))
        return carry

    for part in range(a_ref.shape[0]):
        part_body(part, 0)
    sums = norm_back(mid_ref, acc_ref, g_ref, gm_ref, None, vec_ref[2:3, :], images)
    for place, row in enumerate((2, 3, 6)):
        gvec_ref[row : row + 1, :] = weigh([one[place] for one in sums], share)


def backward_attention(gm_ref, x_ref, vec_ref, attn_ref, share, keep, scratch, gx_ref, gvec_ref, store):
    n1_ref, proj_ref, p_ref, att_ref = keep
    go_ref, acc_ref, ga_ref, dproj_ref = scratch
    images = p_ref.shape[0]
    rows = x_ref.shape[0] // images
    width = x_ref.shape[1]
    pairs = width // (2 * HD)
    scale = HD**-0.5
    go_ref[...] = gm_ref[...].astype(BF16)
    store(0, 3, dot_tn(go_ref[...], att_ref[...]))
    ga_ref[...] = dot_nn(go_ref[...], as_square(attn_ref, 3)).astype(BF16)

    def image_body(image, carry):
        at = block_rows(image, rows)
        for pair in range(pairs):
            lanes = slice(pair * 2 * HD, (pair + 1) * 2 * HD)
            query = stack_heads(proj_ref[0, at, lanes])
            keys = proj_ref[1, at, lanes]
            grad_out = stack_heads(ga_ref[at, lanes])
            probs = p_ref[image, pair]
            grad_probs = dot_nt(grad_out, proj_ref[2, at, lanes])
            dproj_ref[2, at, lanes] = dot_tn(probs, grad_out).astype(BF16)
            wide = probs.astype(F32)
            inner = jnp.sum(grad_probs * wide, axis=-1, keepdims=True)
            grad_scores = (wide * (grad_probs - inner)).astype(BF16)
            dproj_ref[0, at, lanes] = (unstack_heads(dot_nn(grad_scores, keys)) * scale).astype(BF16)
            dproj_ref[1, at, lanes] = (dot_tn(grad_scores, query) * scale).astype(BF16)
        return carry

    for image in range(images):
        image_body(image, 0)
    for part, row in enumerate((4, None, 5)):
        store(0, part, dot_tn(dproj_ref[part], n1_ref[...]))
        value = dot_nn(dproj_ref[part], as_square(attn_ref, part))
        if part == 0:
            acc_ref[...] = value
        else:
            acc_ref[...] += value
        if row is not None:
            sums = [
                fold_rows(dproj_ref[part, image * rows : (image + 1) * rows, :].astype(F32))
                for image in range(images)
            ]
            gvec_ref[row : row + 1, :] = weigh(sums, share)
    sums = norm_back(x_ref, acc_ref, gm_ref, gx_ref, None, vec_ref[0:1, :], images)
    for place, row in enumerate((0, 1)):
        gvec_ref[row : row + 1, :] = weigh([one[place] for one in sums], share)
    store(3, 0, gvec_ref[...])


def coordinates(plan):
    outer, inner = lax.axis_index("dp"), lax.axis_index("mp")
    here = (inner // 2, inner % 2)
    return (outer // 2, outer % 2, *here) if plan.direct else (0, 0, *here)


def counts_shared():
    return lax.axis_index("mp") == 0


def place_weights(plan, pieces, attn_ref, up_ref, down_ref, vec_ref):
    thin, rows = plan.thin, 3 * plan.thin

    def put(owner, block):
        at = owner % plan.inner * plan.outer + owner // plan.inner
        attn_ref[owner] = block[:thin]
        up_ref[at] = block[thin : 2 * thin]
        down_ref[at] = block[2 * thin : 3 * thin]

    if not plan.direct:
        for owner in range(plan.inner):
            put(owner, pieces[0][owner, :rows])
        vec_ref[...] = pieces[0][0, rows:].astype(F32)
        return
    at = coordinates(plan)
    vec = None
    half = plan.zs // 2
    for i, piece in enumerate(pieces):
        c, x, y = i // 2 % 2, i // 4 % 2, i // 8
        low = ((at[1] ^ y) * 2 + (at[2] ^ x)) * 2 + (at[3] ^ c)
        for k in range(half):
            put((at[0] ^ (i % 2 * half + k)) * 8 + low, piece[k * rows : (k + 1) * rows])
        if i % 2 == 1:
            tail = piece[half * rows :].astype(F32)
            vec = tail if vec is None else vec + tail
    vec_ref[...] = vec


def storer(plan, packed_ref, kinds):
    thin, width = plan.thin, plan.width
    per = width // thin
    here = coordinates(plan)

    def put(owner, kind, block):
        c, x, y = owner % 2, owner // 2 % 2, owner // 4 % 2
        row = pl.multiple_of((kinds.index(kind) * plan.zs + owner // 8) * thin, thin)
        packed_ref[c ^ here[3], y ^ here[1], x ^ here[2], pl.ds(row, thin), :] = block

    def store(kind, part, value):
        low = value.astype(BF16)
        if kind == 3:
            for i in range(8):
                packed_ref[i % 2, i // 4, i // 2 % 2, len(kinds) * plan.zs * thin :, :] = low
            return
        blocks = low.reshape(per, thin, width)
        for i in range(per):
            owner = part * per + i if kind == 0 else i * plan.inner + part
            put(owner, kind, blocks[i])

    return store


def start_copies(packed_ref, outs, sems, start, count, before=()):
    at = pl.ds(start, count)
    copies = list(before)
    for i in range(2):
        source, target = packed_ref.at[i, :, :, at], outs[i].at[:, :, at]
        copies.append(pltpu.make_async_copy(source, target, sems.at[len(copies)]))
        copies[-1].start()
    return copies


def wait_all(copies):
    for one in copies:
        one.wait()


def prepare_kernel(plan, attn_ref, up_ref, down_ref, vec_in, keep_in, first_ref, last_ref, line_ref, vec_ref, keep_ref, sems):
    thin, tile, width = plan.thin, plan.tile, plan.width
    outs = (first_ref, last_ref)
    copies = [
        pltpu.make_async_copy(vec_in, vec_ref, sems.at[0]),
        pltpu.make_async_copy(keep_in, keep_ref, sems.at[1]),
    ]
    for kind, ref in enumerate((attn_ref, up_ref, down_ref)):
        for layer, out_ref in enumerate(outs):
            if plan.direct:
                target = out_ref.at[pl.ds(kind * thin, thin)]
                copies.append(pltpu.make_async_copy(ref.at[layer], target, sems.at[len(copies)]))
            else:
                out_ref[kind * thin : (kind + 1) * thin, :] = ref[layer]
    for one in copies:
        one.start()
    count = vec_ref.shape[1]
    device = lax.axis_index("dp") * plan.inner + lax.axis_index("mp")
    row_at = device * count // width
    offset = device * count - row_at * width
    copies[0].wait()
    copies[1].wait()
    kept = jnp.sum(keep_ref[...]) + 2 * keep_ref.shape[0]
    kept = jnp.where(counts_shared(), kept, 0)
    row = lax.broadcasted_iota(jnp.int32, (tile, width), 0)
    here = lax.broadcasted_iota(jnp.int32, (tile, width), 1) == lax.axis_index("dp")
    for layer, out_ref in enumerate(outs):
        line_ref[...] = jnp.zeros_like(line_ref)
        line_ref[0:1, 0:count] = vec_ref[layer : layer + 1, :].astype(F32)
        moved = pltpu.roll(line_ref[...], offset, 1)[0:1]
        piece = jnp.where(row == row_at, moved[:, :width], 0.0)
        piece = jnp.where(row == row_at + 1, moved[:, width:], piece)
        if layer == 1:
            piece = jnp.where(here & (row == 12), (kept >> 5).astype(F32), piece)
            piece = jnp.where(here & (row == 13), (kept & 31).astype(F32), piece)
        out_ref[3 * thin :, :] = piece.astype(BF16)
    for one in copies[2:]:
        one.wait()


def forward_kernel(plan, pieces, x_ref, bias_ref, *refs):
    sources, refs = refs[:pieces], refs[pieces:]
    attn_ref, up_ref, down_ref, vec_ref, mid_ref, out_ref, *refs = refs
    attn_keep, hidden_keep, (h_ref, acc_ref) = refs[:4], refs[4:7], refs[7:]
    place_weights(plan, sources, attn_ref, up_ref, down_ref, vec_ref)
    forward_attention(x_ref, bias_ref, vec_ref, attn_ref, attn_keep, mid_ref)
    forward_hidden(mid_ref, vec_ref, up_ref, down_ref, hidden_keep, (h_ref, acc_ref), out_ref)
    drop_shared((attn_keep[0], attn_keep[3], hidden_keep[0], hidden_keep[1]))


HIDDEN_KINDS, ATTENTION_KINDS, ALL_KINDS = (1, 2), (0,), (1, 2, 0)


def last_hidden_kernel(plan, goal_ref, mid_ref, vec_ref, up_ref, down_ref, *refs):
    keep, gm_ref, gvec_ref, outs, refs = refs[:3], refs[3], refs[4], refs[5:7], refs[7:]
    g_ref, go_ref, gh_ref, acc_ref, h_ref, got_ref, n2t_ref, packed_ref, sems = refs
    high = jnp.sum(vec_ref[12:13, :], axis=-1, keepdims=True)
    rest = jnp.sum(vec_ref[13:14, :], axis=-1, keepdims=True)
    loss_scale = float(plan.slots) / (high * 32.0 + rest)
    g_ref[...] = goal_ref[...].astype(F32) * loss_scale
    gvec_ref[...] = jnp.zeros_like(gvec_ref)
    share = counts_shared().astype(F32)
    store = storer(plan, packed_ref, HIDDEN_KINDS)
    scratch = (go_ref, gh_ref, acc_ref, h_ref, got_ref, n2t_ref)
    backward_hidden(g_ref, mid_ref, vec_ref, up_ref, down_ref, share, keep, scratch, gm_ref, gvec_ref, store)
    wait_all(start_copies(packed_ref, outs, sems, 0, packed_ref.shape[3]))


def last_attention_kernel(plan, gm_ref, x_ref, vec_ref, attn_ref, early_ref, *refs):
    keep, gx_ref, outs, refs = refs[:4], refs[4], refs[5:7], refs[7:]
    gvec_ref, go_ref, acc_ref, ga_ref, dproj_ref, packed_ref, sems = refs
    gvec_ref[...] = early_ref[...]
    share = counts_shared().astype(F32)
    store = storer(plan, packed_ref, ATTENTION_KINDS)
    scratch = (go_ref, acc_ref, ga_ref, dproj_ref)
    backward_attention(gm_ref, x_ref, vec_ref, attn_ref, share, keep, scratch, gx_ref, gvec_ref, store)
    wait_all(start_copies(packed_ref, outs, sems, 0, packed_ref.shape[3]))


def back_kernel(plan, g_ref, x_ref, mid_ref, vec_ref, attn_ref, up_ref, down_ref, *refs):
    attn_keep, hidden_keep, gx_ref, outs, refs = refs[:4], refs[4:7], refs[7], refs[8:10], refs[10:]
    gm_ref, gvec_ref, go_ref, gh_ref, ga_ref, acc_ref, h_ref, got_ref, n2t_ref, dproj_ref, packed_ref, sems = refs
    gvec_ref[...] = jnp.zeros_like(gvec_ref)
    share = counts_shared().astype(F32)
    store = storer(plan, packed_ref, ALL_KINDS)
    scratch = (go_ref, gh_ref, acc_ref, h_ref, got_ref, n2t_ref)
    backward_hidden(g_ref, mid_ref, vec_ref, up_ref, down_ref, share, hidden_keep, scratch, gm_ref, gvec_ref, store)
    hidden_rows = 2 * plan.zs * plan.thin
    copies = start_copies(packed_ref, outs, sems, 0, hidden_rows)
    scratch = (go_ref, acc_ref, ga_ref, dproj_ref)
    backward_attention(gm_ref, x_ref, vec_ref, attn_ref, share, attn_keep, scratch, gx_ref, gvec_ref, store)
    rest = packed_ref.shape[3] - hidden_rows
    wait_all(start_copies(packed_ref, outs, sems, hidden_rows, rest, copies))


def add_kernel(kept_hidden, got_hidden, kept_attn, got_attn, *out_refs):
    count = kept_hidden.shape[2]
    for i, out_ref in enumerate(out_refs):
        at = (i // 2, i % 2)
        total = kept_hidden[at].astype(F32) + got_hidden[at].astype(F32)
        out_ref[0:count, :] = total.astype(BF16)
        total = kept_attn[at].astype(F32) + got_attn[at].astype(F32)
        out_ref[count:, :] = total.astype(BF16)


def finish_kernel(plan, count_of, *refs):
    layers = (refs[:count_of], refs[count_of : 2 * count_of])
    attn_out, vec_out, up_out, down_out, *tiles = refs[2 * count_of :]
    thin, tile, width = plan.thin, plan.tile, plan.width

    count = vec_out.shape[1]
    device = lax.axis_index("dp") * plan.inner + lax.axis_index("mp")
    row = device * count // width
    offset = device * count - row * width
    for layer in range(2):

        def total(start, count, layer=layer):
            return sum(ref[start : start + count, :].astype(F32) for ref in layers[layer])

        attn_out[layer] = total(0, thin)
        up_out[layer] = total(thin, thin)
        down_out[layer] = total(2 * thin, thin)
        tiles[layer][...] = total(3 * thin, tile)
        both = jnp.concatenate(
            [tiles[layer][pl.ds(row, 1), :], tiles[layer][pl.ds(row + 1, 1), :]], axis=1
        )
        both = jnp.broadcast_to(both, (8, 2 * width))
        moved = pltpu.roll(both, 2 * width - offset, 1)
        vec_out[layer : layer + 1, :] = moved[0:1, :count]


def place_kernel(own_ref, *refs):
    others, out_ref = refs[:-1], refs[-1]
    rows = own_ref.shape[0] // 2
    kept = out_ref.shape[1]
    mine = lax.axis_index("mp")
    out_ref[mine] = own_ref[0:rows, :].astype(F32)[:kept]
    for i, ref in enumerate(others):
        out_ref[mine ^ (i + 1)] = ref[...].astype(F32)[:kept]
    out_ref[out_ref.shape[0] - 1] = own_ref[rows : 2 * rows, :].astype(F32)[:kept]


def pack_kernel(slot_ref, own_ref, *refs):
    others, out_ref = refs[:-1], refs[-1]
    rows = own_ref.shape[0] // 2
    sources = [own_ref[0:rows, :]] + [ref[...] for ref in others] + [own_ref[rows : 2 * rows, :]]
    step = 256

    def body(index, carry):
        slots = lax.broadcasted_iota(jnp.int32, (step, rows), 0) + index * step
        total = None
        for i, values in enumerate(sources):
            picks = jnp.where(slots == slot_ref[i], 1.0, 0.0).astype(BF16)
            term = dot_nn(picks, values)
            total = term if total is None else total + term
        out_ref[block_rows(index, step), :] = total
        return carry

    lax.fori_loop(0, out_ref.shape[0] // step, body, 0)


VMEM = pl.BlockSpec(memory_space=pltpu.VMEM)
ANY = pl.BlockSpec(memory_space=pl.ANY)


def call(kernel, operands, specs, outs, out_specs, scratch, flops, limit=26):
    return pl.pallas_call(
        kernel,
        out_shape=[jax.ShapeDtypeStruct(shape, dtype) for shape, dtype in outs],
        in_specs=specs,
        out_specs=out_specs,
        scratch_shapes=scratch,
        compiler_params=pltpu.CompilerParams(vmem_limit_bytes=limit << 20),
        cost_estimate=pl.CostEstimate(flops=flops, bytes_accessed=8 << 20, transcendentals=0),
    )(*operands)


@dataclasses.dataclass(frozen=True)
class Plan:
    outer: int
    inner: int
    thin: int
    tile: int
    width: int
    slots: int
    direct: bool

    @property
    def zs(self):
        return self.outer // 2 if self.direct else 1


def flip(array, mask, devices):
    return lax.ppermute(array, ("dp", "mp"), [(d, d ^ mask) for d in range(devices)])


def column_kernel(plan, *refs):
    blocks, halves = refs[:-2], refs[-2:]
    rows, half = 3 * plan.thin, plan.zs // 2
    for k, ref in enumerate(blocks):
        at = k % half * rows
        halves[k // half][at : at + rows, :] = ref[0:rows, :]
    tail = sum(ref[rows:, :].astype(F32) for ref in blocks)
    halves[1][half * rows :, :] = tail.astype(BF16)


def gather_column(plan, block, devices):
    blocks = [block] + [flip(block, 8 * k, devices) for k in range(1, plan.zs)]
    rows = plan.zs // 2 * 3 * plan.thin
    outs = [((count, plan.width), BF16) for count in (rows, rows + plan.tile)]
    return call(
        functools.partial(column_kernel, plan), blocks, [VMEM] * len(blocks), outs, [VMEM] * 2, [], 1 << 20
    )


def gather_plane(column, devices):
    one, two = column
    x_one, y_two = flip(one, 2, devices), flip(two, 4, devices)
    x_two, y_one = flip(two, 2, devices), flip(one, 4, devices)
    return [one, two, x_one, x_two, y_one, y_two, flip(x_one, 4, devices), flip(y_two, 2, devices)]


def gather_cores(plane, devices):
    pieces = []
    for k in range(0, len(plane), 2):
        halves = plane[k : k + 2]
        pieces += [*halves, *(flip(half, 1, devices) for half in halves)]
    return pieces


def spread(rows, devices):
    across = flip(rows, 2, devices)
    return [flip(rows, 1, devices), across, flip(across, 1, devices)]


def sum_cores(kept, sent, devices):
    got = flip(sent, 1, devices)
    return [(kept[i // 2, i % 2].astype(F32) + got[i // 2, i % 2].astype(F32)).astype(BF16) for i in range(4)]


def plane_kernel(plan, *refs):
    terms, out_refs = refs[:4], refs[4:]
    thin, tile = plan.thin, plan.tile
    zs = len(out_refs)

    def added(start, count):
        return sum(ref[pl.ds(start, count), :].astype(F32) for ref in terms).astype(BF16)

    tail = added(3 * zs * thin, tile)
    for z, out_ref in enumerate(out_refs):
        for kind in range(3):
            row = (ALL_KINDS.index(kind) * zs + (coordinates(plan)[0] ^ z)) * thin
            out_ref[kind * thin : (kind + 1) * thin, :] = added(pl.multiple_of(row, thin), thin)
        out_ref[3 * thin :, :] = tail


def sum_plane(plan, sums, devices):
    zs = devices // 8
    terms = [sums[0]] + [flip(one, mask, devices) for one, mask in zip(sums[1:], (2, 4, 6))]
    outs = [((3 * plan.thin + plan.tile, plan.width), BF16)] * zs
    return call(
        functools.partial(plane_kernel, plan), terms, [VMEM] * 4, outs, [VMEM] * zs, [], 1 << 20
    )


def sum_column(blocks, devices):
    return [one if k == 0 else flip(one, 8 * k, devices) for k, one in enumerate(blocks)]


def shards(patches, targets, keep_mask, attn_weights, vectors, up_weights, down_weights):
    image_count, patch_rows, width = patches.shape
    layers = attn_weights.shape[0]
    dp_size, mp_size = lax.axis_size("dp"), lax.axis_size("mp")
    devices = dp_size * mp_size
    rank = lax.axis_index("mp")
    lane_rank = lax.axis_index("dp")
    device = lane_rank * mp_size + rank
    thin = attn_weights.shape[2]
    vec_rows = vectors.shape[1]
    parts = thin * devices // width
    assert image_count == mp_size + 1 and layers == 2 and parts == mp_size == 4
    direct = thin % 16 == 0 and dp_size % 4 == 0
    images, tile = 2, 16
    rows = -(-patch_rows // 16) * 16
    total = images * rows

    keep_rows = jnp.concatenate([jnp.ones((image_count, 2), jnp.int32), keep_mask], axis=1)
    keep_rows = jnp.pad(keep_rows, ((0, 0), (0, rows - patch_rows)))

    attn_turned = attn_weights.transpose(0, 2, 1)
    down_turned = down_weights.transpose(0, 2, 1)
    packing = Plan(dp_size, mp_size, thin, tile, width, SLOTS * dp_size, direct)
    block_shape = ((3 * thin + tile, width), BF16)
    first_block, last_block = call(
        functools.partial(prepare_kernel, packing),
        (attn_turned, up_weights, down_turned, vectors, keep_mask),
        [ANY if direct else VMEM] * 3 + [ANY] * 2,
        [block_shape, block_shape],
        [VMEM, VMEM],
        [
            pltpu.VMEM((8, 2 * width), F32),
            pltpu.VMEM(vectors.shape, BF16),
            pltpu.VMEM(keep_mask.shape, jnp.int32),
            pltpu.SemaphoreType.DMA((8,)),
        ],
        1 << 20,
        60,
    )
    if direct:
        plan = packing
        first_column = gather_column(plan, first_block, devices)
        first_column, last_block = lax.optimization_barrier((first_column, last_block))
        first_plane = gather_plane(first_column, devices)
        last_column = gather_column(plan, last_block, devices)
        first_plane, last_column = lax.optimization_barrier((first_plane, last_column))
        first_pieces = gather_cores(first_plane, devices)
        last_plane = gather_plane(last_column, devices)
    else:
        plan = Plan(1, parts, width, tile, width, SLOTS * dp_size, False)

        def squares(array):
            return array.reshape(parts, width, width)

        def by_part(array):
            split = array.reshape(dp_size, mp_size, thin, width).transpose(1, 0, 2, 3)
            return squares(split)

        def one_tile(array):
            summed = jnp.sum(array.astype(F32), axis=0).astype(BF16)
            return jnp.pad(summed[None], ((0, parts - 1), (0, 0), (0, 0)))

        def normal(block):
            every = lax.all_gather(block, ("dp", "mp"))
            return jnp.concatenate(
                [
                    squares(every[:, :thin]),
                    by_part(every[:, thin : 2 * thin]),
                    by_part(every[:, 2 * thin : 3 * thin]),
                    one_tile(every[:, 3 * thin :]),
                ],
                axis=1,
            )

        first_pieces, last_pieces = [normal(first_block)], [normal(last_block)]

    flat = keep_rows.reshape(-1)
    slot = jnp.where(flat == 1, jnp.cumsum(flat) - flat, SLOTS).reshape(image_count, 1, rows)

    def mine(array):
        return jnp.concatenate(
            [lax.dynamic_slice_in_dim(array, rank, 1, 0), array[mp_size:]], axis=0
        )

    def padded(array):
        return jnp.pad(mine(array), ((0, 0), (0, rows - patch_rows), (0, 0)))

    kept = mine(keep_rows)
    stream = padded(patches).reshape(total, width)
    bias = jnp.where(kept == 1, 0.0, MASKED).astype(F32)[:, None, :]
    goal = jnp.where((kept == 1)[:, :, None], padded(targets), 0).reshape(total, width)
    slots = jnp.concatenate(
        [lax.dynamic_slice_in_dim(slot, rank ^ k, 1, 0) for k in range(mp_size)] + [slot[mp_size:]],
        axis=0,
    )

    stream, slots, goal = lax.optimization_barrier((stream, slots, goal))

    pairs = width // (2 * HD)
    stream_shape = ((total, width), F32)
    low_shape = ((total, width), BF16)
    pair_shape, low_pair_shape = ((2, total, width), F32), ((2, total, width), BF16)
    three_shape = ((3, total, width), BF16)
    turned_shape = ((width, total), BF16)
    vec_shape = ((tile, width), F32)
    attn_keep = [low_shape, three_shape, ((images, pairs, 2 * rows, rows), BF16), low_shape]
    hidden_keep = [low_shape, ((parts, total, width), BF16), ((parts, total, width), F32)]
    blocks = plan.outer * plan.inner
    weight_shape = ((blocks, plan.thin, width), BF16)
    zs = max(blocks // 8, 1)

    def vmem(shapes):
        return [pltpu.VMEM(shape, dtype) for shape, dtype in shapes]

    layer_flops = 8 * total * parts * width * width
    hidden_rows, attn_rows = 2 * plan.thin * zs, plan.thin * zs + tile

    def half(count):
        return ((2, 2, count, width), BF16)

    def both(count):
        return ((2, 2, 2, count, width), BF16)


    def forward(rows_in, pieces, out_shape):
        results = call(
            functools.partial(forward_kernel, plan, len(pieces)),
            (rows_in, bias, *pieces),
            [VMEM] * (2 + len(pieces)),
            [weight_shape, weight_shape, weight_shape, vec_shape, stream_shape, out_shape]
            + attn_keep
            + hidden_keep,
            [VMEM] * 13,
            vmem([pair_shape, stream_shape]),
            layer_flops,
        )
        return (*results[:6], results[6:10], results[10:])

    attn_full, up_full, down_full, vec, mid, middle, attn_kept, hidden_kept = forward(
        stream, first_pieces, stream_shape
    )
    if direct:
        middle, last_plane = lax.optimization_barrier((middle, last_plane))
        last_pieces = gather_cores(last_plane, devices)
    sems = [pltpu.SemaphoreType.DMA((4,))]
    last_attn, last_up, last_down, last_vec, last_mid, output, last_kept, last_hidden_kept = forward(
        middle, last_pieces, low_shape
    )
    last_mid_grad, last_gvec, *last_hidden = call(
        functools.partial(last_hidden_kernel, plan),
        (goal, last_mid, last_vec, last_up, last_down, *last_hidden_kept),
        [VMEM] * 8,
        [stream_shape, vec_shape, half(hidden_rows), half(hidden_rows)],
        [VMEM] * 2 + [ANY] * 2,
        vmem(
            [stream_shape, low_shape, low_pair_shape, stream_shape, pair_shape]
            + [turned_shape, turned_shape, both(hidden_rows)]
        )
        + sems,
        layer_flops,
    )
    across = flip(output[:rows], 2, devices)
    last_mid_grad, last_gvec, last_hidden, across, output = lax.optimization_barrier(
        (last_mid_grad, last_gvec, last_hidden, across, output)
    )
    grad_middle, *last_attention = call(
        functools.partial(last_attention_kernel, plan),
        (last_mid_grad, middle, last_vec, last_attn, last_gvec, *last_kept),
        [VMEM] * 9,
        [stream_shape, half(attn_rows), half(attn_rows)],
        [VMEM, ANY, ANY],
        vmem([vec_shape, low_shape, stream_shape, low_shape, three_shape, both(attn_rows)]) + sems,
        layer_flops,
    )
    output_pieces = [flip(output[:rows], 1, devices), across, flip(across, 1, devices)]
    if direct:
        terms = []
        for kept_half, sent_half in (last_hidden, last_attention):
            terms += [kept_half, flip(sent_half, 1, devices)]
        message = ((hidden_rows + attn_rows, width), BF16)
        last_sums = call(add_kernel, terms, [VMEM] * 4, [message] * 4, [VMEM] * 4, [], 1 << 20)
        grad_middle, last_sums, output_pieces = lax.optimization_barrier(
            (grad_middle, last_sums, output_pieces)
        )
    grad_first, *first_halves = call(
        functools.partial(back_kernel, plan),
        (grad_middle, stream, mid, vec, attn_full, up_full, down_full, *attn_kept, *hidden_kept),
        [VMEM] * 14,
        [low_shape, half(hidden_rows + attn_rows), half(hidden_rows + attn_rows)],
        [VMEM, ANY, ANY],
        vmem(
            [stream_shape, vec_shape, low_shape, low_pair_shape, low_shape, stream_shape, pair_shape]
            + [turned_shape, turned_shape, three_shape, both(hidden_rows + attn_rows)]
        )
        + sems,
        3 * layer_flops,
    )

    def pack_output(output, output_pieces):
        (activations,) = call(
            pack_kernel,
            (slots, output, *output_pieces),
            [VMEM] * (mp_size + 1),
            [((SLOTS, width), F32)],
            [VMEM],
            [],
            2 * SLOTS * image_count * rows * width,
        )
        return activations

    def place_grads(grad_first, grad_pieces):
        (input_grads,) = call(
            place_kernel,
            (grad_first, *grad_pieces),
            [VMEM] * mp_size,
            [((image_count, patch_rows, width), F32)],
            [VMEM],
            [],
            image_count * patch_rows * width,
        )
        return input_grads

    if direct:
        last_total = sum_plane(plan, last_sums, devices)
        activations = pack_output(output, output_pieces)
        last_total, first_halves, grad_first, activations = lax.optimization_barrier(
            (last_total, first_halves, grad_first, activations)
        )
        across = flip(grad_first[:rows], 2, devices)
        first_sums = sum_cores(*first_halves, devices)
        first_sums, last_total, across, grad_first = lax.optimization_barrier(
            (first_sums, last_total, across, grad_first)
        )
        first_total = sum_plane(plan, first_sums, devices)
        last_terms = sum_column(last_total, devices)
        beside = flip(grad_first[:rows], 1, devices)
        input_grads = place_grads(grad_first, [beside, across, flip(across, 1, devices)])
        first_total, last_terms, input_grads = lax.optimization_barrier(
            (first_total, last_terms, input_grads)
        )
        first_terms = sum_column(first_total, devices)
        terms = (*first_terms, *last_terms)
        turned = (layers, thin, width)
        attn_grads, vector_grads, up_grads, down_grads = call(
            functools.partial(finish_kernel, plan, len(first_terms)),
            terms,
            [VMEM] * len(terms),
            [(turned, F32), (vectors.shape, F32), (turned, F32), (turned, F32)],
            [VMEM] * 4,
            vmem([vec_shape, vec_shape]),
            1 << 20,
        )
        attn_grads, down_grads = attn_grads.transpose(0, 2, 1), down_grads.transpose(0, 2, 1)
    else:
        last_halves = [
            jnp.concatenate(halves, axis=2) for halves in zip(last_hidden, last_attention)
        ]

        def square_blocks(halves):
            stacked = jnp.stack(halves)[:, 0]
            stacked = jnp.stack([stacked[k % 2, k // 2] for k in range(parts)])
            return jnp.stack(
                [lax.dynamic_index_in_dim(stacked, rank ^ k, 0, False) for k in range(parts)]
            )

        def outputs_of(halves):
            def by_owner(array):
                split = array.reshape(mp_size, dp_size, thin, width).transpose(1, 0, 2, 3)
                return split.reshape(devices, thin, width)

            every = square_blocks(halves)
            pieces = [
                every[:, 2 * width : 3 * width].reshape(devices, thin, width),
                by_owner(every[:, :width]),
                by_owner(every[:, width : 2 * width]),
                jnp.broadcast_to(every[0, 3 * width :], (devices, tile, width)),
            ]
            owned = lax.psum_scatter(
                jnp.concatenate(pieces, axis=1), ("dp", "mp"), scatter_dimension=0, tiled=False
            ).astype(F32)
            own_vec = lax.dynamic_slice_in_dim(
                owned[3 * thin :].reshape(-1), device * vec_rows, vec_rows
            )
            return owned[:thin].T, own_vec, owned[thin : 2 * thin], owned[2 * thin : 3 * thin].T

        attn_grads, vector_grads, up_grads, down_grads = (
            jnp.stack([one, two]) for one, two in zip(outputs_of(first_halves), outputs_of(last_halves))
        )
        activations = pack_output(output, output_pieces)
        input_grads = place_grads(grad_first, spread(grad_first[:rows], devices))

    return (activations, input_grads, attn_grads, vector_grads, up_grads, down_grads)


def solution(mesh):
    in_specs = (
        P("dp", None, None),
        P("dp", None, None),
        P("dp", None),
        P(None, None, ("dp", "mp")),
        P(None, ("dp", "mp")),
        P(None, "dp", "mp"),
        P(None, "mp", "dp"),
    )
    out_specs = (
        P("dp", None),
        P("dp", None, None),
        P(None, None, ("dp", "mp")),
        P(None, ("dp", "mp")),
        P(None, "dp", "mp"),
        P(None, "mp", "dp"),
    )
    return jax.shard_map(shards, mesh=mesh, in_specs=in_specs, out_specs=out_specs, check_vma=False)
```

```python
import dataclasses
import functools

import jax
import jax.numpy as jnp
from jax import lax
from jax.experimental import pallas as pl
from jax.experimental.pallas import tpu as pltpu
from jax.sharding import PartitionSpec as P

HD = 64
SLOTS = 1024
EPSILON = 1e-06
MASKED = -1e30
STEP = 16

F32 = jnp.float32
BF16 = jnp.bfloat16


def dot_nn(left, right):
    return lax.dot_general(left, right, (((1,), (0,)), ((), ())), preferred_element_type=F32)


def dot_nt(left, right):
    return lax.dot_general(left, right, (((1,), (1,)), ((), ())), preferred_element_type=F32)


def dot_tn(left, right):
    return lax.dot_general(left, right, (((0,), (0,)), ((), ())), preferred_element_type=F32)


def block_rows(index, step):
    return pl.ds(pl.multiple_of(index * step, step), step)


def fold_rows(values):
    return jnp.sum(values.reshape(values.shape[0] // 8, 8, values.shape[1]), axis=0)


def low_halves(rows):
    lane = lax.broadcasted_iota(jnp.int32, (rows, 2 * HD), 1)
    return lane < HD


def stack_heads(pair):
    low = low_halves(pair.shape[0])
    zero = jnp.zeros_like(pair)
    return jnp.concatenate([jnp.where(low, pair, zero), jnp.where(low, zero, pair)], axis=0)


def unstack_heads(stacked):
    rows = stacked.shape[0] // 2
    return jnp.where(low_halves(rows), stacked[:rows], stacked[rows:])


def norm_rows(x_ref, out_ref, gain, shift):
    def body(index, carry):
        at = block_rows(index, STEP)
        values = x_ref[at, :].astype(F32)
        centred = values - jnp.mean(values, axis=-1, keepdims=True)
        variance = jnp.mean(centred * centred, axis=-1, keepdims=True)
        out_ref[at, :] = (centred * lax.rsqrt(variance + EPSILON) * gain + shift).astype(BF16)
        return carry

    lax.fori_loop(0, x_ref.shape[0] // STEP, body, 0, unroll=True)


def norm_back(x_ref, grad_ref, base_ref, out_ref, low_ref, gain, images):
    rows = x_ref.shape[0] // images
    width = x_ref.shape[1]
    sums = []
    for image in range(images):

        def body(index, carry, image=image):
            at = pl.ds(pl.multiple_of(image * rows + index * STEP, STEP), STEP)
            values = x_ref[at, :].astype(F32)
            grad = grad_ref[at, :]
            centred = values - jnp.mean(values, axis=-1, keepdims=True)
            variance = jnp.mean(centred * centred, axis=-1, keepdims=True)
            inverse = lax.rsqrt(variance + EPSILON)
            unit = centred * inverse
            scaled = grad * gain
            mean_one = jnp.mean(scaled, axis=-1, keepdims=True)
            mean_two = jnp.mean(scaled * unit, axis=-1, keepdims=True)
            out = base_ref[at, :] + inverse * (scaled - mean_one - unit * mean_two)
            out_ref[at, :] = out.astype(out_ref.dtype)
            if low_ref is not None:
                low_ref[at, :] = out.astype(BF16)
            return (
                carry[0] + fold_rows(grad * unit),
                carry[1] + fold_rows(grad),
                carry[2] + fold_rows(out),
            )

        zero = jnp.zeros((8, width), F32)
        sums.append(lax.fori_loop(0, rows // STEP, body, (zero, zero, zero), unroll=True))
    return sums


def weigh(sums, share):
    total = sums[0]
    for more in sums[1:]:
        total = total + more * share
    return jnp.sum(total, axis=0, keepdims=True)


def as_square(ref, part):
    rows, width = ref.shape[1:]
    per = width // rows
    return ref[pl.ds(part * per, per)].reshape(width, width)


def forward_attention(x_ref, bias_ref, vec_ref, attn_ref, keep, mid_ref):
    n1_ref, proj_ref, p_ref, att_ref = keep
    images = bias_ref.shape[0]
    rows = x_ref.shape[0] // images
    width = x_ref.shape[1]
    pairs = width // (2 * HD)
    scale = HD**-0.5

    norm_rows(x_ref, n1_ref, vec_ref[0:1, :], vec_ref[1:2, :])
    for part, bias_row in enumerate((4, None, 5)):
        value = dot_nt(n1_ref[...], as_square(attn_ref, part))
        if bias_row is not None:
            value = value + vec_ref[bias_row : bias_row + 1, :]
        proj_ref[part] = value.astype(BF16)

    def image_body(image, carry):
        at = block_rows(image, rows)
        for pair in range(pairs):
            lanes = slice(pair * 2 * HD, (pair + 1) * 2 * HD)
            query = stack_heads(proj_ref[0, at, lanes])
            scores = dot_nt(query, proj_ref[1, at, lanes]) * scale + bias_ref[image]
            top = jnp.max(scores, axis=-1, keepdims=True)
            powers = jnp.exp(scores - top)
            total = jnp.sum(powers, axis=-1, keepdims=True)
            probs = (powers * (1.0 / total)).astype(BF16)
            p_ref[image, pair] = probs
            att_ref[at, lanes] = unstack_heads(dot_nn(probs, proj_ref[2, at, lanes])).astype(BF16)
        return carry

    for image in range(images):
        image_body(image, 0)
    mid_ref[...] = x_ref[...].astype(F32) + dot_nt(att_ref[...], as_square(attn_ref, 3)) + vec_ref[6:7, :]


def forward_hidden(mid_ref, vec_ref, up_ref, down_ref, keep, scratch, out_ref):
    n2_ref, a_ref, gp_ref = keep
    h_ref, acc_ref = scratch
    norm_rows(mid_ref, n2_ref, vec_ref[2:3, :], vec_ref[3:4, :])
    acc_ref[...] = mid_ref[...] + vec_ref[11:12, :]

    def part_body(part, carry):
        h_ref[part % 2] = dot_nn(n2_ref[...], as_square(up_ref, part))
        bias = vec_ref[pl.ds(7 + part, 1), :]

        def gelu_body(index, inner):
            at = block_rows(index, STEP)
            hidden = h_ref[part % 2, at, :] + bias
            share = 0.5 + 0.5 * lax.erf(hidden * 0.7071067811865476)
            a_ref[part, at, :] = (hidden * share).astype(BF16)
            bell = jnp.exp(-0.5 * hidden * hidden) * 0.3989422804014327
            gp_ref[part, at, :] = (share + hidden * bell).astype(gp_ref.dtype)
            return inner

        lax.fori_loop(0, h_ref.shape[1] // STEP, gelu_body, 0, unroll=True)
        acc_ref[...] += dot_nt(a_ref[part], as_square(down_ref, part))
        return carry

    for part in range(a_ref.shape[0]):
        part_body(part, 0)
    out_ref[...] = acc_ref[...].astype(out_ref.dtype)


def drop_shared(refs):
    @pl.when(jnp.logical_not(counts_shared()))
    def _():
        for ref in refs:
            rows = ref.shape[-2] // 2
            ref[..., rows:, :] = jnp.zeros((*ref.shape[:-2], rows, ref.shape[-1]), ref.dtype)


def backward_hidden(g_ref, mid_ref, vec_ref, up_ref, down_ref, share, keep, scratch, gm_ref, gvec_ref, store):
    n2_ref, a_ref, gp_ref = keep
    go_ref, gh_ref, acc_ref, h_ref, got_ref, n2t_ref = scratch
    images = 2
    rows = mid_ref.shape[0] // images
    width = mid_ref.shape[1]
    zero = jnp.zeros((8, width), F32)
    sums = []
    for image in range(images):

        def low_body(index, carry, image=image):
            at = pl.ds(pl.multiple_of(image * rows + index * STEP, STEP), STEP)
            grad = g_ref[at, :]
            go_ref[at, :] = grad.astype(BF16)
            return carry + fold_rows(grad)

        sums.append(lax.fori_loop(0, rows // STEP, low_body, zero, unroll=True))
    gvec_ref[11:12, :] = weigh(sums, share)
    acc_ref[...] = jnp.zeros_like(acc_ref)
    got_ref[...] = go_ref[...].T
    n2t_ref[...] = n2_ref[...].T

    def part_body(part, carry):
        store(2, part, dot_nn(got_ref[...], a_ref[part]))
        h_ref[part % 2] = dot_nn(go_ref[...], as_square(down_ref, part))
        inner_sums = []
        for image in range(images):

            def hidden_body(index, inner, image=image):
                at = pl.ds(pl.multiple_of(image * rows + index * STEP, STEP), STEP)
                grad = (h_ref[part % 2, at, :] * gp_ref[part, at, :].astype(F32)).astype(BF16)
                gh_ref[part % 2, at, :] = grad
                return inner + fold_rows(grad.astype(F32))

            inner_sums.append(lax.fori_loop(0, rows // STEP, hidden_body, zero, unroll=True))
        gvec_ref[pl.ds(7 + part, 1), :] = weigh(inner_sums, share)
        store(1, part, dot_nn(n2t_ref[...], gh_ref[part % 2]))
        acc_ref[...] += dot_nt(gh_ref[part % 2], as_square(up_ref, part))
        return carry

    for part in range(a_ref.shape[0]):
        part_body(part, 0)
    sums = norm_back(mid_ref, acc_ref, g_ref, gm_ref, None, vec_ref[2:3, :], images)
    for place, row in enumerate((2, 3, 6)):
        gvec_ref[row : row + 1, :] = weigh([one[place] for one in sums], share)


def backward_attention(gm_ref, x_ref, vec_ref, attn_ref, share, keep, scratch, gx_ref, gvec_ref, store):
    n1_ref, proj_ref, p_ref, att_ref = keep
    go_ref, acc_ref, ga_ref, dproj_ref = scratch
    images = p_ref.shape[0]
    rows = x_ref.shape[0] // images
    width = x_ref.shape[1]
    pairs = width // (2 * HD)
    scale = HD**-0.5
    go_ref[...] = gm_ref[...].astype(BF16)
    store(0, 3, dot_tn(go_ref[...], att_ref[...]))
    ga_ref[...] = dot_nn(go_ref[...], as_square(attn_ref, 3)).astype(BF16)

    def image_body(image, carry):
        at = block_rows(image, rows)
        for pair in range(pairs):
            lanes = slice(pair * 2 * HD, (pair + 1) * 2 * HD)
            query = stack_heads(proj_ref[0, at, lanes])
            keys = proj_ref[1, at, lanes]
            grad_out = stack_heads(ga_ref[at, lanes])
            probs = p_ref[image, pair]
            grad_probs = dot_nt(grad_out, proj_ref[2, at, lanes])
            dproj_ref[2, at, lanes] = dot_tn(probs, grad_out).astype(BF16)
            wide = probs.astype(F32)
            inner = jnp.sum(grad_probs * wide, axis=-1, keepdims=True)
            grad_scores = (wide * (grad_probs - inner)).astype(BF16)
            dproj_ref[0, at, lanes] = (unstack_heads(dot_nn(grad_scores, keys)) * scale).astype(BF16)
            dproj_ref[1, at, lanes] = (dot_tn(grad_scores, query) * scale).astype(BF16)
        return carry

    for image in range(images):
        image_body(image, 0)
    for part, row in enumerate((4, None, 5)):
        store(0, part, dot_tn(dproj_ref[part], n1_ref[...]))
        value = dot_nn(dproj_ref[part], as_square(attn_ref, part))
        if part == 0:
            acc_ref[...] = value
        else:
            acc_ref[...] += value
        if row is not None:
            sums = [
                fold_rows(dproj_ref[part, image * rows : (image + 1) * rows, :].astype(F32))
                for image in range(images)
            ]
            gvec_ref[row : row + 1, :] = weigh(sums, share)
    sums = norm_back(x_ref, acc_ref, gm_ref, gx_ref, None, vec_ref[0:1, :], images)
    for place, row in enumerate((0, 1)):
        gvec_ref[row : row + 1, :] = weigh([one[place] for one in sums], share)
    store(3, 0, gvec_ref[...])


def coordinates(plan):
    outer, inner = lax.axis_index("dp"), lax.axis_index("mp")
    here = (inner // 2, inner % 2)
    return (outer // 2, outer % 2, *here) if plan.direct else (0, 0, *here)


def counts_shared():
    return lax.axis_index("mp") == 0


def place_weights(plan, pieces, attn_ref, up_ref, down_ref, vec_ref):
    thin, rows = plan.thin, 3 * plan.thin

    def put(owner, block):
        at = owner % plan.inner * plan.outer + owner // plan.inner
        attn_ref[owner] = block[:thin]
        up_ref[at] = block[thin : 2 * thin]
        down_ref[at] = block[2 * thin : 3 * thin]

    if not plan.direct:
        for owner in range(plan.inner):
            put(owner, pieces[0][owner, :rows])
        vec_ref[...] = pieces[0][0, rows:].astype(F32)
        return
    at = coordinates(plan)
    vec = None
    for i, piece in enumerate(pieces):
        c, x, y = i % 2, i // 2 % 2, i // 4
        low = ((at[1] ^ y) * 2 + (at[2] ^ x)) * 2 + (at[3] ^ c)
        count = piece.shape[0] // rows
        for k in range(count):
            put((at[0] ^ k) * 8 + low, piece[k * rows : (k + 1) * rows])
        tail = piece[count * rows :].astype(F32)
        vec = tail if vec is None else vec + tail
    vec_ref[...] = vec


def storer(plan, packed_ref, kinds):
    thin, width = plan.thin, plan.width
    per = width // thin
    here = coordinates(plan)

    def put(owner, kind, block):
        c, x, y = owner % 2, owner // 2 % 2, owner // 4 % 2
        row = pl.multiple_of((kinds.index(kind) * plan.zs + owner // 8) * thin, thin)
        packed_ref[c ^ here[3], y ^ here[1], x ^ here[2], pl.ds(row, thin), :] = block

    def store(kind, part, value):
        low = value.astype(BF16)
        if kind == 3:
            for i in range(8):
                packed_ref[i % 2, i // 4, i // 2 % 2, len(kinds) * plan.zs * thin :, :] = low
            return
        blocks = low.reshape(per, thin, width)
        for i in range(per):
            owner = part * per + i if kind == 0 else i * plan.inner + part
            put(owner, kind, blocks[i])

    return store


def start_copies(packed_ref, outs, sems, start, count, before=()):
    at = pl.ds(start, count)
    copies = list(before)
    for i in range(2):
        source, target = packed_ref.at[i, :, :, at], outs[i].at[:, :, at]
        copies.append(pltpu.make_async_copy(source, target, sems.at[len(copies)]))
        copies[-1].start()
    return copies


def wait_all(copies):
    for one in copies:
        one.wait()


def prepare_kernel(plan, attn_ref, up_ref, down_ref, vec_in, keep_in, first_ref, last_ref, line_ref, vec_ref, keep_ref, sems):
    thin, tile, width = plan.thin, plan.tile, plan.width
    outs = (first_ref, last_ref)
    copies = [
        pltpu.make_async_copy(vec_in, vec_ref, sems.at[0]),
        pltpu.make_async_copy(keep_in, keep_ref, sems.at[1]),
    ]
    for kind, ref in enumerate((attn_ref, up_ref, down_ref)):
        for layer, out_ref in enumerate(outs):
            if plan.direct:
                target = out_ref.at[pl.ds(kind * thin, thin)]
                copies.append(pltpu.make_async_copy(ref.at[layer], target, sems.at[len(copies)]))
            else:
                out_ref[kind * thin : (kind + 1) * thin, :] = ref[layer]
    for one in copies:
        one.start()
    count = vec_ref.shape[1]
    device = lax.axis_index("dp") * plan.inner + lax.axis_index("mp")
    row_at = device * count // width
    offset = device * count - row_at * width
    copies[0].wait()
    copies[1].wait()
    kept = jnp.sum(keep_ref[...]) + 2 * keep_ref.shape[0]
    kept = jnp.where(counts_shared(), kept, 0)
    row = lax.broadcasted_iota(jnp.int32, (tile, width), 0)
    here = lax.broadcasted_iota(jnp.int32, (tile, width), 1) == lax.axis_index("dp")
    for layer, out_ref in enumerate(outs):
        line_ref[...] = jnp.zeros_like(line_ref)
        line_ref[0:1, 0:count] = vec_ref[layer : layer + 1, :].astype(F32)
        moved = pltpu.roll(line_ref[...], offset, 1)[0:1]
        piece = jnp.where(row == row_at, moved[:, :width], 0.0)
        piece = jnp.where(row == row_at + 1, moved[:, width:], piece)
        if layer == 1:
            piece = jnp.where(here & (row == 12), (kept >> 5).astype(F32), piece)
            piece = jnp.where(here & (row == 13), (kept & 31).astype(F32), piece)
        out_ref[3 * thin :, :] = piece.astype(BF16)
    for one in copies[2:]:
        one.wait()


def forward_kernel(plan, pieces, x_ref, bias_ref, *refs):
    sources, refs = refs[:pieces], refs[pieces:]
    attn_ref, up_ref, down_ref, vec_ref, mid_ref, out_ref, *refs = refs
    attn_keep, hidden_keep, (h_ref, acc_ref) = refs[:4], refs[4:7], refs[7:]
    place_weights(plan, sources, attn_ref, up_ref, down_ref, vec_ref)
    forward_attention(x_ref, bias_ref, vec_ref, attn_ref, attn_keep, mid_ref)
    forward_hidden(mid_ref, vec_ref, up_ref, down_ref, hidden_keep, (h_ref, acc_ref), out_ref)
    drop_shared((attn_keep[0], attn_keep[3], hidden_keep[0], hidden_keep[1]))


HIDDEN_KINDS, ATTENTION_KINDS, ALL_KINDS = (1, 2), (0,), (1, 2, 0)


def last_hidden_kernel(plan, goal_ref, mid_ref, vec_ref, up_ref, down_ref, *refs):
    keep, gm_ref, gvec_ref, outs, refs = refs[:3], refs[3], refs[4], refs[5:7], refs[7:]
    g_ref, go_ref, gh_ref, acc_ref, h_ref, got_ref, n2t_ref, packed_ref, sems = refs
    high = jnp.sum(vec_ref[12:13, :], axis=-1, keepdims=True)
    rest = jnp.sum(vec_ref[13:14, :], axis=-1, keepdims=True)
    loss_scale = float(plan.slots) / (high * 32.0 + rest)
    g_ref[...] = goal_ref[...].astype(F32) * loss_scale
    gvec_ref[...] = jnp.zeros_like(gvec_ref)
    share = counts_shared().astype(F32)
    store = storer(plan, packed_ref, HIDDEN_KINDS)
    scratch = (go_ref, gh_ref, acc_ref, h_ref, got_ref, n2t_ref)
    backward_hidden(g_ref, mid_ref, vec_ref, up_ref, down_ref, share, keep, scratch, gm_ref, gvec_ref, store)
    wait_all(start_copies(packed_ref, outs, sems, 0, packed_ref.shape[3]))


def last_attention_kernel(plan, gm_ref, x_ref, vec_ref, attn_ref, early_ref, *refs):
    keep, gx_ref, outs, refs = refs[:4], refs[4], refs[5:7], refs[7:]
    gvec_ref, go_ref, acc_ref, ga_ref, dproj_ref, packed_ref, sems = refs
    gvec_ref[...] = early_ref[...]
    share = counts_shared().astype(F32)
    store = storer(plan, packed_ref, ATTENTION_KINDS)
    scratch = (go_ref, acc_ref, ga_ref, dproj_ref)
    backward_attention(gm_ref, x_ref, vec_ref, attn_ref, share, keep, scratch, gx_ref, gvec_ref, store)
    wait_all(start_copies(packed_ref, outs, sems, 0, packed_ref.shape[3]))


def back_kernel(plan, g_ref, x_ref, mid_ref, vec_ref, attn_ref, up_ref, down_ref, *refs):
    attn_keep, hidden_keep, gx_ref, outs, refs = refs[:4], refs[4:7], refs[7], refs[8:10], refs[10:]
    gm_ref, gvec_ref, go_ref, gh_ref, ga_ref, acc_ref, h_ref, got_ref, n2t_ref, dproj_ref, packed_ref, sems = refs
    gvec_ref[...] = jnp.zeros_like(gvec_ref)
    share = counts_shared().astype(F32)
    store = storer(plan, packed_ref, ALL_KINDS)
    scratch = (go_ref, gh_ref, acc_ref, h_ref, got_ref, n2t_ref)
    backward_hidden(g_ref, mid_ref, vec_ref, up_ref, down_ref, share, hidden_keep, scratch, gm_ref, gvec_ref, store)
    hidden_rows = 2 * plan.zs * plan.thin
    copies = start_copies(packed_ref, outs, sems, 0, hidden_rows)
    scratch = (go_ref, acc_ref, ga_ref, dproj_ref)
    backward_attention(gm_ref, x_ref, vec_ref, attn_ref, share, attn_keep, scratch, gx_ref, gvec_ref, store)
    rest = packed_ref.shape[3] - hidden_rows
    wait_all(start_copies(packed_ref, outs, sems, hidden_rows, rest, copies))


def add_kernel(kept_hidden, got_hidden, kept_attn, got_attn, *out_refs):
    count = kept_hidden.shape[2]
    for i, out_ref in enumerate(out_refs):
        at = (i // 2, i % 2)
        total = kept_hidden[at].astype(F32) + got_hidden[at].astype(F32)
        out_ref[0:count, :] = total.astype(BF16)
        total = kept_attn[at].astype(F32) + got_attn[at].astype(F32)
        out_ref[count:, :] = total.astype(BF16)


def finish_kernel(plan, count_of, *refs):
    layers = (refs[:count_of], refs[count_of : 2 * count_of])
    attn_out, vec_out, up_out, down_out, *tiles = refs[2 * count_of :]
    thin, tile, width = plan.thin, plan.tile, plan.width

    count = vec_out.shape[1]
    device = lax.axis_index("dp") * plan.inner + lax.axis_index("mp")
    row = device * count // width
    offset = device * count - row * width
    for layer in range(2):

        def total(start, count, layer=layer):
            return sum(ref[start : start + count, :].astype(F32) for ref in layers[layer])

        attn_out[layer] = total(0, thin)
        up_out[layer] = total(thin, thin)
        down_out[layer] = total(2 * thin, thin)
        tiles[layer][...] = total(3 * thin, tile)
        both = jnp.concatenate(
            [tiles[layer][pl.ds(row, 1), :], tiles[layer][pl.ds(row + 1, 1), :]], axis=1
        )
        both = jnp.broadcast_to(both, (8, 2 * width))
        moved = pltpu.roll(both, 2 * width - offset, 1)
        vec_out[layer : layer + 1, :] = moved[0:1, :count]


def place_kernel(own_ref, *refs):
    others, out_ref = refs[:-1], refs[-1]
    rows = own_ref.shape[0] // 2
    kept = out_ref.shape[1]
    mine = lax.axis_index("mp")
    out_ref[mine] = own_ref[0:rows, :].astype(F32)[:kept]
    for i, ref in enumerate(others):
        out_ref[mine ^ (i + 1)] = ref[...].astype(F32)[:kept]
    out_ref[out_ref.shape[0] - 1] = own_ref[rows : 2 * rows, :].astype(F32)[:kept]


def pack_kernel(slot_ref, own_ref, *refs):
    others, out_ref = refs[:-1], refs[-1]
    rows = own_ref.shape[0] // 2
    sources = [own_ref[0:rows, :]] + [ref[...] for ref in others] + [own_ref[rows : 2 * rows, :]]
    step = 256

    def body(index, carry):
        slots = lax.broadcasted_iota(jnp.int32, (step, rows), 0) + index * step
        total = None
        for i, values in enumerate(sources):
            picks = jnp.where(slots == slot_ref[i], 1.0, 0.0).astype(BF16)
            term = dot_nn(picks, values)
            total = term if total is None else total + term
        out_ref[block_rows(index, step), :] = total
        return carry

    lax.fori_loop(0, out_ref.shape[0] // step, body, 0)


VMEM = pl.BlockSpec(memory_space=pltpu.VMEM)
ANY = pl.BlockSpec(memory_space=pl.ANY)


def call(kernel, operands, specs, outs, out_specs, scratch, flops, limit=26):
    return pl.pallas_call(
        kernel,
        out_shape=[jax.ShapeDtypeStruct(shape, dtype) for shape, dtype in outs],
        in_specs=specs,
        out_specs=out_specs,
        scratch_shapes=scratch,
        compiler_params=pltpu.CompilerParams(vmem_limit_bytes=limit << 20),
        cost_estimate=pl.CostEstimate(flops=flops, bytes_accessed=8 << 20, transcendentals=0),
    )(*operands)


@dataclasses.dataclass(frozen=True)
class Plan:
    outer: int
    inner: int
    thin: int
    tile: int
    width: int
    slots: int
    direct: bool

    @property
    def zs(self):
        return self.outer // 2 if self.direct else 1


def flip(array, mask, devices):
    return lax.ppermute(array, ("dp", "mp"), [(d, d ^ mask) for d in range(devices)])


def column_kernel(plan, *refs):
    blocks, out_ref = refs[:-1], refs[-1]
    rows = 3 * plan.thin
    for k, ref in enumerate(blocks):
        out_ref[k * rows : (k + 1) * rows, :] = ref[0:rows, :]
    tail = sum(ref[rows:, :].astype(F32) for ref in blocks)
    out_ref[len(blocks) * rows :, :] = tail.astype(BF16)


def gather_column(plan, block, devices):
    blocks = [block] + [flip(block, 8 * k, devices) for k in range(1, devices // 8)]
    shape = (len(blocks) * 3 * plan.thin + plan.tile, plan.width)
    (column,) = call(
        functools.partial(column_kernel, plan), blocks, [VMEM] * len(blocks), [(shape, BF16)], [VMEM], [], 1 << 20
    )
    return column


def gather_plane(column, devices):
    return [column] + [flip(column, mask, devices) for mask in (2, 4, 6)]


def gather_cores(plane, devices):
    pieces = []
    for piece in plane:
        pieces += [piece, flip(piece, 1, devices)]
    return pieces


def spread(rows, devices):
    across = flip(rows, 2, devices)
    return [flip(rows, 1, devices), across, flip(across, 1, devices)]


def sum_cores(kept, sent, devices):
    got = flip(sent, 1, devices)
    return [(kept[i // 2, i % 2].astype(F32) + got[i // 2, i % 2].astype(F32)).astype(BF16) for i in range(4)]


def plane_kernel(plan, *refs):
    terms, out_refs = refs[:4], refs[4:]
    thin, tile = plan.thin, plan.tile
    zs = len(out_refs)

    def added(start, count):
        return sum(ref[pl.ds(start, count), :].astype(F32) for ref in terms).astype(BF16)

    tail = added(3 * zs * thin, tile)
    for z, out_ref in enumerate(out_refs):
        for kind in range(3):
            row = (ALL_KINDS.index(kind) * zs + (coordinates(plan)[0] ^ z)) * thin
            out_ref[kind * thin : (kind + 1) * thin, :] = added(pl.multiple_of(row, thin), thin)
        out_ref[3 * thin :, :] = tail


def sum_plane(plan, sums, devices):
    zs = devices // 8
    terms = [sums[0]] + [flip(one, mask, devices) for one, mask in zip(sums[1:], (2, 4, 6))]
    outs = [((3 * plan.thin + plan.tile, plan.width), BF16)] * zs
    return call(
        functools.partial(plane_kernel, plan), terms, [VMEM] * 4, outs, [VMEM] * zs, [], 1 << 20
    )


def sum_column(blocks, devices):
    return [one if k == 0 else flip(one, 8 * k, devices) for k, one in enumerate(blocks)]


def shards(patches, targets, keep_mask, attn_weights, vectors, up_weights, down_weights):
    image_count, patch_rows, width = patches.shape
    layers = attn_weights.shape[0]
    dp_size, mp_size = lax.axis_size("dp"), lax.axis_size("mp")
    devices = dp_size * mp_size
    rank = lax.axis_index("mp")
    lane_rank = lax.axis_index("dp")
    device = lane_rank * mp_size + rank
    thin = attn_weights.shape[2]
    vec_rows = vectors.shape[1]
    parts = thin * devices // width
    assert image_count == mp_size + 1 and layers == 2 and parts == mp_size == 4
    direct = thin % 16 == 0
    images, tile = 2, 16
    rows = -(-patch_rows // 16) * 16
    total = images * rows

    keep_rows = jnp.concatenate([jnp.ones((image_count, 2), jnp.int32), keep_mask], axis=1)
    keep_rows = jnp.pad(keep_rows, ((0, 0), (0, rows - patch_rows)))

    attn_turned = attn_weights.transpose(0, 2, 1)
    down_turned = down_weights.transpose(0, 2, 1)
    packing = Plan(dp_size, mp_size, thin, tile, width, SLOTS * dp_size, direct)
    block_shape = ((3 * thin + tile, width), BF16)
    first_block, last_block = call(
        functools.partial(prepare_kernel, packing),
        (attn_turned, up_weights, down_turned, vectors, keep_mask),
        [ANY if direct else VMEM] * 3 + [ANY] * 2,
        [block_shape, block_shape],
        [VMEM, VMEM],
        [
            pltpu.VMEM((8, 2 * width), F32),
            pltpu.VMEM(vectors.shape, BF16),
            pltpu.VMEM(keep_mask.shape, jnp.int32),
            pltpu.SemaphoreType.DMA((8,)),
        ],
        1 << 20,
        60,
    )
    if direct:
        plan = packing
        first_column = gather_column(plan, first_block, devices)
        first_column, last_block = lax.optimization_barrier((first_column, last_block))
        first_plane = gather_plane(first_column, devices)
        last_column = gather_column(plan, last_block, devices)
        first_plane, last_column = lax.optimization_barrier((first_plane, last_column))
        first_pieces = gather_cores(first_plane, devices)
        last_plane = gather_plane(last_column, devices)
    else:
        plan = Plan(1, parts, width, tile, width, SLOTS * dp_size, False)

        def squares(array):
            return array.reshape(parts, width, width)

        def by_part(array):
            split = array.reshape(dp_size, mp_size, thin, width).transpose(1, 0, 2, 3)
            return squares(split)

        def one_tile(array):
            summed = jnp.sum(array.astype(F32), axis=0).astype(BF16)
            return jnp.pad(summed[None], ((0, parts - 1), (0, 0), (0, 0)))

        def normal(block):
            every = lax.all_gather(block, ("dp", "mp"))
            return jnp.concatenate(
                [
                    squares(every[:, :thin]),
                    by_part(every[:, thin : 2 * thin]),
                    by_part(every[:, 2 * thin : 3 * thin]),
                    one_tile(every[:, 3 * thin :]),
                ],
                axis=1,
            )

        first_pieces, last_pieces = [normal(first_block)], [normal(last_block)]

    flat = keep_rows.reshape(-1)
    slot = jnp.where(flat == 1, jnp.cumsum(flat) - flat, SLOTS).reshape(image_count, 1, rows)

    def mine(array):
        return jnp.concatenate(
            [lax.dynamic_slice_in_dim(array, rank, 1, 0), array[mp_size:]], axis=0
        )

    def padded(array):
        return jnp.pad(mine(array), ((0, 0), (0, rows - patch_rows), (0, 0)))

    kept = mine(keep_rows)
    stream = padded(patches).reshape(total, width)
    bias = jnp.where(kept == 1, 0.0, MASKED).astype(F32)[:, None, :]
    goal = jnp.where((kept == 1)[:, :, None], padded(targets), 0).reshape(total, width)
    slots = jnp.concatenate(
        [lax.dynamic_slice_in_dim(slot, rank ^ k, 1, 0) for k in range(mp_size)] + [slot[mp_size:]],
        axis=0,
    )

    stream, slots, goal = lax.optimization_barrier((stream, slots, goal))

    pairs = width // (2 * HD)
    stream_shape = ((total, width), F32)
    low_shape = ((total, width), BF16)
    pair_shape, low_pair_shape = ((2, total, width), F32), ((2, total, width), BF16)
    three_shape = ((3, total, width), BF16)
    turned_shape = ((width, total), BF16)
    vec_shape = ((tile, width), F32)
    attn_keep = [low_shape, three_shape, ((images, pairs, 2 * rows, rows), BF16), low_shape]
    hidden_keep = [low_shape, ((parts, total, width), BF16), ((parts, total, width), F32)]
    blocks = plan.outer * plan.inner
    weight_shape = ((blocks, plan.thin, width), BF16)
    zs = max(blocks // 8, 1)

    def vmem(shapes):
        return [pltpu.VMEM(shape, dtype) for shape, dtype in shapes]

    layer_flops = 8 * total * parts * width * width
    hidden_rows, attn_rows = 2 * plan.thin * zs, plan.thin * zs + tile

    def half(count):
        return ((2, 2, count, width), BF16)

    def both(count):
        return ((2, 2, 2, count, width), BF16)


    def forward(rows_in, pieces, out_shape):
        results = call(
            functools.partial(forward_kernel, plan, len(pieces)),
            (rows_in, bias, *pieces),
            [VMEM] * (2 + len(pieces)),
            [weight_shape, weight_shape, weight_shape, vec_shape, stream_shape, out_shape]
            + attn_keep
            + hidden_keep,
            [VMEM] * 13,
            vmem([pair_shape, stream_shape]),
            layer_flops,
        )
        return (*results[:6], results[6:10], results[10:])

    attn_full, up_full, down_full, vec, mid, middle, attn_kept, hidden_kept = forward(
        stream, first_pieces, stream_shape
    )
    if direct:
        middle, last_plane = lax.optimization_barrier((middle, last_plane))
        last_pieces = gather_cores(last_plane, devices)
    sems = [pltpu.SemaphoreType.DMA((4,))]
    last_attn, last_up, last_down, last_vec, last_mid, output, last_kept, last_hidden_kept = forward(
        middle, last_pieces, low_shape
    )
    last_mid_grad, last_gvec, *last_hidden = call(
        functools.partial(last_hidden_kernel, plan),
        (goal, last_mid, last_vec, last_up, last_down, *last_hidden_kept),
        [VMEM] * 8,
        [stream_shape, vec_shape, half(hidden_rows), half(hidden_rows)],
        [VMEM] * 2 + [ANY] * 2,
        vmem(
            [stream_shape, low_shape, low_pair_shape, stream_shape, pair_shape]
            + [turned_shape, turned_shape, both(hidden_rows)]
        )
        + sems,
        layer_flops,
    )
    across = flip(output[:rows], 2, devices)
    last_mid_grad, last_gvec, last_hidden, across, output = lax.optimization_barrier(
        (last_mid_grad, last_gvec, last_hidden, across, output)
    )
    grad_middle, *last_attention = call(
        functools.partial(last_attention_kernel, plan),
        (last_mid_grad, middle, last_vec, last_attn, last_gvec, *last_kept),
        [VMEM] * 9,
        [stream_shape, half(attn_rows), half(attn_rows)],
        [VMEM, ANY, ANY],
        vmem([vec_shape, low_shape, stream_shape, low_shape, three_shape, both(attn_rows)]) + sems,
        layer_flops,
    )
    output_pieces = [flip(output[:rows], 1, devices), across, flip(across, 1, devices)]
    if direct:
        terms = []
        for kept_half, sent_half in (last_hidden, last_attention):
            terms += [kept_half, flip(sent_half, 1, devices)]
        message = ((hidden_rows + attn_rows, width), BF16)
        last_sums = call(add_kernel, terms, [VMEM] * 4, [message] * 4, [VMEM] * 4, [], 1 << 20)
        grad_middle, last_sums, output_pieces = lax.optimization_barrier(
            (grad_middle, last_sums, output_pieces)
        )
    grad_first, *first_halves = call(
        functools.partial(back_kernel, plan),
        (grad_middle, stream, mid, vec, attn_full, up_full, down_full, *attn_kept, *hidden_kept),
        [VMEM] * 14,
        [low_shape, half(hidden_rows + attn_rows), half(hidden_rows + attn_rows)],
        [VMEM, ANY, ANY],
        vmem(
            [stream_shape, vec_shape, low_shape, low_pair_shape, low_shape, stream_shape, pair_shape]
            + [turned_shape, turned_shape, three_shape, both(hidden_rows + attn_rows)]
        )
        + sems,
        3 * layer_flops,
    )

    def pack_output(output, output_pieces):
        (activations,) = call(
            pack_kernel,
            (slots, output, *output_pieces),
            [VMEM] * (mp_size + 1),
            [((SLOTS, width), F32)],
            [VMEM],
            [],
            2 * SLOTS * image_count * rows * width,
        )
        return activations

    def place_grads(grad_first, grad_pieces):
        (input_grads,) = call(
            place_kernel,
            (grad_first, *grad_pieces),
            [VMEM] * mp_size,
            [((image_count, patch_rows, width), F32)],
            [VMEM],
            [],
            image_count * patch_rows * width,
        )
        return input_grads

    if direct:
        last_total = sum_plane(plan, last_sums, devices)
        activations = pack_output(output, output_pieces)
        last_total, first_halves, grad_first, activations = lax.optimization_barrier(
            (last_total, first_halves, grad_first, activations)
        )
        across = flip(grad_first[:rows], 2, devices)
        first_sums = sum_cores(*first_halves, devices)
        first_sums, last_total, across, grad_first = lax.optimization_barrier(
            (first_sums, last_total, across, grad_first)
        )
        first_total = sum_plane(plan, first_sums, devices)
        last_terms = sum_column(last_total, devices)
        beside = flip(grad_first[:rows], 1, devices)
        input_grads = place_grads(grad_first, [beside, across, flip(across, 1, devices)])
        first_total, last_terms, input_grads = lax.optimization_barrier(
            (first_total, last_terms, input_grads)
        )
        first_terms = sum_column(first_total, devices)
        terms = (*first_terms, *last_terms)
        turned = (layers, thin, width)
        attn_grads, vector_grads, up_grads, down_grads = call(
            functools.partial(finish_kernel, plan, len(first_terms)),
            terms,
            [VMEM] * len(terms),
            [(turned, F32), (vectors.shape, F32), (turned, F32), (turned, F32)],
            [VMEM] * 4,
            vmem([vec_shape, vec_shape]),
            1 << 20,
        )
        attn_grads, down_grads = attn_grads.transpose(0, 2, 1), down_grads.transpose(0, 2, 1)
    else:
        last_halves = [
            jnp.concatenate(halves, axis=2) for halves in zip(last_hidden, last_attention)
        ]

        def square_blocks(halves):
            stacked = jnp.stack(halves)[:, 0]
            stacked = jnp.stack([stacked[k % 2, k // 2] for k in range(parts)])
            return jnp.stack(
                [lax.dynamic_index_in_dim(stacked, rank ^ k, 0, False) for k in range(parts)]
            )

        def outputs_of(halves):
            def by_owner(array):
                split = array.reshape(mp_size, dp_size, thin, width).transpose(1, 0, 2, 3)
                return split.reshape(devices, thin, width)

            every = square_blocks(halves)
            pieces = [
                every[:, 2 * width : 3 * width].reshape(devices, thin, width),
                by_owner(every[:, :width]),
                by_owner(every[:, width : 2 * width]),
                jnp.broadcast_to(every[0, 3 * width :], (devices, tile, width)),
            ]
            owned = lax.psum_scatter(
                jnp.concatenate(pieces, axis=1), ("dp", "mp"), scatter_dimension=0, tiled=False
            ).astype(F32)
            own_vec = lax.dynamic_slice_in_dim(
                owned[3 * thin :].reshape(-1), device * vec_rows, vec_rows
            )
            return owned[:thin].T, own_vec, owned[thin : 2 * thin], owned[2 * thin : 3 * thin].T

        attn_grads, vector_grads, up_grads, down_grads = (
            jnp.stack([one, two]) for one, two in zip(outputs_of(first_halves), outputs_of(last_halves))
        )
        activations = pack_output(output, output_pieces)
        input_grads = place_grads(grad_first, spread(grad_first[:rows], devices))

    return (activations, input_grads, attn_grads, vector_grads, up_grads, down_grads)


def solution(mesh):
    in_specs = (
        P("dp", None, None),
        P("dp", None, None),
        P("dp", None),
        P(None, None, ("dp", "mp")),
        P(None, ("dp", "mp")),
        P(None, "dp", "mp"),
        P(None, "mp", "dp"),
    )
    out_specs = (
        P("dp", None),
        P("dp", None, None),
        P(None, None, ("dp", "mp")),
        P(None, ("dp", "mp")),
        P(None, "dp", "mp"),
        P(None, "mp", "dp"),
    )
    return jax.shard_map(shards, mesh=mesh, in_specs=in_specs, out_specs=out_specs, check_vma=False)
```

```python
import dataclasses
import functools

import jax
import jax.numpy as jnp
from jax import lax
from jax.experimental import pallas as pl
from jax.experimental.pallas import tpu as pltpu
from jax.sharding import PartitionSpec as P

HD = 64
SLOTS = 1024
EPSILON = 1e-06
MASKED = -1e30
STEP = 16

F32 = jnp.float32
BF16 = jnp.bfloat16


def dot_nn(left, right):
    return lax.dot_general(left, right, (((1,), (0,)), ((), ())), preferred_element_type=F32)


def dot_nt(left, right):
    return lax.dot_general(left, right, (((1,), (1,)), ((), ())), preferred_element_type=F32)


def dot_tn(left, right):
    return lax.dot_general(left, right, (((0,), (0,)), ((), ())), preferred_element_type=F32)


def block_rows(index, step):
    return pl.ds(pl.multiple_of(index * step, step), step)


def fold_rows(values):
    return jnp.sum(values.reshape(values.shape[0] // 8, 8, values.shape[1]), axis=0)


def low_halves(rows):
    lane = lax.broadcasted_iota(jnp.int32, (rows, 2 * HD), 1)
    return lane < HD


def stack_heads(pair):
    low = low_halves(pair.shape[0])
    zero = jnp.zeros_like(pair)
    return jnp.concatenate([jnp.where(low, pair, zero), jnp.where(low, zero, pair)], axis=0)


def unstack_heads(stacked):
    rows = stacked.shape[0] // 2
    return jnp.where(low_halves(rows), stacked[:rows], stacked[rows:])


def norm_rows(x_ref, out_ref, gain, shift):
    def body(index, carry):
        at = block_rows(index, STEP)
        values = x_ref[at, :].astype(F32)
        centred = values - jnp.mean(values, axis=-1, keepdims=True)
        variance = jnp.mean(centred * centred, axis=-1, keepdims=True)
        out_ref[at, :] = (centred * lax.rsqrt(variance + EPSILON) * gain + shift).astype(BF16)
        return carry

    lax.fori_loop(0, x_ref.shape[0] // STEP, body, 0, unroll=True)


def norm_back(x_ref, grad_ref, base_ref, out_ref, low_ref, gain, images):
    rows = x_ref.shape[0] // images
    width = x_ref.shape[1]
    sums = []
    for image in range(images):

        def body(index, carry, image=image):
            at = pl.ds(pl.multiple_of(image * rows + index * STEP, STEP), STEP)
            values = x_ref[at, :].astype(F32)
            grad = grad_ref[at, :]
            centred = values - jnp.mean(values, axis=-1, keepdims=True)
            variance = jnp.mean(centred * centred, axis=-1, keepdims=True)
            inverse = lax.rsqrt(variance + EPSILON)
            unit = centred * inverse
            scaled = grad * gain
            mean_one = jnp.mean(scaled, axis=-1, keepdims=True)
            mean_two = jnp.mean(scaled * unit, axis=-1, keepdims=True)
            out = base_ref[at, :] + inverse * (scaled - mean_one - unit * mean_two)
            out_ref[at, :] = out.astype(out_ref.dtype)
            if low_ref is not None:
                low_ref[at, :] = out.astype(BF16)
            return (
                carry[0] + fold_rows(grad * unit),
                carry[1] + fold_rows(grad),
                carry[2] + fold_rows(out),
            )

        zero = jnp.zeros((8, width), F32)
        sums.append(lax.fori_loop(0, rows // STEP, body, (zero, zero, zero), unroll=True))
    return sums


def weigh(sums, share):
    total = sums[0]
    for more in sums[1:]:
        total = total + more * share
    return jnp.sum(total, axis=0, keepdims=True)


def as_square(ref, part):
    rows, width = ref.shape[1:]
    per = width // rows
    return ref[pl.ds(part * per, per)].reshape(width, width)


def forward_attention(x_ref, bias_ref, vec_ref, attn_ref, keep, mid_ref):
    n1_ref, proj_ref, p_ref, att_ref = keep
    images = bias_ref.shape[0]
    rows = x_ref.shape[0] // images
    width = x_ref.shape[1]
    pairs = width // (2 * HD)
    scale = HD**-0.5

    norm_rows(x_ref, n1_ref, vec_ref[0:1, :], vec_ref[1:2, :])
    for part, bias_row in enumerate((4, None, 5)):
        value = dot_nt(n1_ref[...], as_square(attn_ref, part))
        if bias_row is not None:
            value = value + vec_ref[bias_row : bias_row + 1, :]
        proj_ref[part] = value.astype(BF16)

    def image_body(image, carry):
        at = block_rows(image, rows)
        for pair in range(pairs):
            lanes = slice(pair * 2 * HD, (pair + 1) * 2 * HD)
            query = stack_heads(proj_ref[0, at, lanes])
            scores = dot_nt(query, proj_ref[1, at, lanes]) * scale + bias_ref[image]
            top = jnp.max(scores, axis=-1, keepdims=True)
            powers = jnp.exp(scores - top)
            total = jnp.sum(powers, axis=-1, keepdims=True)
            probs = (powers * (1.0 / total)).astype(BF16)
            p_ref[image, pair] = probs
            att_ref[at, lanes] = unstack_heads(dot_nn(probs, proj_ref[2, at, lanes])).astype(BF16)
        return carry

    for image in range(images):
        image_body(image, 0)
    mid_ref[...] = x_ref[...].astype(F32) + dot_nt(att_ref[...], as_square(attn_ref, 3)) + vec_ref[6:7, :]


def forward_hidden(mid_ref, vec_ref, up_ref, down_ref, keep, scratch, out_ref):
    n2_ref, a_ref, gp_ref = keep
    h_ref, acc_ref = scratch
    norm_rows(mid_ref, n2_ref, vec_ref[2:3, :], vec_ref[3:4, :])
    acc_ref[...] = mid_ref[...] + vec_ref[11:12, :]

    def part_body(part, carry):
        h_ref[part % 2] = dot_nn(n2_ref[...], as_square(up_ref, part))
        bias = vec_ref[pl.ds(7 + part, 1), :]

        def gelu_body(index, inner):
            at = block_rows(index, STEP)
            hidden = h_ref[part % 2, at, :] + bias
            share = 0.5 + 0.5 * lax.erf(hidden * 0.7071067811865476)
            a_ref[part, at, :] = (hidden * share).astype(BF16)
            bell = jnp.exp(-0.5 * hidden * hidden) * 0.3989422804014327
            gp_ref[part, at, :] = (share + hidden * bell).astype(gp_ref.dtype)
            return inner

        lax.fori_loop(0, h_ref.shape[1] // STEP, gelu_body, 0, unroll=True)
        acc_ref[...] += dot_nt(a_ref[part], as_square(down_ref, part))
        return carry

    for part in range(a_ref.shape[0]):
        part_body(part, 0)
    out_ref[...] = acc_ref[...].astype(out_ref.dtype)


def drop_shared(refs):
    @pl.when(jnp.logical_not(counts_shared()))
    def _():
        for ref in refs:
            rows = ref.shape[-2] // 2
            ref[..., rows:, :] = jnp.zeros((*ref.shape[:-2], rows, ref.shape[-1]), ref.dtype)


def backward_hidden(g_ref, mid_ref, vec_ref, up_ref, down_ref, share, keep, scratch, gm_ref, gvec_ref, store):
    n2_ref, a_ref, gp_ref = keep
    go_ref, gh_ref, acc_ref, h_ref, got_ref, n2t_ref = scratch
    images = 2
    rows = mid_ref.shape[0] // images
    width = mid_ref.shape[1]
    zero = jnp.zeros((8, width), F32)
    sums = []
    for image in range(images):

        def low_body(index, carry, image=image):
            at = pl.ds(pl.multiple_of(image * rows + index * STEP, STEP), STEP)
            grad = g_ref[at, :]
            go_ref[at, :] = grad.astype(BF16)
            return carry + fold_rows(grad)

        sums.append(lax.fori_loop(0, rows // STEP, low_body, zero, unroll=True))
    gvec_ref[11:12, :] = weigh(sums, share)
    acc_ref[...] = jnp.zeros_like(acc_ref)
    got_ref[...] = go_ref[...].T
    n2t_ref[...] = n2_ref[...].T

    def part_body(part, carry):
        store(2, part, dot_nn(got_ref[...], a_ref[part]))
        h_ref[part % 2] = dot_nn(go_ref[...], as_square(down_ref, part))
        inner_sums = []
        for image in range(images):

            def hidden_body(index, inner, image=image):
                at = pl.ds(pl.multiple_of(image * rows + index * STEP, STEP), STEP)
                grad = (h_ref[part % 2, at, :] * gp_ref[part, at, :].astype(F32)).astype(BF16)
                gh_ref[part % 2, at, :] = grad
                return inner + fold_rows(grad.astype(F32))

            inner_sums.append(lax.fori_loop(0, rows // STEP, hidden_body, zero, unroll=True))
        gvec_ref[pl.ds(7 + part, 1), :] = weigh(inner_sums, share)
        store(1, part, dot_nn(n2t_ref[...], gh_ref[part % 2]))
        acc_ref[...] += dot_nt(gh_ref[part % 2], as_square(up_ref, part))
        return carry

    for part in range(a_ref.shape[0]):
        part_body(part, 0)
    sums = norm_back(mid_ref, acc_ref, g_ref, gm_ref, None, vec_ref[2:3, :], images)
    for place, row in enumerate((2, 3, 6)):
        gvec_ref[row : row + 1, :] = weigh([one[place] for one in sums], share)


def backward_attention(gm_ref, x_ref, vec_ref, attn_ref, share, keep, scratch, gx_ref, gvec_ref, store):
    n1_ref, proj_ref, p_ref, att_ref = keep
    go_ref, acc_ref, ga_ref, dproj_ref = scratch
    images = p_ref.shape[0]
    rows = x_ref.shape[0] // images
    width = x_ref.shape[1]
    pairs = width // (2 * HD)
    scale = HD**-0.5
    go_ref[...] = gm_ref[...].astype(BF16)
    store(0, 3, dot_tn(go_ref[...], att_ref[...]))
    ga_ref[...] = dot_nn(go_ref[...], as_square(attn_ref, 3)).astype(BF16)

    def image_body(image, carry):
        at = block_rows(image, rows)
        for pair in range(pairs):
            lanes = slice(pair * 2 * HD, (pair + 1) * 2 * HD)
            query = stack_heads(proj_ref[0, at, lanes])
            keys = proj_ref[1, at, lanes]
            grad_out = stack_heads(ga_ref[at, lanes])
            probs = p_ref[image, pair]
            grad_probs = dot_nt(grad_out, proj_ref[2, at, lanes])
            dproj_ref[2, at, lanes] = dot_tn(probs, grad_out).astype(BF16)
            wide = probs.astype(F32)
            inner = jnp.sum(grad_probs * wide, axis=-1, keepdims=True)
            grad_scores = (wide * (grad_probs - inner)).astype(BF16)
            dproj_ref[0, at, lanes] = (unstack_heads(dot_nn(grad_scores, keys)) * scale).astype(BF16)
            dproj_ref[1, at, lanes] = (dot_tn(grad_scores, query) * scale).astype(BF16)
        return carry

    for image in range(images):
        image_body(image, 0)
    for part, row in enumerate((4, None, 5)):
        store(0, part, dot_tn(dproj_ref[part], n1_ref[...]))
        value = dot_nn(dproj_ref[part], as_square(attn_ref, part))
        if part == 0:
            acc_ref[...] = value
        else:
            acc_ref[...] += value
        if row is not None:
            sums = [
                fold_rows(dproj_ref[part, image * rows : (image + 1) * rows, :].astype(F32))
                for image in range(images)
            ]
            gvec_ref[row : row + 1, :] = weigh(sums, share)
    sums = norm_back(x_ref, acc_ref, gm_ref, gx_ref, None, vec_ref[0:1, :], images)
    for place, row in enumerate((0, 1)):
        gvec_ref[row : row + 1, :] = weigh([one[place] for one in sums], share)
    store(3, 0, gvec_ref[...])


def coordinates(plan):
    outer, inner = lax.axis_index("dp"), lax.axis_index("mp")
    here = (inner // 2, inner % 2)
    return (outer // 2, outer % 2, *here) if plan.direct else (0, 0, *here)


def counts_shared():
    return lax.axis_index("mp") == 0


def place_weights(plan, pieces, attn_ref, up_ref, down_ref, vec_ref):
    thin, rows = plan.thin, 3 * plan.thin

    def put(owner, block):
        at = owner % plan.inner * plan.outer + owner // plan.inner
        attn_ref[owner] = block[:thin]
        up_ref[at] = block[thin : 2 * thin]
        down_ref[at] = block[2 * thin : 3 * thin]

    if not plan.direct:
        for owner in range(plan.inner):
            put(owner, pieces[0][owner, :rows])
        vec_ref[...] = pieces[0][0, rows:].astype(F32)
        return
    at = coordinates(plan)
    vec = None
    for i, piece in enumerate(pieces):
        c, x, y = i % 2, i // 2 % 2, i // 4
        low = ((at[1] ^ y) * 2 + (at[2] ^ x)) * 2 + (at[3] ^ c)
        count = piece.shape[0] // rows
        for k in range(count):
            put((at[0] ^ k) * 8 + low, piece[k * rows : (k + 1) * rows])
        tail = piece[count * rows :].astype(F32)
        vec = tail if vec is None else vec + tail
    vec_ref[...] = vec


def storer(plan, packed_ref, kinds):
    thin, width = plan.thin, plan.width
    per = width // thin
    here = coordinates(plan)

    def put(owner, kind, block):
        c, x, y = owner % 2, owner // 2 % 2, owner // 4 % 2
        row = pl.multiple_of((kinds.index(kind) * plan.zs + owner // 8) * thin, thin)
        packed_ref[c ^ here[3], y ^ here[1], x ^ here[2], pl.ds(row, thin), :] = block

    def store(kind, part, value):
        low = value.astype(BF16)
        if kind == 3:
            for i in range(8):
                packed_ref[i % 2, i // 4, i // 2 % 2, len(kinds) * plan.zs * thin :, :] = low
            return
        blocks = low.reshape(per, thin, width)
        for i in range(per):
            owner = part * per + i if kind == 0 else i * plan.inner + part
            put(owner, kind, blocks[i])

    return store


def start_copies(packed_ref, outs, sems, start, count, before=()):
    at = pl.ds(start, count)
    copies = list(before)
    for i in range(2):
        source, target = packed_ref.at[i, :, :, at], outs[i].at[:, :, at]
        copies.append(pltpu.make_async_copy(source, target, sems.at[len(copies)]))
        copies[-1].start()
    return copies


def wait_all(copies):
    for one in copies:
        one.wait()


def prepare_kernel(plan, attn_ref, up_ref, down_ref, vec_in, keep_in, first_ref, last_ref, line_ref, vec_ref, keep_ref, sems):
    thin, tile, width = plan.thin, plan.tile, plan.width
    outs = (first_ref, last_ref)
    copies = [
        pltpu.make_async_copy(vec_in, vec_ref, sems.at[0]),
        pltpu.make_async_copy(keep_in, keep_ref, sems.at[1]),
    ]
    for kind, ref in enumerate((attn_ref, up_ref, down_ref)):
        for layer, out_ref in enumerate(outs):
            if plan.direct:
                target = out_ref.at[pl.ds(kind * thin, thin)]
                copies.append(pltpu.make_async_copy(ref.at[layer], target, sems.at[len(copies)]))
            else:
                out_ref[kind * thin : (kind + 1) * thin, :] = ref[layer]
    for one in copies:
        one.start()
    count = vec_ref.shape[1]
    device = lax.axis_index("dp") * plan.inner + lax.axis_index("mp")
    row_at = device * count // width
    offset = device * count - row_at * width
    copies[0].wait()
    copies[1].wait()
    kept = jnp.sum(keep_ref[...]) + 2 * keep_ref.shape[0]
    kept = jnp.where(counts_shared(), kept, 0)
    row = lax.broadcasted_iota(jnp.int32, (tile, width), 0)
    here = lax.broadcasted_iota(jnp.int32, (tile, width), 1) == lax.axis_index("dp")
    for layer, out_ref in enumerate(outs):
        line_ref[...] = jnp.zeros_like(line_ref)
        line_ref[0:1, 0:count] = vec_ref[layer : layer + 1, :].astype(F32)
        moved = pltpu.roll(line_ref[...], offset, 1)[0:1]
        piece = jnp.where(row == row_at, moved[:, :width], 0.0)
        piece = jnp.where(row == row_at + 1, moved[:, width:], piece)
        if layer == 1:
            piece = jnp.where(here & (row == 12), (kept >> 5).astype(F32), piece)
            piece = jnp.where(here & (row == 13), (kept & 31).astype(F32), piece)
        out_ref[3 * thin :, :] = piece.astype(BF16)
    for one in copies[2:]:
        one.wait()


def forward_kernel(plan, pieces, x_ref, bias_ref, *refs):
    sources, refs = refs[:pieces], refs[pieces:]
    attn_ref, up_ref, down_ref, vec_ref, mid_ref, out_ref, *refs = refs
    attn_keep, hidden_keep, (h_ref, acc_ref) = refs[:4], refs[4:7], refs[7:]
    place_weights(plan, sources, attn_ref, up_ref, down_ref, vec_ref)
    forward_attention(x_ref, bias_ref, vec_ref, attn_ref, attn_keep, mid_ref)
    forward_hidden(mid_ref, vec_ref, up_ref, down_ref, hidden_keep, (h_ref, acc_ref), out_ref)
    drop_shared((attn_keep[0], attn_keep[3], hidden_keep[0], hidden_keep[1]))


HIDDEN_KINDS, ATTENTION_KINDS, ALL_KINDS = (1, 2), (0,), (1, 2, 0)


def last_hidden_kernel(plan, goal_ref, mid_ref, vec_ref, up_ref, down_ref, *refs):
    keep, gm_ref, gvec_ref, outs, refs = refs[:3], refs[3], refs[4], refs[5:7], refs[7:]
    g_ref, go_ref, gh_ref, acc_ref, h_ref, got_ref, n2t_ref, packed_ref, sems = refs
    high = jnp.sum(vec_ref[12:13, :], axis=-1, keepdims=True)
    rest = jnp.sum(vec_ref[13:14, :], axis=-1, keepdims=True)
    loss_scale = float(plan.slots) / (high * 32.0 + rest)
    g_ref[...] = goal_ref[...].astype(F32) * loss_scale
    gvec_ref[...] = jnp.zeros_like(gvec_ref)
    share = counts_shared().astype(F32)
    store = storer(plan, packed_ref, HIDDEN_KINDS)
    scratch = (go_ref, gh_ref, acc_ref, h_ref, got_ref, n2t_ref)
    backward_hidden(g_ref, mid_ref, vec_ref, up_ref, down_ref, share, keep, scratch, gm_ref, gvec_ref, store)
    wait_all(start_copies(packed_ref, outs, sems, 0, packed_ref.shape[3]))


def last_attention_kernel(plan, gm_ref, x_ref, vec_ref, attn_ref, early_ref, *refs):
    keep, gx_ref, outs, refs = refs[:4], refs[4], refs[5:7], refs[7:]
    gvec_ref, go_ref, acc_ref, ga_ref, dproj_ref, packed_ref, sems = refs
    gvec_ref[...] = early_ref[...]
    share = counts_shared().astype(F32)
    store = storer(plan, packed_ref, ATTENTION_KINDS)
    scratch = (go_ref, acc_ref, ga_ref, dproj_ref)
    backward_attention(gm_ref, x_ref, vec_ref, attn_ref, share, keep, scratch, gx_ref, gvec_ref, store)
    wait_all(start_copies(packed_ref, outs, sems, 0, packed_ref.shape[3]))


def back_kernel(plan, g_ref, x_ref, mid_ref, vec_ref, attn_ref, up_ref, down_ref, *refs):
    attn_keep, hidden_keep, gx_ref, outs, refs = refs[:4], refs[4:7], refs[7], refs[8:10], refs[10:]
    gm_ref, gvec_ref, go_ref, gh_ref, ga_ref, acc_ref, h_ref, got_ref, n2t_ref, dproj_ref, packed_ref, sems = refs
    gvec_ref[...] = jnp.zeros_like(gvec_ref)
    share = counts_shared().astype(F32)
    store = storer(plan, packed_ref, ALL_KINDS)
    scratch = (go_ref, gh_ref, acc_ref, h_ref, got_ref, n2t_ref)
    backward_hidden(g_ref, mid_ref, vec_ref, up_ref, down_ref, share, hidden_keep, scratch, gm_ref, gvec_ref, store)
    hidden_rows = 2 * plan.zs * plan.thin
    copies = start_copies(packed_ref, outs, sems, 0, hidden_rows)
    scratch = (go_ref, acc_ref, ga_ref, dproj_ref)
    backward_attention(gm_ref, x_ref, vec_ref, attn_ref, share, attn_keep, scratch, gx_ref, gvec_ref, store)
    rest = packed_ref.shape[3] - hidden_rows
    wait_all(start_copies(packed_ref, outs, sems, hidden_rows, rest, copies))


def add_kernel(kept_hidden, got_hidden, kept_attn, got_attn, *out_refs):
    count = kept_hidden.shape[2]
    for i, out_ref in enumerate(out_refs):
        at = (i // 2, i % 2)
        total = kept_hidden[at].astype(F32) + got_hidden[at].astype(F32)
        out_ref[0:count, :] = total.astype(BF16)
        total = kept_attn[at].astype(F32) + got_attn[at].astype(F32)
        out_ref[count:, :] = total.astype(BF16)


def finish_kernel(plan, count_of, *refs):
    layers = (refs[:count_of], refs[count_of : 2 * count_of])
    attn_out, vec_out, up_out, down_out, *tiles = refs[2 * count_of :]
    thin, tile, width = plan.thin, plan.tile, plan.width

    count = vec_out.shape[1]
    device = lax.axis_index("dp") * plan.inner + lax.axis_index("mp")
    row = device * count // width
    offset = device * count - row * width
    for layer in range(2):

        def total(start, count, layer=layer):
            return sum(ref[start : start + count, :].astype(F32) for ref in layers[layer])

        attn_out[layer] = total(0, thin)
        up_out[layer] = total(thin, thin)
        down_out[layer] = total(2 * thin, thin)
        tiles[layer][...] = total(3 * thin, tile)
        both = jnp.concatenate(
            [tiles[layer][pl.ds(row, 1), :], tiles[layer][pl.ds(row + 1, 1), :]], axis=1
        )
        both = jnp.broadcast_to(both, (8, 2 * width))
        moved = pltpu.roll(both, 2 * width - offset, 1)
        vec_out[layer : layer + 1, :] = moved[0:1, :count]


def place_kernel(own_ref, *refs):
    others, out_ref = refs[:-1], refs[-1]
    rows = own_ref.shape[0] // 2
    kept = out_ref.shape[1]
    mine = lax.axis_index("mp")
    out_ref[mine] = own_ref[0:rows, :].astype(F32)[:kept]
    for i, ref in enumerate(others):
        out_ref[mine ^ (i + 1)] = ref[...].astype(F32)[:kept]
    out_ref[out_ref.shape[0] - 1] = own_ref[rows : 2 * rows, :].astype(F32)[:kept]


def pack_kernel(slot_ref, own_ref, *refs):
    others, out_ref = refs[:-1], refs[-1]
    rows = own_ref.shape[0] // 2
    sources = [own_ref[0:rows, :]] + [ref[...] for ref in others] + [own_ref[rows : 2 * rows, :]]
    step = 256

    def body(index, carry):
        slots = lax.broadcasted_iota(jnp.int32, (step, rows), 0) + index * step
        total = None
        for i, values in enumerate(sources):
            picks = jnp.where(slots == slot_ref[i], 1.0, 0.0).astype(BF16)
            term = dot_nn(picks, values)
            total = term if total is None else total + term
        out_ref[block_rows(index, step), :] = total
        return carry

    lax.fori_loop(0, out_ref.shape[0] // step, body, 0)


VMEM = pl.BlockSpec(memory_space=pltpu.VMEM)
ANY = pl.BlockSpec(memory_space=pl.ANY)


def call(kernel, operands, specs, outs, out_specs, scratch, flops, limit=26):
    return pl.pallas_call(
        kernel,
        out_shape=[jax.ShapeDtypeStruct(shape, dtype) for shape, dtype in outs],
        in_specs=specs,
        out_specs=out_specs,
        scratch_shapes=scratch,
        compiler_params=pltpu.CompilerParams(vmem_limit_bytes=limit << 20),
        cost_estimate=pl.CostEstimate(flops=flops, bytes_accessed=8 << 20, transcendentals=0),
    )(*operands)


@dataclasses.dataclass(frozen=True)
class Plan:
    outer: int
    inner: int
    thin: int
    tile: int
    width: int
    slots: int
    direct: bool

    @property
    def zs(self):
        return self.outer // 2 if self.direct else 1


def flip(array, mask, devices):
    return lax.ppermute(array, ("dp", "mp"), [(d, d ^ mask) for d in range(devices)])


def column_kernel(plan, *refs):
    blocks, out_ref = refs[:-1], refs[-1]
    rows = 3 * plan.thin
    for k, ref in enumerate(blocks):
        out_ref[k * rows : (k + 1) * rows, :] = ref[0:rows, :]
    tail = sum(ref[rows:, :].astype(F32) for ref in blocks)
    out_ref[len(blocks) * rows :, :] = tail.astype(BF16)


def gather_column(plan, block, devices):
    blocks = [block] + [flip(block, 8 * k, devices) for k in range(1, devices // 8)]
    shape = (len(blocks) * 3 * plan.thin + plan.tile, plan.width)
    (column,) = call(
        functools.partial(column_kernel, plan), blocks, [VMEM] * len(blocks), [(shape, BF16)], [VMEM], [], 1 << 20
    )
    return column


def gather_plane(column, devices):
    return [column] + [flip(column, mask, devices) for mask in (2, 4, 6)]


def gather_cores(plane, devices):
    pieces = []
    for piece in plane:
        pieces += [piece, flip(piece, 1, devices)]
    return pieces


def spread(rows, devices):
    across = flip(rows, 2, devices)
    return [flip(rows, 1, devices), across, flip(across, 1, devices)]


def sum_cores(kept, sent, devices):
    got = flip(sent, 1, devices)
    return [(kept[i // 2, i % 2].astype(F32) + got[i // 2, i % 2].astype(F32)).astype(BF16) for i in range(4)]


def plane_kernel(plan, counts, *refs):
    terms, out_refs = [], refs[sum(counts) :]
    for k in range(len(counts)):
        start = sum(counts[:k])
        terms.append(refs[start : start + counts[k]])
    thin, tile = plan.thin, plan.tile
    zs, scratch = plan.zs, out_refs[-1]
    rows = scratch.shape[0]
    total = None
    for parts in terms:
        whole = jnp.concatenate([ref[...].astype(F32) for ref in parts], axis=0)
        total = whole if total is None else total + whole
    scratch[...] = total
    tail = scratch[rows - tile :, :].astype(BF16)
    for z, out_ref in enumerate(out_refs[:-1]):
        for kind in range(3):
            row = (ALL_KINDS.index(kind) * zs + (coordinates(plan)[0] ^ z)) * thin
            block = scratch[pl.ds(pl.multiple_of(row, thin), thin), :]
            out_ref[kind * thin : (kind + 1) * thin, :] = block.astype(BF16)
        out_ref[3 * thin :, :] = tail


def sum_plane(plan, sums, devices, relayed):
    rows = sums[0].shape[0]
    if relayed:
        half = rows // 2 // 16 * 16
        own, x_sum, y_sum, both = sums
        x_first, y_first = flip(both[:half], 2, devices), flip(both[half:], 4, devices)

        def joined(one, two):
            return (one.astype(F32) + two.astype(F32)).astype(BF16)

        x_two, y_one = joined(x_sum[half:], y_first), joined(y_sum[:half], x_first)
        x_parts = [flip(x_sum[:half], 2, devices), flip(x_two, 2, devices)]
        y_parts = [flip(y_one, 4, devices), flip(y_sum[half:], 4, devices)]
        terms, counts = [own, *x_parts, *y_parts], (1, 2, 2)
    else:
        terms = [sums[0]] + [flip(one, mask, devices) for one, mask in zip(sums[1:], (2, 4, 6))]
        counts = (1, 1, 1, 1)
    outs = [((3 * plan.thin + plan.tile, plan.width), BF16)] * plan.zs
    return call(
        functools.partial(plane_kernel, plan, counts),
        terms,
        [VMEM] * len(terms),
        outs,
        [VMEM] * plan.zs,
        [pltpu.VMEM((rows, plan.width), F32)],
        1 << 20,
    )


def sum_column(blocks, devices):
    return [one if k == 0 else flip(one, 8 * k, devices) for k, one in enumerate(blocks)]


def shards(patches, targets, keep_mask, attn_weights, vectors, up_weights, down_weights):
    image_count, patch_rows, width = patches.shape
    layers = attn_weights.shape[0]
    dp_size, mp_size = lax.axis_size("dp"), lax.axis_size("mp")
    devices = dp_size * mp_size
    rank = lax.axis_index("mp")
    lane_rank = lax.axis_index("dp")
    device = lane_rank * mp_size + rank
    thin = attn_weights.shape[2]
    vec_rows = vectors.shape[1]
    parts = thin * devices // width
    assert image_count == mp_size + 1 and layers == 2 and parts == mp_size == 4
    direct = thin % 16 == 0
    images, tile = 2, 16
    rows = -(-patch_rows // 16) * 16
    total = images * rows

    keep_rows = jnp.concatenate([jnp.ones((image_count, 2), jnp.int32), keep_mask], axis=1)
    keep_rows = jnp.pad(keep_rows, ((0, 0), (0, rows - patch_rows)))

    attn_turned = attn_weights.transpose(0, 2, 1)
    down_turned = down_weights.transpose(0, 2, 1)
    packing = Plan(dp_size, mp_size, thin, tile, width, SLOTS * dp_size, direct)
    block_shape = ((3 * thin + tile, width), BF16)
    first_block, last_block = call(
        functools.partial(prepare_kernel, packing),
        (attn_turned, up_weights, down_turned, vectors, keep_mask),
        [ANY if direct else VMEM] * 3 + [ANY] * 2,
        [block_shape, block_shape],
        [VMEM, VMEM],
        [
            pltpu.VMEM((8, 2 * width), F32),
            pltpu.VMEM(vectors.shape, BF16),
            pltpu.VMEM(keep_mask.shape, jnp.int32),
            pltpu.SemaphoreType.DMA((8,)),
        ],
        1 << 20,
        60,
    )
    if direct:
        plan = packing
        first_column = gather_column(plan, first_block, devices)
        first_column, last_block = lax.optimization_barrier((first_column, last_block))
        first_plane = gather_plane(first_column, devices)
        last_column = gather_column(plan, last_block, devices)
        first_plane, last_column = lax.optimization_barrier((first_plane, last_column))
        first_pieces = gather_cores(first_plane, devices)
        last_plane = gather_plane(last_column, devices)
    else:
        plan = Plan(1, parts, width, tile, width, SLOTS * dp_size, False)

        def squares(array):
            return array.reshape(parts, width, width)

        def by_part(array):
            split = array.reshape(dp_size, mp_size, thin, width).transpose(1, 0, 2, 3)
            return squares(split)

        def one_tile(array):
            summed = jnp.sum(array.astype(F32), axis=0).astype(BF16)
            return jnp.pad(summed[None], ((0, parts - 1), (0, 0), (0, 0)))

        def normal(block):
            every = lax.all_gather(block, ("dp", "mp"))
            return jnp.concatenate(
                [
                    squares(every[:, :thin]),
                    by_part(every[:, thin : 2 * thin]),
                    by_part(every[:, 2 * thin : 3 * thin]),
                    one_tile(every[:, 3 * thin :]),
                ],
                axis=1,
            )

        first_pieces, last_pieces = [normal(first_block)], [normal(last_block)]

    flat = keep_rows.reshape(-1)
    slot = jnp.where(flat == 1, jnp.cumsum(flat) - flat, SLOTS).reshape(image_count, 1, rows)

    def mine(array):
        return jnp.concatenate(
            [lax.dynamic_slice_in_dim(array, rank, 1, 0), array[mp_size:]], axis=0
        )

    def padded(array):
        return jnp.pad(mine(array), ((0, 0), (0, rows - patch_rows), (0, 0)))

    kept = mine(keep_rows)
    stream = padded(patches).reshape(total, width)
    bias = jnp.where(kept == 1, 0.0, MASKED).astype(F32)[:, None, :]
    goal = jnp.where((kept == 1)[:, :, None], padded(targets), 0).reshape(total, width)
    slots = jnp.concatenate(
        [lax.dynamic_slice_in_dim(slot, rank ^ k, 1, 0) for k in range(mp_size)] + [slot[mp_size:]],
        axis=0,
    )

    stream, slots, goal = lax.optimization_barrier((stream, slots, goal))

    pairs = width // (2 * HD)
    stream_shape = ((total, width), F32)
    low_shape = ((total, width), BF16)
    pair_shape, low_pair_shape = ((2, total, width), F32), ((2, total, width), BF16)
    three_shape = ((3, total, width), BF16)
    turned_shape = ((width, total), BF16)
    vec_shape = ((tile, width), F32)
    attn_keep = [low_shape, three_shape, ((images, pairs, 2 * rows, rows), BF16), low_shape]
    hidden_keep = [low_shape, ((parts, total, width), BF16), ((parts, total, width), F32)]
    blocks = plan.outer * plan.inner
    weight_shape = ((blocks, plan.thin, width), BF16)
    zs = max(blocks // 8, 1)

    def vmem(shapes):
        return [pltpu.VMEM(shape, dtype) for shape, dtype in shapes]

    layer_flops = 8 * total * parts * width * width
    hidden_rows, attn_rows = 2 * plan.thin * zs, plan.thin * zs + tile

    def half(count):
        return ((2, 2, count, width), BF16)

    def both(count):
        return ((2, 2, 2, count, width), BF16)


    def forward(rows_in, pieces, out_shape):
        results = call(
            functools.partial(forward_kernel, plan, len(pieces)),
            (rows_in, bias, *pieces),
            [VMEM] * (2 + len(pieces)),
            [weight_shape, weight_shape, weight_shape, vec_shape, stream_shape, out_shape]
            + attn_keep
            + hidden_keep,
            [VMEM] * 13,
            vmem([pair_shape, stream_shape]),
            layer_flops,
        )
        return (*results[:6], results[6:10], results[10:])

    attn_full, up_full, down_full, vec, mid, middle, attn_kept, hidden_kept = forward(
        stream, first_pieces, stream_shape
    )
    if direct:
        middle, last_plane = lax.optimization_barrier((middle, last_plane))
        last_pieces = gather_cores(last_plane, devices)
    sems = [pltpu.SemaphoreType.DMA((4,))]
    last_attn, last_up, last_down, last_vec, last_mid, output, last_kept, last_hidden_kept = forward(
        middle, last_pieces, low_shape
    )
    last_mid_grad, last_gvec, *last_hidden = call(
        functools.partial(last_hidden_kernel, plan),
        (goal, last_mid, last_vec, last_up, last_down, *last_hidden_kept),
        [VMEM] * 8,
        [stream_shape, vec_shape, half(hidden_rows), half(hidden_rows)],
        [VMEM] * 2 + [ANY] * 2,
        vmem(
            [stream_shape, low_shape, low_pair_shape, stream_shape, pair_shape]
            + [turned_shape, turned_shape, both(hidden_rows)]
        )
        + sems,
        layer_flops,
    )
    across = flip(output[:rows], 2, devices)
    last_mid_grad, last_gvec, last_hidden, across, output = lax.optimization_barrier(
        (last_mid_grad, last_gvec, last_hidden, across, output)
    )
    grad_middle, *last_attention = call(
        functools.partial(last_attention_kernel, plan),
        (last_mid_grad, middle, last_vec, last_attn, last_gvec, *last_kept),
        [VMEM] * 9,
        [stream_shape, half(attn_rows), half(attn_rows)],
        [VMEM, ANY, ANY],
        vmem([vec_shape, low_shape, stream_shape, low_shape, three_shape, both(attn_rows)]) + sems,
        layer_flops,
    )
    output_pieces = [flip(output[:rows], 1, devices), across, flip(across, 1, devices)]
    if direct:
        terms = []
        for kept_half, sent_half in (last_hidden, last_attention):
            terms += [kept_half, flip(sent_half, 1, devices)]
        message = ((hidden_rows + attn_rows, width), BF16)
        last_sums = call(add_kernel, terms, [VMEM] * 4, [message] * 4, [VMEM] * 4, [], 1 << 20)
        grad_middle, last_sums, output_pieces = lax.optimization_barrier(
            (grad_middle, last_sums, output_pieces)
        )
    grad_first, *first_halves = call(
        functools.partial(back_kernel, plan),
        (grad_middle, stream, mid, vec, attn_full, up_full, down_full, *attn_kept, *hidden_kept),
        [VMEM] * 14,
        [low_shape, half(hidden_rows + attn_rows), half(hidden_rows + attn_rows)],
        [VMEM, ANY, ANY],
        vmem(
            [stream_shape, vec_shape, low_shape, low_pair_shape, low_shape, stream_shape, pair_shape]
            + [turned_shape, turned_shape, three_shape, both(hidden_rows + attn_rows)]
        )
        + sems,
        3 * layer_flops,
    )

    def pack_output(output, output_pieces):
        (activations,) = call(
            pack_kernel,
            (slots, output, *output_pieces),
            [VMEM] * (mp_size + 1),
            [((SLOTS, width), F32)],
            [VMEM],
            [],
            2 * SLOTS * image_count * rows * width,
        )
        return activations

    def place_grads(grad_first, grad_pieces):
        (input_grads,) = call(
            place_kernel,
            (grad_first, *grad_pieces),
            [VMEM] * mp_size,
            [((image_count, patch_rows, width), F32)],
            [VMEM],
            [],
            image_count * patch_rows * width,
        )
        return input_grads

    if direct:
        last_total = sum_plane(plan, last_sums, devices, False)
        activations = pack_output(output, output_pieces)
        last_total, first_halves, grad_first, activations = lax.optimization_barrier(
            (last_total, first_halves, grad_first, activations)
        )
        across = flip(grad_first[:rows], 2, devices)
        first_sums = sum_cores(*first_halves, devices)
        first_sums, last_total, across, grad_first = lax.optimization_barrier(
            (first_sums, last_total, across, grad_first)
        )
        first_total = sum_plane(plan, first_sums, devices, True)
        last_terms = sum_column(last_total, devices)
        beside = flip(grad_first[:rows], 1, devices)
        input_grads = place_grads(grad_first, [beside, across, flip(across, 1, devices)])
        first_total, last_terms, input_grads = lax.optimization_barrier(
            (first_total, last_terms, input_grads)
        )
        first_terms = sum_column(first_total, devices)
        terms = (*first_terms, *last_terms)
        turned = (layers, thin, width)
        attn_grads, vector_grads, up_grads, down_grads = call(
            functools.partial(finish_kernel, plan, len(first_terms)),
            terms,
            [VMEM] * len(terms),
            [(turned, F32), (vectors.shape, F32), (turned, F32), (turned, F32)],
            [VMEM] * 4,
            vmem([vec_shape, vec_shape]),
            1 << 20,
        )
        attn_grads, down_grads = attn_grads.transpose(0, 2, 1), down_grads.transpose(0, 2, 1)
    else:
        last_halves = [
            jnp.concatenate(halves, axis=2) for halves in zip(last_hidden, last_attention)
        ]

        def square_blocks(halves):
            stacked = jnp.stack(halves)[:, 0]
            stacked = jnp.stack([stacked[k % 2, k // 2] for k in range(parts)])
            return jnp.stack(
                [lax.dynamic_index_in_dim(stacked, rank ^ k, 0, False) for k in range(parts)]
            )

        def outputs_of(halves):
            def by_owner(array):
                split = array.reshape(mp_size, dp_size, thin, width).transpose(1, 0, 2, 3)
                return split.reshape(devices, thin, width)

            every = square_blocks(halves)
            pieces = [
                every[:, 2 * width : 3 * width].reshape(devices, thin, width),
                by_owner(every[:, :width]),
                by_owner(every[:, width : 2 * width]),
                jnp.broadcast_to(every[0, 3 * width :], (devices, tile, width)),
            ]
            owned = lax.psum_scatter(
                jnp.concatenate(pieces, axis=1), ("dp", "mp"), scatter_dimension=0, tiled=False
            ).astype(F32)
            own_vec = lax.dynamic_slice_in_dim(
                owned[3 * thin :].reshape(-1), device * vec_rows, vec_rows
            )
            return owned[:thin].T, own_vec, owned[thin : 2 * thin], owned[2 * thin : 3 * thin].T

        attn_grads, vector_grads, up_grads, down_grads = (
            jnp.stack([one, two]) for one, two in zip(outputs_of(first_halves), outputs_of(last_halves))
        )
        activations = pack_output(output, output_pieces)
        input_grads = place_grads(grad_first, spread(grad_first[:rows], devices))

    return (activations, input_grads, attn_grads, vector_grads, up_grads, down_grads)


def solution(mesh):
    in_specs = (
        P("dp", None, None),
        P("dp", None, None),
        P("dp", None),
        P(None, None, ("dp", "mp")),
        P(None, ("dp", "mp")),
        P(None, "dp", "mp"),
        P(None, "mp", "dp"),
    )
    out_specs = (
        P("dp", None),
        P("dp", None, None),
        P(None, None, ("dp", "mp")),
        P(None, ("dp", "mp")),
        P(None, "dp", "mp"),
        P(None, "mp", "dp"),
    )
    return jax.shard_map(shards, mesh=mesh, in_specs=in_specs, out_specs=out_specs, check_vma=False)
```

```python
import dataclasses
import functools

import jax
import jax.numpy as jnp
from jax import lax
from jax.experimental import pallas as pl
from jax.experimental.pallas import tpu as pltpu
from jax.sharding import PartitionSpec as P

HD = 64
SLOTS = 1024
EPSILON = 1e-06
MASKED = -1e30
STEP = 16

F32 = jnp.float32
BF16 = jnp.bfloat16


def dot_nn(left, right):
    return lax.dot_general(left, right, (((1,), (0,)), ((), ())), preferred_element_type=F32)


def dot_nt(left, right):
    return lax.dot_general(left, right, (((1,), (1,)), ((), ())), preferred_element_type=F32)


def dot_tn(left, right):
    return lax.dot_general(left, right, (((0,), (0,)), ((), ())), preferred_element_type=F32)


def block_rows(index, step):
    return pl.ds(pl.multiple_of(index * step, step), step)


def fold_rows(values):
    return jnp.sum(values.reshape(values.shape[0] // 8, 8, values.shape[1]), axis=0)


def low_halves(rows):
    lane = lax.broadcasted_iota(jnp.int32, (rows, 2 * HD), 1)
    return lane < HD


def stack_heads(pair):
    low = low_halves(pair.shape[0])
    zero = jnp.zeros_like(pair)
    return jnp.concatenate([jnp.where(low, pair, zero), jnp.where(low, zero, pair)], axis=0)


def unstack_heads(stacked):
    rows = stacked.shape[0] // 2
    return jnp.where(low_halves(rows), stacked[:rows], stacked[rows:])


def norm_rows(x_ref, out_ref, gain, shift):
    def body(index, carry):
        at = block_rows(index, STEP)
        values = x_ref[at, :].astype(F32)
        centred = values - jnp.mean(values, axis=-1, keepdims=True)
        variance = jnp.mean(centred * centred, axis=-1, keepdims=True)
        out_ref[at, :] = (centred * lax.rsqrt(variance + EPSILON) * gain + shift).astype(BF16)
        return carry

    lax.fori_loop(0, x_ref.shape[0] // STEP, body, 0, unroll=True)


def norm_back(x_ref, grad_ref, base_ref, out_ref, low_ref, gain, images):
    rows = x_ref.shape[0] // images
    width = x_ref.shape[1]
    sums = []
    for image in range(images):

        def body(index, carry, image=image):
            at = pl.ds(pl.multiple_of(image * rows + index * STEP, STEP), STEP)
            values = x_ref[at, :].astype(F32)
            grad = grad_ref[at, :]
            centred = values - jnp.mean(values, axis=-1, keepdims=True)
            variance = jnp.mean(centred * centred, axis=-1, keepdims=True)
            inverse = lax.rsqrt(variance + EPSILON)
            unit = centred * inverse
            scaled = grad * gain
            mean_one = jnp.mean(scaled, axis=-1, keepdims=True)
            mean_two = jnp.mean(scaled * unit, axis=-1, keepdims=True)
            out = base_ref[at, :] + inverse * (scaled - mean_one - unit * mean_two)
            out_ref[at, :] = out.astype(out_ref.dtype)
            if low_ref is not None:
                low_ref[at, :] = out.astype(BF16)
            return (
                carry[0] + fold_rows(grad * unit),
                carry[1] + fold_rows(grad),
                carry[2] + fold_rows(out),
            )

        zero = jnp.zeros((8, width), F32)
        sums.append(lax.fori_loop(0, rows // STEP, body, (zero, zero, zero), unroll=True))
    return sums


def weigh(sums, share):
    total = sums[0]
    for more in sums[1:]:
        total = total + more * share
    return jnp.sum(total, axis=0, keepdims=True)


def as_square(ref, part):
    rows, width = ref.shape[1:]
    per = width // rows
    return ref[pl.ds(part * per, per)].reshape(width, width)


def forward_attention(x_ref, bias_ref, vec_ref, attn_ref, keep, mid_ref):
    n1_ref, proj_ref, p_ref, att_ref = keep
    images = bias_ref.shape[0]
    rows = x_ref.shape[0] // images
    width = x_ref.shape[1]
    pairs = width // (2 * HD)
    scale = HD**-0.5

    norm_rows(x_ref, n1_ref, vec_ref[0:1, :], vec_ref[1:2, :])
    for part, bias_row in enumerate((4, None, 5)):
        value = dot_nt(n1_ref[...], as_square(attn_ref, part))
        if bias_row is not None:
            value = value + vec_ref[bias_row : bias_row + 1, :]
        proj_ref[part] = value.astype(BF16)

    def image_body(image, carry):
        at = block_rows(image, rows)
        for pair in range(pairs):
            lanes = slice(pair * 2 * HD, (pair + 1) * 2 * HD)
            query = stack_heads(proj_ref[0, at, lanes])
            scores = dot_nt(query, proj_ref[1, at, lanes]) * scale + bias_ref[image]
            top = jnp.max(scores, axis=-1, keepdims=True)
            powers = jnp.exp(scores - top)
            total = jnp.sum(powers, axis=-1, keepdims=True)
            probs = (powers * (1.0 / total)).astype(BF16)
            p_ref[image, pair] = probs
            att_ref[at, lanes] = unstack_heads(dot_nn(probs, proj_ref[2, at, lanes])).astype(BF16)
        return carry

    for image in range(images):
        image_body(image, 0)
    mid_ref[...] = x_ref[...].astype(F32) + dot_nt(att_ref[...], as_square(attn_ref, 3)) + vec_ref[6:7, :]


def forward_hidden(mid_ref, vec_ref, up_ref, down_ref, keep, scratch, out_ref):
    n2_ref, a_ref, gp_ref = keep
    h_ref, acc_ref = scratch
    norm_rows(mid_ref, n2_ref, vec_ref[2:3, :], vec_ref[3:4, :])
    acc_ref[...] = mid_ref[...] + vec_ref[11:12, :]

    def part_body(part, carry):
        h_ref[part % 2] = dot_nn(n2_ref[...], as_square(up_ref, part))
        bias = vec_ref[pl.ds(7 + part, 1), :]

        def gelu_body(index, inner):
            at = block_rows(index, STEP)
            hidden = h_ref[part % 2, at, :] + bias
            share = 0.5 + 0.5 * lax.erf(hidden * 0.7071067811865476)
            a_ref[part, at, :] = (hidden * share).astype(BF16)
            bell = jnp.exp(-0.5 * hidden * hidden) * 0.3989422804014327
            gp_ref[part, at, :] = (share + hidden * bell).astype(gp_ref.dtype)
            return inner

        lax.fori_loop(0, h_ref.shape[1] // STEP, gelu_body, 0, unroll=True)
        acc_ref[...] += dot_nt(a_ref[part], as_square(down_ref, part))
        return carry

    for part in range(a_ref.shape[0]):
        part_body(part, 0)
    out_ref[...] = acc_ref[...].astype(out_ref.dtype)


def drop_shared(refs):
    @pl.when(jnp.logical_not(counts_shared()))
    def _():
        for ref in refs:
            rows = ref.shape[-2] // 2
            ref[..., rows:, :] = jnp.zeros((*ref.shape[:-2], rows, ref.shape[-1]), ref.dtype)


def backward_hidden(g_ref, mid_ref, vec_ref, up_ref, down_ref, share, keep, scratch, gm_ref, gvec_ref, store):
    n2_ref, a_ref, gp_ref = keep
    go_ref, gh_ref, acc_ref, h_ref, got_ref, n2t_ref = scratch
    images = 2
    rows = mid_ref.shape[0] // images
    width = mid_ref.shape[1]
    zero = jnp.zeros((8, width), F32)
    sums = []
    for image in range(images):

        def low_body(index, carry, image=image):
            at = pl.ds(pl.multiple_of(image * rows + index * STEP, STEP), STEP)
            grad = g_ref[at, :]
            go_ref[at, :] = grad.astype(BF16)
            return carry + fold_rows(grad)

        sums.append(lax.fori_loop(0, rows // STEP, low_body, zero, unroll=True))
    gvec_ref[11:12, :] = weigh(sums, share)
    acc_ref[...] = jnp.zeros_like(acc_ref)
    got_ref[...] = go_ref[...].T
    n2t_ref[...] = n2_ref[...].T

    def part_body(part, carry):
        store(2, part, dot_nn(got_ref[...], a_ref[part]))
        h_ref[part % 2] = dot_nn(go_ref[...], as_square(down_ref, part))
        inner_sums = []
        for image in range(images):

            def hidden_body(index, inner, image=image):
                at = pl.ds(pl.multiple_of(image * rows + index * STEP, STEP), STEP)
                grad = (h_ref[part % 2, at, :] * gp_ref[part, at, :].astype(F32)).astype(BF16)
                gh_ref[part % 2, at, :] = grad
                return inner + fold_rows(grad.astype(F32))

            inner_sums.append(lax.fori_loop(0, rows // STEP, hidden_body, zero, unroll=True))
        gvec_ref[pl.ds(7 + part, 1), :] = weigh(inner_sums, share)
        store(1, part, dot_nn(n2t_ref[...], gh_ref[part % 2]))
        acc_ref[...] += dot_nt(gh_ref[part % 2], as_square(up_ref, part))
        return carry

    for part in range(a_ref.shape[0]):
        part_body(part, 0)
    sums = norm_back(mid_ref, acc_ref, g_ref, gm_ref, None, vec_ref[2:3, :], images)
    for place, row in enumerate((2, 3, 6)):
        gvec_ref[row : row + 1, :] = weigh([one[place] for one in sums], share)


def backward_attention(gm_ref, x_ref, vec_ref, attn_ref, share, keep, scratch, gx_ref, gvec_ref, store):
    n1_ref, proj_ref, p_ref, att_ref = keep
    go_ref, acc_ref, ga_ref, dproj_ref = scratch
    images = p_ref.shape[0]
    rows = x_ref.shape[0] // images
    width = x_ref.shape[1]
    pairs = width // (2 * HD)
    scale = HD**-0.5
    go_ref[...] = gm_ref[...].astype(BF16)
    store(0, 3, dot_tn(go_ref[...], att_ref[...]))
    ga_ref[...] = dot_nn(go_ref[...], as_square(attn_ref, 3)).astype(BF16)

    def image_body(image, carry):
        at = block_rows(image, rows)
        for pair in range(pairs):
            lanes = slice(pair * 2 * HD, (pair + 1) * 2 * HD)
            query = stack_heads(proj_ref[0, at, lanes])
            keys = proj_ref[1, at, lanes]
            grad_out = stack_heads(ga_ref[at, lanes])
            probs = p_ref[image, pair]
            grad_probs = dot_nt(grad_out, proj_ref[2, at, lanes])
            dproj_ref[2, at, lanes] = dot_tn(probs, grad_out).astype(BF16)
            wide = probs.astype(F32)
            inner = jnp.sum(grad_probs * wide, axis=-1, keepdims=True)
            grad_scores = (wide * (grad_probs - inner)).astype(BF16)
            dproj_ref[0, at, lanes] = (unstack_heads(dot_nn(grad_scores, keys)) * scale).astype(BF16)
            dproj_ref[1, at, lanes] = (dot_tn(grad_scores, query) * scale).astype(BF16)
        return carry

    for image in range(images):
        image_body(image, 0)
    for part, row in enumerate((4, None, 5)):
        store(0, part, dot_tn(dproj_ref[part], n1_ref[...]))
        value = dot_nn(dproj_ref[part], as_square(attn_ref, part))
        if part == 0:
            acc_ref[...] = value
        else:
            acc_ref[...] += value
        if row is not None:
            sums = [
                fold_rows(dproj_ref[part, image * rows : (image + 1) * rows, :].astype(F32))
                for image in range(images)
            ]
            gvec_ref[row : row + 1, :] = weigh(sums, share)
    sums = norm_back(x_ref, acc_ref, gm_ref, gx_ref, None, vec_ref[0:1, :], images)
    for place, row in enumerate((0, 1)):
        gvec_ref[row : row + 1, :] = weigh([one[place] for one in sums], share)
    store(3, 0, gvec_ref[...])


def coordinates(plan):
    outer, inner = lax.axis_index("dp"), lax.axis_index("mp")
    here = (inner // 2, inner % 2)
    return (outer // 2, outer % 2, *here) if plan.direct else (0, 0, *here)


def counts_shared():
    return lax.axis_index("mp") == 0


def place_weights(plan, pieces, attn_ref, up_ref, down_ref, vec_ref):
    thin, rows = plan.thin, 3 * plan.thin

    def put(owner, block):
        at = owner % plan.inner * plan.outer + owner // plan.inner
        attn_ref[owner] = block[:thin]
        up_ref[at] = block[thin : 2 * thin]
        down_ref[at] = block[2 * thin : 3 * thin]

    if not plan.direct:
        for owner in range(plan.inner):
            put(owner, pieces[0][owner, :rows])
        vec_ref[...] = pieces[0][0, rows:].astype(F32)
        return
    at = coordinates(plan)
    vec = None
    for i, piece in enumerate(pieces):
        c, x, y = i % 2, i // 2 % 2, i // 4
        low = ((at[1] ^ y) * 2 + (at[2] ^ x)) * 2 + (at[3] ^ c)
        count = piece.shape[0] // rows
        for k in range(count):
            put((at[0] ^ k) * 8 + low, piece[k * rows : (k + 1) * rows])
        tail = piece[count * rows :].astype(F32)
        vec = tail if vec is None else vec + tail
    vec_ref[...] = vec


def storer(plan, packed_ref, kinds):
    thin, width = plan.thin, plan.width
    per = width // thin
    here = coordinates(plan)

    def put(owner, kind, block):
        c, x, y = owner % 2, owner // 2 % 2, owner // 4 % 2
        row = pl.multiple_of((kinds.index(kind) * plan.zs + owner // 8) * thin, thin)
        packed_ref[c ^ here[3], y ^ here[1], x ^ here[2], pl.ds(row, thin), :] = block

    def store(kind, part, value):
        low = value.astype(BF16)
        if kind == 3:
            for i in range(8):
                packed_ref[i % 2, i // 4, i // 2 % 2, len(kinds) * plan.zs * thin :, :] = low
            return
        blocks = low.reshape(per, thin, width)
        for i in range(per):
            owner = part * per + i if kind == 0 else i * plan.inner + part
            put(owner, kind, blocks[i])

    return store


def start_copies(packed_ref, outs, sems, start, count, before=()):
    at = pl.ds(start, count)
    copies = list(before)
    for i in range(2):
        source, target = packed_ref.at[i, :, :, at], outs[i].at[:, :, at]
        copies.append(pltpu.make_async_copy(source, target, sems.at[len(copies)]))
        copies[-1].start()
    return copies


def wait_all(copies):
    for one in copies:
        one.wait()


def prepare_kernel(plan, attn_ref, up_ref, down_ref, vec_in, keep_in, first_ref, last_ref, line_ref, vec_ref, keep_ref, sems):
    thin, tile, width = plan.thin, plan.tile, plan.width
    outs = (first_ref, last_ref)
    copies = [
        pltpu.make_async_copy(vec_in, vec_ref, sems.at[0]),
        pltpu.make_async_copy(keep_in, keep_ref, sems.at[1]),
    ]
    for kind, ref in enumerate((attn_ref, up_ref, down_ref)):
        for layer, out_ref in enumerate(outs):
            if plan.direct:
                target = out_ref.at[pl.ds(kind * thin, thin)]
                copies.append(pltpu.make_async_copy(ref.at[layer], target, sems.at[len(copies)]))
            else:
                out_ref[kind * thin : (kind + 1) * thin, :] = ref[layer]
    for one in copies:
        one.start()
    count = vec_ref.shape[1]
    device = lax.axis_index("dp") * plan.inner + lax.axis_index("mp")
    row_at = device * count // width
    offset = device * count - row_at * width
    copies[0].wait()
    copies[1].wait()
    kept = jnp.sum(keep_ref[...]) + 2 * keep_ref.shape[0]
    kept = jnp.where(counts_shared(), kept, 0)
    row = lax.broadcasted_iota(jnp.int32, (tile, width), 0)
    here = lax.broadcasted_iota(jnp.int32, (tile, width), 1) == lax.axis_index("dp")
    for layer, out_ref in enumerate(outs):
        line_ref[...] = jnp.zeros_like(line_ref)
        line_ref[0:1, 0:count] = vec_ref[layer : layer + 1, :].astype(F32)
        moved = pltpu.roll(line_ref[...], offset, 1)[0:1]
        piece = jnp.where(row == row_at, moved[:, :width], 0.0)
        piece = jnp.where(row == row_at + 1, moved[:, width:], piece)
        if layer == 1:
            piece = jnp.where(here & (row == 12), (kept >> 5).astype(F32), piece)
            piece = jnp.where(here & (row == 13), (kept & 31).astype(F32), piece)
        out_ref[3 * thin :, :] = piece.astype(BF16)
    for one in copies[2:]:
        one.wait()


def forward_kernel(plan, pieces, x_ref, bias_ref, *refs):
    sources, refs = refs[:pieces], refs[pieces:]
    attn_ref, up_ref, down_ref, vec_ref, mid_ref, out_ref, *refs = refs
    attn_keep, hidden_keep, (h_ref, acc_ref) = refs[:4], refs[4:7], refs[7:]
    place_weights(plan, sources, attn_ref, up_ref, down_ref, vec_ref)
    forward_attention(x_ref, bias_ref, vec_ref, attn_ref, attn_keep, mid_ref)
    forward_hidden(mid_ref, vec_ref, up_ref, down_ref, hidden_keep, (h_ref, acc_ref), out_ref)
    drop_shared((attn_keep[0], attn_keep[3], hidden_keep[0], hidden_keep[1]))


HIDDEN_KINDS, ATTENTION_KINDS, ALL_KINDS = (1, 2), (0,), (1, 2, 0)


def last_hidden_kernel(plan, goal_ref, mid_ref, vec_ref, up_ref, down_ref, *refs):
    keep, gm_ref, gvec_ref, outs, refs = refs[:3], refs[3], refs[4], refs[5:7], refs[7:]
    g_ref, go_ref, gh_ref, acc_ref, h_ref, got_ref, n2t_ref, packed_ref, sems = refs
    high = jnp.sum(vec_ref[12:13, :], axis=-1, keepdims=True)
    rest = jnp.sum(vec_ref[13:14, :], axis=-1, keepdims=True)
    loss_scale = float(plan.slots) / (high * 32.0 + rest)
    g_ref[...] = goal_ref[...].astype(F32) * loss_scale
    gvec_ref[...] = jnp.zeros_like(gvec_ref)
    share = counts_shared().astype(F32)
    store = storer(plan, packed_ref, HIDDEN_KINDS)
    scratch = (go_ref, gh_ref, acc_ref, h_ref, got_ref, n2t_ref)
    backward_hidden(g_ref, mid_ref, vec_ref, up_ref, down_ref, share, keep, scratch, gm_ref, gvec_ref, store)
    wait_all(start_copies(packed_ref, outs, sems, 0, packed_ref.shape[3]))


def last_attention_kernel(plan, gm_ref, x_ref, vec_ref, attn_ref, early_ref, *refs):
    keep, gx_ref, outs, refs = refs[:4], refs[4], refs[5:7], refs[7:]
    gvec_ref, go_ref, acc_ref, ga_ref, dproj_ref, packed_ref, sems = refs
    gvec_ref[...] = early_ref[...]
    share = counts_shared().astype(F32)
    store = storer(plan, packed_ref, ATTENTION_KINDS)
    scratch = (go_ref, acc_ref, ga_ref, dproj_ref)
    backward_attention(gm_ref, x_ref, vec_ref, attn_ref, share, keep, scratch, gx_ref, gvec_ref, store)
    wait_all(start_copies(packed_ref, outs, sems, 0, packed_ref.shape[3]))


def back_kernel(plan, g_ref, x_ref, mid_ref, vec_ref, attn_ref, up_ref, down_ref, *refs):
    attn_keep, hidden_keep, gx_ref, outs, refs = refs[:4], refs[4:7], refs[7], refs[8:10], refs[10:]
    gm_ref, gvec_ref, go_ref, gh_ref, ga_ref, acc_ref, h_ref, got_ref, n2t_ref, dproj_ref, packed_ref, sems = refs
    gvec_ref[...] = jnp.zeros_like(gvec_ref)
    share = counts_shared().astype(F32)
    store = storer(plan, packed_ref, ALL_KINDS)
    scratch = (go_ref, gh_ref, acc_ref, h_ref, got_ref, n2t_ref)
    backward_hidden(g_ref, mid_ref, vec_ref, up_ref, down_ref, share, hidden_keep, scratch, gm_ref, gvec_ref, store)
    hidden_rows = 2 * plan.zs * plan.thin
    copies = start_copies(packed_ref, outs, sems, 0, hidden_rows)
    scratch = (go_ref, acc_ref, ga_ref, dproj_ref)
    backward_attention(gm_ref, x_ref, vec_ref, attn_ref, share, attn_keep, scratch, gx_ref, gvec_ref, store)
    rest = packed_ref.shape[3] - hidden_rows
    wait_all(start_copies(packed_ref, outs, sems, hidden_rows, rest, copies))


def add_kernel(kept_hidden, got_hidden, kept_attn, got_attn, *out_refs):
    count = kept_hidden.shape[2]
    for i, out_ref in enumerate(out_refs):
        at = (i // 2, i % 2)
        total = kept_hidden[at].astype(F32) + got_hidden[at].astype(F32)
        out_ref[0:count, :] = total.astype(BF16)
        total = kept_attn[at].astype(F32) + got_attn[at].astype(F32)
        out_ref[count:, :] = total.astype(BF16)


def finish_kernel(plan, *refs):
    late, early = refs[0], refs[1 : 1 + plan.zs]
    attn_out, vec_out, up_out, down_out, *tiles = refs[1 + plan.zs :]
    thin, tile, width = plan.thin, plan.tile, plan.width

    count = vec_out.shape[1]
    device = lax.axis_index("dp") * plan.inner + lax.axis_index("mp")
    row = device * count // width
    offset = device * count - row * width
    for layer in range(2):

        def total(start, count, layer=layer):
            at = slice(start, start + count)
            blocks = [early[k][at, :] if layer == 0 else late[k, at, :] for k in range(plan.zs)]
            return sum(block.astype(F32) for block in blocks)

        attn_out[layer] = total(0, thin)
        up_out[layer] = total(thin, thin)
        down_out[layer] = total(2 * thin, thin)
        tiles[layer][...] = total(3 * thin, tile)
        both = jnp.concatenate(
            [tiles[layer][pl.ds(row, 1), :], tiles[layer][pl.ds(row + 1, 1), :]], axis=1
        )
        both = jnp.broadcast_to(both, (8, 2 * width))
        moved = pltpu.roll(both, 2 * width - offset, 1)
        vec_out[layer : layer + 1, :] = moved[0:1, :count]


def place_kernel(own_ref, *refs):
    others, out_ref = refs[:-1], refs[-1]
    rows = own_ref.shape[0] // 2
    kept = out_ref.shape[1]
    mine = lax.axis_index("mp")
    out_ref[mine] = own_ref[0:rows, :].astype(F32)[:kept]
    for i, ref in enumerate(others):
        out_ref[mine ^ (i + 1)] = ref[...].astype(F32)[:kept]
    out_ref[out_ref.shape[0] - 1] = own_ref[rows : 2 * rows, :].astype(F32)[:kept]


def pack_kernel(slot_ref, own_ref, *refs):
    others, out_ref = refs[:-1], refs[-1]
    rows = own_ref.shape[0] // 2
    sources = [own_ref[0:rows, :]] + [ref[...] for ref in others] + [own_ref[rows : 2 * rows, :]]
    step = 256

    def body(index, carry):
        slots = lax.broadcasted_iota(jnp.int32, (step, rows), 0) + index * step
        total = None
        for i, values in enumerate(sources):
            picks = jnp.where(slots == slot_ref[i], 1.0, 0.0).astype(BF16)
            term = dot_nn(picks, values)
            total = term if total is None else total + term
        out_ref[block_rows(index, step), :] = total
        return carry

    lax.fori_loop(0, out_ref.shape[0] // step, body, 0)


VMEM = pl.BlockSpec(memory_space=pltpu.VMEM)
ANY = pl.BlockSpec(memory_space=pl.ANY)


def call(kernel, operands, specs, outs, out_specs, scratch, flops, limit=26):
    return pl.pallas_call(
        kernel,
        out_shape=[jax.ShapeDtypeStruct(shape, dtype) for shape, dtype in outs],
        in_specs=specs,
        out_specs=out_specs,
        scratch_shapes=scratch,
        compiler_params=pltpu.CompilerParams(vmem_limit_bytes=limit << 20),
        cost_estimate=pl.CostEstimate(flops=flops, bytes_accessed=8 << 20, transcendentals=0),
    )(*operands)


@dataclasses.dataclass(frozen=True)
class Plan:
    outer: int
    inner: int
    thin: int
    tile: int
    width: int
    slots: int
    direct: bool

    @property
    def zs(self):
        return self.outer // 2 if self.direct else 1


def flip(array, mask, devices):
    return lax.ppermute(array, ("dp", "mp"), [(d, d ^ mask) for d in range(devices)])


def column_kernel(plan, *refs):
    blocks, out_ref = refs[:-1], refs[-1]
    rows = 3 * plan.thin
    for k, ref in enumerate(blocks):
        out_ref[k * rows : (k + 1) * rows, :] = ref[0:rows, :]
    tail = sum(ref[rows:, :].astype(F32) for ref in blocks)
    out_ref[len(blocks) * rows :, :] = tail.astype(BF16)


def gather_column(plan, block, devices):
    blocks = [block] + [flip(block, 8 * k, devices) for k in range(1, devices // 8)]
    shape = (len(blocks) * 3 * plan.thin + plan.tile, plan.width)
    (column,) = call(
        functools.partial(column_kernel, plan), blocks, [VMEM] * len(blocks), [(shape, BF16)], [VMEM], [], 1 << 20
    )
    return column


def gather_plane(column, devices):
    return [column] + [flip(column, mask, devices) for mask in (2, 4, 6)]


def gather_cores(plane, devices):
    pieces = []
    for piece in plane:
        pieces += [piece, flip(piece, 1, devices)]
    return pieces


def spread(rows, devices):
    across = flip(rows, 2, devices)
    return [flip(rows, 1, devices), across, flip(across, 1, devices)]


def sum_cores(kept, sent, devices):
    got = flip(sent, 1, devices)
    return [(kept[i // 2, i % 2].astype(F32) + got[i // 2, i % 2].astype(F32)).astype(BF16) for i in range(4)]


def plane_kernel(plan, counts, *refs):
    terms, out_refs = [], refs[sum(counts) :]
    for k in range(len(counts)):
        start = sum(counts[:k])
        terms.append(refs[start : start + counts[k]])
    thin, tile = plan.thin, plan.tile
    zs, scratch = plan.zs, out_refs[-1]
    rows = scratch.shape[0]
    total = None
    for parts in terms:
        whole = jnp.concatenate([ref[...].astype(F32) for ref in parts], axis=0)
        total = whole if total is None else total + whole
    scratch[...] = total
    tail = scratch[rows - tile :, :].astype(BF16)
    one = len(out_refs) == 2
    for z in range(zs):
        for kind in range(3):
            at = z if one else coordinates(plan)[0] ^ z
            row = pl.multiple_of((ALL_KINDS.index(kind) * zs + at) * thin, thin)
            block = scratch[pl.ds(row, thin), :].astype(BF16)
            if one:
                out_refs[0][z, kind * thin : (kind + 1) * thin, :] = block
            else:
                out_refs[z][kind * thin : (kind + 1) * thin, :] = block
        if one:
            out_refs[0][z, 3 * thin :, :] = tail
        else:
            out_refs[z][3 * thin :, :] = tail


def sum_plane(plan, sums, devices, relayed):
    rows = sums[0].shape[0]
    if relayed:
        half = rows // 2 // 16 * 16
        own, x_sum, y_sum, both = sums
        x_first, y_first = flip(both[:half], 2, devices), flip(both[half:], 4, devices)

        def joined(one, two):
            return (one.astype(F32) + two.astype(F32)).astype(BF16)

        x_two, y_one = joined(x_sum[half:], y_first), joined(y_sum[:half], x_first)
        x_parts = [flip(x_sum[:half], 2, devices), flip(x_two, 2, devices)]
        y_parts = [flip(y_one, 4, devices), flip(y_sum[half:], 4, devices)]
        terms, counts = [own, *x_parts, *y_parts], (1, 2, 2)
    else:
        terms = [sums[0]] + [flip(one, mask, devices) for one, mask in zip(sums[1:], (2, 4, 6))]
        counts = (1, 1, 1, 1)
    shape = (3 * plan.thin + plan.tile, plan.width)
    outs = [(shape, BF16)] * plan.zs if relayed else [((plan.zs, *shape), BF16)]
    return call(
        functools.partial(plane_kernel, plan, counts),
        terms,
        [VMEM] * len(terms),
        outs,
        [VMEM] * len(outs),
        [pltpu.VMEM((rows, plan.width), F32)],
        1 << 20,
    )


def sum_column(blocks, devices):
    return [one if k == 0 else flip(one, 8 * k, devices) for k, one in enumerate(blocks)]


def shards(patches, targets, keep_mask, attn_weights, vectors, up_weights, down_weights):
    image_count, patch_rows, width = patches.shape
    layers = attn_weights.shape[0]
    dp_size, mp_size = lax.axis_size("dp"), lax.axis_size("mp")
    devices = dp_size * mp_size
    rank = lax.axis_index("mp")
    lane_rank = lax.axis_index("dp")
    device = lane_rank * mp_size + rank
    thin = attn_weights.shape[2]
    vec_rows = vectors.shape[1]
    parts = thin * devices // width
    assert image_count == mp_size + 1 and layers == 2 and parts == mp_size == 4
    direct = thin % 16 == 0
    images, tile = 2, 16
    rows = -(-patch_rows // 16) * 16
    total = images * rows

    keep_rows = jnp.concatenate([jnp.ones((image_count, 2), jnp.int32), keep_mask], axis=1)
    keep_rows = jnp.pad(keep_rows, ((0, 0), (0, rows - patch_rows)))

    attn_turned = attn_weights.transpose(0, 2, 1)
    down_turned = down_weights.transpose(0, 2, 1)
    packing = Plan(dp_size, mp_size, thin, tile, width, SLOTS * dp_size, direct)
    block_shape = ((3 * thin + tile, width), BF16)
    first_block, last_block = call(
        functools.partial(prepare_kernel, packing),
        (attn_turned, up_weights, down_turned, vectors, keep_mask),
        [ANY if direct else VMEM] * 3 + [ANY] * 2,
        [block_shape, block_shape],
        [VMEM, VMEM],
        [
            pltpu.VMEM((8, 2 * width), F32),
            pltpu.VMEM(vectors.shape, BF16),
            pltpu.VMEM(keep_mask.shape, jnp.int32),
            pltpu.SemaphoreType.DMA((8,)),
        ],
        1 << 20,
        60,
    )
    if direct:
        plan = packing
        first_column = gather_column(plan, first_block, devices)
        first_column, last_block = lax.optimization_barrier((first_column, last_block))
        first_plane = gather_plane(first_column, devices)
        last_column = gather_column(plan, last_block, devices)
        first_plane, last_column = lax.optimization_barrier((first_plane, last_column))
        first_pieces = gather_cores(first_plane, devices)
        last_plane = gather_plane(last_column, devices)
    else:
        plan = Plan(1, parts, width, tile, width, SLOTS * dp_size, False)

        def squares(array):
            return array.reshape(parts, width, width)

        def by_part(array):
            split = array.reshape(dp_size, mp_size, thin, width).transpose(1, 0, 2, 3)
            return squares(split)

        def one_tile(array):
            summed = jnp.sum(array.astype(F32), axis=0).astype(BF16)
            return jnp.pad(summed[None], ((0, parts - 1), (0, 0), (0, 0)))

        def normal(block):
            every = lax.all_gather(block, ("dp", "mp"))
            return jnp.concatenate(
                [
                    squares(every[:, :thin]),
                    by_part(every[:, thin : 2 * thin]),
                    by_part(every[:, 2 * thin : 3 * thin]),
                    one_tile(every[:, 3 * thin :]),
                ],
                axis=1,
            )

        first_pieces, last_pieces = [normal(first_block)], [normal(last_block)]

    flat = keep_rows.reshape(-1)
    slot = jnp.where(flat == 1, jnp.cumsum(flat) - flat, SLOTS).reshape(image_count, 1, rows)

    def mine(array):
        return jnp.concatenate(
            [lax.dynamic_slice_in_dim(array, rank, 1, 0), array[mp_size:]], axis=0
        )

    def padded(array):
        return jnp.pad(mine(array), ((0, 0), (0, rows - patch_rows), (0, 0)))

    kept = mine(keep_rows)
    stream = padded(patches).reshape(total, width)
    bias = jnp.where(kept == 1, 0.0, MASKED).astype(F32)[:, None, :]
    goal = jnp.where((kept == 1)[:, :, None], padded(targets), 0).reshape(total, width)
    slots = jnp.concatenate(
        [lax.dynamic_slice_in_dim(slot, rank ^ k, 1, 0) for k in range(mp_size)] + [slot[mp_size:]],
        axis=0,
    )

    stream, slots, goal = lax.optimization_barrier((stream, slots, goal))

    pairs = width // (2 * HD)
    stream_shape = ((total, width), F32)
    low_shape = ((total, width), BF16)
    pair_shape, low_pair_shape = ((2, total, width), F32), ((2, total, width), BF16)
    three_shape = ((3, total, width), BF16)
    turned_shape = ((width, total), BF16)
    vec_shape = ((tile, width), F32)
    attn_keep = [low_shape, three_shape, ((images, pairs, 2 * rows, rows), BF16), low_shape]
    hidden_keep = [low_shape, ((parts, total, width), BF16), ((parts, total, width), F32)]
    blocks = plan.outer * plan.inner
    weight_shape = ((blocks, plan.thin, width), BF16)
    zs = max(blocks // 8, 1)

    def vmem(shapes):
        return [pltpu.VMEM(shape, dtype) for shape, dtype in shapes]

    layer_flops = 8 * total * parts * width * width
    hidden_rows, attn_rows = 2 * plan.thin * zs, plan.thin * zs + tile

    def half(count):
        return ((2, 2, count, width), BF16)

    def both(count):
        return ((2, 2, 2, count, width), BF16)


    def forward(rows_in, pieces, out_shape):
        results = call(
            functools.partial(forward_kernel, plan, len(pieces)),
            (rows_in, bias, *pieces),
            [VMEM] * (2 + len(pieces)),
            [weight_shape, weight_shape, weight_shape, vec_shape, stream_shape, out_shape]
            + attn_keep
            + hidden_keep,
            [VMEM] * 13,
            vmem([pair_shape, stream_shape]),
            layer_flops,
        )
        return (*results[:6], results[6:10], results[10:])

    attn_full, up_full, down_full, vec, mid, middle, attn_kept, hidden_kept = forward(
        stream, first_pieces, stream_shape
    )
    if direct:
        middle, last_plane = lax.optimization_barrier((middle, last_plane))
        last_pieces = gather_cores(last_plane, devices)
    sems = [pltpu.SemaphoreType.DMA((4,))]
    last_attn, last_up, last_down, last_vec, last_mid, output, last_kept, last_hidden_kept = forward(
        middle, last_pieces, low_shape
    )
    last_mid_grad, last_gvec, *last_hidden = call(
        functools.partial(last_hidden_kernel, plan),
        (goal, last_mid, last_vec, last_up, last_down, *last_hidden_kept),
        [VMEM] * 8,
        [stream_shape, vec_shape, half(hidden_rows), half(hidden_rows)],
        [VMEM] * 2 + [ANY] * 2,
        vmem(
            [stream_shape, low_shape, low_pair_shape, stream_shape, pair_shape]
            + [turned_shape, turned_shape, both(hidden_rows)]
        )
        + sems,
        layer_flops,
    )
    across = flip(output[:rows], 2, devices)
    last_mid_grad, last_gvec, last_hidden, across, output = lax.optimization_barrier(
        (last_mid_grad, last_gvec, last_hidden, across, output)
    )
    grad_middle, *last_attention = call(
        functools.partial(last_attention_kernel, plan),
        (last_mid_grad, middle, last_vec, last_attn, last_gvec, *last_kept),
        [VMEM] * 9,
        [stream_shape, half(attn_rows), half(attn_rows)],
        [VMEM, ANY, ANY],
        vmem([vec_shape, low_shape, stream_shape, low_shape, three_shape, both(attn_rows)]) + sems,
        layer_flops,
    )
    output_pieces = [flip(output[:rows], 1, devices), across, flip(across, 1, devices)]
    if direct:
        terms = []
        for kept_half, sent_half in (last_hidden, last_attention):
            terms += [kept_half, flip(sent_half, 1, devices)]
        message = ((hidden_rows + attn_rows, width), BF16)
        last_sums = call(add_kernel, terms, [VMEM] * 4, [message] * 4, [VMEM] * 4, [], 1 << 20)
        grad_middle, last_sums, output_pieces = lax.optimization_barrier(
            (grad_middle, last_sums, output_pieces)
        )
    grad_first, *first_halves = call(
        functools.partial(back_kernel, plan),
        (grad_middle, stream, mid, vec, attn_full, up_full, down_full, *attn_kept, *hidden_kept),
        [VMEM] * 14,
        [low_shape, half(hidden_rows + attn_rows), half(hidden_rows + attn_rows)],
        [VMEM, ANY, ANY],
        vmem(
            [stream_shape, vec_shape, low_shape, low_pair_shape, low_shape, stream_shape, pair_shape]
            + [turned_shape, turned_shape, three_shape, both(hidden_rows + attn_rows)]
        )
        + sems,
        3 * layer_flops,
    )

    def pack_output(output, output_pieces):
        (activations,) = call(
            pack_kernel,
            (slots, output, *output_pieces),
            [VMEM] * (mp_size + 1),
            [((SLOTS, width), F32)],
            [VMEM],
            [],
            2 * SLOTS * image_count * rows * width,
        )
        return activations

    def place_grads(grad_first, grad_pieces):
        (input_grads,) = call(
            place_kernel,
            (grad_first, *grad_pieces),
            [VMEM] * mp_size,
            [((image_count, patch_rows, width), F32)],
            [VMEM],
            [],
            image_count * patch_rows * width,
        )
        return input_grads

    if direct:
        (last_total,) = sum_plane(plan, last_sums, devices, False)
        activations = pack_output(output, output_pieces)
        last_total, first_halves, grad_first, activations = lax.optimization_barrier(
            (last_total, first_halves, grad_first, activations)
        )
        last_terms = last_total
        if plan.zs > 1:
            columns = [[8 * z + at for z in range(plan.zs)] for at in range(8)]
            last_terms = lax.all_to_all(
                last_total, ("dp", "mp"), 0, 0, axis_index_groups=columns, tiled=True
            )
        across = flip(grad_first[:rows], 2, devices)
        first_sums = sum_cores(*first_halves, devices)
        first_total = sum_plane(plan, first_sums, devices, True)
        beside = flip(grad_first[:rows], 1, devices)
        input_grads = place_grads(grad_first, [beside, across, flip(across, 1, devices)])
        first_total, last_terms, input_grads = lax.optimization_barrier(
            (first_total, last_terms, input_grads)
        )
        first_terms = sum_column(first_total, devices)
        terms = (last_terms, *first_terms)
        turned = (layers, thin, width)
        attn_grads, vector_grads, up_grads, down_grads = call(
            functools.partial(finish_kernel, plan),
            terms,
            [VMEM] * len(terms),
            [(turned, F32), (vectors.shape, F32), (turned, F32), (turned, F32)],
            [VMEM] * 4,
            vmem([vec_shape, vec_shape]),
            1 << 20,
        )
        attn_grads, down_grads = attn_grads.transpose(0, 2, 1), down_grads.transpose(0, 2, 1)
    else:
        last_halves = [
            jnp.concatenate(halves, axis=2) for halves in zip(last_hidden, last_attention)
        ]

        def square_blocks(halves):
            stacked = jnp.stack(halves)[:, 0]
            stacked = jnp.stack([stacked[k % 2, k // 2] for k in range(parts)])
            return jnp.stack(
                [lax.dynamic_index_in_dim(stacked, rank ^ k, 0, False) for k in range(parts)]
            )

        def outputs_of(halves):
            def by_owner(array):
                split = array.reshape(mp_size, dp_size, thin, width).transpose(1, 0, 2, 3)
                return split.reshape(devices, thin, width)

            every = square_blocks(halves)
            pieces = [
                every[:, 2 * width : 3 * width].reshape(devices, thin, width),
                by_owner(every[:, :width]),
                by_owner(every[:, width : 2 * width]),
                jnp.broadcast_to(every[0, 3 * width :], (devices, tile, width)),
            ]
            owned = lax.psum_scatter(
                jnp.concatenate(pieces, axis=1), ("dp", "mp"), scatter_dimension=0, tiled=False
            ).astype(F32)
            own_vec = lax.dynamic_slice_in_dim(
                owned[3 * thin :].reshape(-1), device * vec_rows, vec_rows
            )
            return owned[:thin].T, own_vec, owned[thin : 2 * thin], owned[2 * thin : 3 * thin].T

        attn_grads, vector_grads, up_grads, down_grads = (
            jnp.stack([one, two]) for one, two in zip(outputs_of(first_halves), outputs_of(last_halves))
        )
        activations = pack_output(output, output_pieces)
        input_grads = place_grads(grad_first, spread(grad_first[:rows], devices))

    return (activations, input_grads, attn_grads, vector_grads, up_grads, down_grads)


def solution(mesh):
    in_specs = (
        P("dp", None, None),
        P("dp", None, None),
        P("dp", None),
        P(None, None, ("dp", "mp")),
        P(None, ("dp", "mp")),
        P(None, "dp", "mp"),
        P(None, "mp", "dp"),
    )
    out_specs = (
        P("dp", None),
        P("dp", None, None),
        P(None, None, ("dp", "mp")),
        P(None, ("dp", "mp")),
        P(None, "dp", "mp"),
        P(None, "mp", "dp"),
    )
    return jax.shard_map(shards, mesh=mesh, in_specs=in_specs, out_specs=out_specs, check_vma=False)
```

```python
import dataclasses
import functools

import jax
import jax.numpy as jnp
from jax import lax
from jax.experimental import pallas as pl
from jax.experimental.pallas import tpu as pltpu
from jax.sharding import PartitionSpec as P

HD = 64
SLOTS = 1024
EPSILON = 1e-06
MASKED = -1e30
STEP = 16

F32 = jnp.float32
BF16 = jnp.bfloat16


def dot_nn(left, right):
    return lax.dot_general(left, right, (((1,), (0,)), ((), ())), preferred_element_type=F32)


def dot_nt(left, right):
    return lax.dot_general(left, right, (((1,), (1,)), ((), ())), preferred_element_type=F32)


def dot_tn(left, right):
    return lax.dot_general(left, right, (((0,), (0,)), ((), ())), preferred_element_type=F32)


def block_rows(index, step):
    return pl.ds(pl.multiple_of(index * step, step), step)


def fold_rows(values):
    return jnp.sum(values.reshape(values.shape[0] // 8, 8, values.shape[1]), axis=0)


def low_halves(rows):
    lane = lax.broadcasted_iota(jnp.int32, (rows, 2 * HD), 1)
    return lane < HD


def stack_heads(pair):
    low = low_halves(pair.shape[0])
    zero = jnp.zeros_like(pair)
    return jnp.concatenate([jnp.where(low, pair, zero), jnp.where(low, zero, pair)], axis=0)


def unstack_heads(stacked):
    rows = stacked.shape[0] // 2
    return jnp.where(low_halves(rows), stacked[:rows], stacked[rows:])


def norm_rows(x_ref, out_ref, gain, shift):
    def body(index, carry):
        at = block_rows(index, STEP)
        values = x_ref[at, :].astype(F32)
        centred = values - jnp.mean(values, axis=-1, keepdims=True)
        variance = jnp.mean(centred * centred, axis=-1, keepdims=True)
        out_ref[at, :] = (centred * lax.rsqrt(variance + EPSILON) * gain + shift).astype(BF16)
        return carry

    lax.fori_loop(0, x_ref.shape[0] // STEP, body, 0, unroll=True)


def norm_back(x_ref, grad_ref, base_ref, out_ref, low_ref, gain, images):
    rows = x_ref.shape[0] // images
    width = x_ref.shape[1]
    sums = []
    for image in range(images):

        def body(index, carry, image=image):
            at = pl.ds(pl.multiple_of(image * rows + index * STEP, STEP), STEP)
            values = x_ref[at, :].astype(F32)
            grad = grad_ref[at, :]
            centred = values - jnp.mean(values, axis=-1, keepdims=True)
            variance = jnp.mean(centred * centred, axis=-1, keepdims=True)
            inverse = lax.rsqrt(variance + EPSILON)
            unit = centred * inverse
            scaled = grad * gain
            mean_one = jnp.mean(scaled, axis=-1, keepdims=True)
            mean_two = jnp.mean(scaled * unit, axis=-1, keepdims=True)
            out = base_ref[at, :] + inverse * (scaled - mean_one - unit * mean_two)
            out_ref[at, :] = out.astype(out_ref.dtype)
            if low_ref is not None:
                low_ref[at, :] = out.astype(BF16)
            return (
                carry[0] + fold_rows(grad * unit),
                carry[1] + fold_rows(grad),
                carry[2] + fold_rows(out),
            )

        zero = jnp.zeros((8, width), F32)
        sums.append(lax.fori_loop(0, rows // STEP, body, (zero, zero, zero), unroll=True))
    return sums


def weigh(sums, share):
    total = sums[0]
    for more in sums[1:]:
        total = total + more * share
    return jnp.sum(total, axis=0, keepdims=True)


def as_square(ref, part):
    rows, width = ref.shape[1:]
    per = width // rows
    return ref[pl.ds(part * per, per)].reshape(width, width)


def forward_attention(x_ref, bias_ref, vec_ref, attn_ref, keep, mid_ref):
    n1_ref, proj_ref, p_ref, att_ref = keep
    images = bias_ref.shape[0]
    rows = x_ref.shape[0] // images
    width = x_ref.shape[1]
    pairs = width // (2 * HD)
    scale = HD**-0.5

    norm_rows(x_ref, n1_ref, vec_ref[0:1, :], vec_ref[1:2, :])
    for part, bias_row in enumerate((4, None, 5)):
        value = dot_nt(n1_ref[...], as_square(attn_ref, part))
        if bias_row is not None:
            value = value + vec_ref[bias_row : bias_row + 1, :]
        proj_ref[part] = value.astype(BF16)

    def image_body(image, carry):
        at = block_rows(image, rows)
        for pair in range(pairs):
            lanes = slice(pair * 2 * HD, (pair + 1) * 2 * HD)
            query = stack_heads(proj_ref[0, at, lanes])
            scores = dot_nt(query, proj_ref[1, at, lanes]) * scale + bias_ref[image]
            top = jnp.max(scores, axis=-1, keepdims=True)
            powers = jnp.exp(scores - top)
            total = jnp.sum(powers, axis=-1, keepdims=True)
            probs = (powers * (1.0 / total)).astype(BF16)
            p_ref[image, pair] = probs
            att_ref[at, lanes] = unstack_heads(dot_nn(probs, proj_ref[2, at, lanes])).astype(BF16)
        return carry

    for image in range(images):
        image_body(image, 0)
    mid_ref[...] = x_ref[...].astype(F32) + dot_nt(att_ref[...], as_square(attn_ref, 3)) + vec_ref[6:7, :]


def forward_hidden(mid_ref, vec_ref, up_ref, down_ref, keep, scratch, out_ref):
    n2_ref, a_ref, gp_ref = keep
    h_ref, acc_ref = scratch
    norm_rows(mid_ref, n2_ref, vec_ref[2:3, :], vec_ref[3:4, :])
    acc_ref[...] = mid_ref[...] + vec_ref[11:12, :]

    def part_body(part, carry):
        h_ref[part % 2] = dot_nn(n2_ref[...], as_square(up_ref, part))
        bias = vec_ref[pl.ds(7 + part, 1), :]

        def gelu_body(index, inner):
            at = block_rows(index, STEP)
            hidden = h_ref[part % 2, at, :] + bias
            share = 0.5 + 0.5 * lax.erf(hidden * 0.7071067811865476)
            a_ref[part, at, :] = (hidden * share).astype(BF16)
            bell = jnp.exp(-0.5 * hidden * hidden) * 0.3989422804014327
            gp_ref[part, at, :] = (share + hidden * bell).astype(gp_ref.dtype)
            return inner

        lax.fori_loop(0, h_ref.shape[1] // STEP, gelu_body, 0, unroll=True)
        acc_ref[...] += dot_nt(a_ref[part], as_square(down_ref, part))
        return carry

    for part in range(a_ref.shape[0]):
        part_body(part, 0)
    out_ref[...] = acc_ref[...].astype(out_ref.dtype)


def drop_shared(refs):
    @pl.when(jnp.logical_not(counts_shared()))
    def _():
        for ref in refs:
            rows = ref.shape[-2] // 2
            ref[..., rows:, :] = jnp.zeros((*ref.shape[:-2], rows, ref.shape[-1]), ref.dtype)


def backward_hidden(g_ref, mid_ref, vec_ref, up_ref, down_ref, share, keep, scratch, gm_ref, gvec_ref, store):
    n2_ref, a_ref, gp_ref = keep
    go_ref, gh_ref, acc_ref, h_ref, got_ref, n2t_ref = scratch
    images = 2
    rows = mid_ref.shape[0] // images
    width = mid_ref.shape[1]
    zero = jnp.zeros((8, width), F32)
    sums = []
    for image in range(images):

        def low_body(index, carry, image=image):
            at = pl.ds(pl.multiple_of(image * rows + index * STEP, STEP), STEP)
            grad = g_ref[at, :]
            go_ref[at, :] = grad.astype(BF16)
            return carry + fold_rows(grad)

        sums.append(lax.fori_loop(0, rows // STEP, low_body, zero, unroll=True))
    gvec_ref[11:12, :] = weigh(sums, share)
    acc_ref[...] = jnp.zeros_like(acc_ref)
    got_ref[...] = go_ref[...].T
    n2t_ref[...] = n2_ref[...].T

    def part_body(part, carry):
        store(2, part, dot_nn(got_ref[...], a_ref[part]))
        h_ref[part % 2] = dot_nn(go_ref[...], as_square(down_ref, part))
        inner_sums = []
        for image in range(images):

            def hidden_body(index, inner, image=image):
                at = pl.ds(pl.multiple_of(image * rows + index * STEP, STEP), STEP)
                grad = (h_ref[part % 2, at, :] * gp_ref[part, at, :].astype(F32)).astype(BF16)
                gh_ref[part % 2, at, :] = grad
                return inner + fold_rows(grad.astype(F32))

            inner_sums.append(lax.fori_loop(0, rows // STEP, hidden_body, zero, unroll=True))
        gvec_ref[pl.ds(7 + part, 1), :] = weigh(inner_sums, share)
        store(1, part, dot_nn(n2t_ref[...], gh_ref[part % 2]))
        acc_ref[...] += dot_nt(gh_ref[part % 2], as_square(up_ref, part))
        return carry

    for part in range(a_ref.shape[0]):
        part_body(part, 0)
    sums = norm_back(mid_ref, acc_ref, g_ref, gm_ref, None, vec_ref[2:3, :], images)
    for place, row in enumerate((2, 3, 6)):
        gvec_ref[row : row + 1, :] = weigh([one[place] for one in sums], share)


def backward_attention(gm_ref, x_ref, vec_ref, attn_ref, share, keep, scratch, gx_ref, gvec_ref, store):
    n1_ref, proj_ref, p_ref, att_ref = keep
    go_ref, acc_ref, ga_ref, dproj_ref = scratch
    images = p_ref.shape[0]
    rows = x_ref.shape[0] // images
    width = x_ref.shape[1]
    pairs = width // (2 * HD)
    scale = HD**-0.5
    go_ref[...] = gm_ref[...].astype(BF16)
    store(0, 3, dot_tn(go_ref[...], att_ref[...]))
    ga_ref[...] = dot_nn(go_ref[...], as_square(attn_ref, 3)).astype(BF16)

    def image_body(image, carry):
        at = block_rows(image, rows)
        for pair in range(pairs):
            lanes = slice(pair * 2 * HD, (pair + 1) * 2 * HD)
            query = stack_heads(proj_ref[0, at, lanes])
            keys = proj_ref[1, at, lanes]
            grad_out = stack_heads(ga_ref[at, lanes])
            probs = p_ref[image, pair]
            grad_probs = dot_nt(grad_out, proj_ref[2, at, lanes])
            dproj_ref[2, at, lanes] = dot_tn(probs, grad_out).astype(BF16)
            wide = probs.astype(F32)
            inner = jnp.sum(grad_probs * wide, axis=-1, keepdims=True)
            grad_scores = (wide * (grad_probs - inner)).astype(BF16)
            dproj_ref[0, at, lanes] = (unstack_heads(dot_nn(grad_scores, keys)) * scale).astype(BF16)
            dproj_ref[1, at, lanes] = (dot_tn(grad_scores, query) * scale).astype(BF16)
        return carry

    for image in range(images):
        image_body(image, 0)
    for part, row in enumerate((4, None, 5)):
        store(0, part, dot_tn(dproj_ref[part], n1_ref[...]))
        value = dot_nn(dproj_ref[part], as_square(attn_ref, part))
        if part == 0:
            acc_ref[...] = value
        else:
            acc_ref[...] += value
        if row is not None:
            sums = [
                fold_rows(dproj_ref[part, image * rows : (image + 1) * rows, :].astype(F32))
                for image in range(images)
            ]
            gvec_ref[row : row + 1, :] = weigh(sums, share)
    sums = norm_back(x_ref, acc_ref, gm_ref, gx_ref, None, vec_ref[0:1, :], images)
    for place, row in enumerate((0, 1)):
        gvec_ref[row : row + 1, :] = weigh([one[place] for one in sums], share)
    store(3, 0, gvec_ref[...])


def coordinates(plan):
    outer, inner = lax.axis_index("dp"), lax.axis_index("mp")
    here = (inner // 2, inner % 2)
    return (outer // 2, outer % 2, *here) if plan.direct else (0, 0, *here)


def counts_shared():
    return lax.axis_index("mp") == 0


def place_weights(plan, pieces, attn_ref, up_ref, down_ref, vec_ref):
    thin, rows = plan.thin, 3 * plan.thin

    def put(owner, block):
        at = owner % plan.inner * plan.outer + owner // plan.inner
        attn_ref[owner] = block[:thin]
        up_ref[at] = block[thin : 2 * thin]
        down_ref[at] = block[2 * thin : 3 * thin]

    if not plan.direct:
        for owner in range(plan.inner):
            put(owner, pieces[0][owner, :rows])
        vec_ref[...] = pieces[0][0, rows:].astype(F32)
        return
    at = coordinates(plan)
    vec = None
    for i, piece in enumerate(pieces):
        c, x, y = i % 2, i // 2 % 2, i // 4
        low = ((at[1] ^ y) * 2 + (at[2] ^ x)) * 2 + (at[3] ^ c)
        count = piece.shape[0] // rows
        for k in range(count):
            put((at[0] ^ k) * 8 + low, piece[k * rows : (k + 1) * rows])
        tail = piece[count * rows :].astype(F32)
        vec = tail if vec is None else vec + tail
    vec_ref[...] = vec


def storer(plan, packed_ref, kinds):
    thin, width = plan.thin, plan.width
    per = width // thin
    here = coordinates(plan)

    def put(owner, kind, block):
        c, x, y = owner % 2, owner // 2 % 2, owner // 4 % 2
        row = pl.multiple_of((kinds.index(kind) * plan.zs + owner // 8) * thin, thin)
        packed_ref[c ^ here[3], y ^ here[1], x ^ here[2], pl.ds(row, thin), :] = block

    def store(kind, part, value):
        low = value.astype(BF16)
        if kind == 3:
            for i in range(8):
                packed_ref[i % 2, i // 4, i // 2 % 2, len(kinds) * plan.zs * thin :, :] = low
            return
        blocks = low.reshape(per, thin, width)
        for i in range(per):
            owner = part * per + i if kind == 0 else i * plan.inner + part
            put(owner, kind, blocks[i])

    return store


def start_copies(packed_ref, outs, sems, start, count, before=()):
    at = pl.ds(start, count)
    copies = list(before)
    for i in range(2):
        source, target = packed_ref.at[i, :, :, at], outs[i].at[:, :, at]
        copies.append(pltpu.make_async_copy(source, target, sems.at[len(copies)]))
        copies[-1].start()
    return copies


def wait_all(copies):
    for one in copies:
        one.wait()


def prepare_kernel(plan, attn_ref, up_ref, down_ref, vec_in, keep_in, first_ref, last_ref, line_ref, vec_ref, keep_ref, sems):
    thin, tile, width = plan.thin, plan.tile, plan.width
    outs = (first_ref, last_ref)
    copies = [
        pltpu.make_async_copy(vec_in, vec_ref, sems.at[0]),
        pltpu.make_async_copy(keep_in, keep_ref, sems.at[1]),
    ]
    for kind, ref in enumerate((attn_ref, up_ref, down_ref)):
        for layer, out_ref in enumerate(outs):
            if plan.direct:
                target = out_ref.at[pl.ds(kind * thin, thin)]
                copies.append(pltpu.make_async_copy(ref.at[layer], target, sems.at[len(copies)]))
            else:
                out_ref[kind * thin : (kind + 1) * thin, :] = ref[layer]
    for one in copies:
        one.start()
    count = vec_ref.shape[1]
    device = lax.axis_index("dp") * plan.inner + lax.axis_index("mp")
    row_at = device * count // width
    offset = device * count - row_at * width
    copies[0].wait()
    copies[1].wait()
    kept = jnp.sum(keep_ref[...]) + 2 * keep_ref.shape[0]
    kept = jnp.where(counts_shared(), kept, 0)
    row = lax.broadcasted_iota(jnp.int32, (tile, width), 0)
    here = lax.broadcasted_iota(jnp.int32, (tile, width), 1) == lax.axis_index("dp")
    for layer, out_ref in enumerate(outs):
        line_ref[...] = jnp.zeros_like(line_ref)
        line_ref[0:1, 0:count] = vec_ref[layer : layer + 1, :].astype(F32)
        moved = pltpu.roll(line_ref[...], offset, 1)[0:1]
        piece = jnp.where(row == row_at, moved[:, :width], 0.0)
        piece = jnp.where(row == row_at + 1, moved[:, width:], piece)
        if layer == 1:
            piece = jnp.where(here & (row == 12), (kept >> 5).astype(F32), piece)
            piece = jnp.where(here & (row == 13), (kept & 31).astype(F32), piece)
        out_ref[3 * thin :, :] = piece.astype(BF16)
    for one in copies[2:]:
        one.wait()


def forward_kernel(plan, pieces, x_ref, bias_ref, *refs):
    sources, refs = refs[:pieces], refs[pieces:]
    attn_ref, up_ref, down_ref, vec_ref, mid_ref, out_ref, *refs = refs
    attn_keep, hidden_keep, (h_ref, acc_ref) = refs[:4], refs[4:7], refs[7:]
    place_weights(plan, sources, attn_ref, up_ref, down_ref, vec_ref)
    forward_attention(x_ref, bias_ref, vec_ref, attn_ref, attn_keep, mid_ref)
    forward_hidden(mid_ref, vec_ref, up_ref, down_ref, hidden_keep, (h_ref, acc_ref), out_ref)
    drop_shared((attn_keep[0], attn_keep[3], hidden_keep[0], hidden_keep[1]))


HIDDEN_KINDS, ATTENTION_KINDS, ALL_KINDS = (1, 2), (0,), (1, 2, 0)


def last_hidden_kernel(plan, goal_ref, mid_ref, vec_ref, up_ref, down_ref, *refs):
    keep, gm_ref, gvec_ref, outs, refs = refs[:3], refs[3], refs[4], refs[5:7], refs[7:]
    g_ref, go_ref, gh_ref, acc_ref, h_ref, got_ref, n2t_ref, packed_ref, sems = refs
    high = jnp.sum(vec_ref[12:13, :], axis=-1, keepdims=True)
    rest = jnp.sum(vec_ref[13:14, :], axis=-1, keepdims=True)
    loss_scale = float(plan.slots) / (high * 32.0 + rest)
    g_ref[...] = goal_ref[...].astype(F32) * loss_scale
    gvec_ref[...] = jnp.zeros_like(gvec_ref)
    share = counts_shared().astype(F32)
    store = storer(plan, packed_ref, HIDDEN_KINDS)
    scratch = (go_ref, gh_ref, acc_ref, h_ref, got_ref, n2t_ref)
    backward_hidden(g_ref, mid_ref, vec_ref, up_ref, down_ref, share, keep, scratch, gm_ref, gvec_ref, store)
    wait_all(start_copies(packed_ref, outs, sems, 0, packed_ref.shape[3]))


def last_attention_kernel(plan, gm_ref, x_ref, vec_ref, attn_ref, early_ref, *refs):
    keep, gx_ref, outs, refs = refs[:4], refs[4], refs[5:7], refs[7:]
    gvec_ref, go_ref, acc_ref, ga_ref, dproj_ref, packed_ref, sems = refs
    gvec_ref[...] = early_ref[...]
    share = counts_shared().astype(F32)
    store = storer(plan, packed_ref, ATTENTION_KINDS)
    scratch = (go_ref, acc_ref, ga_ref, dproj_ref)
    backward_attention(gm_ref, x_ref, vec_ref, attn_ref, share, keep, scratch, gx_ref, gvec_ref, store)
    wait_all(start_copies(packed_ref, outs, sems, 0, packed_ref.shape[3]))


def back_kernel(plan, g_ref, x_ref, mid_ref, vec_ref, attn_ref, up_ref, down_ref, *refs):
    attn_keep, hidden_keep, gx_ref, outs, refs = refs[:4], refs[4:7], refs[7], refs[8:10], refs[10:]
    gm_ref, gvec_ref, go_ref, gh_ref, ga_ref, acc_ref, h_ref, got_ref, n2t_ref, dproj_ref, packed_ref, sems = refs
    gvec_ref[...] = jnp.zeros_like(gvec_ref)
    share = counts_shared().astype(F32)
    store = storer(plan, packed_ref, ALL_KINDS)
    scratch = (go_ref, gh_ref, acc_ref, h_ref, got_ref, n2t_ref)
    backward_hidden(g_ref, mid_ref, vec_ref, up_ref, down_ref, share, hidden_keep, scratch, gm_ref, gvec_ref, store)
    hidden_rows = 2 * plan.zs * plan.thin
    copies = start_copies(packed_ref, outs, sems, 0, hidden_rows)
    scratch = (go_ref, acc_ref, ga_ref, dproj_ref)
    backward_attention(gm_ref, x_ref, vec_ref, attn_ref, share, attn_keep, scratch, gx_ref, gvec_ref, store)
    rest = packed_ref.shape[3] - hidden_rows
    wait_all(start_copies(packed_ref, outs, sems, hidden_rows, rest, copies))


def add_kernel(kept_hidden, got_hidden, kept_attn, got_attn, *out_refs):
    count = kept_hidden.shape[2]
    for i, out_ref in enumerate(out_refs):
        at = (i // 2, i % 2)
        total = kept_hidden[at].astype(F32) + got_hidden[at].astype(F32)
        out_ref[0:count, :] = total.astype(BF16)
        total = kept_attn[at].astype(F32) + got_attn[at].astype(F32)
        out_ref[count:, :] = total.astype(BF16)


def finish_kernel(plan, count_of, *refs):
    layers = (refs[:count_of], refs[count_of : 2 * count_of])
    attn_out, vec_out, up_out, down_out, *tiles = refs[2 * count_of :]
    thin, tile, width = plan.thin, plan.tile, plan.width

    count = vec_out.shape[1]
    device = lax.axis_index("dp") * plan.inner + lax.axis_index("mp")
    row = device * count // width
    offset = device * count - row * width
    for layer in range(2):

        def total(start, count, layer=layer):
            return sum(ref[start : start + count, :].astype(F32) for ref in layers[layer])

        attn_out[layer] = total(0, thin)
        up_out[layer] = total(thin, thin)
        down_out[layer] = total(2 * thin, thin)
        tiles[layer][...] = total(3 * thin, tile)
        both = jnp.concatenate(
            [tiles[layer][pl.ds(row, 1), :], tiles[layer][pl.ds(row + 1, 1), :]], axis=1
        )
        both = jnp.broadcast_to(both, (8, 2 * width))
        moved = pltpu.roll(both, 2 * width - offset, 1)
        vec_out[layer : layer + 1, :] = moved[0:1, :count]


def place_kernel(own_ref, *refs):
    others, out_ref = refs[:-1], refs[-1]
    rows = own_ref.shape[0] // 2
    kept = out_ref.shape[1]
    mine = lax.axis_index("mp")
    out_ref[mine] = own_ref[0:rows, :].astype(F32)[:kept]
    for i, ref in enumerate(others):
        out_ref[mine ^ (i + 1)] = ref[...].astype(F32)[:kept]
    out_ref[out_ref.shape[0] - 1] = own_ref[rows : 2 * rows, :].astype(F32)[:kept]


def pack_kernel(slot_ref, own_ref, *refs):
    others, out_ref = refs[:-1], refs[-1]
    rows = own_ref.shape[0] // 2
    sources = [own_ref[0:rows, :]] + [ref[...] for ref in others] + [own_ref[rows : 2 * rows, :]]
    step = 256

    def body(index, carry):
        slots = lax.broadcasted_iota(jnp.int32, (step, rows), 0) + index * step
        total = None
        for i, values in enumerate(sources):
            picks = jnp.where(slots == slot_ref[i], 1.0, 0.0).astype(BF16)
            term = dot_nn(picks, values)
            total = term if total is None else total + term
        out_ref[block_rows(index, step), :] = total
        return carry

    lax.fori_loop(0, out_ref.shape[0] // step, body, 0)


VMEM = pl.BlockSpec(memory_space=pltpu.VMEM)
ANY = pl.BlockSpec(memory_space=pl.ANY)


def call(kernel, operands, specs, outs, out_specs, scratch, flops, limit=26):
    return pl.pallas_call(
        kernel,
        out_shape=[jax.ShapeDtypeStruct(shape, dtype) for shape, dtype in outs],
        in_specs=specs,
        out_specs=out_specs,
        scratch_shapes=scratch,
        compiler_params=pltpu.CompilerParams(vmem_limit_bytes=limit << 20),
        cost_estimate=pl.CostEstimate(flops=flops, bytes_accessed=8 << 20, transcendentals=0),
    )(*operands)


@dataclasses.dataclass(frozen=True)
class Plan:
    outer: int
    inner: int
    thin: int
    tile: int
    width: int
    slots: int
    direct: bool

    @property
    def zs(self):
        return self.outer // 2 if self.direct else 1


def flip(array, mask, devices):
    return lax.ppermute(array, ("dp", "mp"), [(d, d ^ mask) for d in range(devices)])


def column_kernel(plan, *refs):
    blocks, out_ref = refs[:-1], refs[-1]
    rows = 3 * plan.thin
    for k, ref in enumerate(blocks):
        out_ref[k * rows : (k + 1) * rows, :] = ref[0:rows, :]
    tail = sum(ref[rows:, :].astype(F32) for ref in blocks)
    out_ref[len(blocks) * rows :, :] = tail.astype(BF16)


def gather_column(plan, block, devices):
    blocks = [block] + [flip(block, 8 * k, devices) for k in range(1, devices // 8)]
    shape = (len(blocks) * 3 * plan.thin + plan.tile, plan.width)
    (column,) = call(
        functools.partial(column_kernel, plan), blocks, [VMEM] * len(blocks), [(shape, BF16)], [VMEM], [], 1 << 20
    )
    return column


def gather_plane(column, devices):
    return [column] + [flip(column, mask, devices) for mask in (2, 4, 6)]


def gather_cores(plane, devices):
    pieces = []
    for piece in plane:
        pieces += [piece, flip(piece, 1, devices)]
    return pieces


def spread(rows, devices):
    across = flip(rows, 2, devices)
    return [flip(rows, 1, devices), across, flip(across, 1, devices)]


def sum_cores(kept, sent, devices):
    got = flip(sent, 1, devices)
    return [(kept[i // 2, i % 2].astype(F32) + got[i // 2, i % 2].astype(F32)).astype(BF16) for i in range(4)]


def plane_kernel(plan, *refs):
    terms, out_refs = refs[:4], refs[4:]
    thin, tile = plan.thin, plan.tile
    zs = len(out_refs)

    def added(start, count):
        return sum(ref[pl.ds(start, count), :].astype(F32) for ref in terms).astype(BF16)

    tail = added(3 * zs * thin, tile)
    for z, out_ref in enumerate(out_refs):
        for kind in range(3):
            row = (ALL_KINDS.index(kind) * zs + (coordinates(plan)[0] ^ z)) * thin
            out_ref[kind * thin : (kind + 1) * thin, :] = added(pl.multiple_of(row, thin), thin)
        out_ref[3 * thin :, :] = tail


def sum_plane(plan, sums, devices):
    zs = devices // 8
    terms = [sums[0]] + [flip(one, mask, devices) for one, mask in zip(sums[1:], (2, 4, 6))]
    outs = [((3 * plan.thin + plan.tile, plan.width), BF16)] * zs
    return call(
        functools.partial(plane_kernel, plan), terms, [VMEM] * 4, outs, [VMEM] * zs, [], 1 << 20
    )


def sum_column(blocks, devices):
    return [one if k == 0 else flip(one, 8 * k, devices) for k, one in enumerate(blocks)]


def shards(patches, targets, keep_mask, attn_weights, vectors, up_weights, down_weights):
    image_count, patch_rows, width = patches.shape
    layers = attn_weights.shape[0]
    dp_size, mp_size = lax.axis_size("dp"), lax.axis_size("mp")
    devices = dp_size * mp_size
    rank = lax.axis_index("mp")
    lane_rank = lax.axis_index("dp")
    device = lane_rank * mp_size + rank
    thin = attn_weights.shape[2]
    vec_rows = vectors.shape[1]
    parts = thin * devices // width
    assert image_count == mp_size + 1 and layers == 2 and parts == mp_size == 4
    direct = thin % 16 == 0
    images, tile = 2, 16
    rows = -(-patch_rows // 16) * 16
    total = images * rows

    keep_rows = jnp.concatenate([jnp.ones((image_count, 2), jnp.int32), keep_mask], axis=1)
    keep_rows = jnp.pad(keep_rows, ((0, 0), (0, rows - patch_rows)))

    attn_turned = attn_weights.transpose(0, 2, 1)
    down_turned = down_weights.transpose(0, 2, 1)
    packing = Plan(dp_size, mp_size, thin, tile, width, SLOTS * dp_size, direct)
    block_shape = ((3 * thin + tile, width), BF16)
    first_block, last_block = call(
        functools.partial(prepare_kernel, packing),
        (attn_turned, up_weights, down_turned, vectors, keep_mask),
        [ANY if direct else VMEM] * 3 + [ANY] * 2,
        [block_shape, block_shape],
        [VMEM, VMEM],
        [
            pltpu.VMEM((8, 2 * width), F32),
            pltpu.VMEM(vectors.shape, BF16),
            pltpu.VMEM(keep_mask.shape, jnp.int32),
            pltpu.SemaphoreType.DMA((8,)),
        ],
        1 << 20,
        60,
    )
    if direct:
        plan = packing
        first_column = gather_column(plan, first_block, devices)
        first_column, last_block = lax.optimization_barrier((first_column, last_block))
        first_plane = gather_plane(first_column, devices)
        last_column = gather_column(plan, last_block, devices)
        first_plane, last_column = lax.optimization_barrier((first_plane, last_column))
        first_pieces = gather_cores(first_plane, devices)
        last_plane = gather_plane(last_column, devices)
    else:
        plan = Plan(1, parts, width, tile, width, SLOTS * dp_size, False)

        def squares(array):
            return array.reshape(parts, width, width)

        def by_part(array):
            split = array.reshape(dp_size, mp_size, thin, width).transpose(1, 0, 2, 3)
            return squares(split)

        def one_tile(array):
            summed = jnp.sum(array.astype(F32), axis=0).astype(BF16)
            return jnp.pad(summed[None], ((0, parts - 1), (0, 0), (0, 0)))

        def normal(block):
            every = lax.all_gather(block, ("dp", "mp"))
            return jnp.concatenate(
                [
                    squares(every[:, :thin]),
                    by_part(every[:, thin : 2 * thin]),
                    by_part(every[:, 2 * thin : 3 * thin]),
                    one_tile(every[:, 3 * thin :]),
                ],
                axis=1,
            )

        first_pieces, last_pieces = [normal(first_block)], [normal(last_block)]

    flat = keep_rows.reshape(-1)
    slot = jnp.where(flat == 1, jnp.cumsum(flat) - flat, SLOTS).reshape(image_count, 1, rows)

    def mine(array):
        return jnp.concatenate(
            [lax.dynamic_slice_in_dim(array, rank, 1, 0), array[mp_size:]], axis=0
        )

    def padded(array):
        return jnp.pad(mine(array), ((0, 0), (0, rows - patch_rows), (0, 0)))

    kept = mine(keep_rows)
    stream = padded(patches).reshape(total, width)
    bias = jnp.where(kept == 1, 0.0, MASKED).astype(F32)[:, None, :]
    goal = jnp.where((kept == 1)[:, :, None], padded(targets), 0).reshape(total, width)
    slots = jnp.concatenate(
        [lax.dynamic_slice_in_dim(slot, rank ^ k, 1, 0) for k in range(mp_size)] + [slot[mp_size:]],
        axis=0,
    )

    stream, slots, goal = lax.optimization_barrier((stream, slots, goal))

    pairs = width // (2 * HD)
    stream_shape = ((total, width), F32)
    low_shape = ((total, width), BF16)
    pair_shape, low_pair_shape = ((2, total, width), F32), ((2, total, width), BF16)
    three_shape = ((3, total, width), BF16)
    turned_shape = ((width, total), BF16)
    vec_shape = ((tile, width), F32)
    attn_keep = [low_shape, three_shape, ((images, pairs, 2 * rows, rows), BF16), low_shape]
    hidden_keep = [low_shape, ((parts, total, width), BF16), ((parts, total, width), F32)]
    blocks = plan.outer * plan.inner
    weight_shape = ((blocks, plan.thin, width), BF16)
    zs = max(blocks // 8, 1)

    def vmem(shapes):
        return [pltpu.VMEM(shape, dtype) for shape, dtype in shapes]

    layer_flops = 8 * total * parts * width * width
    hidden_rows, attn_rows = 2 * plan.thin * zs, plan.thin * zs + tile

    def half(count):
        return ((2, 2, count, width), BF16)

    def both(count):
        return ((2, 2, 2, count, width), BF16)


    def forward(rows_in, pieces, out_shape):
        results = call(
            functools.partial(forward_kernel, plan, len(pieces)),
            (rows_in, bias, *pieces),
            [VMEM] * (2 + len(pieces)),
            [weight_shape, weight_shape, weight_shape, vec_shape, stream_shape, out_shape]
            + attn_keep
            + hidden_keep,
            [VMEM] * 13,
            vmem([pair_shape, stream_shape]),
            layer_flops,
        )
        return (*results[:6], results[6:10], results[10:])

    attn_full, up_full, down_full, vec, mid, middle, attn_kept, hidden_kept = forward(
        stream, first_pieces, stream_shape
    )
    if direct:
        middle, last_plane = lax.optimization_barrier((middle, last_plane))
        last_pieces = gather_cores(last_plane, devices)
    sems = [pltpu.SemaphoreType.DMA((4,))]
    last_attn, last_up, last_down, last_vec, last_mid, output, last_kept, last_hidden_kept = forward(
        middle, last_pieces, low_shape
    )
    last_mid_grad, last_gvec, *last_hidden = call(
        functools.partial(last_hidden_kernel, plan),
        (goal, last_mid, last_vec, last_up, last_down, *last_hidden_kept),
        [VMEM] * 8,
        [stream_shape, vec_shape, half(hidden_rows), half(hidden_rows)],
        [VMEM] * 2 + [ANY] * 2,
        vmem(
            [stream_shape, low_shape, low_pair_shape, stream_shape, pair_shape]
            + [turned_shape, turned_shape, both(hidden_rows)]
        )
        + sems,
        layer_flops,
    )
    across = flip(output[:rows], 2, devices)
    last_mid_grad, last_gvec, last_hidden, across, output = lax.optimization_barrier(
        (last_mid_grad, last_gvec, last_hidden, across, output)
    )
    grad_middle, *last_attention = call(
        functools.partial(last_attention_kernel, plan),
        (last_mid_grad, middle, last_vec, last_attn, last_gvec, *last_kept),
        [VMEM] * 9,
        [stream_shape, half(attn_rows), half(attn_rows)],
        [VMEM, ANY, ANY],
        vmem([vec_shape, low_shape, stream_shape, low_shape, three_shape, both(attn_rows)]) + sems,
        layer_flops,
    )
    output_pieces = [flip(output[:rows], 1, devices), across, flip(across, 1, devices)]
    if direct:
        terms = []
        for kept_half, sent_half in (last_hidden, last_attention):
            terms += [kept_half, flip(sent_half, 1, devices)]
        message = ((hidden_rows + attn_rows, width), BF16)
        last_sums = call(add_kernel, terms, [VMEM] * 4, [message] * 4, [VMEM] * 4, [], 1 << 20)
        grad_middle, last_sums, output_pieces = lax.optimization_barrier(
            (grad_middle, last_sums, output_pieces)
        )
    grad_first, *first_halves = call(
        functools.partial(back_kernel, plan),
        (grad_middle, stream, mid, vec, attn_full, up_full, down_full, *attn_kept, *hidden_kept),
        [VMEM] * 14,
        [low_shape, half(hidden_rows + attn_rows), half(hidden_rows + attn_rows)],
        [VMEM, ANY, ANY],
        vmem(
            [stream_shape, vec_shape, low_shape, low_pair_shape, low_shape, stream_shape, pair_shape]
            + [turned_shape, turned_shape, three_shape, both(hidden_rows + attn_rows)]
        )
        + sems,
        3 * layer_flops,
    )

    def pack_output(output, output_pieces):
        (activations,) = call(
            pack_kernel,
            (slots, output, *output_pieces),
            [VMEM] * (mp_size + 1),
            [((SLOTS, width), F32)],
            [VMEM],
            [],
            2 * SLOTS * image_count * rows * width,
        )
        return activations

    def place_grads(grad_first, grad_pieces):
        (input_grads,) = call(
            place_kernel,
            (grad_first, *grad_pieces),
            [VMEM] * mp_size,
            [((image_count, patch_rows, width), F32)],
            [VMEM],
            [],
            image_count * patch_rows * width,
        )
        return input_grads

    if direct:
        last_total = sum_plane(plan, last_sums, devices)
        activations = pack_output(output, output_pieces)
        last_total, first_halves, grad_first, activations = lax.optimization_barrier(
            (last_total, first_halves, grad_first, activations)
        )
        across = flip(grad_first[:rows], 2, devices)
        first_sums = sum_cores(*first_halves, devices)
        first_sums, last_total = lax.optimization_barrier((first_sums, last_total))
        first_total = sum_plane(plan, first_sums, devices)
        last_terms = sum_column(last_total, devices)
        beside = flip(grad_first[:rows], 1, devices)
        input_grads = place_grads(grad_first, [beside, across, flip(across, 1, devices)])
        first_total, last_terms, input_grads = lax.optimization_barrier(
            (first_total, last_terms, input_grads)
        )
        first_terms = sum_column(first_total, devices)
        terms = (*first_terms, *last_terms)
        turned = (layers, thin, width)
        attn_grads, vector_grads, up_grads, down_grads = call(
            functools.partial(finish_kernel, plan, len(first_terms)),
            terms,
            [VMEM] * len(terms),
            [(turned, F32), (vectors.shape, F32), (turned, F32), (turned, F32)],
            [VMEM] * 4,
            vmem([vec_shape, vec_shape]),
            1 << 20,
        )
        attn_grads, down_grads = attn_grads.transpose(0, 2, 1), down_grads.transpose(0, 2, 1)
    else:
        last_halves = [
            jnp.concatenate(halves, axis=2) for halves in zip(last_hidden, last_attention)
        ]

        def square_blocks(halves):
            stacked = jnp.stack(halves)[:, 0]
            stacked = jnp.stack([stacked[k % 2, k // 2] for k in range(parts)])
            return jnp.stack(
                [lax.dynamic_index_in_dim(stacked, rank ^ k, 0, False) for k in range(parts)]
            )

        def outputs_of(halves):
            def by_owner(array):
                split = array.reshape(mp_size, dp_size, thin, width).transpose(1, 0, 2, 3)
                return split.reshape(devices, thin, width)

            every = square_blocks(halves)
            pieces = [
                every[:, 2 * width : 3 * width].reshape(devices, thin, width),
                by_owner(every[:, :width]),
                by_owner(every[:, width : 2 * width]),
                jnp.broadcast_to(every[0, 3 * width :], (devices, tile, width)),
            ]
            owned = lax.psum_scatter(
                jnp.concatenate(pieces, axis=1), ("dp", "mp"), scatter_dimension=0, tiled=False
            ).astype(F32)
            own_vec = lax.dynamic_slice_in_dim(
                owned[3 * thin :].reshape(-1), device * vec_rows, vec_rows
            )
            return owned[:thin].T, own_vec, owned[thin : 2 * thin], owned[2 * thin : 3 * thin].T

        attn_grads, vector_grads, up_grads, down_grads = (
            jnp.stack([one, two]) for one, two in zip(outputs_of(first_halves), outputs_of(last_halves))
        )
        activations = pack_output(output, output_pieces)
        input_grads = place_grads(grad_first, spread(grad_first[:rows], devices))

    return (activations, input_grads, attn_grads, vector_grads, up_grads, down_grads)


def solution(mesh):
    in_specs = (
        P("dp", None, None),
        P("dp", None, None),
        P("dp", None),
        P(None, None, ("dp", "mp")),
        P(None, ("dp", "mp")),
        P(None, "dp", "mp"),
        P(None, "mp", "dp"),
    )
    out_specs = (
        P("dp", None),
        P("dp", None, None),
        P(None, None, ("dp", "mp")),
        P(None, ("dp", "mp")),
        P(None, "dp", "mp"),
        P(None, "mp", "dp"),
    )
    return jax.shard_map(shards, mesh=mesh, in_specs=in_specs, out_specs=out_specs, check_vma=False)
```

```python
import dataclasses
import functools

import jax
import jax.numpy as jnp
from jax import lax
from jax.experimental import pallas as pl
from jax.experimental.pallas import tpu as pltpu
from jax.sharding import PartitionSpec as P

HD = 64
SLOTS = 1024
EPSILON = 1e-06
MASKED = -1e30
STEP = 16

F32 = jnp.float32
BF16 = jnp.bfloat16


def dot_nn(left, right):
    return lax.dot_general(left, right, (((1,), (0,)), ((), ())), preferred_element_type=F32)


def dot_nt(left, right):
    return lax.dot_general(left, right, (((1,), (1,)), ((), ())), preferred_element_type=F32)


def dot_tn(left, right):
    return lax.dot_general(left, right, (((0,), (0,)), ((), ())), preferred_element_type=F32)


def block_rows(index, step):
    return pl.ds(pl.multiple_of(index * step, step), step)


def fold_rows(values):
    return jnp.sum(values.reshape(values.shape[0] // 8, 8, values.shape[1]), axis=0)


def low_halves(rows):
    lane = lax.broadcasted_iota(jnp.int32, (rows, 2 * HD), 1)
    return lane < HD


def stack_heads(pair):
    low = low_halves(pair.shape[0])
    zero = jnp.zeros_like(pair)
    return jnp.concatenate([jnp.where(low, pair, zero), jnp.where(low, zero, pair)], axis=0)


def unstack_heads(stacked):
    rows = stacked.shape[0] // 2
    return jnp.where(low_halves(rows), stacked[:rows], stacked[rows:])


def norm_rows(x_ref, out_ref, gain, shift):
    def body(index, carry):
        at = block_rows(index, STEP)
        values = x_ref[at, :].astype(F32)
        centred = values - jnp.mean(values, axis=-1, keepdims=True)
        variance = jnp.mean(centred * centred, axis=-1, keepdims=True)
        out_ref[at, :] = (centred * lax.rsqrt(variance + EPSILON) * gain + shift).astype(BF16)
        return carry

    lax.fori_loop(0, x_ref.shape[0] // STEP, body, 0, unroll=True)


def norm_back(x_ref, grad_ref, base_ref, out_ref, low_ref, gain, images):
    rows = x_ref.shape[0] // images
    width = x_ref.shape[1]
    sums = []
    for image in range(images):

        def body(index, carry, image=image):
            at = pl.ds(pl.multiple_of(image * rows + index * STEP, STEP), STEP)
            values = x_ref[at, :].astype(F32)
            grad = grad_ref[at, :]
            centred = values - jnp.mean(values, axis=-1, keepdims=True)
            variance = jnp.mean(centred * centred, axis=-1, keepdims=True)
            inverse = lax.rsqrt(variance + EPSILON)
            unit = centred * inverse
            scaled = grad * gain
            mean_one = jnp.mean(scaled, axis=-1, keepdims=True)
            mean_two = jnp.mean(scaled * unit, axis=-1, keepdims=True)
            out = base_ref[at, :] + inverse * (scaled - mean_one - unit * mean_two)
            out_ref[at, :] = out.astype(out_ref.dtype)
            if low_ref is not None:
                low_ref[at, :] = out.astype(BF16)
            return (
                carry[0] + fold_rows(grad * unit),
                carry[1] + fold_rows(grad),
                carry[2] + fold_rows(out),
            )

        zero = jnp.zeros((8, width), F32)
        sums.append(lax.fori_loop(0, rows // STEP, body, (zero, zero, zero), unroll=True))
    return sums


def weigh(sums, share):
    total = sums[0]
    for more in sums[1:]:
        total = total + more * share
    return jnp.sum(total, axis=0, keepdims=True)


def as_square(ref, part):
    rows, width = ref.shape[1:]
    per = width // rows
    return ref[pl.ds(part * per, per)].reshape(width, width)


def forward_attention(x_ref, bias_ref, vec_ref, attn_ref, keep, mid_ref):
    n1_ref, proj_ref, p_ref, att_ref = keep
    images = bias_ref.shape[0]
    rows = x_ref.shape[0] // images
    width = x_ref.shape[1]
    pairs = width // (2 * HD)
    scale = HD**-0.5

    norm_rows(x_ref, n1_ref, vec_ref[0:1, :], vec_ref[1:2, :])
    for part, bias_row in enumerate((4, None, 5)):
        value = dot_nt(n1_ref[...], as_square(attn_ref, part))
        if bias_row is not None:
            value = value + vec_ref[bias_row : bias_row + 1, :]
        proj_ref[part] = value.astype(BF16)

    def image_body(image, carry):
        at = block_rows(image, rows)
        for pair in range(pairs):
            lanes = slice(pair * 2 * HD, (pair + 1) * 2 * HD)
            query = stack_heads(proj_ref[0, at, lanes])
            scores = dot_nt(query, proj_ref[1, at, lanes]) * scale + bias_ref[image]
            top = jnp.max(scores, axis=-1, keepdims=True)
            powers = jnp.exp(scores - top)
            total = jnp.sum(powers, axis=-1, keepdims=True)
            probs = (powers * (1.0 / total)).astype(BF16)
            p_ref[image, pair] = probs
            att_ref[at, lanes] = unstack_heads(dot_nn(probs, proj_ref[2, at, lanes])).astype(BF16)
        return carry

    for image in range(images):
        image_body(image, 0)
    mid_ref[...] = x_ref[...].astype(F32) + dot_nt(att_ref[...], as_square(attn_ref, 3)) + vec_ref[6:7, :]


def forward_hidden(mid_ref, vec_ref, up_ref, down_ref, keep, scratch, out_ref):
    n2_ref, a_ref, gp_ref = keep
    h_ref, acc_ref = scratch
    norm_rows(mid_ref, n2_ref, vec_ref[2:3, :], vec_ref[3:4, :])
    acc_ref[...] = mid_ref[...] + vec_ref[11:12, :]

    def part_body(part, carry):
        h_ref[part % 2] = dot_nn(n2_ref[...], as_square(up_ref, part))
        bias = vec_ref[pl.ds(7 + part, 1), :]

        def gelu_body(index, inner):
            at = block_rows(index, STEP)
            hidden = h_ref[part % 2, at, :] + bias
            share = 0.5 + 0.5 * lax.erf(hidden * 0.7071067811865476)
            a_ref[part, at, :] = (hidden * share).astype(BF16)
            bell = jnp.exp(-0.5 * hidden * hidden) * 0.3989422804014327
            gp_ref[part, at, :] = (share + hidden * bell).astype(gp_ref.dtype)
            return inner

        lax.fori_loop(0, h_ref.shape[1] // STEP, gelu_body, 0, unroll=True)
        acc_ref[...] += dot_nt(a_ref[part], as_square(down_ref, part))
        return carry

    for part in range(a_ref.shape[0]):
        part_body(part, 0)
    out_ref[...] = acc_ref[...].astype(out_ref.dtype)


def drop_shared(refs):
    @pl.when(jnp.logical_not(counts_shared()))
    def _():
        for ref in refs:
            rows = ref.shape[-2] // 2
            ref[..., rows:, :] = jnp.zeros((*ref.shape[:-2], rows, ref.shape[-1]), ref.dtype)


def backward_hidden(g_ref, mid_ref, vec_ref, up_ref, down_ref, share, keep, scratch, gm_ref, gvec_ref, store):
    n2_ref, a_ref, gp_ref = keep
    go_ref, gh_ref, acc_ref, h_ref, got_ref, n2t_ref = scratch
    images = 2
    rows = mid_ref.shape[0] // images
    width = mid_ref.shape[1]
    zero = jnp.zeros((8, width), F32)
    sums = []
    for image in range(images):

        def low_body(index, carry, image=image):
            at = pl.ds(pl.multiple_of(image * rows + index * STEP, STEP), STEP)
            grad = g_ref[at, :]
            go_ref[at, :] = grad.astype(BF16)
            return carry + fold_rows(grad)

        sums.append(lax.fori_loop(0, rows // STEP, low_body, zero, unroll=True))
    gvec_ref[11:12, :] = weigh(sums, share)
    acc_ref[...] = jnp.zeros_like(acc_ref)
    got_ref[...] = go_ref[...].T
    n2t_ref[...] = n2_ref[...].T

    def part_body(part, carry):
        store(2, part, dot_nn(got_ref[...], a_ref[part]))
        h_ref[part % 2] = dot_nn(go_ref[...], as_square(down_ref, part))
        inner_sums = []
        for image in range(images):

            def hidden_body(index, inner, image=image):
                at = pl.ds(pl.multiple_of(image * rows + index * STEP, STEP), STEP)
                grad = (h_ref[part % 2, at, :] * gp_ref[part, at, :].astype(F32)).astype(BF16)
                gh_ref[part % 2, at, :] = grad
                return inner + fold_rows(grad.astype(F32))

            inner_sums.append(lax.fori_loop(0, rows // STEP, hidden_body, zero, unroll=True))
        gvec_ref[pl.ds(7 + part, 1), :] = weigh(inner_sums, share)
        store(1, part, dot_nn(n2t_ref[...], gh_ref[part % 2]))
        acc_ref[...] += dot_nt(gh_ref[part % 2], as_square(up_ref, part))
        return carry

    for part in range(a_ref.shape[0]):
        part_body(part, 0)
    sums = norm_back(mid_ref, acc_ref, g_ref, gm_ref, None, vec_ref[2:3, :], images)
    for place, row in enumerate((2, 3, 6)):
        gvec_ref[row : row + 1, :] = weigh([one[place] for one in sums], share)


def backward_attention(gm_ref, x_ref, vec_ref, attn_ref, share, keep, scratch, gx_ref, gvec_ref, store):
    n1_ref, proj_ref, p_ref, att_ref = keep
    go_ref, acc_ref, ga_ref, dproj_ref = scratch
    images = p_ref.shape[0]
    rows = x_ref.shape[0] // images
    width = x_ref.shape[1]
    pairs = width // (2 * HD)
    scale = HD**-0.5
    go_ref[...] = gm_ref[...].astype(BF16)
    store(0, 3, dot_tn(go_ref[...], att_ref[...]))
    ga_ref[...] = dot_nn(go_ref[...], as_square(attn_ref, 3)).astype(BF16)

    def image_body(image, carry):
        at = block_rows(image, rows)
        for pair in range(pairs):
            lanes = slice(pair * 2 * HD, (pair + 1) * 2 * HD)
            query = stack_heads(proj_ref[0, at, lanes])
            keys = proj_ref[1, at, lanes]
            grad_out = stack_heads(ga_ref[at, lanes])
            probs = p_ref[image, pair]
            grad_probs = dot_nt(grad_out, proj_ref[2, at, lanes])
            dproj_ref[2, at, lanes] = dot_tn(probs, grad_out).astype(BF16)
            wide = probs.astype(F32)
            inner = jnp.sum(grad_probs * wide, axis=-1, keepdims=True)
            grad_scores = (wide * (grad_probs - inner)).astype(BF16)
            dproj_ref[0, at, lanes] = (unstack_heads(dot_nn(grad_scores, keys)) * scale).astype(BF16)
            dproj_ref[1, at, lanes] = (dot_tn(grad_scores, query) * scale).astype(BF16)
        return carry

    for image in range(images):
        image_body(image, 0)
    for part, row in enumerate((4, None, 5)):
        store(0, part, dot_tn(dproj_ref[part], n1_ref[...]))
        value = dot_nn(dproj_ref[part], as_square(attn_ref, part))
        if part == 0:
            acc_ref[...] = value
        else:
            acc_ref[...] += value
        if row is not None:
            sums = [
                fold_rows(dproj_ref[part, image * rows : (image + 1) * rows, :].astype(F32))
                for image in range(images)
            ]
            gvec_ref[row : row + 1, :] = weigh(sums, share)
    sums = norm_back(x_ref, acc_ref, gm_ref, gx_ref, None, vec_ref[0:1, :], images)
    for place, row in enumerate((0, 1)):
        gvec_ref[row : row + 1, :] = weigh([one[place] for one in sums], share)
    store(3, 0, gvec_ref[...])


def coordinates(plan):
    outer, inner = lax.axis_index("dp"), lax.axis_index("mp")
    here = (inner // 2, inner % 2)
    return (outer // 2, outer % 2, *here) if plan.direct else (0, 0, *here)


def counts_shared():
    return lax.axis_index("mp") == 0


def place_weights(plan, pieces, attn_ref, up_ref, down_ref, vec_ref):
    thin, rows = plan.thin, 3 * plan.thin

    def put(owner, block):
        at = owner % plan.inner * plan.outer + owner // plan.inner
        attn_ref[owner] = block[:thin]
        up_ref[at] = block[thin : 2 * thin]
        down_ref[at] = block[2 * thin : 3 * thin]

    if not plan.direct:
        for owner in range(plan.inner):
            put(owner, pieces[0][owner, :rows])
        vec_ref[...] = pieces[0][0, rows:].astype(F32)
        return
    at = coordinates(plan)
    vec = None
    for i, piece in enumerate(pieces):
        c, x, y = i % 2, i // 2 % 2, i // 4
        low = ((at[1] ^ y) * 2 + (at[2] ^ x)) * 2 + (at[3] ^ c)
        count = piece.shape[0] // rows
        for k in range(count):
            put((at[0] ^ k) * 8 + low, piece[k * rows : (k + 1) * rows])
        tail = piece[count * rows :].astype(F32)
        vec = tail if vec is None else vec + tail
    vec_ref[...] = vec


def storer(plan, packed_ref, kinds):
    thin, width = plan.thin, plan.width
    per = width // thin
    here = coordinates(plan)

    def put(owner, kind, block):
        c, x, y = owner % 2, owner // 2 % 2, owner // 4 % 2
        row = pl.multiple_of((kinds.index(kind) * plan.zs + owner // 8) * thin, thin)
        packed_ref[c ^ here[3], y ^ here[1], x ^ here[2], pl.ds(row, thin), :] = block

    def store(kind, part, value):
        low = value.astype(BF16)
        if kind == 3:
            for i in range(8):
                packed_ref[i % 2, i // 4, i // 2 % 2, len(kinds) * plan.zs * thin :, :] = low
            return
        blocks = low.reshape(per, thin, width)
        for i in range(per):
            owner = part * per + i if kind == 0 else i * plan.inner + part
            put(owner, kind, blocks[i])

    return store


def start_copies(packed_ref, outs, sems, start, count, before=()):
    at = pl.ds(start, count)
    copies = list(before)
    for i in range(2):
        source, target = packed_ref.at[i, :, :, at], outs[i].at[:, :, at]
        copies.append(pltpu.make_async_copy(source, target, sems.at[len(copies)]))
        copies[-1].start()
    return copies


def wait_all(copies):
    for one in copies:
        one.wait()


def prepare_kernel(plan, attn_ref, up_ref, down_ref, vec_in, keep_in, first_ref, last_ref, line_ref, vec_ref, keep_ref, sems):
    thin, tile, width = plan.thin, plan.tile, plan.width
    outs = (first_ref, last_ref)
    copies = [
        pltpu.make_async_copy(vec_in, vec_ref, sems.at[0]),
        pltpu.make_async_copy(keep_in, keep_ref, sems.at[1]),
    ]
    for kind, ref in enumerate((attn_ref, up_ref, down_ref)):
        for layer, out_ref in enumerate(outs):
            if plan.direct:
                target = out_ref.at[pl.ds(kind * thin, thin)]
                copies.append(pltpu.make_async_copy(ref.at[layer], target, sems.at[len(copies)]))
            else:
                out_ref[kind * thin : (kind + 1) * thin, :] = ref[layer]
    for one in copies:
        one.start()
    count = vec_ref.shape[1]
    device = lax.axis_index("dp") * plan.inner + lax.axis_index("mp")
    row_at = device * count // width
    offset = device * count - row_at * width
    copies[0].wait()
    copies[1].wait()
    kept = jnp.sum(keep_ref[...]) + 2 * keep_ref.shape[0]
    kept = jnp.where(counts_shared(), kept, 0)
    row = lax.broadcasted_iota(jnp.int32, (tile, width), 0)
    here = lax.broadcasted_iota(jnp.int32, (tile, width), 1) == lax.axis_index("dp")
    for layer, out_ref in enumerate(outs):
        line_ref[...] = jnp.zeros_like(line_ref)
        line_ref[0:1, 0:count] = vec_ref[layer : layer + 1, :].astype(F32)
        moved = pltpu.roll(line_ref[...], offset, 1)[0:1]
        piece = jnp.where(row == row_at, moved[:, :width], 0.0)
        piece = jnp.where(row == row_at + 1, moved[:, width:], piece)
        if layer == 1:
            piece = jnp.where(here & (row == 12), (kept >> 5).astype(F32), piece)
            piece = jnp.where(here & (row == 13), (kept & 31).astype(F32), piece)
        out_ref[3 * thin :, :] = piece.astype(BF16)
    for one in copies[2:]:
        one.wait()


def forward_kernel(plan, pieces, x_ref, bias_ref, *refs):
    sources, refs = refs[:pieces], refs[pieces:]
    attn_ref, up_ref, down_ref, vec_ref, mid_ref, out_ref, *refs = refs
    attn_keep, hidden_keep, (h_ref, acc_ref) = refs[:4], refs[4:7], refs[7:]
    place_weights(plan, sources, attn_ref, up_ref, down_ref, vec_ref)
    forward_attention(x_ref, bias_ref, vec_ref, attn_ref, attn_keep, mid_ref)
    forward_hidden(mid_ref, vec_ref, up_ref, down_ref, hidden_keep, (h_ref, acc_ref), out_ref)
    drop_shared((attn_keep[0], attn_keep[3], hidden_keep[0], hidden_keep[1]))


HIDDEN_KINDS, ATTENTION_KINDS, ALL_KINDS = (1, 2), (0,), (1, 2, 0)


def last_hidden_kernel(plan, goal_ref, mid_ref, vec_ref, up_ref, down_ref, *refs):
    keep, gm_ref, gvec_ref, outs, refs = refs[:3], refs[3], refs[4], refs[5:7], refs[7:]
    g_ref, go_ref, gh_ref, acc_ref, h_ref, got_ref, n2t_ref, packed_ref, sems = refs
    high = jnp.sum(vec_ref[12:13, :], axis=-1, keepdims=True)
    rest = jnp.sum(vec_ref[13:14, :], axis=-1, keepdims=True)
    loss_scale = float(plan.slots) / (high * 32.0 + rest)
    g_ref[...] = goal_ref[...].astype(F32) * loss_scale
    gvec_ref[...] = jnp.zeros_like(gvec_ref)
    share = counts_shared().astype(F32)
    store = storer(plan, packed_ref, HIDDEN_KINDS)
    scratch = (go_ref, gh_ref, acc_ref, h_ref, got_ref, n2t_ref)
    backward_hidden(g_ref, mid_ref, vec_ref, up_ref, down_ref, share, keep, scratch, gm_ref, gvec_ref, store)
    wait_all(start_copies(packed_ref, outs, sems, 0, packed_ref.shape[3]))


def last_attention_kernel(plan, gm_ref, x_ref, vec_ref, attn_ref, early_ref, *refs):
    keep, gx_ref, outs, refs = refs[:4], refs[4], refs[5:7], refs[7:]
    gvec_ref, go_ref, acc_ref, ga_ref, dproj_ref, packed_ref, sems = refs
    gvec_ref[...] = early_ref[...]
    share = counts_shared().astype(F32)
    store = storer(plan, packed_ref, ATTENTION_KINDS)
    scratch = (go_ref, acc_ref, ga_ref, dproj_ref)
    backward_attention(gm_ref, x_ref, vec_ref, attn_ref, share, keep, scratch, gx_ref, gvec_ref, store)
    wait_all(start_copies(packed_ref, outs, sems, 0, packed_ref.shape[3]))


def back_kernel(plan, g_ref, x_ref, mid_ref, vec_ref, attn_ref, up_ref, down_ref, *refs):
    attn_keep, hidden_keep, gx_ref, outs, refs = refs[:4], refs[4:7], refs[7], refs[8:10], refs[10:]
    gm_ref, gvec_ref, go_ref, gh_ref, ga_ref, acc_ref, h_ref, got_ref, n2t_ref, dproj_ref, packed_ref, sems = refs
    gvec_ref[...] = jnp.zeros_like(gvec_ref)
    share = counts_shared().astype(F32)
    store = storer(plan, packed_ref, ALL_KINDS)
    scratch = (go_ref, gh_ref, acc_ref, h_ref, got_ref, n2t_ref)
    backward_hidden(g_ref, mid_ref, vec_ref, up_ref, down_ref, share, hidden_keep, scratch, gm_ref, gvec_ref, store)
    hidden_rows = 2 * plan.zs * plan.thin
    copies = start_copies(packed_ref, outs, sems, 0, hidden_rows)
    scratch = (go_ref, acc_ref, ga_ref, dproj_ref)
    backward_attention(gm_ref, x_ref, vec_ref, attn_ref, share, attn_keep, scratch, gx_ref, gvec_ref, store)
    rest = packed_ref.shape[3] - hidden_rows
    wait_all(start_copies(packed_ref, outs, sems, hidden_rows, rest, copies))


def add_kernel(kept_hidden, got_hidden, kept_attn, got_attn, *out_refs):
    count = kept_hidden.shape[2]
    for i, out_ref in enumerate(out_refs):
        at = (i // 2, i % 2)
        total = kept_hidden[at].astype(F32) + got_hidden[at].astype(F32)
        out_ref[0:count, :] = total.astype(BF16)
        total = kept_attn[at].astype(F32) + got_attn[at].astype(F32)
        out_ref[count:, :] = total.astype(BF16)


def finish_kernel(plan, *refs):
    late, early = refs[0], refs[1 : 1 + plan.zs]
    attn_out, vec_out, up_out, down_out, *tiles = refs[1 + plan.zs :]
    thin, tile, width = plan.thin, plan.tile, plan.width

    count = vec_out.shape[1]
    device = lax.axis_index("dp") * plan.inner + lax.axis_index("mp")
    row = device * count // width
    offset = device * count - row * width
    for layer in range(2):

        def total(start, count, layer=layer):
            at = slice(start, start + count)
            blocks = [early[k][at, :] if layer == 0 else late[k, at, :] for k in range(plan.zs)]
            return sum(block.astype(F32) for block in blocks)

        attn_out[layer] = total(0, thin)
        up_out[layer] = total(thin, thin)
        down_out[layer] = total(2 * thin, thin)
        tiles[layer][...] = total(3 * thin, tile)
        both = jnp.concatenate(
            [tiles[layer][pl.ds(row, 1), :], tiles[layer][pl.ds(row + 1, 1), :]], axis=1
        )
        both = jnp.broadcast_to(both, (8, 2 * width))
        moved = pltpu.roll(both, 2 * width - offset, 1)
        vec_out[layer : layer + 1, :] = moved[0:1, :count]


def place_kernel(own_ref, *refs):
    others, out_ref = refs[:-1], refs[-1]
    rows = own_ref.shape[0] // 2
    kept = out_ref.shape[1]
    mine = lax.axis_index("mp")
    out_ref[mine] = own_ref[0:rows, :].astype(F32)[:kept]
    for i, ref in enumerate(others):
        out_ref[mine ^ (i + 1)] = ref[...].astype(F32)[:kept]
    out_ref[out_ref.shape[0] - 1] = own_ref[rows : 2 * rows, :].astype(F32)[:kept]


def pack_kernel(slot_ref, own_ref, *refs):
    others, out_ref = refs[:-1], refs[-1]
    rows = own_ref.shape[0] // 2
    sources = [own_ref[0:rows, :]] + [ref[...] for ref in others] + [own_ref[rows : 2 * rows, :]]
    step = 256

    def body(index, carry):
        slots = lax.broadcasted_iota(jnp.int32, (step, rows), 0) + index * step
        total = None
        for i, values in enumerate(sources):
            picks = jnp.where(slots == slot_ref[i], 1.0, 0.0).astype(BF16)
            term = dot_nn(picks, values)
            total = term if total is None else total + term
        out_ref[block_rows(index, step), :] = total
        return carry

    lax.fori_loop(0, out_ref.shape[0] // step, body, 0)


VMEM = pl.BlockSpec(memory_space=pltpu.VMEM)
ANY = pl.BlockSpec(memory_space=pl.ANY)


def call(kernel, operands, specs, outs, out_specs, scratch, flops, limit=26):
    return pl.pallas_call(
        kernel,
        out_shape=[jax.ShapeDtypeStruct(shape, dtype) for shape, dtype in outs],
        in_specs=specs,
        out_specs=out_specs,
        scratch_shapes=scratch,
        compiler_params=pltpu.CompilerParams(vmem_limit_bytes=limit << 20),
        cost_estimate=pl.CostEstimate(flops=flops, bytes_accessed=8 << 20, transcendentals=0),
    )(*operands)


@dataclasses.dataclass(frozen=True)
class Plan:
    outer: int
    inner: int
    thin: int
    tile: int
    width: int
    slots: int
    direct: bool

    @property
    def zs(self):
        return self.outer // 2 if self.direct else 1


def flip(array, mask, devices):
    return lax.ppermute(array, ("dp", "mp"), [(d, d ^ mask) for d in range(devices)])


def column_kernel(plan, *refs):
    blocks, out_ref = refs[:-1], refs[-1]
    rows = 3 * plan.thin
    for k, ref in enumerate(blocks):
        out_ref[k * rows : (k + 1) * rows, :] = ref[0:rows, :]
    tail = sum(ref[rows:, :].astype(F32) for ref in blocks)
    out_ref[len(blocks) * rows :, :] = tail.astype(BF16)


def gather_column(plan, block, devices):
    blocks = [block] + [flip(block, 8 * k, devices) for k in range(1, devices // 8)]
    shape = (len(blocks) * 3 * plan.thin + plan.tile, plan.width)
    (column,) = call(
        functools.partial(column_kernel, plan), blocks, [VMEM] * len(blocks), [(shape, BF16)], [VMEM], [], 1 << 20
    )
    return column


def gather_plane(column, devices):
    return [column] + [flip(column, mask, devices) for mask in (2, 4, 6)]


def gather_cores(plane, devices):
    pieces = []
    for piece in plane:
        pieces += [piece, flip(piece, 1, devices)]
    return pieces


def spread(rows, devices):
    across = flip(rows, 2, devices)
    return [flip(rows, 1, devices), across, flip(across, 1, devices)]


def sum_cores(kept, sent, devices):
    got = flip(sent, 1, devices)
    return [(kept[i // 2, i % 2].astype(F32) + got[i // 2, i % 2].astype(F32)).astype(BF16) for i in range(4)]


def plane_kernel(plan, counts, *refs):
    terms, out_refs = [], refs[sum(counts) :]
    for k in range(len(counts)):
        start = sum(counts[:k])
        terms.append(refs[start : start + counts[k]])
    thin, tile = plan.thin, plan.tile
    zs, scratch = plan.zs, out_refs[-1]
    rows = scratch.shape[0]
    total = None
    for parts in terms:
        whole = jnp.concatenate([ref[...].astype(F32) for ref in parts], axis=0)
        total = whole if total is None else total + whole
    scratch[...] = total
    tail = scratch[rows - tile :, :].astype(BF16)
    one = len(out_refs) == 2
    for z in range(zs):
        for kind in range(3):
            at = z if one else coordinates(plan)[0] ^ z
            row = pl.multiple_of((ALL_KINDS.index(kind) * zs + at) * thin, thin)
            block = scratch[pl.ds(row, thin), :].astype(BF16)
            if one:
                out_refs[0][z, kind * thin : (kind + 1) * thin, :] = block
            else:
                out_refs[z][kind * thin : (kind + 1) * thin, :] = block
        if one:
            out_refs[0][z, 3 * thin :, :] = tail
        else:
            out_refs[z][3 * thin :, :] = tail


def sum_plane(plan, sums, devices, relayed):
    rows = sums[0].shape[0]
    if relayed:
        half = rows // 2 // 16 * 16
        own, x_sum, y_sum, both = sums
        x_first, y_first = flip(both[:half], 2, devices), flip(both[half:], 4, devices)

        def joined(one, two):
            return (one.astype(F32) + two.astype(F32)).astype(BF16)

        x_two, y_one = joined(x_sum[half:], y_first), joined(y_sum[:half], x_first)
        x_parts = [flip(x_sum[:half], 2, devices), flip(x_two, 2, devices)]
        y_parts = [flip(y_one, 4, devices), flip(y_sum[half:], 4, devices)]
        terms, counts = [own, *x_parts, *y_parts], (1, 2, 2)
    else:
        terms = [sums[0]] + [flip(one, mask, devices) for one, mask in zip(sums[1:], (2, 4, 6))]
        counts = (1, 1, 1, 1)
    shape = (3 * plan.thin + plan.tile, plan.width)
    outs = [(shape, BF16)] * plan.zs if relayed else [((plan.zs, *shape), BF16)]
    return call(
        functools.partial(plane_kernel, plan, counts),
        terms,
        [VMEM] * len(terms),
        outs,
        [VMEM] * len(outs),
        [pltpu.VMEM((rows, plan.width), F32)],
        1 << 20,
    )


def sum_column(blocks, devices):
    return [one if k == 0 else flip(one, 8 * k, devices) for k, one in enumerate(blocks)]


def shards(patches, targets, keep_mask, attn_weights, vectors, up_weights, down_weights):
    image_count, patch_rows, width = patches.shape
    layers = attn_weights.shape[0]
    dp_size, mp_size = lax.axis_size("dp"), lax.axis_size("mp")
    devices = dp_size * mp_size
    rank = lax.axis_index("mp")
    lane_rank = lax.axis_index("dp")
    device = lane_rank * mp_size + rank
    thin = attn_weights.shape[2]
    vec_rows = vectors.shape[1]
    parts = thin * devices // width
    assert image_count == mp_size + 1 and layers == 2 and parts == mp_size == 4
    direct = thin % 16 == 0
    images, tile = 2, 16
    rows = -(-patch_rows // 16) * 16
    total = images * rows

    keep_rows = jnp.concatenate([jnp.ones((image_count, 2), jnp.int32), keep_mask], axis=1)
    keep_rows = jnp.pad(keep_rows, ((0, 0), (0, rows - patch_rows)))

    attn_turned = attn_weights.transpose(0, 2, 1)
    down_turned = down_weights.transpose(0, 2, 1)
    packing = Plan(dp_size, mp_size, thin, tile, width, SLOTS * dp_size, direct)
    block_shape = ((3 * thin + tile, width), BF16)
    first_block, last_block = call(
        functools.partial(prepare_kernel, packing),
        (attn_turned, up_weights, down_turned, vectors, keep_mask),
        [ANY if direct else VMEM] * 3 + [ANY] * 2,
        [block_shape, block_shape],
        [VMEM, VMEM],
        [
            pltpu.VMEM((8, 2 * width), F32),
            pltpu.VMEM(vectors.shape, BF16),
            pltpu.VMEM(keep_mask.shape, jnp.int32),
            pltpu.SemaphoreType.DMA((8,)),
        ],
        1 << 20,
        60,
    )
    if direct:
        plan = packing
        first_column = gather_column(plan, first_block, devices)
        first_column, last_block = lax.optimization_barrier((first_column, last_block))
        first_plane = gather_plane(first_column, devices)
        last_column = gather_column(plan, last_block, devices)
        first_plane, last_column = lax.optimization_barrier((first_plane, last_column))
        first_pieces = gather_cores(first_plane, devices)
        last_plane = gather_plane(last_column, devices)
    else:
        plan = Plan(1, parts, width, tile, width, SLOTS * dp_size, False)

        def squares(array):
            return array.reshape(parts, width, width)

        def by_part(array):
            split = array.reshape(dp_size, mp_size, thin, width).transpose(1, 0, 2, 3)
            return squares(split)

        def one_tile(array):
            summed = jnp.sum(array.astype(F32), axis=0).astype(BF16)
            return jnp.pad(summed[None], ((0, parts - 1), (0, 0), (0, 0)))

        def normal(block):
            every = lax.all_gather(block, ("dp", "mp"))
            return jnp.concatenate(
                [
                    squares(every[:, :thin]),
                    by_part(every[:, thin : 2 * thin]),
                    by_part(every[:, 2 * thin : 3 * thin]),
                    one_tile(every[:, 3 * thin :]),
                ],
                axis=1,
            )

        first_pieces, last_pieces = [normal(first_block)], [normal(last_block)]

    flat = keep_rows.reshape(-1)
    slot = jnp.where(flat == 1, jnp.cumsum(flat) - flat, SLOTS).reshape(image_count, 1, rows)

    def mine(array):
        return jnp.concatenate(
            [lax.dynamic_slice_in_dim(array, rank, 1, 0), array[mp_size:]], axis=0
        )

    def padded(array):
        return jnp.pad(mine(array), ((0, 0), (0, rows - patch_rows), (0, 0)))

    kept = mine(keep_rows)
    stream = padded(patches).reshape(total, width)
    bias = jnp.where(kept == 1, 0.0, MASKED).astype(F32)[:, None, :]
    goal = jnp.where((kept == 1)[:, :, None], padded(targets), 0).reshape(total, width)
    slots = jnp.concatenate(
        [lax.dynamic_slice_in_dim(slot, rank ^ k, 1, 0) for k in range(mp_size)] + [slot[mp_size:]],
        axis=0,
    )

    stream, slots, goal = lax.optimization_barrier((stream, slots, goal))

    pairs = width // (2 * HD)
    stream_shape = ((total, width), F32)
    low_shape = ((total, width), BF16)
    pair_shape, low_pair_shape = ((2, total, width), F32), ((2, total, width), BF16)
    three_shape = ((3, total, width), BF16)
    turned_shape = ((width, total), BF16)
    vec_shape = ((tile, width), F32)
    attn_keep = [low_shape, three_shape, ((images, pairs, 2 * rows, rows), BF16), low_shape]
    hidden_keep = [low_shape, ((parts, total, width), BF16), ((parts, total, width), F32)]
    blocks = plan.outer * plan.inner
    weight_shape = ((blocks, plan.thin, width), BF16)
    zs = max(blocks // 8, 1)

    def vmem(shapes):
        return [pltpu.VMEM(shape, dtype) for shape, dtype in shapes]

    layer_flops = 8 * total * parts * width * width
    hidden_rows, attn_rows = 2 * plan.thin * zs, plan.thin * zs + tile

    def half(count):
        return ((2, 2, count, width), BF16)

    def both(count):
        return ((2, 2, 2, count, width), BF16)


    def forward(rows_in, pieces, out_shape):
        results = call(
            functools.partial(forward_kernel, plan, len(pieces)),
            (rows_in, bias, *pieces),
            [VMEM] * (2 + len(pieces)),
            [weight_shape, weight_shape, weight_shape, vec_shape, stream_shape, out_shape]
            + attn_keep
            + hidden_keep,
            [VMEM] * 13,
            vmem([pair_shape, stream_shape]),
            layer_flops,
        )
        return (*results[:6], results[6:10], results[10:])

    attn_full, up_full, down_full, vec, mid, middle, attn_kept, hidden_kept = forward(
        stream, first_pieces, stream_shape
    )
    if direct:
        middle, last_plane = lax.optimization_barrier((middle, last_plane))
        last_pieces = gather_cores(last_plane, devices)
    sems = [pltpu.SemaphoreType.DMA((4,))]
    last_attn, last_up, last_down, last_vec, last_mid, output, last_kept, last_hidden_kept = forward(
        middle, last_pieces, low_shape
    )
    last_mid_grad, last_gvec, *last_hidden = call(
        functools.partial(last_hidden_kernel, plan),
        (goal, last_mid, last_vec, last_up, last_down, *last_hidden_kept),
        [VMEM] * 8,
        [stream_shape, vec_shape, half(hidden_rows), half(hidden_rows)],
        [VMEM] * 2 + [ANY] * 2,
        vmem(
            [stream_shape, low_shape, low_pair_shape, stream_shape, pair_shape]
            + [turned_shape, turned_shape, both(hidden_rows)]
        )
        + sems,
        layer_flops,
    )
    across = flip(output[:rows], 2, devices)
    last_mid_grad, last_gvec, last_hidden, across, output = lax.optimization_barrier(
        (last_mid_grad, last_gvec, last_hidden, across, output)
    )
    grad_middle, *last_attention = call(
        functools.partial(last_attention_kernel, plan),
        (last_mid_grad, middle, last_vec, last_attn, last_gvec, *last_kept),
        [VMEM] * 9,
        [stream_shape, half(attn_rows), half(attn_rows)],
        [VMEM, ANY, ANY],
        vmem([vec_shape, low_shape, stream_shape, low_shape, three_shape, both(attn_rows)]) + sems,
        layer_flops,
    )
    output_pieces = [flip(output[:rows], 1, devices), across, flip(across, 1, devices)]
    if direct:
        terms = []
        for kept_half, sent_half in (last_hidden, last_attention):
            terms += [kept_half, flip(sent_half, 1, devices)]
        message = ((hidden_rows + attn_rows, width), BF16)
        last_sums = call(add_kernel, terms, [VMEM] * 4, [message] * 4, [VMEM] * 4, [], 1 << 20)
        grad_middle, last_sums, output_pieces = lax.optimization_barrier(
            (grad_middle, last_sums, output_pieces)
        )
    grad_first, *first_halves = call(
        functools.partial(back_kernel, plan),
        (grad_middle, stream, mid, vec, attn_full, up_full, down_full, *attn_kept, *hidden_kept),
        [VMEM] * 14,
        [low_shape, half(hidden_rows + attn_rows), half(hidden_rows + attn_rows)],
        [VMEM, ANY, ANY],
        vmem(
            [stream_shape, vec_shape, low_shape, low_pair_shape, low_shape, stream_shape, pair_shape]
            + [turned_shape, turned_shape, three_shape, both(hidden_rows + attn_rows)]
        )
        + sems,
        3 * layer_flops,
    )

    def pack_output(output, output_pieces):
        (activations,) = call(
            pack_kernel,
            (slots, output, *output_pieces),
            [VMEM] * (mp_size + 1),
            [((SLOTS, width), F32)],
            [VMEM],
            [],
            2 * SLOTS * image_count * rows * width,
        )
        return activations

    def place_grads(grad_first, grad_pieces):
        (input_grads,) = call(
            place_kernel,
            (grad_first, *grad_pieces),
            [VMEM] * mp_size,
            [((image_count, patch_rows, width), F32)],
            [VMEM],
            [],
            image_count * patch_rows * width,
        )
        return input_grads

    if direct:
        (last_total,) = sum_plane(plan, last_sums, devices, False)
        activations = pack_output(output, output_pieces)
        last_total, first_halves, grad_first, activations = lax.optimization_barrier(
            (last_total, first_halves, grad_first, activations)
        )
        last_terms = last_total
        if plan.zs > 1:
            columns = [[8 * z + at for z in range(plan.zs)] for at in range(8)]
            last_terms = lax.all_to_all(
                last_total, ("dp", "mp"), 0, 0, axis_index_groups=columns, tiled=True
            )
        across = flip(grad_first[:rows], 2, devices)
        first_sums = sum_cores(*first_halves, devices)
        first_sums, across, grad_first = lax.optimization_barrier((first_sums, across, grad_first))
        first_total = sum_plane(plan, first_sums, devices, True)
        beside = flip(grad_first[:rows], 1, devices)
        input_grads = place_grads(grad_first, [beside, across, flip(across, 1, devices)])
        first_total, last_terms, input_grads = lax.optimization_barrier(
            (first_total, last_terms, input_grads)
        )
        first_terms = sum_column(first_total, devices)
        terms = (last_terms, *first_terms)
        turned = (layers, thin, width)
        attn_grads, vector_grads, up_grads, down_grads = call(
            functools.partial(finish_kernel, plan),
            terms,
            [VMEM] * len(terms),
            [(turned, F32), (vectors.shape, F32), (turned, F32), (turned, F32)],
            [VMEM] * 4,
            vmem([vec_shape, vec_shape]),
            1 << 20,
        )
        attn_grads, down_grads = attn_grads.transpose(0, 2, 1), down_grads.transpose(0, 2, 1)
    else:
        last_halves = [
            jnp.concatenate(halves, axis=2) for halves in zip(last_hidden, last_attention)
        ]

        def square_blocks(halves):
            stacked = jnp.stack(halves)[:, 0]
            stacked = jnp.stack([stacked[k % 2, k // 2] for k in range(parts)])
            return jnp.stack(
                [lax.dynamic_index_in_dim(stacked, rank ^ k, 0, False) for k in range(parts)]
            )

        def outputs_of(halves):
            def by_owner(array):
                split = array.reshape(mp_size, dp_size, thin, width).transpose(1, 0, 2, 3)
                return split.reshape(devices, thin, width)

            every = square_blocks(halves)
            pieces = [
                every[:, 2 * width : 3 * width].reshape(devices, thin, width),
                by_owner(every[:, :width]),
                by_owner(every[:, width : 2 * width]),
                jnp.broadcast_to(every[0, 3 * width :], (devices, tile, width)),
            ]
            owned = lax.psum_scatter(
                jnp.concatenate(pieces, axis=1), ("dp", "mp"), scatter_dimension=0, tiled=False
            ).astype(F32)
            own_vec = lax.dynamic_slice_in_dim(
                owned[3 * thin :].reshape(-1), device * vec_rows, vec_rows
            )
            return owned[:thin].T, own_vec, owned[thin : 2 * thin], owned[2 * thin : 3 * thin].T

        attn_grads, vector_grads, up_grads, down_grads = (
            jnp.stack([one, two]) for one, two in zip(outputs_of(first_halves), outputs_of(last_halves))
        )
        activations = pack_output(output, output_pieces)
        input_grads = place_grads(grad_first, spread(grad_first[:rows], devices))

    return (activations, input_grads, attn_grads, vector_grads, up_grads, down_grads)


def solution(mesh):
    in_specs = (
        P("dp", None, None),
        P("dp", None, None),
        P("dp", None),
        P(None, None, ("dp", "mp")),
        P(None, ("dp", "mp")),
        P(None, "dp", "mp"),
        P(None, "mp", "dp"),
    )
    out_specs = (
        P("dp", None),
        P("dp", None, None),
        P(None, None, ("dp", "mp")),
        P(None, ("dp", "mp")),
        P(None, "dp", "mp"),
        P(None, "mp", "dp"),
    )
    return jax.shard_map(shards, mesh=mesh, in_specs=in_specs, out_specs=out_specs, check_vma=False)
```
